32 devices in a mesh: lon: 4 (over y, x), lat: 8 (over z, core).
Axes of the slice: x: 2, y: 2, z: 4, core: 2. Of those that a mesh axis runs over, the one named last changes fastest.
Arguments:
- tracers: float32 [2, 16, 256, 512], P(None, None, 'lat', 'lon'), may hold values from -6 to 6
- velocity: float32 [2, 16, 256, 512], P(None, None, 'lat', 'lon'), may hold values from -3 to 3
- land_mask: int32 [256, 512], P('lat', 'lon'), may hold values 0 or 1
- mixing: float32 [256, 512], P('lat', 'lon'), may hold values from 0.05 to 0.25
- owners: int32 [1024, 1], P(('lon', 'lat')), may hold values from 0 to 31; in each aligned block of 32 rows (0 to 31, 32 to 63, ...) at most 2 rows name the same one
- atm_row: int32 [1024], P(('lon', 'lat')), may hold values from 0 to 31
Outputs:
- tracers_out: float32 [2, 16, 256, 512], P(None, None, 'lat', 'lon')
- velocity_out: float32 [2, 16, 256, 512], P(None, None, 'lat', 'lon')
- atm_surface: float32 [4, 1024, 128], P(None, ('lon', 'lat'))
- atm_cover: float32 [1024, 128], P(('lon', 'lat'))
The draws below stay inside these ranges and needn't reach their ends.
Inputs may be any that keep to these rules, and one draw needn't show every extreme that they name: `owners`: among the 32 blocks of one device at most 2 name the same owner, and in every draw some owner is named by exactly 2 blocks of some device.
All inputs are finite; a program needn't handle non-finite values. No bound on the sum of `land_mask` on one device may be relied on, other than what follows from the above.
Results may differ from the reference program's by a relative error of at most 0.00007.
Values sent between devices are 32-bit elements; how exact they have to be, the bound alone decides.
No kernel may reach another device: no remote copies, remote signals or barrier semaphores. Data moves between devices by JAX's collectives and lax.ppermute only.
A program may use at most 64 MiB of HBM per device.

```python
import math
import jax
import jax.numpy as jnp
import numpy as np

CX = 128
CY = 32
KZ = 16
STEPS = 2
ATM_ROWS = 32
NX = 512
NY = 256
NB = 32
NBT = 1024
CAP = 2
N_LON = 4
N_LAT = 8


def set_ends(drawn, stream_key, least, top_value):
    place = [jax.random.randint(jax.random.fold_in(stream_key, axis), (), 0, length) for axis, length in enumerate(drawn.shape)]
    longest = drawn.shape.index(max(drawn.shape))
    next_to = place[:longest] + [(place[longest] + 1) % drawn.shape[longest]] + place[longest + 1:]
    return drawn.at[tuple(place)].set(least).at[tuple(next_to)].set(top_value)


def steps_of(own_key, dims, pieces, smallest, top_value):
    def one(axis_at, parts):
        heights = jax.random.uniform(jax.random.fold_in(jax.random.fold_in(own_key, 6), axis_at), (parts,), jnp.float32, smallest / len(pieces), top_value / len(pieces))
        return jnp.repeat(jnp.exp(heights), dims[axis_at] // parts).reshape((-1,) + (1,) * (len(dims) - axis_at - 1))

    factor_of = one(*pieces[0])
    for cut in pieces[1:]:
        factor_of = factor_of * one(*cut)
    return factor_of


def shared_out(rng, own, number, rows, number_of, top, reach, slope):
    order = jax.random.permutation(rng, number_of)
    heavy_load, common = shares(number_of, rows * top, reach, slope, True), shares(number_of, rows * top, reach, slope, False)
    places = jnp.arange(number_of)

    def named(sizes, offset_by):
        used = int((sizes > 0).sum())
        fixed = max(1, used // 4)
        passed = fixed + (places - fixed + offset_by * (used - fixed)) % max(1, number_of - fixed)
        return jnp.zeros((number_of,), jnp.int32).at[order[jnp.where(places < fixed, places, passed)]].set(jnp.asarray(sizes, jnp.int32))

    sizes = jnp.where(number % 4 == 0, named(heavy_load, number // 4), named(common, number - number // 4 - 1))
    mixed = jax.random.permutation(jax.random.fold_in(own, 3), number_of)
    giver, taker = mixed[0:number_of // 2 * 2:2], mixed[1:number_of // 2 * 2:2]
    margin = jnp.minimum(sizes[giver] - 1, reach - sizes[taker]) // 2
    margin = jnp.where((giver == order[0]) | (taker == order[0]) | (sizes[taker] == 0), 0, jnp.maximum(margin, 0))
    passed = jax.random.randint(jax.random.fold_in(own, 4), (number_of // 2,), 0, 1 << 20) % (margin + 1)
    sizes = sizes.at[giver].add(-passed).at[taker].add(passed)
    items = jnp.searchsorted(jnp.cumsum(sizes), jnp.arange(rows * top), side="right").astype(jnp.int32)
    table = items.reshape(top, rows).T
    table = table[jax.random.permutation(jax.random.fold_in(own, 1), rows)]
    offset_by = jax.random.randint(jax.random.fold_in(own, 2), (rows, 1), 0, top)
    return jnp.take_along_axis(table, (jnp.arange(top)[None, :] + offset_by) % top, axis=1)


def shares(number_of, total, bound, lean, full):
    weights = [(1 << 20) // math.isqrt(grade ** lean) + 1 for grade in range(1, number_of + 1)]
    largest = bound if full else min(bound, max(-(-total // number_of), total * weights[0] // sum(weights)))
    least = 1 if total - largest >= number_of - 1 else 0
    holding, spare = [largest] + [least] * (number_of - 1), total - largest - least * (number_of - 1)
    while spare > 0:
        movable = [i for i in range(1, number_of) if holding[i] < largest] or [i for i in range(1, number_of) if holding[i] < bound]
        whole, remaining = sum([weights[i] for i in movable]), spare
        for i in movable:
            more = min(bound - holding[i], max(1, remaining * weights[i] // whole), spare)
            holding[i] = holding[i] + more
            spare = spare - more
    return np.array(holding)


def scatter_about(stream_key, extent, spread, reach, cuts=(), held_as=jnp.bfloat16):
    gain = steps_of(stream_key, extent, cuts, -0.22, 0.18) if cuts else 1.0
    result = jax.random.normal(stream_key, extent, jnp.float32) * spread * gain
    return jnp.minimum(jnp.maximum(result, -reach), reach).astype(held_as)


def setup_inputs(seed: int = 0) -> dict:
    key_list = jax.random.split(jax.random.key(seed), 7)
    tracers = scatter_about(key_list[0], (2, KZ, NY, NX), 1.0, 6.0, ((2, 8), (3, 4)), jnp.float32)
    velocity = scatter_about(key_list[1], (2, KZ, NY, NX), 0.5, 3.0, ((2, 8), (3, 4)), jnp.float32)
    land_mask = set_ends((jax.random.randint(key_list[2], (NY, NX), 0, 4) < 3).astype(jnp.int32), jax.random.fold_in(key_list[2], 1), 0, 1)
    mixing = jnp.clip(jnp.exp(math.log(0.25) - 1.609438 * jax.random.uniform(key_list[3], (NY, NX), jnp.float32) ** steps_of(key_list[3], (NY, NX), ((0, 8), (1, 4)), -0.2, 0.2)), 0.05, 0.25)
    owners_keys = jax.random.split(jax.random.fold_in(key_list[4], 1), NBT // NB)
    owners_turns = jax.random.permutation(jax.random.fold_in(key_list[4], 3), NBT // NB)
    owners = jax.vmap(lambda own, number: shared_out(jax.random.fold_in(key_list[4], 2), own, number, NB, N_LON * N_LAT, 1, CAP, 2))(owners_keys, owners_turns).reshape((NBT, 1))
    atm_row = set_ends(jax.random.randint(key_list[5], (NBT,), 0, ATM_ROWS), jax.random.fold_in(key_list[5], 1), 0, ATM_ROWS - 1).astype(jnp.int32)
    return dict(tracers=tracers, velocity=velocity, land_mask=land_mask, mixing=mixing, owners=owners, atm_row=atm_row)


THERMAL = 0.2
HALINE = 0.15
GRAVITY = 0.2
TIMESTEP = 0.8
VERTICAL_MIX = 0.1
VISCOSITY = 0.2
CORIOLIS_MAX = 0.3


def split_state(stacked):
    levels = (stacked.shape[0] - 1) // 4
    return stacked[:-1].reshape(4, levels, stacked.shape[1], stacked.shape[2]), stacked[-1]


def pressure(fields):
    density = HALINE * fields[1] - THERMAL * fields[0]
    return GRAVITY * (jnp.cumsum(density, axis=0) - 0.5 * density)


def coriolis_table(latitude, total_rows):
    return CORIOLIS_MAX * jnp.sin(math.pi * (-0.43 + 0.93 * (latitude + 0.5) / total_rows))


def advance(center, east_side, west_side, north_side, south_side, diffusivity, coriolis):
    fields, wet_mask = split_state(center)
    fields_east, wet_east = split_state(east_side)
    fields_west, wet_west = split_state(west_side)
    fields_north, wet_north = split_state(north_side)
    fields_south, wet_south = split_state(south_side)
    laplace = wet_east * (fields_east - fields) + wet_west * (fields_west - fields)
    laplace = laplace + wet_north * (fields_north - fields) + wet_south * (fields_south - fields)
    zonal_vel = fields[2]
    merid_vel = fields[3]
    advect = 0.5 * (zonal_vel * (fields_east - fields_west) + merid_vel * (fields_north - fields_south))
    level_above = jnp.concatenate([fields[:, :1], fields[:, :-1]], axis=1)
    level_below = jnp.concatenate([fields[:, 1:], fields[:, -1:]], axis=1)
    vertical = level_above + level_below - 2.0 * fields
    grad_east = 0.5 * (pressure(fields_east) - pressure(fields_west))
    grad_north = 0.5 * (pressure(fields_north) - pressure(fields_south))
    tend_temp = -advect[0] + diffusivity * laplace[0] + VERTICAL_MIX * vertical[0]
    tend_salt = -advect[1] + diffusivity * laplace[1] + VERTICAL_MIX * vertical[1]
    tend_zonal = -advect[2] + coriolis * merid_vel - grad_east + VISCOSITY * laplace[2] + VERTICAL_MIX * vertical[2]
    tend_merid = -advect[3] - coriolis * zonal_vel - grad_north + VISCOSITY * laplace[3] + VERTICAL_MIX * vertical[3]
    tendency = jnp.stack([tend_temp, tend_salt, tend_zonal, tend_merid])
    updated = wet_mask * (fields + TIMESTEP * tendency)
    return jnp.concatenate([updated.reshape(-1, center.shape[1], center.shape[2]), wet_mask[None]], axis=0)


def initial_state(tracers, velocity, wet_mask):
    levels = tracers.shape[1]
    rows_here, cols_here = wet_mask.shape
    return jnp.concatenate([(tracers * wet_mask).reshape(2 * levels, rows_here, cols_here),
                            (velocity * wet_mask).reshape(2 * levels, rows_here, cols_here),
                            wet_mask[None]], axis=0)


def fold_signs(levels):
    return jnp.concatenate([jnp.ones((2 * levels,), jnp.float32), -jnp.ones((2 * levels,), jnp.float32),
                            jnp.ones((1,), jnp.float32)])[:, None]


def reference(tracers, velocity, land_mask, mixing, owners, atm_row):
    wet_mask = land_mask.astype(jnp.float32)
    levels = tracers.shape[1]
    rows_total, cols_total = land_mask.shape
    stacked = initial_state(tracers, velocity, wet_mask)
    sign_rows = fold_signs(levels)
    coriolis = coriolis_table(jnp.arange(rows_total).astype(jnp.float32), rows_total)[:, None]
    for step_index in range(STEPS):
        fold_row = sign_rows * stacked[:, -1, ::-1]
        north_side = jnp.concatenate([stacked[:, 1:], fold_row[:, None]], axis=1)
        south_side = jnp.concatenate([jnp.zeros_like(stacked[:, :1]), stacked[:, :-1]], axis=1)
        east_side = jnp.roll(stacked, -1, axis=2)
        west_side = jnp.roll(stacked, 1, axis=2)
        stacked = advance(stacked, east_side, west_side, north_side, south_side, mixing, coriolis)
    fields = stacked[:-1].reshape(4, levels, rows_total, cols_total)
    surface = jnp.concatenate([fields[:, 0], wet_mask[None]], axis=0)
    blocks = surface.reshape(5, N_LAT, CY, N_LON, CX // 128, 128).transpose(3, 1, 2, 4, 0, 5).reshape(-1, 5, 128)
    segment_key = owners[:, 0] * ATM_ROWS + atm_row
    totals = jax.ops.segment_sum(blocks, segment_key, num_segments=N_LON * N_LAT * ATM_ROWS)
    ocean_count = totals[:, 4]
    atm_surface = (totals[:, :4] / jnp.maximum(ocean_count, 1.0)[:, None]).transpose(1, 0, 2)
    return fields[:2], fields[2:], atm_surface, ocean_count
```

```python
import functools
import math

import jax
import jax.numpy as jnp
from jax import lax
from jax.experimental import pallas as pl
from jax.experimental.pallas import tpu as pltpu
from jax.sharding import PartitionSpec as P

ATM_ROWS = 32
CAP = 2

THERMAL = 0.2
HALINE = 0.15
GRAVITY = 0.2
TIMESTEP = 0.8
VERTICAL_MIX = 0.1
VISCOSITY = 0.2
CORIOLIS_MAX = 0.3

LANES = 128
PAD = 8
EXACT = lax.Precision.HIGHEST
F32 = jnp.float32
VMEM_LIMIT = 48 * 1024 * 1024


def iota(shape, dim):
    return lax.broadcasted_iota(jnp.int32, shape, dim)


def dot(a, b, dims=(((1,), (0,)), ((), ()))):
    return lax.dot_general(a, b, dims, precision=EXACT, preferred_element_type=F32)


def is_lower():
    return lax.axis_index("lon") < lax.axis_size("lon") // 2


def pack_kernel(rows, fields, devices, tr, ve, mask, mix, own, arow, east, west, up, down, info):
    half = fields // 2
    wet = mask[...].astype(F32)
    lane = iota((rows, LANES), 1)
    pair = lane >> 1

    def columns(ref, base, carry):
        def body(f, carry):
            to_east, to_west = carry
            x = ref[pl.ds(pl.multiple_of(f * rows, rows), rows), :] * wet
            keep = pair == base + f
            low = 2 * (base + f)
            to_east = jnp.where(keep, pltpu.roll(x, (low + 2) & (LANES - 1), 1), to_east)
            to_west = jnp.where(keep, pltpu.roll(x, low, 1), to_west)
            return to_east, to_west

        return lax.fori_loop(0, half, body, carry, unroll=8)

    zero = jnp.zeros((rows, LANES), F32)
    to_east, to_west = columns(ve, half, columns(tr, 0, (zero, zero)))
    east[0:rows, :] = to_east
    west[0:rows, :] = to_west
    mixing = mix[...]
    east[rows : 2 * rows, :] = jnp.where(
        lane == 0,
        pltpu.roll(wet, 1, 1),
        jnp.where(lane == 1, pltpu.roll(wet, 3, 1), pltpu.roll(mixing, 3, 1)),
    )
    west[rows : 2 * rows, :] = jnp.where(lane <= 1, wet, pltpu.roll(mixing, 2, 1))

    lower = is_lower()
    top, bottom = (rows - 1, rows - 2), (0, 1)
    for buf, first, second in ((up, top, bottom), (down, bottom, top)):
        near = jnp.where(lower, first[0], second[0])
        far = jnp.where(lower, first[1], second[1])
        for place, line in ((0, near), (fields, far)):
            row_wet = mask[pl.ds(line, 1), :].astype(F32)
            buf[place : place + half, :] = tr[pl.ds(line, half, stride=rows), :] * row_wet
            buf[place + half : place + fields, :] = ve[pl.ds(line, half, stride=rows), :] * row_wet
        buf[2 * fields : 2 * fields + 8, :] = jnp.zeros((8, LANES), F32)
        buf[2 * fields : 2 * fields + 1, :] = mask[pl.ds(near, 1), :].astype(F32)
        buf[2 * fields + 1 : 2 * fields + 2, :] = mask[pl.ds(far, 1), :].astype(F32)
        buf[2 * fields + 2 : 2 * fields + 3, :] = mix[pl.ds(near, 1), :]

    blocks = own.shape[1]
    info[0:rows, :] = mask[...]
    info[rows : rows + 8, :] = jnp.zeros((8, LANES), jnp.int32)
    info[rows : rows + 1, 0:blocks] = own[...]
    info[rows + 1 : rows + 2, 0:blocks] = arow[...]


def corner_kernel(rows, up_in, down_in, from_east, from_west, up, down):
    lower = is_lower()
    lane = iota((1, LANES), 1)
    for src, dst, first, second in ((up_in, up, rows - 1, 0), (down_in, down, 0, rows - 1)):
        near = jnp.where(lower, first, second)
        dst[...] = src[...]
        dst[3:4, :] = jnp.where(
            (lane & 1) == 0, from_east[pl.ds(near, 1), :], from_west[pl.ds(near, 1), :]
        )
        wet_east = from_east[pl.ds(rows + near, 1), :]
        wet_west = from_west[pl.ds(rows + near, 1), :]
        dst[4:5, :] = jnp.where(
            lane == 0,
            jnp.broadcast_to(wet_east[:, 0:1], (1, LANES)),
            jnp.broadcast_to(wet_west[:, 0:1], (1, LANES)),
        )


def level_matrix(kind, levels, source, target):
    if kind == "mix":
        above = (source == jnp.maximum(target - 1, 0)).astype(F32)
        below = (source == jnp.minimum(target + 1, levels - 1)).astype(F32)
        return above + below - 2.0 * (source == target).astype(F32)
    full = jnp.where(source < target, 1.0, jnp.where(source == target, 0.5, 0.0))
    return (0.5 * GRAVITY) * full


def density_weight(group):
    return jnp.where(group == 0, -THERMAL, jnp.where(group == 1, HALINE, 0.0)).astype(F32)


def advance_columns(levels, mid, outer, inner, corner_n, corner_s, wets, mixing, coriolis):
    rows = mid.shape[0]
    wet_mid, wet_out, wet_in, wet_corner_n, wet_corner_s = wets
    lane = iota((rows, LANES), 1)
    row = iota((rows, LANES), 0)
    even = (lane & 1) == 0
    group = lane // (2 * levels)

    def sides(outside, inside):
        return jnp.where(even, outside, inside), jnp.where(even, inside, outside)

    def shifted(x, north, south):
        n = jnp.where(row == rows - 1, north, pltpu.roll(x, rows - 1, 0))
        s = jnp.where(row == 0, south, pltpu.roll(x, 1, 0))
        return n, s

    e, w = sides(outer, inner)
    wet_e, wet_w = sides(wet_out, wet_in)
    n, s = shifted(mid, corner_n, corner_s)
    wet_n, wet_s = shifted(wet_mid, wet_corner_n, wet_corner_s)
    lap = wet_e * (e - mid) + wet_w * (w - mid) + wet_n * (n - mid) + wet_s * (s - mid)
    de, dn = e - w, n - s
    span = 2 * levels
    one, two, three = (pltpu.roll(mid, i * span, 1) for i in (1, 2, 3))

    def pick(a, b, c, d):
        return jnp.where(group == 0, a, jnp.where(group == 1, b, jnp.where(group == 2, c, d)))

    u = pick(two, three, mid, one)
    v = pick(one, two, three, mid)
    adv = 0.5 * (u * de + v * dn)
    src, dst = iota((LANES, LANES), 0), iota((LANES, LANES), 1)
    src_group, dst_group = src // span, dst // span
    src_level, dst_level = (src // 2) % levels, (dst // 2) % levels
    same_side = (src & 1) == (dst & 1)
    mix_map = jnp.where(
        same_side & (src_group == dst_group), level_matrix("mix", levels, src_level, dst_level), 0.0
    )
    press = level_matrix("pressure", levels, src_level, dst_level) * density_weight(src_group)
    press_x = jnp.where(same_side & (dst_group == 2), press, 0.0)
    press_y = jnp.where(same_side & (dst_group == 3), press, 0.0)
    vertical = dot(mid, mix_map)
    grad = dot(de, press_x) + dot(dn, press_y)
    zero = jnp.zeros_like(mid)
    turn = pick(zero, zero, coriolis * v, -coriolis * u)
    kappa = jnp.where(group < 2, mixing, VISCOSITY)
    tend = turn - adv - grad + kappa * lap + VERTICAL_MIX * vertical
    return wet_mid * (mid + TIMESTEP * tend)


def advance_row(levels, north_side, mid, outer, inner, corner_e, corner_w, wets, mixing, coriolis):
    fields = mid.shape[0]
    wet_mid, wet_out, wet_in, wet_corner_e, wet_corner_w = wets
    lane = iota((fields, LANES), 1)
    lane8 = iota((8, LANES), 1)

    def sides(x, east, west, at):
        e = jnp.where(at == LANES - 1, east, pltpu.roll(x, LANES - 1, 1))
        w = jnp.where(at == 0, west, pltpu.roll(x, 1, 1))
        return e, w

    e, w = sides(mid, corner_e, corner_w, lane)
    wet_e, wet_w = sides(
        jnp.broadcast_to(wet_mid, (8, LANES)), wet_corner_e, wet_corner_w, lane8
    )
    wet_e, wet_w = wet_e[0:1], wet_w[0:1]
    n, s = (outer, inner) if north_side else (inner, outer)
    wet_n, wet_s = (wet_out, wet_in) if north_side else (wet_in, wet_out)
    lap = wet_e * (e - mid) + wet_w * (w - mid) + wet_n * (n - mid) + wet_s * (s - mid)
    de, dn = e - w, n - s
    u, v = mid[2 * levels : 3 * levels], mid[3 * levels :]
    adv = 0.5 * (jnp.concatenate([u] * 4, axis=0) * de + jnp.concatenate([v] * 4, axis=0) * dn)
    dst, src = iota((fields, fields), 0), iota((fields, fields), 1)
    mix_map = jnp.where(
        dst // levels == src // levels, level_matrix("mix", levels, src % levels, dst % levels), 0.0
    )
    dst, src = iota((levels, fields), 0), iota((levels, fields), 1)
    press = level_matrix("pressure", levels, src % levels, dst) * density_weight(src // levels)
    vertical = dot(mix_map, mid)
    zero = jnp.zeros((2 * levels, LANES), F32)
    turn = jnp.concatenate(
        [zero, coriolis * v - dot(press, de), -coriolis * u - dot(press, dn)], axis=0
    )
    kappa = jnp.concatenate(
        [jnp.broadcast_to(mixing, (2 * levels, LANES)), jnp.full((2 * levels, LANES), VISCOSITY)],
        axis=0,
    )
    tend = turn - adv + kappa * lap + VERTICAL_MIX * vertical
    return wet_mid * (mid + TIMESTEP * tend)


def advance_level(k, count, levels, rows, src, sides, wets, mixing, coriolis, acc):
    pitch = rows + 2 * PAD
    wet, wet_e, wet_w, wet_n, wet_s = wets
    lane = iota((rows, LANES), 1)
    first, last = lane == 0, lane == LANES - 1
    above_k = jnp.maximum(k - 1, 0)
    below_k = jnp.minimum(k + 1, levels - 1)

    def load(q, level, shift):
        return src[pl.ds((q * count + level) * pitch + PAD + shift, rows), :]

    center, lap, de, dn, vertical = [], [], [], [], []
    for q in range(4):
        c = load(q, k, 0)
        n, s = load(q, k, 1), load(q, k, -1)
        edge = pltpu.roll(sides, (LANES - 1 - 2 * (q * levels + k)) & (LANES - 1), 1)
        e = jnp.where(last, edge, pltpu.roll(c, LANES - 1, 1))
        w = jnp.where(first, edge, pltpu.roll(c, 1, 1))
        center.append(c)
        lap.append(wet_e * (e - c) + wet_w * (w - c) + wet_n * (n - c) + wet_s * (s - c))
        de.append(e - w)
        dn.append(n - s)
        vertical.append(load(q, above_k, 0) + load(q, below_k, 0) - 2.0 * c)
    u, v = center[2], center[3]
    dens_x = HALINE * de[1] - THERMAL * de[0]
    dens_y = HALINE * dn[1] - THERMAL * dn[0]
    acc_x, acc_y = acc
    grad_x = (0.5 * GRAVITY) * (acc_x + 0.5 * dens_x)
    grad_y = (0.5 * GRAVITY) * (acc_y + 0.5 * dens_y)
    extra = (None, None, coriolis * v - grad_x, -coriolis * u - grad_y)
    new = []
    for q in range(4):
        tend = (mixing if q < 2 else VISCOSITY) * lap[q] - 0.5 * (u * de[q] + v * dn[q])
        tend = tend + VERTICAL_MIX * vertical[q]
        if extra[q] is not None:
            tend = tend + extra[q]
        new.append(wet * (center[q] + TIMESTEP * tend))
    return new, (acc_x + dens_x, acc_y + dens_y)


class Halo:
    def __init__(self, rows, fields):
        at = 0
        for name, size in (
            ("side0", rows), ("side1", rows), ("north0", fields), ("south0", fields),
            ("north1", fields), ("south1", fields), ("wet_e", rows), ("wet_w", rows),
            ("wet_n", rows), ("wet_s", rows), ("coriolis", rows),
        ):
            setattr(self, name, slice(at, at + size))
            at += size
        self.size = at


def surface_kernel(
    rows, levels, lat_count,
    tr, ve, mask, mix, east, west, from_east, from_west, from_up, from_down, up, down, own,
    halo, out, now, later, wet_pad, stage,
):
    fields = 4 * levels
    at = Halo(rows, fields)
    lat = lax.axis_index("lat")
    lower = is_lower()
    fold = lat == lat_count - 1
    wet = mask[...].astype(F32)
    mixing = mix[...]
    lane = iota((rows, LANES), 1)
    even = (lane & 1) == 0

    latitude = lat * rows - PAD + iota((rows + 2 * PAD, LANES), 0)
    total = lat_count * rows
    latitude = jnp.where(latitude >= total, 2 * total - 1 - latitude, latitude).astype(F32)
    table = CORIOLIS_MAX * jnp.sin(math.pi * (-0.43 + 0.93 * (latitude + 0.5) / total))
    coriolis = table[PAD : PAD + rows]

    got_up, got_down = from_up[...], from_down[...]
    north, south = jnp.where(lower, got_down, got_up), jnp.where(lower, got_up, got_down)
    length = 2 * fields + 8
    back = jnp.broadcast_to(LANES - 1 - iota((8, LANES), 1), (8, LANES))
    flipped = jnp.concatenate(
        [
            jnp.take_along_axis(north[i : i + 8], back, axis=1)
            * (-1.0 if i < 2 * fields and i % fields >= fields // 2 else 1.0)
            for i in range(0, length, 8)
        ],
        axis=0,
    )
    straight = north
    north = jnp.where(fold, flipped, straight)
    lane1 = iota((1, LANES), 1)
    even1 = (lane1 & 1) == 0
    tail_n, tail_s = straight[2 * fields :], south[2 * fields :]
    swapped = jnp.where(
        iota((8, LANES), 1) & 1 == 0, pltpu.roll(tail_n, LANES - 1, 1), pltpu.roll(tail_n, 1, 1)
    )
    sign = jnp.where(lane1 >= LANES // 2, -1.0, 1.0)
    corner_n = jnp.where(fold, swapped[3:4] * sign, tail_n[3:4])
    corner_s = tail_s[3:4]
    wet_corner_n = jnp.where(fold, swapped[4:5], tail_n[4:5])
    wet_corner_s = tail_s[4:5]

    def corner_wet(x):
        east_wet = jnp.broadcast_to(x[:, 0:1], (1, LANES))
        west_wet = jnp.broadcast_to(x[:, 1:2], (1, LANES))
        return east_wet, west_wet, jnp.where(even1, east_wet, west_wet)

    wet_ne, wet_nw, wet_n_lanes = corner_wet(wet_corner_n)
    wet_se, wet_sw, wet_s_lanes = corner_wet(wet_corner_s)

    north_rows = (north[0:fields], north[fields : 2 * fields], north[2 * fields :])
    south_rows = (south[0:fields], south[fields : 2 * fields], south[2 * fields :])
    halo[at.north0] = north_rows[0]
    halo[at.south0] = south_rows[0]

    wet_pad[PAD : PAD + rows, :] = wet
    wet_pad[PAD - 1 : PAD, :] = south_rows[2][0:1]
    wet_pad[PAD + rows : PAD + rows + 1, :] = north_rows[2][0:1]
    wet_n = wet_pad[PAD + 1 : PAD + 1 + rows, :]
    wet_s = wet_pad[PAD - 1 : PAD - 1 + rows, :]

    def spread(x, i):
        return jnp.broadcast_to(x[:, i : i + 1], (rows, LANES))

    aux_e, aux_w = from_east[rows:, :], from_west[rows:, :]
    wet_col_e, wet_col_w = spread(aux_e, 0), spread(aux_w, 0)
    wet_e = jnp.where(lane == LANES - 1, wet_col_e, pltpu.roll(wet, LANES - 1, 1))
    wet_w = jnp.where(lane == 0, wet_col_w, pltpu.roll(wet, 1, 1))
    halo[at.wet_e] = wet_e
    halo[at.wet_w] = wet_w
    halo[at.wet_n] = wet_n
    halo[at.wet_s] = wet_s
    halo[at.coriolis] = coriolis

    got_e, got_w = from_east[0:rows, :], from_west[0:rows, :]
    side = jnp.where(even, got_e, got_w)
    outer = jnp.where(even, pltpu.roll(got_e, LANES - 1, 1), pltpu.roll(got_w, 1, 1))
    inner = jnp.where(
        even, pltpu.roll(east[0:rows, :], LANES - 1, 1), pltpu.roll(west[0:rows, :], 1, 1)
    )
    halo[at.side0] = side
    side_new = advance_columns(
        levels, side, outer, inner, corner_n, corner_s,
        (
            jnp.where(even, wet_col_e, wet_col_w),
            jnp.where(even, spread(aux_e, 1), spread(aux_w, 1)),
            jnp.where(even, spread(wet, LANES - 1), spread(wet, 0)),
            wet_n_lanes,
            wet_s_lanes,
        ),
        jnp.where(even, spread(aux_e, 2), spread(aux_w, 2)),
        coriolis,
    )
    halo[at.side1] = side_new

    field_lane = iota((fields, LANES), 1)
    field_id = iota((fields, LANES), 0)

    def to_sublanes(x, parity):
        here = field_lane == 2 * field_id + parity
        return jnp.sum(jnp.where(here, x, 0.0), axis=1, keepdims=True)

    own_up, own_down = up[...], down[...]
    for north_side, (mid, outside, tail), inside, corner, corner_wets, line, lat_row, place in (
        (
            True, north_rows, jnp.where(lower, own_up, own_down), corner_n, (wet_ne, wet_nw),
            rows - 1, PAD + rows, at.north1,
        ),
        (
            False, south_rows, jnp.where(lower, own_down, own_up), corner_s, (wet_se, wet_sw),
            0, PAD - 1, at.south1,
        ),
    ):
        halo[place] = advance_row(
            levels, north_side, mid, outside, inside,
            to_sublanes(corner, 0), to_sublanes(corner, 1),
            (tail[0:1], tail[1:2], wet[line : line + 1], *corner_wets),
            tail[2:3], table[lat_row : lat_row + 1],
        )

    count = now.shape[0] // (4 * (rows + 2 * PAD))
    pitch = rows + 2 * PAD
    for q in range(4):
        ref = tr if q < 2 else ve
        for k in range(count):
            base = (q * count + k) * pitch
            field = q * levels + k
            now[base + PAD : base + PAD + rows, :] = ref[q % 2, k * rows : (k + 1) * rows, :] * wet
            for buf, north_at, south_at in (
                (now, at.north0, at.south0),
                (later, at.north1, at.south1),
            ):
                n, s = north_at.start + field, south_at.start + field
                buf[base + PAD + rows : base + PAD + rows + 1, :] = halo[n : n + 1, :]
                buf[base + PAD - 1 : base + PAD, :] = halo[s : s + 1, :]
    wets = (wet, wet_e, wet_w, wet_n, wet_s)
    none = jnp.zeros((rows, LANES), F32)
    acc = (none, none)
    for k in range(count - 1):
        new, acc = advance_level(
            k, count, levels, rows, now, side, wets, mixing, coriolis, acc
        )
        for q in range(4):
            base = (q * count + k) * pitch + PAD
            later[base : base + rows, :] = new[q]
    new, _ = advance_level(
        0, count, levels, rows, later, side_new, wets, mixing, coriolis, (none, none)
    )
    for q in range(4):
        stage[pl.ds(q, rows, stride=4), :] = new[q]

    out[...] = jnp.zeros(out.shape, F32)
    for r in range(rows):
        place = pl.multiple_of(own[r] * (4 * CAP), 4 * CAP)
        out[pl.ds(place, 4), :] = stage[4 * r : 4 * r + 4, :]
    for r in reversed(range(rows)):
        place = pl.multiple_of(own[r] * (4 * CAP), 4 * CAP)
        out[pl.ds(place + 4, 4), :] = stage[4 * r : 4 * r + 4, :]


def main_kernel(
    rows, levels, devices, tr, ve, mask, mix, halo, info, tr_out, ve_out, slots, cover, now, later
):
    fields = 4 * levels
    half = fields // 2
    pitch = rows + 2 * PAD
    at = Halo(rows, fields)
    wet = mask[...].astype(F32)
    mixing = mix[...]
    wets = (wet, halo[at.wet_e], halo[at.wet_w], halo[at.wet_n], halo[at.wet_s])
    coriolis = halo[at.coriolis]
    for buf, north, south in ((now, at.north0, at.south0), (later, at.north1, at.south1)):
        buf[pl.ds(PAD - 1, fields, stride=pitch), :] = halo[south]
        buf[pl.ds(PAD + rows, fields, stride=pitch), :] = halo[north]

    for ref, base in ((tr, 0), (ve, half)):

        def fill(f, carry, ref=ref, base=base):
            x = ref[pl.ds(pl.multiple_of(f * rows, rows), rows), :] * wet
            now[pl.ds(pl.multiple_of((base + f) * pitch + PAD, 8), rows), :] = x
            return carry

        lax.fori_loop(0, half, fill, 0, unroll=4)

    none = jnp.zeros((rows, LANES), F32)

    def first(k, acc):
        new, acc = advance_level(
            k, levels, levels, rows, now, halo[at.side0], wets, mixing, coriolis, acc
        )
        for q in range(4):
            place = pl.multiple_of((q * levels + k) * pitch + PAD, 8)
            later[pl.ds(place, rows), :] = new[q]
        return acc

    def second(k, acc):
        new, acc = advance_level(
            k, levels, levels, rows, later, halo[at.side1], wets, mixing, coriolis, acc
        )
        for q in range(4):
            ref = tr_out if q < 2 else ve_out
            place = pl.multiple_of(((q % 2) * levels + k) * rows, 8)
            ref[pl.ds(place, rows), :] = new[q]
        return acc

    lax.fori_loop(0, levels, first, (none, none))
    lax.fori_loop(0, levels, second, (none, none))

    me = lax.axis_index("lon") * lax.axis_size("lat") + lax.axis_index("lat")
    pitch = rows + 8
    owner = info[pl.ds(rows, devices, stride=pitch), :]
    target = info[pl.ds(rows + 1, devices, stride=pitch), :]
    lane = iota((devices, LANES), 1)
    mine = (owner == me) & (lane < rows)
    last = jnp.max(jnp.where(mine, lane, -1), axis=1, keepdims=True)
    start = jnp.min(jnp.where(mine, lane, LANES), axis=1, keepdims=True)
    for i, block in enumerate((last, start)):
        line = jnp.sum(jnp.where(lane == block, target, 0), axis=1, keepdims=True)
        keep = (last >= 0) if i == 0 else (last > start)
        slots[i * devices : (i + 1) * devices, :] = ((lane == line) & keep).astype(F32)

    atm_row = iota((ATM_ROWS, rows), 0)

    def count(d, total):
        base = pl.multiple_of(d * pitch, 8)
        extra = info[pl.ds(base + rows, 8), :]
        here = (extra[1:2, 0:rows] == atm_row) & (extra[0:1, 0:rows] == me)
        wet_rows = info[pl.ds(base, rows), :].astype(F32)
        return total + jnp.dot(
            here.astype(F32).astype(jnp.bfloat16), wet_rows.astype(jnp.bfloat16),
            preferred_element_type=F32,
        )

    cover[...] = lax.fori_loop(0, devices, count, jnp.zeros((ATM_ROWS, LANES), F32), unroll=4)


def reduce_kernel(devices, data, slots, cover, surface, cover_out):
    ocean = cover[...]
    cover_out[...] = ocean
    share = 1.0 / jnp.maximum(ocean, 1.0)
    totals = None
    for i in range(CAP):
        fields = [data[pl.ds(4 * i + q, devices, stride=4 * CAP), :] for q in range(4)]
        to_rows = slots[i * devices : (i + 1) * devices, :]
        part = dot(to_rows, jnp.concatenate(fields, axis=1), (((0,), (0,)), ((), ())))
        totals = part if totals is None else totals + part
    for q in range(4):
        surface[q] = totals[0:ATM_ROWS, q * LANES : (q + 1) * LANES] * share


def call(kernel, out_shape, **kwargs):
    return pl.pallas_call(
        kernel,
        out_shape=out_shape,
        compiler_params=pltpu.CompilerParams(vmem_limit_bytes=VMEM_LIMIT),
        **kwargs,
    )


def shaped(*shape, dtype=F32):
    return jax.ShapeDtypeStruct(shape, dtype)


def local(tracers, velocity, land_mask, mixing, owners, atm_row):
    levels = tracers.shape[1]
    rows, cols = land_mask.shape
    fields = 4 * levels
    lon_count, lat_count = lax.axis_size("lon"), lax.axis_size("lat")
    devices = lon_count * lat_count
    assert cols == LANES and rows % 8 == 0 and 2 * fields == LANES and lon_count % 2 == 0
    tr = tracers.reshape(2, levels * rows, cols)
    ve = velocity.reshape(2, levels * rows, cols)
    tr_flat, ve_flat = tr.reshape(-1, cols), ve.reshape(-1, cols)
    owner_list = owners.reshape(rows)
    length = 2 * fields + 8

    east, west, up, down, info = call(
        functools.partial(pack_kernel, rows, fields, devices),
        [
            shaped(2 * rows, cols),
            shaped(2 * rows, cols),
            shaped(length, cols),
            shaped(length, cols),
            shaped(rows + 8, cols, dtype=jnp.int32),
        ],
    )(tr_flat, ve_flat, land_mask, mixing, owners.reshape(1, rows), atm_row.reshape(1, rows))
    info = lax.all_gather(info, ("lon", "lat"), axis=0, tiled=True)

    ring = [(i, (i + 1) % lon_count) for i in range(lon_count)]
    from_west = lax.ppermute(east, "lon", ring)
    from_east = lax.ppermute(west, "lon", [(j, i) for i, j in ring])

    tail = pl.BlockSpec((8, cols), lambda i: (length // 8 - 1, 0))
    whole = pl.BlockSpec((2 * rows, cols), lambda i: (0, 0))
    up, down = call(
        functools.partial(corner_kernel, rows),
        [shaped(length, cols), shaped(length, cols)],
        grid=(1,),
        in_specs=[tail, tail, whole, whole],
        out_specs=[tail, tail],
        input_output_aliases={0: 0, 1: 1},
    )(up, down, from_east, from_west)

    path = []
    for i in range(lon_count // 2):
        line = [i * lat_count + a for a in range(lat_count)]
        line += [(lon_count - 1 - i) * lat_count + a for a in reversed(range(lat_count))]
        path += list(zip(line[:-1], line[1:]))
    from_up = lax.ppermute(up, ("lon", "lat"), path)
    from_down = lax.ppermute(down, ("lon", "lat"), [(j, i) for i, j in path])

    at = Halo(rows, fields)
    count = min(3, levels)
    pitch = rows + 2 * PAD

    def full(*shape):
        return pl.BlockSpec(shape, lambda i: (0,) * len(shape))

    top = full(2, count * rows, cols)
    halo, outgoing = call(
        functools.partial(surface_kernel, rows, levels, lat_count),
        [shaped(at.size, cols), shaped(devices * CAP * 4, cols)],
        grid=(1,),
        in_specs=[top, top, full(rows, cols), full(rows, cols)]
        + [full(2 * rows, cols)] * 4
        + [full(length, cols)] * 2
        + [full(fields, cols)] * 2
        + [pl.BlockSpec(memory_space=pltpu.SMEM)],
        out_specs=[full(at.size, cols), full(devices * CAP * 4, cols)],
        scratch_shapes=[
            pltpu.VMEM((4 * count * pitch, cols), F32),
            pltpu.VMEM((4 * count * pitch, cols), F32),
            pltpu.VMEM((pitch, cols), F32),
            pltpu.VMEM((4 * rows, cols), F32),
        ],
    )(tr, ve, land_mask, mixing, east, west, from_east, from_west, from_up, from_down, up, down,
      owner_list)
    incoming = lax.all_to_all(
        outgoing.reshape(devices, CAP * 4, cols), ("lon", "lat"), 0, 0, tiled=True
    ).reshape(devices * CAP * 4, cols)

    tr_out, ve_out, slots, cover = call(
        functools.partial(main_kernel, rows, levels, devices),
        [
            shaped(2 * levels * rows, cols),
            shaped(2 * levels * rows, cols),
            shaped(CAP * devices, cols),
            shaped(ATM_ROWS, cols),
        ],
        scratch_shapes=[
            pltpu.VMEM((fields * pitch, cols), F32),
            pltpu.VMEM((fields * pitch, cols), F32),
        ],
        cost_estimate=pl.CostEstimate(
            flops=80 * fields * rows * cols, bytes_accessed=5 << 20, transcendentals=0
        ),
    )(tr_flat, ve_flat, land_mask, mixing, halo, info)
    surface, cover = call(
        functools.partial(reduce_kernel, devices),
        [shaped(4, ATM_ROWS, cols), shaped(ATM_ROWS, cols)],
    )(incoming, slots, cover)
    shape = (2, levels, rows, cols)
    return tr_out.reshape(shape), ve_out.reshape(shape), surface, cover


def solution(mesh):
    in_specs = (
        P(None, None, "lat", "lon"),
        P(None, None, "lat", "lon"),
        P("lat", "lon"),
        P("lat", "lon"),
        P(("lon", "lat"), None),
        P(("lon", "lat")),
    )
    out_specs = (
        P(None, None, "lat", "lon"),
        P(None, None, "lat", "lon"),
        P(None, ("lon", "lat"), None),
        P(("lon", "lat"), None),
    )
    return jax.shard_map(local, mesh=mesh, in_specs=in_specs, out_specs=out_specs, check_vma=False)
```

```python
import functools
import math

import jax
import jax.numpy as jnp
from jax import lax
from jax.experimental import pallas as pl
from jax.experimental.pallas import tpu as pltpu
from jax.sharding import PartitionSpec as P

ATM_ROWS = 32
CAP = 2

THERMAL = 0.2
HALINE = 0.15
GRAVITY = 0.2
TIMESTEP = 0.8
VERTICAL_MIX = 0.1
VISCOSITY = 0.2
CORIOLIS_MAX = 0.3

LANES = 128
PAD = 8
EXACT = lax.Precision.HIGHEST
F32 = jnp.float32
VMEM_LIMIT = 48 * 1024 * 1024


def iota(shape, dim):
    return lax.broadcasted_iota(jnp.int32, shape, dim)


def dot(a, b, dims=(((1,), (0,)), ((), ()))):
    return lax.dot_general(a, b, dims, precision=EXACT, preferred_element_type=F32)


def is_even(axis):
    return lax.rem(lax.axis_index(axis), 2) == 0


def start_copies(pairs, sems):
    copies = [pltpu.make_async_copy(src, dst, sems.at[i]) for i, (src, dst) in enumerate(pairs)]
    for copy in copies:
        copy.start()
    return copies


def pack_kernel(
    rows, fields, chunks,
    tr_hbm, ve_hbm, mask_hbm, mix_hbm,
    lon_a, lon_b, lat_a, lat_b, state, wet_out, mix,
    tr, ve, mask, sems,
):
    half = fields // 2
    size = half // chunks
    pairs = [(mask_hbm, mask), (mix_hbm, mix)]
    for src, dst in ((tr_hbm, tr), (ve_hbm, ve)):
        for i in range(chunks):
            part = slice(i * size * rows, (i + 1) * size * rows)
            pairs.append((src.at[part], dst.at[part]))
    copies = start_copies(pairs, sems)
    copies[0].wait()
    copies[1].wait()
    wet = mask[...].astype(F32)
    wet_out[...] = wet
    lane = iota((rows, LANES), 1)
    pair = lane >> 1

    def columns(ref, base, carry):
        def body(f, carry):
            to_east, to_west = carry
            x = ref[pl.ds(pl.multiple_of(f * rows, rows), rows), :] * wet
            state[pl.ds(pl.multiple_of((base + f) * rows, 8), rows), :] = x
            keep = pair == base + f
            low = 2 * (base + f)
            to_east = jnp.where(keep, pltpu.roll(x, (low + 2) & (LANES - 1), 1), to_east)
            to_west = jnp.where(keep, pltpu.roll(x, low, 1), to_west)
            return to_east, to_west

        return body

    carry = (jnp.zeros((rows, LANES), F32), jnp.zeros((rows, LANES), F32))
    for n, (ref, base) in enumerate(((tr, 0), (ve, half))):
        for i in range(chunks):
            copies[2 + n * chunks + i].wait()
            carry = lax.fori_loop(
                i * size, (i + 1) * size, columns(ref, base, carry), carry, unroll=8
            )
    to_east, to_west = carry
    mixing = mix[...]
    aux_east = jnp.where(
        lane == 0,
        pltpu.roll(wet, 1, 1),
        jnp.where(lane == 1, pltpu.roll(wet, 3, 1), pltpu.roll(mixing, 3, 1)),
    )
    aux_west = jnp.where(lane <= 1, wet, pltpu.roll(mixing, 2, 1))
    even = is_even("lon")
    lon_a[0:rows, :] = jnp.where(even, to_east, to_west)
    lon_b[0:rows, :] = jnp.where(even, to_west, to_east)
    lon_a[rows : 2 * rows, :] = jnp.where(even, aux_east, aux_west)
    lon_b[rows : 2 * rows, :] = jnp.where(even, aux_west, aux_east)

    even = is_even("lat")
    top, bottom = (rows - 1, rows - 2), (0, 1)
    for buf, first, second in ((lat_a, top, bottom), (lat_b, bottom, top)):
        near = jnp.where(even, first[0], second[0])
        far = jnp.where(even, first[1], second[1])
        for place, line in ((0, near), (fields, far)):
            buf[place : place + fields, :] = state[pl.ds(line, fields, stride=rows), :]
        buf[2 * fields : 2 * fields + 8, :] = jnp.zeros((8, LANES), F32)
        buf[2 * fields : 2 * fields + 1, :] = wet_out[pl.ds(near, 1), :]
        buf[2 * fields + 1 : 2 * fields + 2, :] = wet_out[pl.ds(far, 1), :]
        buf[2 * fields + 2 : 2 * fields + 3, :] = mix[pl.ds(near, 1), :]


def corner_kernel(rows, a_in, b_in, got_a, got_b, a_out, b_out):
    even, even_lon = is_even("lat"), is_even("lon")
    lane = iota((1, LANES), 1)
    for src, dst, first, second in ((a_in, a_out, rows - 1, 0), (b_in, b_out, 0, rows - 1)):
        near = jnp.where(even, first, second)
        dst[...] = src[...]

        def sides(line):
            a, b = got_a[pl.ds(line, 1), :], got_b[pl.ds(line, 1), :]
            return jnp.where(even_lon, a, b), jnp.where(even_lon, b, a)

        east, west = sides(near)
        dst[3:4, :] = jnp.where((lane & 1) == 0, east, west)
        east, west = sides(rows + near)
        dst[4:5, :] = jnp.where(
            lane == 0,
            jnp.broadcast_to(east[:, 0:1], (1, LANES)),
            jnp.broadcast_to(west[:, 0:1], (1, LANES)),
        )


def level_matrix(kind, levels, source, target):
    if kind == "mix":
        above = (source == jnp.maximum(target - 1, 0)).astype(F32)
        below = (source == jnp.minimum(target + 1, levels - 1)).astype(F32)
        return above + below - 2.0 * (source == target).astype(F32)
    full = jnp.where(source < target, 1.0, jnp.where(source == target, 0.5, 0.0))
    return (0.5 * GRAVITY) * full


def density_weight(group):
    return jnp.where(group == 0, -THERMAL, jnp.where(group == 1, HALINE, 0.0)).astype(F32)


def advance_columns(levels, mid, outer, inner, corner_n, corner_s, wets, mixing, coriolis):
    rows = mid.shape[0]
    wet_mid, wet_out, wet_in, wet_corner_n, wet_corner_s = wets
    lane = iota((rows, LANES), 1)
    row = iota((rows, LANES), 0)
    even = (lane & 1) == 0
    group = lane // (2 * levels)

    def sides(outside, inside):
        return jnp.where(even, outside, inside), jnp.where(even, inside, outside)

    def shifted(x, north, south):
        n = jnp.where(row == rows - 1, north, pltpu.roll(x, rows - 1, 0))
        s = jnp.where(row == 0, south, pltpu.roll(x, 1, 0))
        return n, s

    e, w = sides(outer, inner)
    wet_e, wet_w = sides(wet_out, wet_in)
    n, s = shifted(mid, corner_n, corner_s)
    wet_n, wet_s = shifted(wet_mid, wet_corner_n, wet_corner_s)
    lap = wet_e * (e - mid) + wet_w * (w - mid) + wet_n * (n - mid) + wet_s * (s - mid)
    de, dn = e - w, n - s
    span = 2 * levels
    one, two, three = (pltpu.roll(mid, i * span, 1) for i in (1, 2, 3))

    def pick(a, b, c, d):
        return jnp.where(group == 0, a, jnp.where(group == 1, b, jnp.where(group == 2, c, d)))

    u = pick(two, three, mid, one)
    v = pick(one, two, three, mid)
    adv = 0.5 * (u * de + v * dn)
    src, dst = iota((LANES, LANES), 0), iota((LANES, LANES), 1)
    src_group, dst_group = src // span, dst // span
    src_level, dst_level = (src // 2) % levels, (dst // 2) % levels
    same_side = (src & 1) == (dst & 1)
    mix_map = jnp.where(
        same_side & (src_group == dst_group), level_matrix("mix", levels, src_level, dst_level), 0.0
    )
    press = level_matrix("pressure", levels, src_level, dst_level) * density_weight(src_group)
    press_x = jnp.where(same_side & (dst_group == 2), press, 0.0)
    press_y = jnp.where(same_side & (dst_group == 3), press, 0.0)
    vertical = dot(mid, mix_map)
    grad = dot(de, press_x) + dot(dn, press_y)
    zero = jnp.zeros_like(mid)
    turn = pick(zero, zero, coriolis * v, -coriolis * u)
    kappa = jnp.where(group < 2, mixing, VISCOSITY)
    tend = turn - adv - grad + kappa * lap + VERTICAL_MIX * vertical
    return wet_mid * (mid + TIMESTEP * tend)


def advance_row(levels, north_side, mid, outer, inner, corner_e, corner_w, wets, mixing, coriolis):
    fields = mid.shape[0]
    wet_mid, wet_out, wet_in, wet_corner_e, wet_corner_w = wets
    lane = iota((fields, LANES), 1)
    lane8 = iota((8, LANES), 1)

    def sides(x, east, west, at):
        e = jnp.where(at == LANES - 1, east, pltpu.roll(x, LANES - 1, 1))
        w = jnp.where(at == 0, west, pltpu.roll(x, 1, 1))
        return e, w

    e, w = sides(mid, corner_e, corner_w, lane)
    wet_e, wet_w = sides(
        jnp.broadcast_to(wet_mid, (8, LANES)), wet_corner_e, wet_corner_w, lane8
    )
    wet_e, wet_w = wet_e[0:1], wet_w[0:1]
    n, s = (outer, inner) if north_side else (inner, outer)
    wet_n, wet_s = (wet_out, wet_in) if north_side else (wet_in, wet_out)
    lap = wet_e * (e - mid) + wet_w * (w - mid) + wet_n * (n - mid) + wet_s * (s - mid)
    de, dn = e - w, n - s
    u, v = mid[2 * levels : 3 * levels], mid[3 * levels :]
    adv = 0.5 * (jnp.concatenate([u] * 4, axis=0) * de + jnp.concatenate([v] * 4, axis=0) * dn)
    dst, src = iota((fields, fields), 0), iota((fields, fields), 1)
    mix_map = jnp.where(
        dst // levels == src // levels, level_matrix("mix", levels, src % levels, dst % levels), 0.0
    )
    dst, src = iota((levels, fields), 0), iota((levels, fields), 1)
    press = level_matrix("pressure", levels, src % levels, dst) * density_weight(src // levels)
    vertical = dot(mix_map, mid)
    zero = jnp.zeros((2 * levels, LANES), F32)
    turn = jnp.concatenate(
        [zero, coriolis * v - dot(press, de), -coriolis * u - dot(press, dn)], axis=0
    )
    kappa = jnp.concatenate(
        [jnp.broadcast_to(mixing, (2 * levels, LANES)), jnp.full((2 * levels, LANES), VISCOSITY)],
        axis=0,
    )
    tend = turn - adv + kappa * lap + VERTICAL_MIX * vertical
    return wet_mid * (mid + TIMESTEP * tend)


COEFFICIENTS = ("te", "tw", "tn", "ts", "tc", "ve", "vw", "vn", "vs", "vc", "adv", "mix", "turn")


class Halo:
    def __init__(self, rows, fields):
        at = 0
        sizes = [("side0", rows), ("side1", rows)]
        sizes += [(name, fields) for name in ("north0", "south0", "north1", "south1")]
        for name, size in sizes + [(name, rows) for name in COEFFICIENTS]:
            setattr(self, name, slice(at, at + size))
            at += size
        self.size = at


def coefficients(wet, neighbours, mixing, coriolis):
    made = {}
    for name, kappa in (("t", mixing), ("v", VISCOSITY)):
        rest = wet * (1.0 - 2.0 * TIMESTEP * VERTICAL_MIX)
        for side, wet_n in zip("ewns", neighbours):
            made[name + side] = TIMESTEP * kappa * wet * wet_n
            rest = rest - made[name + side]
        made[name + "c"] = rest
    made["adv"] = (0.5 * TIMESTEP) * wet
    made["mix"] = (TIMESTEP * VERTICAL_MIX) * wet
    made["turn"] = TIMESTEP * coriolis * wet
    return made


def advance_level(k, count, levels, rows, src, sides, coef, acc):
    pitch = rows + 2 * PAD
    lane = iota((rows, LANES), 1)
    first, last = lane == 0, lane == LANES - 1
    above_k = jnp.maximum(k - 1, 0)
    below_k = jnp.minimum(k + 1, levels - 1)

    def load(q, level, shift):
        return src[pl.ds((q * count + level) * pitch + PAD + shift, rows), :]

    def base(q):
        return pl.multiple_of((q * count + k) * pitch + PAD, 8)

    center = [load(q, k, 0) for q in range(4)]
    u, v = coef("adv") * center[2], coef("adv") * center[3]
    sums, de, dn = [], [], []
    for q in range(4):
        c = center[q]
        n, s = load(q, k, 1), load(q, k, -1)
        edge = pltpu.roll(sides, (LANES - 1 - 2 * (q * levels + k)) & (LANES - 1), 1)
        e = jnp.where(last, edge, pltpu.roll(c, LANES - 1, 1))
        w = jnp.where(first, edge, pltpu.roll(c, 1, 1))
        kind = "t" if q < 2 else "v"
        lap = coef(kind + "c") * c + coef(kind + "e") * e + coef(kind + "w") * w
        lap = lap + coef(kind + "n") * n + coef(kind + "s") * s
        de.append(e - w)
        dn.append(n - s)
        sums.append(lap - (u * de[q] + v * dn[q]))
    scale = 0.5 * GRAVITY / VERTICAL_MIX
    dens_x = (scale * HALINE) * de[1] - (scale * THERMAL) * de[0]
    dens_y = (scale * HALINE) * dn[1] - (scale * THERMAL) * dn[0]
    acc_x, acc_y = acc
    grad = (None, None, acc_x + 0.5 * dens_x, acc_y + 0.5 * dens_y)
    turn = (None, None, coef("turn") * center[3], -coef("turn") * center[2])
    new = []
    for q in range(4):
        vertical = load(q, above_k, 0) + load(q, below_k, 0)
        if grad[q] is not None:
            vertical = vertical - grad[q]
        total = sums[q] + coef("mix") * vertical
        new.append(total if turn[q] is None else total + turn[q])
    return new, (acc_x + dens_x, acc_y + dens_y)


def surface_kernel(
    rows, levels, lat_count, devices,
    state, wet_in, mix_in, lon_a, lon_b, got_lon_a, got_lon_b, lat_a, lat_b, got_lat_a, got_lat_b,
    own, atm_row,
    halo, out, now, later, wet_pad, stage, used,
):
    fields = 4 * levels
    pitch = rows + 2 * PAD
    at = Halo(rows, fields)
    lat = lax.axis_index("lat")
    even_lat, even_lon = is_even("lat"), is_even("lon")
    fold = lat == lat_count - 1
    wet = wet_in[...]
    mixing = mix_in[...]
    lane = iota((rows, LANES), 1)
    even = (lane & 1) == 0

    def ordered(flag, a, b):
        return jnp.where(flag, a, b), jnp.where(flag, b, a)

    slot_rows = out.shape[0] // (devices * CAP)

    def clear(d, carry):
        used[d] = 0
        return carry

    lax.fori_loop(0, devices, clear, 0, unroll=8)
    out[...] = jnp.zeros(out.shape, F32)
    stage[...] = jnp.zeros(stage.shape, F32)
    stage[pl.ds(4, rows, stride=slot_rows), :] = wet
    for r in range(rows):
        line = jnp.full((1, LANES), atm_row[r], jnp.int32)
        stage[r * slot_rows + 5 : r * slot_rows + 6, :] = line.astype(F32)

    latitude = lat * rows - PAD + iota((rows + 2 * PAD, LANES), 0)
    total = lat_count * rows
    latitude = jnp.where(latitude >= total, 2 * total - 1 - latitude, latitude).astype(F32)
    table = CORIOLIS_MAX * jnp.sin(math.pi * (-0.43 + 0.93 * (latitude + 0.5) / total))
    coriolis = table[PAD : PAD + rows]

    north, south = ordered(even_lat, got_lat_a[...], got_lat_b[...])
    length = 2 * fields + 8
    back = LANES - 1 - iota((8, LANES), 1)
    flipped = jnp.concatenate(
        [
            jnp.take_along_axis(north[i : i + 8], back, axis=1)
            * (-1.0 if i < 2 * fields and i % fields >= fields // 2 else 1.0)
            for i in range(0, length, 8)
        ],
        axis=0,
    )
    straight = north
    north = jnp.where(fold, flipped, straight)
    lane1 = iota((1, LANES), 1)
    even1 = (lane1 & 1) == 0
    tail_n, tail_s = straight[2 * fields :], south[2 * fields :]
    swapped = jnp.where(
        iota((8, LANES), 1) & 1 == 0, pltpu.roll(tail_n, LANES - 1, 1), pltpu.roll(tail_n, 1, 1)
    )
    sign = jnp.where(lane1 >= LANES // 2, -1.0, 1.0)
    corner_n = jnp.where(fold, swapped[3:4] * sign, tail_n[3:4])
    corner_s = tail_s[3:4]
    wet_corner_n = jnp.where(fold, swapped[4:5], tail_n[4:5])
    wet_corner_s = tail_s[4:5]

    def corner_wet(x):
        east_wet = jnp.broadcast_to(x[:, 0:1], (1, LANES))
        west_wet = jnp.broadcast_to(x[:, 1:2], (1, LANES))
        return east_wet, west_wet, jnp.where(even1, east_wet, west_wet)

    wet_ne, wet_nw, wet_n_lanes = corner_wet(wet_corner_n)
    wet_se, wet_sw, wet_s_lanes = corner_wet(wet_corner_s)

    north_rows = (north[0:fields], north[fields : 2 * fields], north[2 * fields :])
    south_rows = (south[0:fields], south[fields : 2 * fields], south[2 * fields :])
    halo[at.north0] = north_rows[0]
    halo[at.south0] = south_rows[0]

    wet_pad[PAD : PAD + rows, :] = wet
    wet_pad[PAD - 1 : PAD, :] = south_rows[2][0:1]
    wet_pad[PAD + rows : PAD + rows + 1, :] = north_rows[2][0:1]
    wet_n = wet_pad[PAD + 1 : PAD + 1 + rows, :]
    wet_s = wet_pad[PAD - 1 : PAD - 1 + rows, :]

    def spread(x, i):
        return jnp.broadcast_to(x[:, i : i + 1], (rows, LANES))

    aux_e, aux_w = ordered(even_lon, got_lon_a[rows:, :], got_lon_b[rows:, :])
    wet_col_e, wet_col_w = spread(aux_e, 0), spread(aux_w, 0)
    wet_e = jnp.where(lane == LANES - 1, wet_col_e, pltpu.roll(wet, LANES - 1, 1))
    wet_w = jnp.where(lane == 0, wet_col_w, pltpu.roll(wet, 1, 1))
    made = coefficients(wet, (wet_e, wet_w, wet_n, wet_s), mixing, coriolis)
    for name in COEFFICIENTS:
        halo[getattr(at, name)] = made[name]

    def coef(name):
        return halo[getattr(at, name)]

    got_e, got_w = ordered(even_lon, got_lon_a[0:rows, :], got_lon_b[0:rows, :])
    sent_e, sent_w = ordered(even_lon, lon_a[0:rows, :], lon_b[0:rows, :])
    side = jnp.where(even, got_e, got_w)
    outer = jnp.where(even, pltpu.roll(got_e, LANES - 1, 1), pltpu.roll(got_w, 1, 1))
    inner = jnp.where(even, pltpu.roll(sent_e, LANES - 1, 1), pltpu.roll(sent_w, 1, 1))
    halo[at.side0] = side
    halo[at.side1] = advance_columns(
        levels, side, outer, inner, corner_n, corner_s,
        (
            jnp.where(even, wet_col_e, wet_col_w),
            jnp.where(even, spread(aux_e, 1), spread(aux_w, 1)),
            jnp.where(even, spread(wet, LANES - 1), spread(wet, 0)),
            wet_n_lanes,
            wet_s_lanes,
        ),
        jnp.where(even, spread(aux_e, 2), spread(aux_w, 2)),
        coriolis,
    )

    field_lane = iota((fields, LANES), 1)
    field_id = iota((fields, LANES), 0)

    def to_sublanes(x, parity):
        here = field_lane == 2 * field_id + parity
        return jnp.sum(jnp.where(here, x, 0.0), axis=1, keepdims=True)

    inside_n, inside_s = ordered(even_lat, lat_a[0:fields, :], lat_b[0:fields, :])
    for north_side, (mid, outside, tail), inside, corner, corner_wets, line, lat_row, place in (
        (True, north_rows, inside_n, corner_n, (wet_ne, wet_nw), rows - 1, PAD + rows, at.north1),
        (False, south_rows, inside_s, corner_s, (wet_se, wet_sw), 0, PAD - 1, at.south1),
    ):
        halo[place] = advance_row(
            levels, north_side, mid, outside, inside,
            to_sublanes(corner, 0), to_sublanes(corner, 1),
            (tail[0:1], tail[1:2], wet[line : line + 1], *corner_wets),
            tail[2:3], table[lat_row : lat_row + 1],
        )

    count = now.shape[0] // (4 * pitch)

    def put(buf, q, k, value, north, south):
        base = (q * count + k) * pitch + PAD
        n, s = north.start + q * levels + k, south.start + q * levels + k
        buf[base : base + rows, :] = value
        buf[base + rows : base + rows + 1, :] = halo[n : n + 1, :]
        buf[base - 1 : base, :] = halo[s : s + 1, :]

    for q in range(4):
        for k in range(count):
            field = (q * levels + k) * rows
            put(now, q, k, state[field : field + rows, :], at.north0, at.south0)
    none = jnp.zeros((rows, LANES), F32)
    acc = (none, none)
    for k in range(count - 1):
        new, acc = advance_level(k, count, levels, rows, now, halo[at.side0], coef, acc)
        for q in range(4):
            put(later, q, k, new[q], at.north1, at.south1)
    new, _ = advance_level(0, count, levels, rows, later, halo[at.side1], coef, (none, none))
    for q in range(4):
        stage[pl.ds(q, rows, stride=slot_rows), :] = new[q]
    for r in range(rows):
        owner = own[r]
        slot = used[owner]
        used[owner] = slot + 1
        place = pl.multiple_of((owner * CAP + slot) * slot_rows, 8)
        out[pl.ds(place, slot_rows), :] = stage[r * slot_rows : (r + 1) * slot_rows, :]


def main_kernel(
    rows, levels, chunks, state, halo, tr_hbm, ve_hbm, now, later, tr_out, ve_out, sems
):
    fields = 4 * levels
    pitch = rows + 2 * PAD
    at = Halo(rows, fields)
    for buf, north, south in ((now, at.north0, at.south0), (later, at.north1, at.south1)):
        buf[pl.ds(PAD - 1, fields, stride=pitch), :] = halo[south]
        buf[pl.ds(PAD + rows, fields, stride=pitch), :] = halo[north]

    def fill(f, carry):
        x = state[pl.ds(pl.multiple_of(f * rows, 8), rows), :]
        now[pl.ds(pl.multiple_of(f * pitch + PAD, 8), rows), :] = x
        return carry

    lax.fori_loop(0, fields, fill, 0, unroll=8)

    def coef(name):
        return halo[getattr(at, name)]

    def first(k, acc):
        new, acc = advance_level(k, levels, levels, rows, now, halo[at.side0], coef, acc)
        for q in range(4):
            place = pl.multiple_of((q * levels + k) * pitch + PAD, 8)
            later[pl.ds(place, rows), :] = new[q]
        return acc

    def second(k, acc):
        new, acc = advance_level(k, levels, levels, rows, later, halo[at.side1], coef, acc)
        for q in range(4):
            ref = tr_out if q < 2 else ve_out
            place = pl.multiple_of(((q % 2) * levels + k) * rows, 8)
            ref[pl.ds(place, rows), :] = new[q]
        return acc

    none = jnp.zeros((rows, LANES), F32)
    lax.fori_loop(0, levels, first, (none, none), unroll=2)
    acc = (none, none)
    size = levels // chunks
    copies = []
    for i in range(chunks):
        acc = lax.fori_loop(i * size, (i + 1) * size, second, acc, unroll=2)
        for src, dst in ((tr_out, tr_hbm), (ve_out, ve_hbm)):
            for q in range(2):
                start = (q * levels + i * size) * rows
                part = slice(start, start + size * rows)
                copy = pltpu.make_async_copy(src.at[part], dst.at[part], sems.at[len(copies)])
                copy.start()
                copies.append(copy)
    for copy in copies:
        copy.wait()


def reduce_kernel(devices, data, surface, cover):
    slot_rows = data.shape[0] // (devices * CAP)
    slots = devices * CAP
    lines = data[pl.ds(5, slots, stride=slot_rows), :]
    to_rows = (lines == iota((slots, LANES), 1).astype(F32)).astype(F32)
    values = [data[pl.ds(q, slots, stride=slot_rows), :] for q in range(5)]
    totals = dot(to_rows, jnp.concatenate(values, axis=1), (((0,), (0,)), ((), ())))
    totals = totals[0:ATM_ROWS]
    ocean = totals[:, 4 * LANES :]
    cover[...] = ocean
    share = jnp.maximum(ocean, 1.0)
    for q in range(4):
        surface[q] = totals[:, q * LANES : (q + 1) * LANES] / share


def call(kernel, out_shape, **kwargs):
    return pl.pallas_call(
        kernel,
        out_shape=out_shape,
        compiler_params=pltpu.CompilerParams(vmem_limit_bytes=VMEM_LIMIT),
        **kwargs,
    )


def shaped(*shape, dtype=F32):
    return jax.ShapeDtypeStruct(shape, dtype)


def pairs_of(lon_count, lat_count):
    lon_a = [(i, i ^ 1) for i in range(lon_count)]
    lon_b = [(i, (i + 1 if i % 2 else i - 1) % lon_count) for i in range(lon_count)]
    lat_a, lat_b = [], []
    for i in range(lon_count):
        for a in range(lat_count):
            here = i * lat_count + a
            lat_a.append((here, i * lat_count + (a ^ 1)))
            if a == lat_count - 1:
                lat_b.append((here, (lon_count - 1 - i) * lat_count + a))
            elif a > 0:
                lat_b.append((here, here + 1 if a % 2 else here - 1))
    return lon_a, lon_b, lat_a, lat_b


def local(tracers, velocity, land_mask, mixing, owners, atm_row):
    levels = tracers.shape[1]
    rows, cols = land_mask.shape
    fields = 4 * levels
    lon_count, lat_count = lax.axis_size("lon"), lax.axis_size("lat")
    devices = lon_count * lat_count
    assert cols == LANES and rows % 8 == 0 and 2 * fields == LANES
    assert lon_count % 2 == 0 and lat_count % 2 == 0
    length = 2 * fields + 8
    pitch = rows + 2 * PAD
    flat = 2 * levels * rows
    hbm = pl.BlockSpec(memory_space=pltpu.HBM)
    smem = pl.BlockSpec(memory_space=pltpu.SMEM)
    vmem = pl.BlockSpec(memory_space=pltpu.VMEM)

    chunks = 2
    lon_a, lon_b, lat_a, lat_b, state, wet, mix = call(
        functools.partial(pack_kernel, rows, fields, chunks),
        [shaped(2 * rows, cols)] * 2
        + [shaped(length, cols)] * 2
        + [shaped(fields * rows, cols), shaped(rows, cols), shaped(rows, cols)],
        in_specs=[hbm] * 4,
        scratch_shapes=[
            pltpu.VMEM((flat, cols), F32),
            pltpu.VMEM((flat, cols), F32),
            pltpu.VMEM((rows, cols), jnp.int32),
            pltpu.SemaphoreType.DMA((2 + 2 * chunks,)),
        ],
    )(tracers.reshape(flat, cols), velocity.reshape(flat, cols), land_mask, mixing)

    swaps = pairs_of(lon_count, lat_count)
    got_lon_a = lax.ppermute(lon_a, "lon", swaps[0])
    got_lon_b = lax.ppermute(lon_b, "lon", swaps[1])

    tail = pl.BlockSpec((8, cols), lambda i: (length // 8 - 1, 0))
    whole = pl.BlockSpec((2 * rows, cols), lambda i: (0, 0))
    lat_a, lat_b = call(
        functools.partial(corner_kernel, rows),
        [shaped(length, cols), shaped(length, cols)],
        grid=(1,),
        in_specs=[tail, tail, whole, whole],
        out_specs=[tail, tail],
        input_output_aliases={0: 0, 1: 1},
    )(lat_a, lat_b, got_lon_a, got_lon_b)
    got_lat_a = lax.ppermute(lat_a, ("lon", "lat"), swaps[2])
    got_lat_b = lax.ppermute(lat_b, ("lon", "lat"), swaps[3])

    at = Halo(rows, fields)
    slot_rows = 8
    count = min(3, levels)
    halo, outgoing = call(
        functools.partial(surface_kernel, rows, levels, lat_count, devices),
        [shaped(at.size, cols), shaped(devices * CAP * slot_rows, cols)],
        in_specs=[vmem] * 11 + [smem] * 2,
        scratch_shapes=[
            pltpu.VMEM((4 * count * pitch, cols), F32),
            pltpu.VMEM((4 * count * pitch, cols), F32),
            pltpu.VMEM((pitch, cols), F32),
            pltpu.VMEM((rows * slot_rows, cols), F32),
            pltpu.SMEM((devices,), jnp.int32),
        ],
    )(state, wet, mix, lon_a, lon_b, got_lon_a, got_lon_b, lat_a, lat_b, got_lat_a, got_lat_b,
      owners.reshape(rows), atm_row)
    incoming = lax.all_to_all(
        outgoing.reshape(devices, CAP * slot_rows, cols), ("lon", "lat"), 0, 0, tiled=True
    )

    chunks = 4
    tr_out, ve_out = call(
        functools.partial(main_kernel, rows, levels, chunks),
        [shaped(flat, cols), shaped(flat, cols)],
        in_specs=[vmem] * 2,
        out_specs=[hbm] * 2,
        scratch_shapes=[
            pltpu.VMEM((fields * pitch, cols), F32),
            pltpu.VMEM((fields * pitch, cols), F32),
            pltpu.VMEM((flat, cols), F32),
            pltpu.VMEM((flat, cols), F32),
            pltpu.SemaphoreType.DMA((4 * chunks,)),
        ],
        cost_estimate=pl.CostEstimate(
            flops=80 * fields * rows * cols, bytes_accessed=5 << 20, transcendentals=0
        ),
    )(state, halo)
    surface, cover = call(
        functools.partial(reduce_kernel, devices),
        [shaped(4, ATM_ROWS, cols), shaped(ATM_ROWS, cols)],
    )(incoming.reshape(devices * CAP * slot_rows, cols))
    shape = (2, levels, rows, cols)
    return tr_out.reshape(shape), ve_out.reshape(shape), surface, cover


def solution(mesh):
    in_specs = (
        P(None, None, "lat", "lon"),
        P(None, None, "lat", "lon"),
        P("lat", "lon"),
        P("lat", "lon"),
        P(("lon", "lat"), None),
        P(("lon", "lat")),
    )
    out_specs = (
        P(None, None, "lat", "lon"),
        P(None, None, "lat", "lon"),
        P(None, ("lon", "lat"), None),
        P(("lon", "lat"), None),
    )
    return jax.shard_map(local, mesh=mesh, in_specs=in_specs, out_specs=out_specs, check_vma=False)
```

```python
import functools
import math

import jax
import jax.numpy as jnp
from jax import lax
from jax.experimental import pallas as pl
from jax.experimental.pallas import tpu as pltpu
from jax.sharding import PartitionSpec as P

ATM_ROWS = 32
CAP = 2

THERMAL = 0.2
HALINE = 0.15
GRAVITY = 0.2
TIMESTEP = 0.8
VERTICAL_MIX = 0.1
VISCOSITY = 0.2
CORIOLIS_MAX = 0.3

LANES = 128
PAD = 8
EXACT = lax.Precision.HIGHEST
F32 = jnp.float32
VMEM_LIMIT = 32 * 1024 * 1024
VMEM_ALL = 63 * 1024 * 1024


def iota(shape, dim):
    return lax.broadcasted_iota(jnp.int32, shape, dim)


def dot(a, b, dims=(((1,), (0,)), ((), ()))):
    return lax.dot_general(a, b, dims, precision=EXACT, preferred_element_type=F32)


def is_even(axis):
    return lax.rem(lax.axis_index(axis), 2) == 0


def start_copies(pairs, sems):
    copies = [pltpu.make_async_copy(src, dst, sems.at[i]) for i, (src, dst) in enumerate(pairs)]
    for copy in copies:
        copy.start()
    return copies


def pack_kernel(
    rows, fields, chunks, tr_hbm, ve_hbm, mask_hbm, mix_hbm, lon_a, lon_b, tr, ve, mask, mix, sems
):
    half = fields // 2
    size = half // chunks
    pairs = [(mask_hbm, mask), (mix_hbm, mix)]
    for src, dst in ((tr_hbm, tr), (ve_hbm, ve)):
        for i in range(chunks):
            part = slice(i * size * rows, (i + 1) * size * rows)
            pairs.append((src.at[part], dst.at[part]))
    copies = start_copies(pairs, sems)
    copies[0].wait()
    copies[1].wait()
    wet = mask[...].astype(F32)
    lane = iota((rows, LANES), 1)
    pair = lane >> 1

    def columns(ref, base):
        def body(f, carry):
            to_east, to_west = carry
            x = ref[pl.ds(pl.multiple_of(f * rows, rows), rows), :]
            keep = pair == base + f
            low = 2 * (base + f)
            to_east = jnp.where(keep, pltpu.roll(x, (low + 2) & (LANES - 1), 1), to_east)
            to_west = jnp.where(keep, pltpu.roll(x, low, 1), to_west)
            return to_east, to_west

        return body

    carry = (jnp.zeros((rows, LANES), F32), jnp.zeros((rows, LANES), F32))
    for n, (ref, base) in enumerate(((tr, 0), (ve, half))):
        for i in range(chunks):
            copies[2 + n * chunks + i].wait()
            carry = lax.fori_loop(i * size, (i + 1) * size, columns(ref, base), carry, unroll=8)
    mixing = mix[...]
    aux_east = jnp.where(
        lane == 0,
        pltpu.roll(wet, 1, 1),
        jnp.where(lane == 1, pltpu.roll(wet, 3, 1), pltpu.roll(mixing, 3, 1)),
    )
    aux_west = jnp.where(lane <= 1, wet, pltpu.roll(mixing, 2, 1))

    def spread(x, i):
        return jnp.broadcast_to(x[:, i : i + 1], (rows, LANES))

    odd = (lane & 1) == 1
    to_east = carry[0] * jnp.where(odd, spread(wet, LANES - 1), spread(wet, LANES - 2))
    to_west = carry[1] * jnp.where(odd, spread(wet, 1), spread(wet, 0))
    even = is_even("lon")
    lon_a[0:rows, :] = jnp.where(even, to_east, to_west)
    lon_b[0:rows, :] = jnp.where(even, to_west, to_east)
    lon_a[rows : 2 * rows, :] = jnp.where(even, aux_east, aux_west)
    lon_b[rows : 2 * rows, :] = jnp.where(even, aux_west, aux_east)


def prepare_kernel(
    rows, levels, devices, tr, ve, mask, mix, own, atm_row,
    state, lat_a, lat_b, base, col_map, row_map, out, ids, used,
):
    fields = 4 * levels
    half = fields // 2
    wet = mask[...].astype(F32)
    base[0:rows, :] = wet
    base[rows : 2 * rows, :] = mix[...]
    for ref, first in ((tr, 0), (ve, half)):

        def fill(f, carry, ref=ref, first=first):
            x = ref[pl.ds(pl.multiple_of(f * rows, 8), rows), :] * wet
            state[pl.ds(pl.multiple_of((first + f) * rows, 8), rows), :] = x
            return carry

        lax.fori_loop(0, half, fill, 0, unroll=8)

    even = is_even("lat")
    top, bottom = (rows - 1, rows - 2), (0, 1)
    for buf, first, second in ((lat_a, top, bottom), (lat_b, bottom, top)):
        near = jnp.where(even, first[0], second[0])
        far = jnp.where(even, first[1], second[1])
        for place, line in ((0, near), (fields, far)):
            buf[place : place + fields, :] = state[pl.ds(line, fields, stride=rows), :]
        buf[2 * fields : 2 * fields + 8, :] = jnp.zeros((8, LANES), F32)
        buf[2 * fields : 2 * fields + 1, :] = base[pl.ds(near, 1), :]
        buf[2 * fields + 1 : 2 * fields + 2, :] = base[pl.ds(far, 1), :]
        buf[2 * fields + 2 : 2 * fields + 3, :] = base[pl.ds(rows + near, 1), :]

    total = lax.axis_size("lat") * rows
    latitude = lax.axis_index("lat") * rows - PAD + iota((rows + 2 * PAD, LANES), 0)
    latitude = jnp.where(latitude >= total, 2 * total - 1 - latitude, latitude).astype(F32)
    table = CORIOLIS_MAX * jnp.sin(math.pi * (-0.43 + 0.93 * (latitude + 0.5) / total))
    base[2 * rows :, :] = table

    span = 2 * levels
    src, dst = iota((LANES, LANES), 0), iota((LANES, LANES), 1)
    src_group, dst_group = src // span, dst // span
    src_level, dst_level = (src // 2) % levels, (dst // 2) % levels
    same_side = (src & 1) == (dst & 1)
    mixes = VERTICAL_MIX * level_matrix("mix", levels, src_level, dst_level)
    press = level_matrix("pressure", levels, src_level, dst_level) * density_weight(src_group)
    col_map[0:LANES, :] = jnp.where(same_side & (src_group == dst_group), mixes, 0.0)
    col_map[LANES : 2 * LANES, :] = jnp.where(same_side & (dst_group == 2), -press, 0.0)
    col_map[2 * LANES :, :] = jnp.where(same_side & (dst_group == 3), -press, 0.0)

    dst, src = iota((fields, fields), 0), iota((fields, fields), 1)
    mixes = VERTICAL_MIX * level_matrix("mix", levels, src % levels, dst % levels)
    row_map[0:fields, 0:fields] = jnp.where(dst // levels == src // levels, mixes, 0.0)
    dst, src = iota((levels, fields), 0), iota((levels, fields), 1)
    press = level_matrix("pressure", levels, src % levels, dst) * density_weight(src // levels)
    row_map[fields:, 0:fields] = press

    slot_rows = out.shape[0] // devices

    def clear(d, carry):
        used[d] = 0
        return carry

    lax.fori_loop(0, devices, clear, 0, unroll=8)
    out[...] = jnp.zeros(out.shape, F32)
    lane1 = iota((1, LANES), 1)
    places = jnp.zeros((1, LANES), jnp.int32)
    for r in range(rows):
        owner = own[r]
        slot = used[owner]
        used[owner] = slot + 1
        start = owner * slot_rows
        places = jnp.where(lane1 == r, start + 4 * slot, places)
        out[pl.ds(start + 4 * CAP + slot, 1), :] = base[r : r + 1, :]
        line = out[pl.ds(start + 5 * CAP, 1), :]
        target = jnp.full((1, LANES), atm_row[r], jnp.int32).astype(F32)
        out[pl.ds(start + 5 * CAP, 1), :] = jnp.where(lane1 // (LANES // CAP) == slot, target, line)
    ids[...] = jnp.zeros(ids.shape, jnp.int32)
    ids[0:1, :] = places


def corner_kernel(rows, a_in, b_in, got_a, got_b, a_out, b_out):
    even, even_lon = is_even("lat"), is_even("lon")
    lane = iota((1, LANES), 1)
    for src, dst, first, second in ((a_in, a_out, rows - 1, 0), (b_in, b_out, 0, rows - 1)):
        near = jnp.where(even, first, second)
        dst[...] = src[...]

        def sides(line):
            a, b = got_a[pl.ds(line, 1), :], got_b[pl.ds(line, 1), :]
            return jnp.where(even_lon, a, b), jnp.where(even_lon, b, a)

        east, west = sides(near)
        dst[3:4, :] = jnp.where((lane & 1) == 0, east, west)
        east, west = sides(rows + near)
        dst[4:5, :] = jnp.where(
            lane == 0,
            jnp.broadcast_to(east[:, 0:1], (1, LANES)),
            jnp.broadcast_to(west[:, 0:1], (1, LANES)),
        )


def level_matrix(kind, levels, source, target):
    if kind == "mix":
        above = (source == jnp.maximum(target - 1, 0)).astype(F32)
        below = (source == jnp.minimum(target + 1, levels - 1)).astype(F32)
        return above + below - 2.0 * (source == target).astype(F32)
    full = jnp.where(source < target, 1.0, jnp.where(source == target, 0.5, 0.0))
    return (0.5 * GRAVITY) * full


def density_weight(group):
    return jnp.where(group == 0, -THERMAL, jnp.where(group == 1, HALINE, 0.0)).astype(F32)


def advance_columns(mid, outer, inner, corner_n, corner_s, wets, mixing, coriolis, level_map):
    rows = mid.shape[0]
    wet_mid, wet_out, wet_in, wet_corner_n, wet_corner_s = wets
    lane = iota((rows, LANES), 1)
    row = iota((rows, LANES), 0)
    even = (lane & 1) == 0
    span = LANES // 4
    group = lane // span

    def sides(outside, inside):
        return jnp.where(even, outside, inside), jnp.where(even, inside, outside)

    def shifted(x, north, south):
        n = jnp.where(row == rows - 1, north, pltpu.roll(x, rows - 1, 0))
        s = jnp.where(row == 0, south, pltpu.roll(x, 1, 0))
        return n, s

    e, w = sides(outer, inner)
    wet_e, wet_w = sides(wet_out, wet_in)
    n, s = shifted(mid, corner_n, corner_s)
    wet_n, wet_s = shifted(wet_mid, wet_corner_n, wet_corner_s)
    lap = wet_e * (e - mid) + wet_w * (w - mid) + wet_n * (n - mid) + wet_s * (s - mid)
    de, dn = e - w, n - s
    one, two, three = (pltpu.roll(mid, i * span, 1) for i in (1, 2, 3))

    def pick(a, b, c, d):
        return jnp.where(group == 0, a, jnp.where(group == 1, b, jnp.where(group == 2, c, d)))

    u = pick(two, three, mid, one)
    v = pick(one, two, three, mid)
    adv = 0.5 * (u * de + v * dn)
    linear = dot(jnp.concatenate([mid, de, dn], axis=1), level_map)
    zero = jnp.zeros_like(mid)
    turn = pick(zero, zero, coriolis * v, -coriolis * u)
    kappa = jnp.where(group < 2, mixing, VISCOSITY)
    tend = turn - adv + kappa * lap + linear
    return wet_mid * (mid + TIMESTEP * tend)


def advance_rows(levels, parts, level_map):
    fields = 4 * levels
    lane = iota((fields, LANES), 1)
    lane8 = iota((8, LANES), 1)

    def sides(x, east, west, at):
        e = jnp.where(at == LANES - 1, east, pltpu.roll(x, LANES - 1, 1))
        w = jnp.where(at == 0, west, pltpu.roll(x, 1, 1))
        return e, w

    mids, gaps = [], []
    for mid, n, s, (corner_e, corner_w), *_ in parts:
        e, w = sides(mid, corner_e, corner_w, lane)
        mids.append((mid, e, w, n, s))
        gaps += [e - w, n - s]
    vertical = dot(level_map[0:fields, 0:fields], jnp.concatenate([m[0] for m in mids], axis=1))
    grads = dot(level_map[fields:, 0:fields], jnp.concatenate(gaps, axis=1))
    done = []
    for i, (mid, e, w, n, s) in enumerate(mids):
        *_, wets, mixing, coriolis = parts[i]
        wet_mid, wet_n, wet_s, wet_corner_e, wet_corner_w = wets
        wet_e, wet_w = sides(
            jnp.broadcast_to(wet_mid, (8, LANES)), wet_corner_e, wet_corner_w, lane8
        )
        lap = wet_e[0:1] * (e - mid) + wet_w[0:1] * (w - mid)
        lap = lap + wet_n * (n - mid) + wet_s * (s - mid)
        de, dn = gaps[2 * i], gaps[2 * i + 1]
        u, v = mid[2 * levels : 3 * levels], mid[3 * levels :]
        adv = jnp.concatenate([u] * 4, axis=0) * de + jnp.concatenate([v] * 4, axis=0) * dn
        grad_x = grads[:, 2 * i * LANES : (2 * i + 1) * LANES]
        grad_y = grads[:, (2 * i + 1) * LANES : (2 * i + 2) * LANES]
        zero = jnp.zeros((2 * levels, LANES), F32)
        turn = jnp.concatenate([zero, coriolis * v - grad_x, -coriolis * u - grad_y], axis=0)
        kappa = jnp.concatenate(
            [jnp.broadcast_to(mixing, (2 * levels, LANES)), jnp.full(zero.shape, VISCOSITY)],
            axis=0,
        )
        tend = turn - 0.5 * adv + kappa * lap + vertical[:, i * LANES : (i + 1) * LANES]
        done.append(wet_mid * (mid + TIMESTEP * tend))
    return done


COEFFICIENTS = ("te", "tw", "tn", "ts", "tc", "ve", "vw", "vn", "vs", "vc", "adv", "mix", "turn")


class Halo:
    def __init__(self, rows, fields):
        at = 0
        sizes = [("side0", rows), ("side1", rows)]
        sizes += [(name, fields) for name in ("north0", "south0", "north1", "south1")]
        for name, size in sizes + [(name, rows) for name in COEFFICIENTS]:
            setattr(self, name, slice(at, at + size))
            at += size
        self.size = at


def coefficients(wet, neighbours, mixing, coriolis):
    made = {}
    for name, kappa in (("t", mixing), ("v", VISCOSITY)):
        rest = wet * (1.0 - 2.0 * TIMESTEP * VERTICAL_MIX)
        for side, wet_n in zip("ewns", neighbours):
            made[name + side] = TIMESTEP * kappa * wet * wet_n
            rest = rest - made[name + side]
        made[name + "c"] = rest
    made["adv"] = (0.5 * TIMESTEP) * wet
    made["mix"] = (TIMESTEP * VERTICAL_MIX) * wet
    made["turn"] = TIMESTEP * coriolis * wet
    return made


def advance_level(k, count, levels, rows, src, sides, coef, acc):
    pitch = rows + 2 * PAD
    lane = iota((rows, LANES), 1)
    first, last = lane == 0, lane == LANES - 1
    above_k = jnp.maximum(k - 1, 0)
    below_k = jnp.minimum(k + 1, levels - 1)

    def load(q, level, shift):
        return src[pl.ds((q * count + level) * pitch + PAD + shift, rows), :]

    def base(q):
        return pl.multiple_of((q * count + k) * pitch + PAD, 8)

    center = [load(q, k, 0) for q in range(4)]
    u, v = coef("adv") * center[2], coef("adv") * center[3]
    sums, de, dn = [], [], []
    for q in range(4):
        c = center[q]
        n, s = load(q, k, 1), load(q, k, -1)
        edge = pltpu.roll(sides, (LANES - 1 - 2 * (q * levels + k)) & (LANES - 1), 1)
        e = jnp.where(last, edge, pltpu.roll(c, LANES - 1, 1))
        w = jnp.where(first, edge, pltpu.roll(c, 1, 1))
        kind = "t" if q < 2 else "v"
        lap = coef(kind + "c") * c + coef(kind + "e") * e + coef(kind + "w") * w
        lap = lap + coef(kind + "n") * n + coef(kind + "s") * s
        de.append(e - w)
        dn.append(n - s)
        sums.append(lap - (u * de[q] + v * dn[q]))
    scale = 0.5 * GRAVITY / VERTICAL_MIX
    dens_x = (scale * HALINE) * de[1] - (scale * THERMAL) * de[0]
    dens_y = (scale * HALINE) * dn[1] - (scale * THERMAL) * dn[0]
    acc_x, acc_y = acc
    grad = (None, None, acc_x + 0.5 * dens_x, acc_y + 0.5 * dens_y)
    turn = (None, None, coef("turn") * center[3], -coef("turn") * center[2])
    new = []
    for q in range(4):
        vertical = load(q, above_k, 0) + load(q, below_k, 0)
        if grad[q] is not None:
            vertical = vertical - grad[q]
        total = sums[q] + coef("mix") * vertical
        new.append(total if turn[q] is None else total + turn[q])
    return new, (acc_x + dens_x, acc_y + dens_y)


def surface_kernel(
    rows, levels, lat_count,
    state, base, col_map, row_map, lon_a, lon_b, got_lon_a, got_lon_b, lat_a, lat_b, got_lat_a,
    got_lat_b, out_in, ids,
    halo, out, now, later, wet_pad, stage, places, sem,
):
    fields = 4 * levels
    pitch = rows + 2 * PAD
    at = Halo(rows, fields)
    to_scalars = pltpu.make_async_copy(ids, places, sem)
    to_scalars.start()
    out[...] = out_in[...]
    lat = lax.axis_index("lat")
    even_lat, even_lon = is_even("lat"), is_even("lon")
    fold = lat == lat_count - 1
    wet = base[0:rows, :]
    mixing = base[rows : 2 * rows, :]
    table = base[2 * rows :, :]
    coriolis = table[PAD : PAD + rows]
    lane = iota((rows, LANES), 1)
    even = (lane & 1) == 0

    def ordered(flag, a, b):
        return jnp.where(flag, a, b), jnp.where(flag, b, a)

    north, south = ordered(even_lat, got_lat_a[...], got_lat_b[...])
    length = 2 * fields + 8
    back = LANES - 1 - iota((8, LANES), 1)
    flipped = jnp.concatenate(
        [
            jnp.take_along_axis(north[i : i + 8], back, axis=1)
            * (-1.0 if i < 2 * fields and i % fields >= fields // 2 else 1.0)
            for i in range(0, length, 8)
        ],
        axis=0,
    )
    straight = north
    north = jnp.where(fold, flipped, straight)
    lane1 = iota((1, LANES), 1)
    even1 = (lane1 & 1) == 0
    tail_n, tail_s = straight[2 * fields :], south[2 * fields :]
    swapped = jnp.where(
        iota((8, LANES), 1) & 1 == 0, pltpu.roll(tail_n, LANES - 1, 1), pltpu.roll(tail_n, 1, 1)
    )
    sign = jnp.where(lane1 >= LANES // 2, -1.0, 1.0)
    corner_n = jnp.where(fold, swapped[3:4] * sign, tail_n[3:4])
    corner_s = tail_s[3:4]
    wet_corner_n = jnp.where(fold, swapped[4:5], tail_n[4:5])
    wet_corner_s = tail_s[4:5]

    def corner_wet(x):
        east_wet = jnp.broadcast_to(x[:, 0:1], (1, LANES))
        west_wet = jnp.broadcast_to(x[:, 1:2], (1, LANES))
        return east_wet, west_wet, jnp.where(even1, east_wet, west_wet)

    wet_ne, wet_nw, wet_n_lanes = corner_wet(wet_corner_n)
    wet_se, wet_sw, wet_s_lanes = corner_wet(wet_corner_s)

    north_rows = (north[0:fields], north[fields : 2 * fields], north[2 * fields :])
    south_rows = (south[0:fields], south[fields : 2 * fields], south[2 * fields :])
    halo[at.north0] = north_rows[0]
    halo[at.south0] = south_rows[0]

    wet_pad[PAD : PAD + rows, :] = wet
    wet_pad[PAD - 1 : PAD, :] = south_rows[2][0:1]
    wet_pad[PAD + rows : PAD + rows + 1, :] = north_rows[2][0:1]
    wet_n = wet_pad[PAD + 1 : PAD + 1 + rows, :]
    wet_s = wet_pad[PAD - 1 : PAD - 1 + rows, :]

    def spread(x, i):
        return jnp.broadcast_to(x[:, i : i + 1], (rows, LANES))

    aux_e, aux_w = ordered(even_lon, got_lon_a[rows:, :], got_lon_b[rows:, :])
    wet_col_e, wet_col_w = spread(aux_e, 0), spread(aux_w, 0)
    wet_e = jnp.where(lane == LANES - 1, wet_col_e, pltpu.roll(wet, LANES - 1, 1))
    wet_w = jnp.where(lane == 0, wet_col_w, pltpu.roll(wet, 1, 1))
    made = coefficients(wet, (wet_e, wet_w, wet_n, wet_s), mixing, coriolis)
    for name in COEFFICIENTS:
        halo[getattr(at, name)] = made[name]

    def coef(name):
        return halo[getattr(at, name)]

    got_e, got_w = ordered(even_lon, got_lon_a[0:rows, :], got_lon_b[0:rows, :])
    sent_e, sent_w = ordered(even_lon, lon_a[0:rows, :], lon_b[0:rows, :])
    side = jnp.where(even, got_e, got_w)
    outer = jnp.where(even, pltpu.roll(got_e, LANES - 1, 1), pltpu.roll(got_w, 1, 1))
    inner = jnp.where(even, pltpu.roll(sent_e, LANES - 1, 1), pltpu.roll(sent_w, 1, 1))
    halo[at.side0] = side
    halo[at.side1] = advance_columns(
        side, outer, inner, corner_n, corner_s,
        (
            jnp.where(even, wet_col_e, wet_col_w),
            jnp.where(even, spread(aux_e, 1), spread(aux_w, 1)),
            jnp.where(even, spread(wet, LANES - 1), spread(wet, 0)),
            wet_n_lanes,
            wet_s_lanes,
        ),
        jnp.where(even, spread(aux_e, 2), spread(aux_w, 2)),
        coriolis, col_map[...],
    )

    field_lane = iota((fields, LANES), 1)
    field_id = iota((fields, LANES), 0)

    def to_sublanes(x, parity):
        here = field_lane == 2 * field_id + parity
        return jnp.sum(jnp.where(here, x, 0.0), axis=1, keepdims=True)

    inside_n, inside_s = ordered(even_lat, lat_a[0:fields, :], lat_b[0:fields, :])
    parts = []
    for north_side, (mid, outside, tail), inside, corner, corner_wets, line, lat_row in (
        (True, north_rows, inside_n, corner_n, (wet_ne, wet_nw), rows - 1, PAD + rows),
        (False, south_rows, inside_s, corner_s, (wet_se, wet_sw), 0, PAD - 1),
    ):
        pair = (outside, inside), (tail[1:2], wet[line : line + 1])
        (n, s), (wet_n1, wet_s1) = pair if north_side else [x[::-1] for x in pair]
        parts.append(
            (
                mid, n, s, (to_sublanes(corner, 0), to_sublanes(corner, 1)),
                (tail[0:1], wet_n1, wet_s1, *corner_wets),
                tail[2:3], table[lat_row : lat_row + 1],
            )
        )
    halo[at.north1], halo[at.south1] = advance_rows(levels, parts, row_map[...])

    count = now.shape[0] // (4 * pitch)

    def put(buf, q, k, value, north, south):
        base = (q * count + k) * pitch + PAD
        n, s = north.start + q * levels + k, south.start + q * levels + k
        buf[base : base + rows, :] = value
        buf[base + rows : base + rows + 1, :] = halo[n : n + 1, :]
        buf[base - 1 : base, :] = halo[s : s + 1, :]

    for q in range(4):
        for k in range(count):
            field = (q * levels + k) * rows
            put(now, q, k, state[field : field + rows, :], at.north0, at.south0)
    none = jnp.zeros((rows, LANES), F32)
    acc = (none, none)
    for k in range(count - 1):
        new, acc = advance_level(k, count, levels, rows, now, halo[at.side0], coef, acc)
        for q in range(4):
            put(later, q, k, new[q], at.north1, at.south1)
    new, _ = advance_level(0, count, levels, rows, later, halo[at.side1], coef, (none, none))
    for q in range(4):
        stage[pl.ds(q, rows, stride=4), :] = new[q]
    to_scalars.wait()
    for r in range(rows):
        out[pl.ds(places[0, r], 4), :] = stage[4 * r : 4 * r + 4, :]


def main_kernel(
    rows, levels, chunks, state, halo, tr_hbm, ve_hbm, now, later, tr_out, ve_out, sems
):
    fields = 4 * levels
    pitch = rows + 2 * PAD
    at = Halo(rows, fields)
    for buf, north, south in ((now, at.north0, at.south0), (later, at.north1, at.south1)):
        buf[pl.ds(PAD - 1, fields, stride=pitch), :] = halo[south]
        buf[pl.ds(PAD + rows, fields, stride=pitch), :] = halo[north]

    def fill(f, carry):
        x = state[pl.ds(pl.multiple_of(f * rows, 8), rows), :]
        now[pl.ds(pl.multiple_of(f * pitch + PAD, 8), rows), :] = x
        return carry

    lax.fori_loop(0, fields, fill, 0, unroll=8)

    def coef(name):
        return halo[getattr(at, name)]

    def first(k, acc):
        new, acc = advance_level(k, levels, levels, rows, now, halo[at.side0], coef, acc)
        for q in range(4):
            place = pl.multiple_of((q * levels + k) * pitch + PAD, 8)
            later[pl.ds(place, rows), :] = new[q]
        return acc

    def second(k, acc):
        new, acc = advance_level(k, levels, levels, rows, later, halo[at.side1], coef, acc)
        for q in range(4):
            ref = tr_out if q < 2 else ve_out
            place = pl.multiple_of(((q % 2) * levels + k) * rows, 8)
            ref[pl.ds(place, rows), :] = new[q]
        return acc

    none = jnp.zeros((rows, LANES), F32)
    lax.fori_loop(0, levels, first, (none, none), unroll=2)
    acc = (none, none)
    size = levels // chunks
    copies = []
    for i in range(chunks):
        acc = lax.fori_loop(i * size, (i + 1) * size, second, acc, unroll=2)
        for src, dst in ((tr_out, tr_hbm), (ve_out, ve_hbm)):
            for q in range(2):
                start = (q * levels + i * size) * rows
                part = slice(start, start + size * rows)
                copy = pltpu.make_async_copy(src.at[part], dst.at[part], sems.at[len(copies)])
                copy.start()
                copies.append(copy)
    for copy in copies:
        copy.wait()


def reduce_kernel(devices, data, surface, cover):
    slot_rows = data.shape[0] // devices

    def rows_of(i):
        return data[pl.ds(i, devices, stride=slot_rows), :]

    width = LANES // CAP
    lines = rows_of(5 * CAP)
    named = (lines == (iota((devices, LANES), 1) % width).astype(F32)).astype(F32)
    to_rows, values = [], []
    for slot in range(CAP):
        to_rows.append(named[:, slot * width : slot * width + ATM_ROWS])
        parts = [rows_of(4 * slot + q) for q in range(4)] + [rows_of(4 * CAP + slot)]
        values.append(jnp.concatenate(parts, axis=1))
    totals = dot(
        jnp.concatenate(to_rows, axis=0), jnp.concatenate(values, axis=0), (((0,), (0,)), ((), ()))
    )
    ocean = totals[:, 4 * LANES :]
    cover[...] = ocean
    share = jnp.maximum(ocean, 1.0)
    for q in range(4):
        surface[q] = totals[:, q * LANES : (q + 1) * LANES] / share


def call(kernel, out_shape, limit=VMEM_LIMIT, **kwargs):
    return pl.pallas_call(
        kernel,
        out_shape=out_shape,
        compiler_params=pltpu.CompilerParams(vmem_limit_bytes=limit),
        **kwargs,
    )


def shaped(*shape, dtype=F32):
    return jax.ShapeDtypeStruct(shape, dtype)


def pairs_of(lon_count, lat_count):
    lon_a = [(i, i ^ 1) for i in range(lon_count)]
    lon_b = [(i, (i + 1 if i % 2 else i - 1) % lon_count) for i in range(lon_count)]
    lat_a, lat_b = [], []
    for i in range(lon_count):
        for a in range(lat_count):
            here = i * lat_count + a
            lat_a.append((here, i * lat_count + (a ^ 1)))
            if a == lat_count - 1:
                lat_b.append((here, (lon_count - 1 - i) * lat_count + a))
            elif a > 0:
                lat_b.append((here, here + 1 if a % 2 else here - 1))
    return lon_a, lon_b, lat_a, lat_b


def local(tracers, velocity, land_mask, mixing, owners, atm_row):
    levels = tracers.shape[1]
    rows, cols = land_mask.shape
    fields = 4 * levels
    lon_count, lat_count = lax.axis_size("lon"), lax.axis_size("lat")
    devices = lon_count * lat_count
    assert cols == LANES and rows % 8 == 0 and 2 * fields == LANES
    assert lon_count % 2 == 0 and lat_count % 2 == 0
    length = 2 * fields + 8
    pitch = rows + 2 * PAD
    flat = 2 * levels * rows
    hbm = pl.BlockSpec(memory_space=pltpu.HBM)
    smem = pl.BlockSpec(memory_space=pltpu.SMEM)
    vmem = pl.BlockSpec(memory_space=pltpu.VMEM)

    chunks = 2
    tr, ve = tracers.reshape(flat, cols), velocity.reshape(flat, cols)
    lon_a, lon_b = call(
        functools.partial(pack_kernel, rows, fields, chunks),
        [shaped(2 * rows, cols)] * 2,
        limit=VMEM_ALL,
        in_specs=[hbm] * 4,
        scratch_shapes=[
            pltpu.VMEM((flat, cols), F32),
            pltpu.VMEM((flat, cols), F32),
            pltpu.VMEM((rows, cols), jnp.int32),
            pltpu.VMEM((rows, cols), F32),
            pltpu.SemaphoreType.DMA((2 + 2 * chunks,)),
        ],
    )(tr, ve, land_mask, mixing)

    slot_rows = 5 * CAP + 1
    state, lat_a, lat_b, base, col_map, row_map, outgoing, ids = call(
        functools.partial(prepare_kernel, rows, levels, devices),
        [shaped(fields * rows, cols)]
        + [shaped(length, cols)] * 2
        + [
            shaped(2 * rows + pitch, cols),
            shaped(3 * cols, cols),
            shaped(fields + levels, cols),
            shaped(devices * slot_rows, cols),
            shaped(8, cols, dtype=jnp.int32),
        ],
        in_specs=[vmem] * 4 + [smem] * 2,
        scratch_shapes=[pltpu.SMEM((devices,), jnp.int32)],
    )(tr, ve, land_mask, mixing, owners.reshape(rows), atm_row)

    swaps = pairs_of(lon_count, lat_count)
    got_lon_a = lax.ppermute(lon_a, "lon", swaps[0])
    got_lon_b = lax.ppermute(lon_b, "lon", swaps[1])

    tail = pl.BlockSpec((8, cols), lambda i: (length // 8 - 1, 0))
    whole = pl.BlockSpec((2 * rows, cols), lambda i: (0, 0))
    lat_a, lat_b = call(
        functools.partial(corner_kernel, rows),
        [shaped(length, cols), shaped(length, cols)],
        grid=(1,),
        in_specs=[tail, tail, whole, whole],
        out_specs=[tail, tail],
        input_output_aliases={0: 0, 1: 1},
    )(lat_a, lat_b, got_lon_a, got_lon_b)
    got_lat_a = lax.ppermute(lat_a, ("lon", "lat"), swaps[2])
    got_lat_b = lax.ppermute(lat_b, ("lon", "lat"), swaps[3])

    at = Halo(rows, fields)
    count = min(3, levels)
    halo, outgoing = call(
        functools.partial(surface_kernel, rows, levels, lat_count),
        [shaped(at.size, cols), shaped(devices * slot_rows, cols)],
        in_specs=[vmem] * 14,
        scratch_shapes=[
            pltpu.VMEM((4 * count * pitch, cols), F32),
            pltpu.VMEM((4 * count * pitch, cols), F32),
            pltpu.VMEM((pitch, cols), F32),
            pltpu.VMEM((4 * rows, cols), F32),
            pltpu.SMEM((8, cols), jnp.int32),
            pltpu.SemaphoreType.DMA,
        ],
    )(state, base, col_map, row_map, lon_a, lon_b, got_lon_a, got_lon_b, lat_a, lat_b, got_lat_a,
      got_lat_b, outgoing, ids)
    incoming = lax.all_to_all(
        outgoing.reshape(devices, slot_rows, 1, cols), ("lon", "lat"), 0, 0, tiled=True
    ).reshape(devices * slot_rows, cols)

    chunks = 4
    tr_out, ve_out = call(
        functools.partial(main_kernel, rows, levels, chunks),
        [shaped(flat, cols), shaped(flat, cols)],
        in_specs=[vmem] * 2,
        out_specs=[hbm] * 2,
        scratch_shapes=[
            pltpu.VMEM((fields * pitch, cols), F32),
            pltpu.VMEM((fields * pitch, cols), F32),
            pltpu.VMEM((flat, cols), F32),
            pltpu.VMEM((flat, cols), F32),
            pltpu.SemaphoreType.DMA((4 * chunks,)),
        ],
        cost_estimate=pl.CostEstimate(
            flops=80 * fields * rows * cols, bytes_accessed=5 << 20, transcendentals=0
        ),
    )(state, halo)
    surface, cover = call(
        functools.partial(reduce_kernel, devices),
        [shaped(4, ATM_ROWS, cols), shaped(ATM_ROWS, cols)],
    )(incoming)
    shape = (2, levels, rows, cols)
    return tr_out.reshape(shape), ve_out.reshape(shape), surface, cover


def solution(mesh):
    in_specs = (
        P(None, None, "lat", "lon"),
        P(None, None, "lat", "lon"),
        P("lat", "lon"),
        P("lat", "lon"),
        P(("lon", "lat"), None),
        P(("lon", "lat")),
    )
    out_specs = (
        P(None, None, "lat", "lon"),
        P(None, None, "lat", "lon"),
        P(None, ("lon", "lat"), None),
        P(("lon", "lat"), None),
    )
    return jax.shard_map(local, mesh=mesh, in_specs=in_specs, out_specs=out_specs, check_vma=False)
```

```python
import functools
import math

import jax
import jax.numpy as jnp
from jax import lax
from jax.experimental import pallas as pl
from jax.experimental.pallas import tpu as pltpu
from jax.sharding import PartitionSpec as P

ATM_ROWS = 32
CAP = 2

THERMAL = 0.2
HALINE = 0.15
GRAVITY = 0.2
TIMESTEP = 0.8
VERTICAL_MIX = 0.1
VISCOSITY = 0.2
CORIOLIS_MAX = 0.3

LANES = 128
PAD = 8
EXACT = lax.Precision.HIGHEST
F32 = jnp.float32
VMEM_LIMIT = 32 * 1024 * 1024
VMEM_ALL = 63 * 1024 * 1024


def iota(shape, dim):
    return lax.broadcasted_iota(jnp.int32, shape, dim)


def dot(a, b, dims=(((1,), (0,)), ((), ()))):
    return lax.dot_general(a, b, dims, precision=EXACT, preferred_element_type=F32)


def is_even(axis):
    return lax.rem(lax.axis_index(axis), 2) == 0


def start_copies(pairs, sems):
    copies = [pltpu.make_async_copy(src, dst, sems.at[i]) for i, (src, dst) in enumerate(pairs)]
    for copy in copies:
        copy.start()
    return copies


def edge_kernel(rows, fields, tr_hbm, ve_hbm, mask_hbm, mix_hbm, lat_a, lat_b, edges, mask, mix, sems):
    half = fields // 2
    pairs = [(mask_hbm, mask), (mix_hbm, mix)]
    for n, src in enumerate((tr_hbm, ve_hbm)):
        for side, first in enumerate((0, rows - 8)):
            part = edges.at[side, n * half : (n + 1) * half]
            pairs.append((src.at[:, first : first + 8, :], part))
    for copy in start_copies(pairs, sems):
        copy.wait()
    flat = edges.reshape(2 * fields * 8, LANES)
    even = is_even("lat")
    top = ((rows - 1, 8 * fields + 7), (rows - 2, 8 * fields + 6))
    bottom = ((0, 0), (1, 1))
    for buf, first, second in ((lat_a, top, bottom), (lat_b, bottom, top)):
        (near, near_at), (far, far_at) = [
            [jnp.where(even, x, y) for x, y in zip(one, other)] for one, other in zip(first, second)
        ]
        wet_near = mask[pl.ds(near, 1), :].astype(F32)
        wet_far = mask[pl.ds(far, 1), :].astype(F32)
        buf[0:fields, :] = flat[pl.ds(near_at, fields, stride=8), :] * wet_near
        buf[fields : 2 * fields, :] = flat[pl.ds(far_at, fields, stride=8), :] * wet_far
        buf[2 * fields : 2 * fields + 8, :] = jnp.zeros((8, LANES), F32)
        buf[2 * fields : 2 * fields + 1, :] = wet_near
        buf[2 * fields + 1 : 2 * fields + 2, :] = wet_far
        buf[2 * fields + 2 : 2 * fields + 3, :] = mix[pl.ds(near, 1), :]


def pack_kernel(rows, fields, tr, ve, mask, mix, lon_a, lon_b):
    half = fields // 2
    wet = mask[...].astype(F32)
    lane = iota((rows, LANES), 1)
    pair = lane >> 1

    def columns(ref, base):
        def body(f, carry):
            to_east, to_west = carry
            x = ref[pl.ds(pl.multiple_of(f * rows, rows), rows), :]
            keep = pair == base + f
            low = 2 * (base + f)
            to_east = jnp.where(keep, pltpu.roll(x, (low + 2) & (LANES - 1), 1), to_east)
            to_west = jnp.where(keep, pltpu.roll(x, low, 1), to_west)
            return to_east, to_west

        return body

    carry = (jnp.zeros((rows, LANES), F32), jnp.zeros((rows, LANES), F32))
    for ref, base in ((tr, 0), (ve, half)):
        carry = lax.fori_loop(0, half, columns(ref, base), carry, unroll=8)
    mixing = mix[...]
    aux_east = jnp.where(
        lane == 0,
        pltpu.roll(wet, 1, 1),
        jnp.where(lane == 1, pltpu.roll(wet, 3, 1), pltpu.roll(mixing, 3, 1)),
    )
    aux_west = jnp.where(lane <= 1, wet, pltpu.roll(mixing, 2, 1))

    def spread(x, i):
        return jnp.broadcast_to(x[:, i : i + 1], (rows, LANES))

    odd = (lane & 1) == 1
    to_east = carry[0] * jnp.where(odd, spread(wet, LANES - 1), spread(wet, LANES - 2))
    to_west = carry[1] * jnp.where(odd, spread(wet, 1), spread(wet, 0))
    even = is_even("lon")
    lon_a[0:rows, :] = jnp.where(even, to_east, to_west)
    lon_b[0:rows, :] = jnp.where(even, to_west, to_east)
    lon_a[rows : 2 * rows, :] = jnp.where(even, aux_east, aux_west)
    lon_b[rows : 2 * rows, :] = jnp.where(even, aux_west, aux_east)


def prepare_kernel(
    rows, levels, devices, tr, ve, mask, mix, own, atm_row,
    state, base, col_map, row_map, out, ids, used,
):
    fields = 4 * levels
    half = fields // 2
    wet = mask[...].astype(F32)
    base[0:rows, :] = wet
    base[rows : 2 * rows, :] = mix[...]
    for ref, first in ((tr, 0), (ve, half)):

        def fill(f, carry, ref=ref, first=first):
            x = ref[pl.ds(pl.multiple_of(f * rows, 8), rows), :] * wet
            state[pl.ds(pl.multiple_of((first + f) * rows, 8), rows), :] = x
            return carry

        lax.fori_loop(0, half, fill, 0, unroll=8)

    total = lax.axis_size("lat") * rows
    latitude = lax.axis_index("lat") * rows - PAD + iota((rows + 2 * PAD, LANES), 0)
    latitude = jnp.where(latitude >= total, 2 * total - 1 - latitude, latitude).astype(F32)
    table = CORIOLIS_MAX * jnp.sin(math.pi * (-0.43 + 0.93 * (latitude + 0.5) / total))
    base[2 * rows :, :] = table

    span = 2 * levels
    src, dst = iota((LANES, LANES), 0), iota((LANES, LANES), 1)
    src_group, dst_group = src // span, dst // span
    src_level, dst_level = (src // 2) % levels, (dst // 2) % levels
    same_side = (src & 1) == (dst & 1)
    mixes = VERTICAL_MIX * level_matrix("mix", levels, src_level, dst_level)
    press = level_matrix("pressure", levels, src_level, dst_level) * density_weight(src_group)
    col_map[0:LANES, :] = jnp.where(same_side & (src_group == dst_group), mixes, 0.0)
    col_map[LANES : 2 * LANES, :] = jnp.where(same_side & (dst_group == 2), -press, 0.0)
    col_map[2 * LANES :, :] = jnp.where(same_side & (dst_group == 3), -press, 0.0)

    dst, src = iota((fields, fields), 0), iota((fields, fields), 1)
    mixes = VERTICAL_MIX * level_matrix("mix", levels, src % levels, dst % levels)
    row_map[0:fields, 0:fields] = jnp.where(dst // levels == src // levels, mixes, 0.0)
    dst, src = iota((levels, fields), 0), iota((levels, fields), 1)
    press = level_matrix("pressure", levels, src % levels, dst) * density_weight(src // levels)
    row_map[fields:, 0:fields] = press

    slot_rows = out.shape[0] // devices

    def clear(d, carry):
        used[d] = 0
        return carry

    lax.fori_loop(0, devices, clear, 0, unroll=8)
    out[...] = jnp.zeros(out.shape, F32)
    lane1 = iota((1, LANES), 1)
    places = jnp.zeros((1, LANES), jnp.int32)
    for r in range(rows):
        owner = own[r]
        slot = used[owner]
        used[owner] = slot + 1
        start = owner * slot_rows
        places = jnp.where(lane1 == r, start + 4 * slot, places)
        out[pl.ds(start + 4 * CAP + slot, 1), :] = base[r : r + 1, :]
        line = out[pl.ds(start + 5 * CAP, 1), :]
        target = jnp.full((1, LANES), atm_row[r], jnp.int32).astype(F32)
        out[pl.ds(start + 5 * CAP, 1), :] = jnp.where(lane1 // (LANES // CAP) == slot, target, line)
    ids[...] = jnp.zeros(ids.shape, jnp.int32)
    ids[0:1, :] = places


def corner_kernel(lat_count, fields, got_a, got_b, north, south, corners):
    fold = lax.axis_index("lat") == lat_count - 1
    even = is_even("lat")
    a, b = got_a[...], got_b[...]
    straight = jnp.where(even, a, b)
    south[...] = jnp.where(even, b, a)
    back = LANES - 1 - iota((8, LANES), 1)
    flipped = jnp.concatenate(
        [
            jnp.take_along_axis(straight[i : i + 8], back, axis=1)
            * (-1.0 if i < 2 * fields and i % fields >= fields // 2 else 1.0)
            for i in range(0, straight.shape[0], 8)
        ],
        axis=0,
    )
    north[...] = jnp.where(fold, flipped, straight)
    lane, field = iota((fields, LANES), 1), iota((fields, LANES), 0)
    lane1 = iota((1, LANES), 1)
    corners[...] = jnp.zeros(corners.shape, F32)
    for i, ref in enumerate((north, south)):
        near = ref[0:fields, :]
        ends = jnp.where(
            lane == 2 * field, near[:, 0:1], jnp.where(lane == 2 * field + 1, near[:, LANES - 1 :], 0.0)
        )
        corners[i : i + 1, :] = jnp.sum(ends, axis=0, keepdims=True)
        wet = ref[2 * fields : 2 * fields + 1, :]
        corners[2 + i : 3 + i, :] = jnp.where(lane1 == 0, wet[:, 0:1], wet[:, LANES - 1 :])


def level_matrix(kind, levels, source, target):
    if kind == "mix":
        above = (source == jnp.maximum(target - 1, 0)).astype(F32)
        below = (source == jnp.minimum(target + 1, levels - 1)).astype(F32)
        return above + below - 2.0 * (source == target).astype(F32)
    full = jnp.where(source < target, 1.0, jnp.where(source == target, 0.5, 0.0))
    return (0.5 * GRAVITY) * full


def density_weight(group):
    return jnp.where(group == 0, -THERMAL, jnp.where(group == 1, HALINE, 0.0)).astype(F32)


def advance_columns(mid, outer, inner, corner_n, corner_s, wets, mixing, coriolis, level_map):
    rows = mid.shape[0]
    wet_mid, wet_out, wet_in, wet_corner_n, wet_corner_s = wets
    lane = iota((rows, LANES), 1)
    row = iota((rows, LANES), 0)
    even = (lane & 1) == 0
    span = LANES // 4
    group = lane // span

    def sides(outside, inside):
        return jnp.where(even, outside, inside), jnp.where(even, inside, outside)

    def shifted(x, north, south):
        n = jnp.where(row == rows - 1, north, pltpu.roll(x, rows - 1, 0))
        s = jnp.where(row == 0, south, pltpu.roll(x, 1, 0))
        return n, s

    e, w = sides(outer, inner)
    wet_e, wet_w = sides(wet_out, wet_in)
    n, s = shifted(mid, corner_n, corner_s)
    wet_n, wet_s = shifted(wet_mid, wet_corner_n, wet_corner_s)
    lap = wet_e * (e - mid) + wet_w * (w - mid) + wet_n * (n - mid) + wet_s * (s - mid)
    de, dn = e - w, n - s
    one, two, three = (pltpu.roll(mid, i * span, 1) for i in (1, 2, 3))

    def pick(a, b, c, d):
        return jnp.where(group == 0, a, jnp.where(group == 1, b, jnp.where(group == 2, c, d)))

    u = pick(two, three, mid, one)
    v = pick(one, two, three, mid)
    adv = 0.5 * (u * de + v * dn)
    linear = dot(jnp.concatenate([mid, de, dn], axis=1), level_map)
    zero = jnp.zeros_like(mid)
    turn = pick(zero, zero, coriolis * v, -coriolis * u)
    kappa = jnp.where(group < 2, mixing, VISCOSITY)
    tend = turn - adv + kappa * lap + linear
    return wet_mid * (mid + TIMESTEP * tend)


def advance_rows(levels, parts, level_map):
    fields = 4 * levels
    lane = iota((fields, LANES), 1)
    lane8 = iota((8, LANES), 1)

    def sides(x, east, west, at):
        e = jnp.where(at == LANES - 1, east, pltpu.roll(x, LANES - 1, 1))
        w = jnp.where(at == 0, west, pltpu.roll(x, 1, 1))
        return e, w

    mids, gaps = [], []
    for mid, n, s, (corner_e, corner_w), *_ in parts:
        e, w = sides(mid, corner_e, corner_w, lane)
        mids.append((mid, e, w, n, s))
        gaps += [e - w, n - s]
    vertical = dot(level_map[0:fields, 0:fields], jnp.concatenate([m[0] for m in mids], axis=1))
    grads = dot(level_map[fields:, 0:fields], jnp.concatenate(gaps, axis=1))
    done = []
    for i, (mid, e, w, n, s) in enumerate(mids):
        *_, wets, mixing, coriolis = parts[i]
        wet_mid, wet_n, wet_s, wet_corner_e, wet_corner_w = wets
        wet_e, wet_w = sides(
            jnp.broadcast_to(wet_mid, (8, LANES)), wet_corner_e, wet_corner_w, lane8
        )
        lap = wet_e[0:1] * (e - mid) + wet_w[0:1] * (w - mid)
        lap = lap + wet_n * (n - mid) + wet_s * (s - mid)
        de, dn = gaps[2 * i], gaps[2 * i + 1]
        u, v = mid[2 * levels : 3 * levels], mid[3 * levels :]
        adv = jnp.concatenate([u] * 4, axis=0) * de + jnp.concatenate([v] * 4, axis=0) * dn
        grad_x = grads[:, 2 * i * LANES : (2 * i + 1) * LANES]
        grad_y = grads[:, (2 * i + 1) * LANES : (2 * i + 2) * LANES]
        zero = jnp.zeros((2 * levels, LANES), F32)
        turn = jnp.concatenate([zero, coriolis * v - grad_x, -coriolis * u - grad_y], axis=0)
        kappa = jnp.concatenate(
            [jnp.broadcast_to(mixing, (2 * levels, LANES)), jnp.full(zero.shape, VISCOSITY)],
            axis=0,
        )
        tend = turn - 0.5 * adv + kappa * lap + vertical[:, i * LANES : (i + 1) * LANES]
        done.append(wet_mid * (mid + TIMESTEP * tend))
    return done


COEFFICIENTS = ("te", "tw", "tn", "ts", "tc", "ve", "vw", "vn", "vs", "vc", "adv", "mix", "turn")


def place_of(name, rows):
    i = COEFFICIENTS.index(name)
    return slice(i * rows, (i + 1) * rows)


def coefficients(wet, neighbours, mixing, coriolis):
    made = {}
    for name, kappa in (("t", mixing), ("v", VISCOSITY)):
        rest = wet * (1.0 - 2.0 * TIMESTEP * VERTICAL_MIX)
        for side, wet_n in zip("ewns", neighbours):
            made[name + side] = TIMESTEP * kappa * wet * wet_n
            rest = rest - made[name + side]
        made[name + "c"] = rest
    made["adv"] = (0.5 * TIMESTEP) * wet
    made["mix"] = (TIMESTEP * VERTICAL_MIX) * wet
    made["turn"] = TIMESTEP * coriolis * wet
    return made


def advance_level(k, count, levels, rows, src, sides, coef, acc):
    pitch = rows + 2 * PAD
    lane = iota((rows, LANES), 1)
    first, last = lane == 0, lane == LANES - 1
    above_k = jnp.maximum(k - 1, 0)
    below_k = jnp.minimum(k + 1, levels - 1)

    def load(q, level, shift):
        return src[pl.ds((q * count + level) * pitch + PAD + shift, rows), :]

    def base(q):
        return pl.multiple_of((q * count + k) * pitch + PAD, 8)

    center = [load(q, k, 0) for q in range(4)]
    u, v = coef("adv") * center[2], coef("adv") * center[3]
    sums, de, dn = [], [], []
    for q in range(4):
        c = center[q]
        n, s = load(q, k, 1), load(q, k, -1)
        edge = pltpu.roll(sides, (LANES - 1 - 2 * (q * levels + k)) & (LANES - 1), 1)
        e = jnp.where(last, edge, pltpu.roll(c, LANES - 1, 1))
        w = jnp.where(first, edge, pltpu.roll(c, 1, 1))
        kind = "t" if q < 2 else "v"
        lap = coef(kind + "c") * c + coef(kind + "e") * e + coef(kind + "w") * w
        lap = lap + coef(kind + "n") * n + coef(kind + "s") * s
        de.append(e - w)
        dn.append(n - s)
        sums.append(lap - (u * de[q] + v * dn[q]))
    scale = 0.5 * GRAVITY / VERTICAL_MIX
    dens_x = (scale * HALINE) * de[1] - (scale * THERMAL) * de[0]
    dens_y = (scale * HALINE) * dn[1] - (scale * THERMAL) * dn[0]
    acc_x, acc_y = acc
    grad = (None, None, acc_x + 0.5 * dens_x, acc_y + 0.5 * dens_y)
    turn = (None, None, coef("turn") * center[3], -coef("turn") * center[2])
    new = []
    for q in range(4):
        vertical = load(q, above_k, 0) + load(q, below_k, 0)
        if grad[q] is not None:
            vertical = vertical - grad[q]
        total = sums[q] + coef("mix") * vertical
        new.append(total if turn[q] is None else total + turn[q])
    return new, (acc_x + dens_x, acc_y + dens_y)


def ordered(flag, a, b):
    return jnp.where(flag, a, b), jnp.where(flag, b, a)


def padded(buf, count, levels, rows, q, k, value, north, south):
    at = (q * count + k) * (rows + 2 * PAD) + PAD
    field = q * levels + k
    buf[at : at + rows, :] = value
    buf[at + rows : at + rows + 1, :] = north[field : field + 1, :]
    buf[at - 1 : at, :] = south[field : field + 1, :]


def first_kernel(
    rows, levels, state, base, got_lon_a, got_lon_b, north, south, coef, side, top, now, wet_pad
):
    fields = 4 * levels
    even_lon = is_even("lon")
    wet = base[0:rows, :]
    mixing = base[rows : 2 * rows, :]
    coriolis = base[2 * rows + PAD : 3 * rows + PAD, :]
    lane = iota((rows, LANES), 1)
    wet_pad[PAD : PAD + rows, :] = wet
    wet_pad[PAD - 1 : PAD, :] = south[2 * fields : 2 * fields + 1, :]
    wet_pad[PAD + rows : PAD + rows + 1, :] = north[2 * fields : 2 * fields + 1, :]
    wet_n = wet_pad[PAD + 1 : PAD + 1 + rows, :]
    wet_s = wet_pad[PAD - 1 : PAD - 1 + rows, :]
    aux_e, aux_w = ordered(even_lon, got_lon_a[rows:, :], got_lon_b[rows:, :])
    wet_e = jnp.where(lane == LANES - 1, aux_e[:, 0:1], pltpu.roll(wet, LANES - 1, 1))
    wet_w = jnp.where(lane == 0, aux_w[:, 0:1], pltpu.roll(wet, 1, 1))
    made = coefficients(wet, (wet_e, wet_w, wet_n, wet_s), mixing, coriolis)
    for name in COEFFICIENTS:
        coef[place_of(name, rows)] = made[name]
    got_e, got_w = ordered(even_lon, got_lon_a[0:rows, :], got_lon_b[0:rows, :])
    side[...] = jnp.where((lane & 1) == 0, got_e, got_w)

    count = now.shape[0] // (4 * (rows + 2 * PAD))
    for q in range(4):
        for k in range(count):
            field = (q * levels + k) * rows
            padded(now, count, levels, rows, q, k, state[field : field + rows, :], north, south)
    none = jnp.zeros((rows, LANES), F32)
    acc = (none, none)
    for k in range(count - 1):
        new, acc = advance_level(
            k, count, levels, rows, now, side[...], lambda x: coef[place_of(x, rows)], acc
        )
        for q in range(4):
            at = (q * (count - 1) + k) * rows
            top[at : at + rows, :] = new[q]


def surface_kernel(
    rows, levels,
    state, base, col_map, row_map, coef, side, top, lon_a, lon_b, got_lon_a, got_lon_b, north, south,
    got_corner_a, got_corner_b, out_in, ids,
    side_new, north_new, south_new, out, later, stage, places, sem,
):
    fields = 4 * levels
    to_scalars = pltpu.make_async_copy(ids, places, sem)
    to_scalars.start()
    out[...] = out_in[...]
    even_lon = is_even("lon")
    wet = base[0:rows, :]
    table = base[2 * rows :, :]
    lane = iota((rows, LANES), 1)
    even = (lane & 1) == 0
    lane1 = iota((1, LANES), 1)
    even1 = (lane1 & 1) == 0

    corner_e, corner_w = ordered(even_lon, got_corner_a[...], got_corner_b[...])

    def corner(i):
        wets = corner_e[2 + i : 3 + i, 0:1], corner_w[2 + i : 3 + i, 1:2]
        return jnp.where(even1, corner_e[i : i + 1], corner_w[i : i + 1]), *wets

    corner_n, wet_ne, wet_nw = corner(0)
    corner_s, wet_se, wet_sw = corner(1)

    def spread(x, i):
        return jnp.broadcast_to(x[:, i : i + 1], (rows, LANES))

    aux_e, aux_w = ordered(even_lon, got_lon_a[rows:, :], got_lon_b[rows:, :])
    got_e, got_w = ordered(even_lon, got_lon_a[0:rows, :], got_lon_b[0:rows, :])
    sent_e, sent_w = ordered(even_lon, lon_a[0:rows, :], lon_b[0:rows, :])
    outer = jnp.where(even, pltpu.roll(got_e, LANES - 1, 1), pltpu.roll(got_w, 1, 1))
    inner = jnp.where(even, pltpu.roll(sent_e, LANES - 1, 1), pltpu.roll(sent_w, 1, 1))
    side_new[...] = advance_columns(
        side[...], outer, inner, corner_n, corner_s,
        (
            jnp.where(even, spread(aux_e, 0), spread(aux_w, 0)),
            jnp.where(even, spread(aux_e, 1), spread(aux_w, 1)),
            jnp.where(even, spread(wet, LANES - 1), spread(wet, 0)),
            jnp.where(even1, wet_ne, wet_nw),
            jnp.where(even1, wet_se, wet_sw),
        ),
        jnp.where(even, spread(aux_e, 2), spread(aux_w, 2)),
        table[PAD : PAD + rows], col_map[...],
    )

    field_lane = iota((fields, LANES), 1)
    field_id = iota((fields, LANES), 0)

    def to_sublanes(x, parity):
        here = field_lane == 2 * field_id + parity
        return jnp.sum(jnp.where(here, x, 0.0), axis=1, keepdims=True)

    parts = []
    for north_side, ref, ends, corner_wets, line, lat_row in (
        (True, north, corner_n, (wet_ne, wet_nw), rows - 1, PAD + rows),
        (False, south, corner_s, (wet_se, wet_sw), 0, PAD - 1),
    ):
        inside = state[pl.ds(line, fields, stride=rows), :]
        tail = ref[2 * fields :, :]
        pair = (ref[fields : 2 * fields, :], inside), (tail[1:2], wet[line : line + 1])
        (n, s), (wet_n, wet_s) = pair if north_side else [x[::-1] for x in pair]
        parts.append(
            (
                ref[0:fields, :], n, s, (to_sublanes(ends, 0), to_sublanes(ends, 1)),
                (tail[0:1], wet_n, wet_s, *corner_wets),
                tail[2:3], table[lat_row : lat_row + 1],
            )
        )
    north_new[...], south_new[...] = advance_rows(levels, parts, row_map[...])

    count = later.shape[0] // (4 * (rows + 2 * PAD))
    for q in range(4):
        for k in range(count):
            at = (q * count + k) * rows
            padded(
                later, count, levels, rows, q, k, top[at : at + rows, :], north_new, south_new
            )
    none = jnp.zeros((rows, LANES), F32)
    new, _ = advance_level(
        0, count, levels, rows, later, side_new[...], lambda x: coef[place_of(x, rows)], (none, none)
    )
    for q in range(4):
        stage[pl.ds(q, rows, stride=4), :] = new[q]
    to_scalars.wait()
    for r in range(rows):
        out[pl.ds(places[0, r], 4), :] = stage[4 * r : 4 * r + 4, :]


def main_kernel(
    rows, levels, chunks,
    state, coefs, side, side_new, north, south, north_new, south_new,
    tr_hbm, ve_hbm, now, later, tr_out, ve_out, sems,
):
    fields = 4 * levels
    pitch = rows + 2 * PAD
    for buf, n, s in ((now, north, south), (later, north_new, south_new)):
        buf[pl.ds(PAD - 1, fields, stride=pitch), :] = s[0:fields, :]
        buf[pl.ds(PAD + rows, fields, stride=pitch), :] = n[0:fields, :]

    def fill(f, carry):
        x = state[pl.ds(pl.multiple_of(f * rows, 8), rows), :]
        now[pl.ds(pl.multiple_of(f * pitch + PAD, 8), rows), :] = x
        return carry

    lax.fori_loop(0, fields, fill, 0, unroll=8)

    def coef(name):
        return coefs[place_of(name, rows)]

    def first(k, acc):
        new, acc = advance_level(k, levels, levels, rows, now, side[...], coef, acc)
        for q in range(4):
            place = pl.multiple_of((q * levels + k) * pitch + PAD, 8)
            later[pl.ds(place, rows), :] = new[q]
        return acc

    def second(k, acc):
        new, acc = advance_level(k, levels, levels, rows, later, side_new[...], coef, acc)
        for q in range(4):
            ref = tr_out if q < 2 else ve_out
            place = pl.multiple_of(((q % 2) * levels + k) * rows, 8)
            ref[pl.ds(place, rows), :] = new[q]
        return acc

    none = jnp.zeros((rows, LANES), F32)
    lax.fori_loop(0, levels, first, (none, none), unroll=2)
    acc = (none, none)
    size = levels // chunks
    copies = []
    for i in range(chunks):
        acc = lax.fori_loop(i * size, (i + 1) * size, second, acc, unroll=2)
        for src, dst in ((tr_out, tr_hbm), (ve_out, ve_hbm)):
            for q in range(2):
                start = (q * levels + i * size) * rows
                part = slice(start, start + size * rows)
                copy = pltpu.make_async_copy(src.at[part], dst.at[part], sems.at[len(copies)])
                copy.start()
                copies.append(copy)
    for copy in copies:
        copy.wait()


def reduce_kernel(devices, data, surface, cover):
    slot_rows = data.shape[0] // devices

    def rows_of(i):
        return data[pl.ds(i, devices, stride=slot_rows), :]

    width = LANES // CAP
    lines = rows_of(5 * CAP)
    named = (lines == (iota((devices, LANES), 1) % width).astype(F32)).astype(F32)
    to_rows, values = [], []
    for slot in range(CAP):
        to_rows.append(named[:, slot * width : slot * width + ATM_ROWS])
        parts = [rows_of(4 * slot + q) for q in range(4)] + [rows_of(4 * CAP + slot)]
        values.append(jnp.concatenate(parts, axis=1))
    totals = dot(
        jnp.concatenate(to_rows, axis=0), jnp.concatenate(values, axis=0), (((0,), (0,)), ((), ()))
    )
    ocean = totals[:, 4 * LANES :]
    cover[...] = ocean
    share = jnp.maximum(ocean, 1.0)
    for q in range(4):
        surface[q] = totals[:, q * LANES : (q + 1) * LANES] / share


def call(kernel, out_shape, limit=VMEM_LIMIT, **kwargs):
    return pl.pallas_call(
        kernel,
        out_shape=out_shape,
        compiler_params=pltpu.CompilerParams(vmem_limit_bytes=limit),
        **kwargs,
    )


def shaped(*shape, dtype=F32):
    return jax.ShapeDtypeStruct(shape, dtype)


def pairs_of(lon_count, lat_count):
    lon_a = [(i, i ^ 1) for i in range(lon_count)]
    lon_b = [(i, (i + 1 if i % 2 else i - 1) % lon_count) for i in range(lon_count)]
    lat_a, lat_b = [], []
    for i in range(lon_count):
        for a in range(lat_count):
            here = i * lat_count + a
            lat_a.append((here, i * lat_count + (a ^ 1)))
            if a == lat_count - 1:
                lat_b.append((here, (lon_count - 1 - i) * lat_count + a))
            elif a > 0:
                lat_b.append((here, here + 1 if a % 2 else here - 1))
    return lon_a, lon_b, lat_a, lat_b


def local(tracers, velocity, land_mask, mixing, owners, atm_row):
    levels = tracers.shape[1]
    rows, cols = land_mask.shape
    fields = 4 * levels
    lon_count, lat_count = lax.axis_size("lon"), lax.axis_size("lat")
    devices = lon_count * lat_count
    assert cols == LANES and rows % 8 == 0 and 2 * fields == LANES
    assert lon_count % 2 == 0 and lat_count % 2 == 0
    length = 2 * fields + 8
    pitch = rows + 2 * PAD
    flat = 2 * levels * rows
    hbm = pl.BlockSpec(memory_space=pltpu.HBM)
    smem = pl.BlockSpec(memory_space=pltpu.SMEM)
    vmem = pl.BlockSpec(memory_space=pltpu.VMEM)

    deep = (2 * levels, rows, cols)
    lat_a, lat_b = call(
        functools.partial(edge_kernel, rows, fields),
        [shaped(length, cols)] * 2,
        limit=VMEM_ALL,
        in_specs=[hbm] * 4,
        scratch_shapes=[
            pltpu.VMEM((2, fields, 8, cols), F32),
            pltpu.VMEM((rows, cols), jnp.int32),
            pltpu.VMEM((rows, cols), F32),
            pltpu.SemaphoreType.DMA((6,)),
        ],
    )(tracers.reshape(deep), velocity.reshape(deep), land_mask, mixing)
    swaps = pairs_of(lon_count, lat_count)
    got_lat_b = lax.ppermute(lat_b, ("lon", "lat"), swaps[3])
    got_lat_a = lax.ppermute(lat_a, ("lon", "lat"), swaps[2])

    tr, ve = tracers.reshape(flat, cols), velocity.reshape(flat, cols)
    lon_a, lon_b = call(
        functools.partial(pack_kernel, rows, fields),
        [shaped(2 * rows, cols)] * 2,
        in_specs=[vmem] * 4,
    )(tr, ve, land_mask, mixing)
    got_lon_a = lax.ppermute(lon_a, "lon", swaps[0])
    got_lon_b = lax.ppermute(lon_b, "lon", swaps[1])

    slot_rows = 5 * CAP + 1
    state, base, col_map, row_map, outgoing, ids = call(
        functools.partial(prepare_kernel, rows, levels, devices),
        [
            shaped(fields * rows, cols),
            shaped(2 * rows + pitch, cols),
            shaped(3 * cols, cols),
            shaped(fields + levels, cols),
            shaped(devices * slot_rows, cols),
            shaped(8, cols, dtype=jnp.int32),
        ],
        in_specs=[vmem] * 4 + [smem] * 2,
        scratch_shapes=[pltpu.SMEM((devices,), jnp.int32)],
    )(tr, ve, land_mask, mixing, owners.reshape(rows), atm_row)

    north, south, corners = call(
        functools.partial(corner_kernel, lat_count, fields),
        [shaped(length, cols), shaped(length, cols), shaped(8, cols)],
    )(got_lat_a, got_lat_b)
    got_corner_a = lax.ppermute(corners, "lon", swaps[0])
    got_corner_b = lax.ppermute(corners, "lon", swaps[1])

    count = min(3, levels)
    coefs, side, top = call(
        functools.partial(first_kernel, rows, levels),
        [
            shaped(len(COEFFICIENTS) * rows, cols),
            shaped(rows, cols),
            shaped(4 * (count - 1) * rows, cols),
        ],
        scratch_shapes=[
            pltpu.VMEM((4 * count * pitch, cols), F32),
            pltpu.VMEM((pitch, cols), F32),
        ],
    )(state, base, got_lon_a, got_lon_b, north, south)

    side_new, north_new, south_new, outgoing = call(
        functools.partial(surface_kernel, rows, levels),
        [
            shaped(rows, cols),
            shaped(fields, cols),
            shaped(fields, cols),
            shaped(devices * slot_rows, cols),
        ],
        scratch_shapes=[
            pltpu.VMEM((4 * (count - 1) * pitch, cols), F32),
            pltpu.VMEM((4 * rows, cols), F32),
            pltpu.SMEM((8, cols), jnp.int32),
            pltpu.SemaphoreType.DMA,
        ],
    )(state, base, col_map, row_map, coefs, side, top, lon_a, lon_b, got_lon_a, got_lon_b, north,
      south, got_corner_a, got_corner_b, outgoing, ids)
    incoming = lax.all_to_all(
        outgoing.reshape(devices, slot_rows, 1, cols), ("lon", "lat"), 0, 0, tiled=True
    ).reshape(devices * slot_rows, cols)

    chunks = 4
    tr_out, ve_out = call(
        functools.partial(main_kernel, rows, levels, chunks),
        [shaped(flat, cols), shaped(flat, cols)],
        in_specs=[vmem] * 8,
        out_specs=[hbm] * 2,
        scratch_shapes=[
            pltpu.VMEM((fields * pitch, cols), F32),
            pltpu.VMEM((fields * pitch, cols), F32),
            pltpu.VMEM((flat, cols), F32),
            pltpu.VMEM((flat, cols), F32),
            pltpu.SemaphoreType.DMA((4 * chunks,)),
        ],
        cost_estimate=pl.CostEstimate(
            flops=80 * fields * rows * cols, bytes_accessed=5 << 20, transcendentals=0
        ),
    )(state, coefs, side, side_new, north, south, north_new, south_new)
    surface, cover = call(
        functools.partial(reduce_kernel, devices),
        [shaped(4, ATM_ROWS, cols), shaped(ATM_ROWS, cols)],
    )(incoming)
    shape = (2, levels, rows, cols)
    return tr_out.reshape(shape), ve_out.reshape(shape), surface, cover


def solution(mesh):
    in_specs = (
        P(None, None, "lat", "lon"),
        P(None, None, "lat", "lon"),
        P("lat", "lon"),
        P("lat", "lon"),
        P(("lon", "lat"), None),
        P(("lon", "lat")),
    )
    out_specs = (
        P(None, None, "lat", "lon"),
        P(None, None, "lat", "lon"),
        P(None, ("lon", "lat"), None),
        P(("lon", "lat"), None),
    )
    return jax.shard_map(local, mesh=mesh, in_specs=in_specs, out_specs=out_specs, check_vma=False)
```

```python
import functools
import math

import jax
import jax.numpy as jnp
from jax import lax
from jax.experimental import pallas as pl
from jax.experimental.pallas import tpu as pltpu
from jax.sharding import PartitionSpec as P

ATM_ROWS = 32
CAP = 2

THERMAL = 0.2
HALINE = 0.15
GRAVITY = 0.2
TIMESTEP = 0.8
VERTICAL_MIX = 0.1
VISCOSITY = 0.2
CORIOLIS_MAX = 0.3

LANES = 128
PAD = 8
EXACT = lax.Precision.HIGHEST
F32 = jnp.float32
VMEM_LIMIT = 32 * 1024 * 1024
VMEM_ALL = 62 * 1024 * 1024


def iota(shape, dim):
    return lax.broadcasted_iota(jnp.int32, shape, dim)


def dot(a, b, dims=(((1,), (0,)), ((), ()))):
    return lax.dot_general(a, b, dims, precision=EXACT, preferred_element_type=F32)


def is_even(axis):
    return lax.rem(lax.axis_index(axis), 2) == 0


def start_copies(pairs, sems):
    copies = [pltpu.make_async_copy(src, dst, sems.at[i]) for i, (src, dst) in enumerate(pairs)]
    for copy in copies:
        copy.start()
    return copies


def edge_kernel(rows, fields, tr_hbm, ve_hbm, mask_hbm, mix_hbm, lat_a, lat_b, edges, mask, mix, sems):
    half = fields // 2
    pairs = [(mask_hbm, mask), (mix_hbm, mix)]
    for n, src in enumerate((tr_hbm, ve_hbm)):
        for side, first in enumerate((0, rows - 8)):
            part = edges.at[side, n * half : (n + 1) * half]
            pairs.append((src.at[:, first : first + 8, :], part))
    for copy in start_copies(pairs, sems):
        copy.wait()
    flat = edges.reshape(2 * fields * 8, LANES)
    even = is_even("lat")
    top = ((rows - 1, 8 * fields + 7), (rows - 2, 8 * fields + 6))
    bottom = ((0, 0), (1, 1))
    for buf, first, second in ((lat_a, top, bottom), (lat_b, bottom, top)):
        (near, near_at), (far, far_at) = [
            [jnp.where(even, x, y) for x, y in zip(one, other)] for one, other in zip(first, second)
        ]
        wet_near = mask[pl.ds(near, 1), :].astype(F32)
        wet_far = mask[pl.ds(far, 1), :].astype(F32)
        buf[0:fields, :] = flat[pl.ds(near_at, fields, stride=8), :] * wet_near
        buf[fields : 2 * fields, :] = flat[pl.ds(far_at, fields, stride=8), :] * wet_far
        buf[2 * fields : 2 * fields + 8, :] = jnp.zeros((8, LANES), F32)
        buf[2 * fields : 2 * fields + 1, :] = wet_near
        buf[2 * fields + 1 : 2 * fields + 2, :] = wet_far
        buf[2 * fields + 2 : 2 * fields + 3, :] = mix[pl.ds(near, 1), :]


def pack_kernel(rows, fields, tr, ve, mask, mix, cols):
    half = fields // 2
    wet = mask[...].astype(F32)
    lane = iota((rows, LANES), 1)
    pair = lane >> 1

    def columns(ref, base):
        def body(f, carry):
            to_east, to_west = carry
            x = ref[pl.ds(pl.multiple_of(f * rows, rows), rows), :]
            keep = pair == base + f
            low = 2 * (base + f)
            to_east = jnp.where(keep, pltpu.roll(x, (low + 2) & (LANES - 1), 1), to_east)
            to_west = jnp.where(keep, pltpu.roll(x, low, 1), to_west)
            return to_east, to_west

        return body

    carry = (jnp.zeros((rows, LANES), F32), jnp.zeros((rows, LANES), F32))
    for ref, base in ((tr, 0), (ve, half)):
        carry = lax.fori_loop(0, half, columns(ref, base), carry, unroll=8)
    def spread(x, i):
        return jnp.broadcast_to(x[:, i : i + 1], (rows, LANES))

    odd = (lane & 1) == 1
    cols[0:rows, :] = carry[0] * jnp.where(odd, spread(wet, LANES - 1), spread(wet, LANES - 2))
    cols[rows : 2 * rows, :] = carry[1] * jnp.where(odd, spread(wet, 1), spread(wet, 0))
    cols[2 * rows :, :] = jnp.zeros((8, LANES), F32)
    row = iota((rows, LANES), 0)
    mixing = mix[...]
    for i, (near, far) in enumerate(((LANES - 1, LANES - 2), (0, 1))):
        line = jnp.zeros((rows, LANES), F32)
        for part, column in enumerate((wet[:, near], wet[:, far], mixing[:, near])):
            line = jnp.where(lane == part * rows + row, column[:, None], line)
        cols[2 * rows + i : 2 * rows + i + 1, :] = jnp.sum(line, axis=0, keepdims=True)


def prepare_kernel(
    rows, levels, devices, tr, ve, mask, mix, own, atm_row,
    state, base, col_map, row_map, out, ids, used,
):
    fields = 4 * levels
    half = fields // 2
    wet = mask[...].astype(F32)
    base[0:rows, :] = wet
    base[rows : 2 * rows, :] = mix[...]
    for ref, first in ((tr, 0), (ve, half)):

        def fill(f, carry, ref=ref, first=first):
            x = ref[pl.ds(pl.multiple_of(f * rows, 8), rows), :] * wet
            state[pl.ds(pl.multiple_of((first + f) * rows, 8), rows), :] = x
            return carry

        lax.fori_loop(0, half, fill, 0, unroll=8)

    total = lax.axis_size("lat") * rows
    latitude = lax.axis_index("lat") * rows - PAD + iota((rows + 2 * PAD, LANES), 0)
    latitude = jnp.where(latitude >= total, 2 * total - 1 - latitude, latitude).astype(F32)
    table = CORIOLIS_MAX * jnp.sin(math.pi * (-0.43 + 0.93 * (latitude + 0.5) / total))
    base[2 * rows :, :] = table

    span = 2 * levels
    src, dst = iota((LANES, LANES), 0), iota((LANES, LANES), 1)
    src_group, dst_group = src // span, dst // span
    src_level, dst_level = (src // 2) % levels, (dst // 2) % levels
    same_side = (src & 1) == (dst & 1)
    mixes = VERTICAL_MIX * level_matrix("mix", levels, src_level, dst_level)
    press = level_matrix("pressure", levels, src_level, dst_level) * density_weight(src_group)
    col_map[0:LANES, :] = jnp.where(same_side & (src_group == dst_group), mixes, 0.0)
    col_map[LANES : 2 * LANES, :] = jnp.where(same_side & (dst_group == 2), -press, 0.0)
    col_map[2 * LANES :, :] = jnp.where(same_side & (dst_group == 3), -press, 0.0)

    dst, src = iota((fields, fields), 0), iota((fields, fields), 1)
    mixes = VERTICAL_MIX * level_matrix("mix", levels, src % levels, dst % levels)
    row_map[0:fields, 0:fields] = jnp.where(dst // levels == src // levels, mixes, 0.0)
    dst, src = iota((levels, fields), 0), iota((levels, fields), 1)
    press = level_matrix("pressure", levels, src % levels, dst) * density_weight(src // levels)
    row_map[fields:, 0:fields] = press

    slot_rows = out.shape[0] // devices

    def clear(d, carry):
        used[d] = 0
        return carry

    lax.fori_loop(0, devices, clear, 0, unroll=8)
    out[...] = jnp.zeros(out.shape, F32)
    lane1 = iota((1, LANES), 1)
    places = jnp.zeros((1, LANES), jnp.int32)
    for r in range(rows):
        owner = own[r]
        slot = used[owner]
        used[owner] = slot + 1
        start = owner * slot_rows
        places = jnp.where(lane1 == r, start + 4 * slot, places)
        out[pl.ds(start + 4 * CAP + slot, 1), :] = base[r : r + 1, :]
        line = out[pl.ds(start + 5 * CAP, 1), :]
        target = jnp.full((1, LANES), atm_row[r], jnp.int32).astype(F32)
        out[pl.ds(start + 5 * CAP, 1), :] = jnp.where(lane1 // (LANES // CAP) == slot, target, line)
    ids[...] = jnp.zeros(ids.shape, jnp.int32)
    ids[0:1, :] = places


def corner_kernel(lat_count, lon_count, rows, fields, got_a, got_b, cols, north, south, message):
    fold = lax.axis_index("lat") == lat_count - 1
    even = is_even("lat")
    a, b = got_a[...], got_b[...]
    straight = jnp.where(even, a, b)
    south[...] = jnp.where(even, b, a)
    back = LANES - 1 - iota((8, LANES), 1)
    flipped = jnp.concatenate(
        [
            jnp.take_along_axis(straight[i : i + 8], back, axis=1)
            * (-1.0 if i < 2 * fields and i % fields >= fields // 2 else 1.0)
            for i in range(0, straight.shape[0], 8)
        ],
        axis=0,
    )
    north[...] = jnp.where(fold, flipped, straight)
    lane, field = iota((fields, LANES), 1), iota((fields, LANES), 0)
    lane1 = iota((1, LANES), 1)
    corners = []
    for ref in (north, south):
        near = ref[0:fields, :]
        ends = jnp.where(
            lane == 2 * field, near[:, 0:1], jnp.where(lane == 2 * field + 1, near[:, LANES - 1 :], 0.0)
        )
        corners.append(jnp.sum(ends, axis=0, keepdims=True))
    for ref in (north, south):
        wet = ref[2 * fields : 2 * fields + 1, :]
        corners.append(jnp.where(lane1 == 0, wet[:, 0:1], wet[:, LANES - 1 :]))
    message[...] = jnp.zeros(message.shape, F32)
    me = lax.axis_index("lon")
    for i, step in enumerate((1, lon_count - 1)):
        start = pl.multiple_of(lax.rem(me + step, lon_count) * (rows + 8), 8)
        message[pl.ds(start, rows), :] = cols[i * rows : (i + 1) * rows, :]
        extra = [*corners, cols[2 * rows + i : 2 * rows + i + 1, :], jnp.zeros((3, LANES), F32)]
        message[pl.ds(start + rows, 8), :] = jnp.concatenate(extra, axis=0)


class Sides:
    def __init__(self, rows, lon_count, got, cols):
        me = lax.axis_index("lon")
        lane, row = iota((rows, LANES), 1), iota((rows, LANES), 0)
        self.even = (lane & 1) == 0
        self.even1 = (iota((1, LANES), 1) & 1) == 0
        halves, extras = [], []
        for step in (1, lon_count - 1):
            start = pl.multiple_of(lax.rem(me + step, lon_count) * (rows + 8), 8)
            halves.append(got[pl.ds(start, rows), :])
            extras.append(got[pl.ds(start + rows, 8), :])
        self.got, self.extras, self.cols, self.rows = halves, extras, cols, rows
        self.columns = [
            [
                jnp.sum(jnp.where(lane == i * rows + row, x[4:5], 0.0), axis=1, keepdims=True)
                for i in range(3)
            ]
            for x in extras
        ]

    def near(self):
        return jnp.where(self.even, *self.got)

    def far_and_inner(self):
        east, west = self.got
        mine_e, mine_w = self.cols[0 : self.rows, :], self.cols[self.rows : 2 * self.rows, :]
        far = jnp.where(self.even, pltpu.roll(east, LANES - 1, 1), pltpu.roll(west, 1, 1))
        inner = jnp.where(self.even, pltpu.roll(mine_e, LANES - 1, 1), pltpu.roll(mine_w, 1, 1))
        return far, inner

    def corner(self, i):
        east, west = self.extras
        wets = east[2 + i : 3 + i, 0:1], west[2 + i : 3 + i, 1:2]
        return jnp.where(self.even1, east[i : i + 1], west[i : i + 1]), *wets

    def lanes(self, i):
        return jnp.where(self.even, self.columns[0][i], self.columns[1][i])


def level_matrix(kind, levels, source, target):
    if kind == "mix":
        above = (source == jnp.maximum(target - 1, 0)).astype(F32)
        below = (source == jnp.minimum(target + 1, levels - 1)).astype(F32)
        return above + below - 2.0 * (source == target).astype(F32)
    full = jnp.where(source < target, 1.0, jnp.where(source == target, 0.5, 0.0))
    return (0.5 * GRAVITY) * full


def density_weight(group):
    return jnp.where(group == 0, -THERMAL, jnp.where(group == 1, HALINE, 0.0)).astype(F32)


def advance_columns(sides, wet, coriolis, level_map):
    rows = wet.shape[0]
    mid = sides.near()
    outer, inner = sides.far_and_inner()
    (corner_n, wet_ne, wet_nw), (corner_s, wet_se, wet_sw) = sides.corner(0), sides.corner(1)
    wet_mid, wet_out = sides.lanes(0), sides.lanes(1)
    wet_in = jnp.where(sides.even, wet[:, LANES - 1 :], wet[:, 0:1])
    wet_corner_n = jnp.where(sides.even1, wet_ne, wet_nw)
    wet_corner_s = jnp.where(sides.even1, wet_se, wet_sw)
    mixing = sides.lanes(2)
    lane = iota((rows, LANES), 1)
    row = iota((rows, LANES), 0)
    span = LANES // 4
    group = lane // span

    def ends(outside, inside):
        return jnp.where(sides.even, outside, inside), jnp.where(sides.even, inside, outside)

    def shifted(x, north, south):
        n = jnp.where(row == rows - 1, north, pltpu.roll(x, rows - 1, 0))
        s = jnp.where(row == 0, south, pltpu.roll(x, 1, 0))
        return n, s

    e, w = ends(outer, inner)
    wet_e, wet_w = ends(wet_out, wet_in)
    n, s = shifted(mid, corner_n, corner_s)
    wet_n, wet_s = shifted(wet_mid, wet_corner_n, wet_corner_s)
    lap = wet_e * (e - mid) + wet_w * (w - mid) + wet_n * (n - mid) + wet_s * (s - mid)
    de, dn = e - w, n - s
    one, two, three = (pltpu.roll(mid, i * span, 1) for i in (1, 2, 3))

    def pick(a, b, c, d):
        return jnp.where(group == 0, a, jnp.where(group == 1, b, jnp.where(group == 2, c, d)))

    u = pick(two, three, mid, one)
    v = pick(one, two, three, mid)
    adv = 0.5 * (u * de + v * dn)
    zero = jnp.zeros_like(mid)
    if level_map is None:
        grad_x = HALINE * pltpu.roll(de, span, 1) - THERMAL * pltpu.roll(de, 2 * span, 1)
        grad_y = HALINE * pltpu.roll(dn, 2 * span, 1) - THERMAL * pltpu.roll(dn, 3 * span, 1)
        linear = VERTICAL_MIX * (pltpu.roll(mid, LANES - 2, 1) - mid)
        linear = linear - (0.25 * GRAVITY) * pick(zero, zero, grad_x, grad_y)
    else:
        linear = dot(jnp.concatenate([mid, de, dn], axis=1), level_map)
    turn = pick(zero, zero, coriolis * v, -coriolis * u)
    kappa = jnp.where(group < 2, mixing, VISCOSITY)
    tend = turn - adv + kappa * lap + linear
    return wet_mid * (mid + TIMESTEP * tend)


def advance_rows(levels, parts, level_map):
    fields = 4 * levels
    lane = iota((fields, LANES), 1)
    lane8 = iota((8, LANES), 1)

    def sides(x, east, west, at):
        e = jnp.where(at == LANES - 1, east, pltpu.roll(x, LANES - 1, 1))
        w = jnp.where(at == 0, west, pltpu.roll(x, 1, 1))
        return e, w

    mids, gaps = [], []
    for mid, n, s, (corner_e, corner_w), *_ in parts:
        e, w = sides(mid, corner_e, corner_w, lane)
        mids.append((mid, e, w, n, s))
        gaps += [e - w, n - s]
    vertical = dot(level_map[0:fields, 0:fields], jnp.concatenate([m[0] for m in mids], axis=1))
    grads = dot(level_map[fields:, 0:fields], jnp.concatenate(gaps, axis=1))
    done = []
    for i, (mid, e, w, n, s) in enumerate(mids):
        *_, wets, mixing, coriolis = parts[i]
        wet_mid, wet_n, wet_s, wet_corner_e, wet_corner_w = wets
        wet_e, wet_w = sides(
            jnp.broadcast_to(wet_mid, (8, LANES)), wet_corner_e, wet_corner_w, lane8
        )
        lap = wet_e[0:1] * (e - mid) + wet_w[0:1] * (w - mid)
        lap = lap + wet_n * (n - mid) + wet_s * (s - mid)
        de, dn = gaps[2 * i], gaps[2 * i + 1]
        u, v = mid[2 * levels : 3 * levels], mid[3 * levels :]
        adv = jnp.concatenate([u] * 4, axis=0) * de + jnp.concatenate([v] * 4, axis=0) * dn
        grad_x = grads[:, 2 * i * LANES : (2 * i + 1) * LANES]
        grad_y = grads[:, (2 * i + 1) * LANES : (2 * i + 2) * LANES]
        zero = jnp.zeros((2 * levels, LANES), F32)
        turn = jnp.concatenate([zero, coriolis * v - grad_x, -coriolis * u - grad_y], axis=0)
        kappa = jnp.concatenate(
            [jnp.broadcast_to(mixing, (2 * levels, LANES)), jnp.full(zero.shape, VISCOSITY)],
            axis=0,
        )
        tend = turn - 0.5 * adv + kappa * lap + vertical[:, i * LANES : (i + 1) * LANES]
        done.append(wet_mid * (mid + TIMESTEP * tend))
    return done


COEFFICIENTS = ("te", "tw", "tn", "ts", "tc", "ve", "vw", "vn", "vs", "vc", "adv", "mix", "turn")


def place_of(name, rows):
    i = COEFFICIENTS.index(name)
    return slice(i * rows, (i + 1) * rows)


def coefficients(wet, neighbours, mixing, coriolis):
    made = {}
    for name, kappa in (("t", mixing), ("v", VISCOSITY)):
        rest = wet * (1.0 - 2.0 * TIMESTEP * VERTICAL_MIX)
        for side, wet_n in zip("ewns", neighbours):
            made[name + side] = TIMESTEP * kappa * wet * wet_n
            rest = rest - made[name + side]
        made[name + "c"] = rest
    made["adv"] = (0.5 * TIMESTEP) * wet
    made["mix"] = (TIMESTEP * VERTICAL_MIX) * wet
    made["turn"] = TIMESTEP * coriolis * wet
    return made


def advance_level(k, count, levels, rows, src, sides, coef, acc):
    pitch = rows + 2 * PAD
    lane = iota((rows, LANES), 1)
    first, last = lane == 0, lane == LANES - 1
    above_k = jnp.maximum(k - 1, 0)
    below_k = jnp.minimum(k + 1, levels - 1)

    def load(q, level, shift):
        return src[pl.ds((q * count + level) * pitch + PAD + shift, rows), :]

    def base(q):
        return pl.multiple_of((q * count + k) * pitch + PAD, 8)

    center = [load(q, k, 0) for q in range(4)]
    u, v = coef("adv") * center[2], coef("adv") * center[3]
    sums, de, dn = [], [], []
    for q in range(4):
        c = center[q]
        n, s = load(q, k, 1), load(q, k, -1)
        edge = pltpu.roll(sides, (LANES - 1 - 2 * (q * levels + k)) & (LANES - 1), 1)
        e = jnp.where(last, edge, pltpu.roll(c, LANES - 1, 1))
        w = jnp.where(first, edge, pltpu.roll(c, 1, 1))
        kind = "t" if q < 2 else "v"
        lap = coef(kind + "c") * c + coef(kind + "e") * e + coef(kind + "w") * w
        lap = lap + coef(kind + "n") * n + coef(kind + "s") * s
        de.append(e - w)
        dn.append(n - s)
        sums.append(lap - (u * de[q] + v * dn[q]))
    scale = 0.5 * GRAVITY / VERTICAL_MIX
    dens_x = (scale * HALINE) * de[1] - (scale * THERMAL) * de[0]
    dens_y = (scale * HALINE) * dn[1] - (scale * THERMAL) * dn[0]
    acc_x, acc_y = acc
    grad = (None, None, acc_x + 0.5 * dens_x, acc_y + 0.5 * dens_y)
    turn = (None, None, coef("turn") * center[3], -coef("turn") * center[2])
    new = []
    for q in range(4):
        vertical = load(q, above_k, 0) + load(q, below_k, 0)
        if grad[q] is not None:
            vertical = vertical - grad[q]
        total = sums[q] + coef("mix") * vertical
        new.append(total if turn[q] is None else total + turn[q])
    return new, (acc_x + dens_x, acc_y + dens_y)


def advance_top_rows(levels, sides, north, south, state, wet, rows, table):
    fields = 4 * levels

    def both(a, b):
        return jnp.concatenate([a, b], axis=0)

    def rows_at(first):
        return both(
            north[pl.ds(first, 4, stride=levels), :], south[pl.ds(first, 4, stride=levels), :]
        )

    lane, row = iota((8, LANES), 1), iota((8, LANES), 0)
    upper = row < 4
    field = row & 3
    inside_n = state[pl.ds(rows - 1, 4, stride=levels * rows), :]
    inside_s = state[pl.ds(0, 4, stride=levels * rows), :]
    mid, below, outer = rows_at(0), rows_at(1), rows_at(fields)
    n = both(outer[0:4], inside_s)
    s = both(inside_n, outer[4:8])
    (corner_n, wet_ne, wet_nw), (corner_s, wet_se, wet_sw) = sides.corner(0), sides.corner(1)
    corner = jnp.where(upper, corner_n, corner_s)
    at = 2 * levels * field

    def end(parity):
        return jnp.sum(jnp.where(lane == at + parity, corner, 0.0), axis=1, keepdims=True)

    def west_east(x, east, west):
        return (
            jnp.where(lane == LANES - 1, east, pltpu.roll(x, LANES - 1, 1)),
            jnp.where(lane == 0, west, pltpu.roll(x, 1, 1)),
        )

    def tail(i):
        place = slice(2 * fields + i, 2 * fields + i + 1)
        return north[place, :], south[place, :]

    e, w = west_east(mid, end(0), end(1))
    wet_mid = jnp.where(upper, *tail(0))
    wet_e, wet_w = west_east(
        wet_mid, jnp.where(upper, wet_ne, wet_se), jnp.where(upper, wet_nw, wet_sw)
    )
    out_n, out_s = tail(1)
    wet_n = jnp.where(upper, out_n, wet[0:1])
    wet_s = jnp.where(upper, wet[rows - 1 : rows], out_s)
    lap = wet_e * (e - mid) + wet_w * (w - mid) + wet_n * (n - mid) + wet_s * (s - mid)
    de, dn = e - w, n - s

    def of(x, i):
        return jnp.where(upper, x[i : i + 1], x[4 + i : 5 + i])

    u, v = of(mid, 2), of(mid, 3)
    coriolis = jnp.where(upper, table[PAD + rows : PAD + rows + 1], table[PAD - 1 : PAD])
    grad_x = (0.25 * GRAVITY) * (HALINE * of(de, 1) - THERMAL * of(de, 0))
    grad_y = (0.25 * GRAVITY) * (HALINE * of(dn, 1) - THERMAL * of(dn, 0))
    turn = jnp.where(
        field < 2, 0.0, jnp.where(field == 2, coriolis * v - grad_x, -coriolis * u - grad_y)
    )
    kappa = jnp.where(field < 2, jnp.where(upper, *tail(2)), VISCOSITY)
    tend = turn - 0.5 * (u * de + v * dn) + kappa * lap + VERTICAL_MIX * (below - mid)
    return wet_mid * (mid + TIMESTEP * tend)


def surface_kernel(
    rows, levels, lon_count,
    state, base, cols, got, north, south, out_in, ids,
    coef, side, out, now, later, wet_pad, stage, places, sem,
):
    fields = 4 * levels
    pitch = rows + 2 * PAD
    to_scalars = pltpu.make_async_copy(ids, places, sem)
    to_scalars.start()
    out[...] = out_in[...]
    wet = base[0:rows, :]
    mixing = base[rows : 2 * rows, :]
    table = base[2 * rows :, :]
    coriolis = table[PAD : PAD + rows]
    lane = iota((rows, LANES), 1)
    sides = Sides(rows, lon_count, got, cols)
    wet_pad[PAD : PAD + rows, :] = wet
    wet_pad[PAD - 1 : PAD, :] = south[2 * fields : 2 * fields + 1, :]
    wet_pad[PAD + rows : PAD + rows + 1, :] = north[2 * fields : 2 * fields + 1, :]
    wet_n = wet_pad[PAD + 1 : PAD + 1 + rows, :]
    wet_s = wet_pad[PAD - 1 : PAD - 1 + rows, :]
    wet_e = jnp.where(lane == LANES - 1, sides.columns[0][0], pltpu.roll(wet, LANES - 1, 1))
    wet_w = jnp.where(lane == 0, sides.columns[1][0], pltpu.roll(wet, 1, 1))
    made = coefficients(wet, (wet_e, wet_w, wet_n, wet_s), mixing, coriolis)
    for name in COEFFICIENTS:
        coef[place_of(name, rows)] = made[name]
    near = sides.near()
    side[...] = near

    count = now.shape[0] // (4 * pitch)
    for q in range(4):
        for k in range(count):
            field = (q * levels + k) * rows
            at = (q * count + k) * pitch + PAD
            now[at : at + rows, :] = state[field : field + rows, :]
            now[at + rows : at + rows + 1, :] = north[q * levels + k : q * levels + k + 1, :]
            now[at - 1 : at, :] = south[q * levels + k : q * levels + k + 1, :]

    def read(name):
        return coef[place_of(name, rows)]

    none = jnp.zeros((rows, LANES), F32)
    acc = (none, none)
    edge_rows = advance_top_rows(levels, sides, north, south, state, wet, rows, table)
    edge_cols = advance_columns(sides, wet, coriolis, None)
    for k in range(count - 1):
        new, acc = advance_level(k, count, levels, rows, now, near, read, acc)
        for q in range(4):
            at = (q * count + k) * pitch + PAD
            later[at : at + rows, :] = new[q]
            if k == 0:
                later[at + rows : at + rows + 1, :] = edge_rows[q : q + 1]
                later[at - 1 : at, :] = edge_rows[4 + q : 5 + q]
    new, _ = advance_level(0, count, levels, rows, later, edge_cols, read, (none, none))
    for q in range(4):
        stage[pl.ds(q, rows, stride=4), :] = new[q]
    to_scalars.wait()
    for r in range(rows):
        out[pl.ds(places[0, r], 4), :] = stage[4 * r : 4 * r + 4, :]


def halo_after_first(rows, levels, sides, north, south, state, wet, table, col_map, row_map):
    fields = 4 * levels
    side_new = advance_columns(sides, wet, table[PAD : PAD + rows], col_map)
    lane, field = iota((fields, LANES), 1), iota((fields, LANES), 0)

    def to_sublanes(x, parity):
        here = lane == 2 * field + parity
        return jnp.sum(jnp.where(here, x, 0.0), axis=1, keepdims=True)

    parts = []
    for north_side, ref, line, lat_row in (
        (True, north, rows - 1, PAD + rows),
        (False, south, 0, PAD - 1),
    ):
        corner, *corner_wets = sides.corner(0 if north_side else 1)
        inside = state[pl.ds(line, fields, stride=rows), :]
        tail = ref[2 * fields :, :]
        pair = (ref[fields : 2 * fields, :], inside), (tail[1:2], wet[line : line + 1])
        (n, s), (wet_n, wet_s) = pair if north_side else [x[::-1] for x in pair]
        parts.append(
            (
                ref[0:fields, :], n, s, (to_sublanes(corner, 0), to_sublanes(corner, 1)),
                (tail[0:1], wet_n, wet_s, *corner_wets),
                tail[2:3], table[lat_row : lat_row + 1],
            )
        )
    return side_new, *advance_rows(levels, parts, row_map)


def main_kernel(
    rows, levels, lon_count, chunks,
    state, base, cols, got, north, south, col_map, row_map, coefs, side,
    tr_hbm, ve_hbm, now, later, side_new, tr_out, ve_out, sems,
):
    fields = 4 * levels
    pitch = rows + 2 * PAD
    sides = Sides(rows, lon_count, got, cols)
    side_new[...], north_new, south_new = halo_after_first(
        rows, levels, sides, north, south, state, base[0:rows, :], base[2 * rows :, :],
        col_map[...], row_map[...],
    )
    edges = (now, north[0:fields, :], south[0:fields, :]), (later, north_new, south_new)
    for buf, n, s in edges:
        buf[pl.ds(PAD - 1, fields, stride=pitch), :] = s
        buf[pl.ds(PAD + rows, fields, stride=pitch), :] = n

    def fill(f, carry):
        x = state[pl.ds(pl.multiple_of(f * rows, 8), rows), :]
        now[pl.ds(pl.multiple_of(f * pitch + PAD, 8), rows), :] = x
        return carry

    lax.fori_loop(0, fields, fill, 0, unroll=8)

    def coef(name):
        return coefs[place_of(name, rows)]

    def first(k, acc):
        new, acc = advance_level(k, levels, levels, rows, now, side[...], coef, acc)
        for q in range(4):
            place = pl.multiple_of((q * levels + k) * pitch + PAD, 8)
            later[pl.ds(place, rows), :] = new[q]
        return acc

    def second(k, acc):
        new, acc = advance_level(k, levels, levels, rows, later, side_new[...], coef, acc)
        for q in range(4):
            ref = tr_out if q < 2 else ve_out
            place = pl.multiple_of(((q % 2) * levels + k) * rows, 8)
            ref[pl.ds(place, rows), :] = new[q]
        return acc

    none = jnp.zeros((rows, LANES), F32)
    lax.fori_loop(0, levels, first, (none, none), unroll=2)
    acc = (none, none)
    size = levels // chunks
    copies = []
    for i in range(chunks):
        acc = lax.fori_loop(i * size, (i + 1) * size, second, acc, unroll=2)
        for src, dst in ((tr_out, tr_hbm), (ve_out, ve_hbm)):
            for q in range(2):
                start = (q * levels + i * size) * rows
                part = slice(start, start + size * rows)
                copy = pltpu.make_async_copy(src.at[part], dst.at[part], sems.at[len(copies)])
                copy.start()
                copies.append(copy)
    for copy in copies:
        copy.wait()


def reduce_kernel(devices, data, surface, cover):
    slot_rows = data.shape[0] // devices

    def rows_of(i):
        return data[pl.ds(i, devices, stride=slot_rows), :]

    width = LANES // CAP
    lines = rows_of(5 * CAP)
    named = (lines == (iota((devices, LANES), 1) % width).astype(F32)).astype(F32)
    to_rows, values = [], []
    for slot in range(CAP):
        to_rows.append(named[:, slot * width : slot * width + ATM_ROWS])
        parts = [rows_of(4 * slot + q) for q in range(4)] + [rows_of(4 * CAP + slot)]
        values.append(jnp.concatenate(parts, axis=1))
    totals = dot(
        jnp.concatenate(to_rows, axis=0), jnp.concatenate(values, axis=0), (((0,), (0,)), ((), ()))
    )
    ocean = totals[:, 4 * LANES :]
    cover[...] = ocean
    share = jnp.maximum(ocean, 1.0)
    for q in range(4):
        surface[q] = totals[:, q * LANES : (q + 1) * LANES] / share


def call(kernel, out_shape, limit=VMEM_LIMIT, **kwargs):
    return pl.pallas_call(
        kernel,
        out_shape=out_shape,
        compiler_params=pltpu.CompilerParams(vmem_limit_bytes=limit),
        **kwargs,
    )


def shaped(*shape, dtype=F32):
    return jax.ShapeDtypeStruct(shape, dtype)


def lat_swaps(lon_count, lat_count):
    swap_a, swap_b = [], []
    for i in range(lon_count):
        for a in range(lat_count):
            here = i * lat_count + a
            swap_a.append((here, i * lat_count + (a ^ 1)))
            if a == lat_count - 1:
                swap_b.append((here, (lon_count - 1 - i) * lat_count + a))
            elif a > 0:
                swap_b.append((here, here + 1 if a % 2 else here - 1))
    return swap_a, swap_b


def local(tracers, velocity, land_mask, mixing, owners, atm_row):
    levels = tracers.shape[1]
    rows, cols = land_mask.shape
    fields = 4 * levels
    lon_count, lat_count = lax.axis_size("lon"), lax.axis_size("lat")
    devices = lon_count * lat_count
    assert cols == LANES and rows % 8 == 0 and 2 * fields == LANES
    assert lon_count > 2 and lat_count % 2 == 0 and 3 * rows <= LANES
    length = 2 * fields + 8
    pitch = rows + 2 * PAD
    flat = 2 * levels * rows
    hbm = pl.BlockSpec(memory_space=pltpu.HBM)
    smem = pl.BlockSpec(memory_space=pltpu.SMEM)
    vmem = pl.BlockSpec(memory_space=pltpu.VMEM)

    deep = (2 * levels, rows, cols)
    lat_a, lat_b = call(
        functools.partial(edge_kernel, rows, fields),
        [shaped(length, cols)] * 2,
        limit=VMEM_ALL,
        in_specs=[hbm] * 4,
        scratch_shapes=[
            pltpu.VMEM((2, fields, 8, cols), F32),
            pltpu.VMEM((rows, cols), jnp.int32),
            pltpu.VMEM((rows, cols), F32),
            pltpu.SemaphoreType.DMA((6,)),
        ],
    )(tracers.reshape(deep), velocity.reshape(deep), land_mask, mixing)
    swap_a, swap_b = lat_swaps(lon_count, lat_count)
    got_lat_b = lax.ppermute(lat_b, ("lon", "lat"), swap_b)
    got_lat_a = lax.ppermute(lat_a, ("lon", "lat"), swap_a)

    tr, ve = tracers.reshape(flat, cols), velocity.reshape(flat, cols)
    columns = call(
        functools.partial(pack_kernel, rows, fields),
        shaped(2 * rows + 8, cols),
        in_specs=[vmem] * 4,
    )(tr, ve, land_mask, mixing)

    slot_rows = 5 * CAP + 1
    state, base, col_map, row_map, outgoing, ids = call(
        functools.partial(prepare_kernel, rows, levels, devices),
        [
            shaped(fields * rows, cols),
            shaped(2 * rows + pitch, cols),
            shaped(3 * cols, cols),
            shaped(fields + levels, cols),
            shaped(devices * slot_rows, cols),
            shaped(8, cols, dtype=jnp.int32),
        ],
        in_specs=[vmem] * 4 + [smem] * 2,
        scratch_shapes=[pltpu.SMEM((devices,), jnp.int32)],
    )(tr, ve, land_mask, mixing, owners.reshape(rows), atm_row)

    size = rows + 8
    north, south, message = call(
        functools.partial(corner_kernel, lat_count, lon_count, rows, fields),
        [shaped(length, cols), shaped(length, cols), shaped(lon_count * size, cols)],
    )(got_lat_a, got_lat_b, columns)
    got = lax.all_to_all(
        message.reshape(lon_count, size, cols), "lon", 0, 0, tiled=True
    ).reshape(lon_count * size, cols)

    count = min(3, levels)
    coefs, side, outgoing = call(
        functools.partial(surface_kernel, rows, levels, lon_count),
        [
            shaped(len(COEFFICIENTS) * rows, cols),
            shaped(rows, cols),
            shaped(devices * slot_rows, cols),
        ],
        scratch_shapes=[
            pltpu.VMEM((4 * count * pitch, cols), F32),
            pltpu.VMEM((4 * count * pitch, cols), F32),
            pltpu.VMEM((pitch, cols), F32),
            pltpu.VMEM((4 * rows, cols), F32),
            pltpu.SMEM((8, cols), jnp.int32),
            pltpu.SemaphoreType.DMA,
        ],
    )(state, base, columns, got, north, south, outgoing, ids)
    incoming = lax.all_to_all(
        outgoing.reshape(devices, slot_rows, 1, cols), ("lon", "lat"), 0, 0, tiled=True
    ).reshape(devices * slot_rows, cols)

    chunks = 4
    tr_out, ve_out = call(
        functools.partial(main_kernel, rows, levels, lon_count, chunks),
        [shaped(flat, cols), shaped(flat, cols)],
        in_specs=[vmem] * 10,
        out_specs=[hbm] * 2,
        scratch_shapes=[
            pltpu.VMEM((fields * pitch, cols), F32),
            pltpu.VMEM((fields * pitch, cols), F32),
            pltpu.VMEM((rows, cols), F32),
            pltpu.VMEM((flat, cols), F32),
            pltpu.VMEM((flat, cols), F32),
            pltpu.SemaphoreType.DMA((4 * chunks,)),
        ],
        cost_estimate=pl.CostEstimate(
            flops=80 * fields * rows * cols, bytes_accessed=5 << 20, transcendentals=0
        ),
    )(state, base, columns, got, north, south, col_map, row_map, coefs, side)
    surface, cover = call(
        functools.partial(reduce_kernel, devices),
        [shaped(4, ATM_ROWS, cols), shaped(ATM_ROWS, cols)],
    )(incoming)
    shape = (2, levels, rows, cols)
    return tr_out.reshape(shape), ve_out.reshape(shape), surface, cover


def solution(mesh):
    in_specs = (
        P(None, None, "lat", "lon"),
        P(None, None, "lat", "lon"),
        P("lat", "lon"),
        P("lat", "lon"),
        P(("lon", "lat"), None),
        P(("lon", "lat")),
    )
    out_specs = (
        P(None, None, "lat", "lon"),
        P(None, None, "lat", "lon"),
        P(None, ("lon", "lat"), None),
        P(("lon", "lat"), None),
    )
    return jax.shard_map(local, mesh=mesh, in_specs=in_specs, out_specs=out_specs, check_vma=False)
```

```python
import functools
import math

import jax
import jax.numpy as jnp
from jax import lax
from jax.experimental import pallas as pl
from jax.experimental.pallas import tpu as pltpu
from jax.sharding import PartitionSpec as P

ATM_ROWS = 32
CAP = 2

THERMAL = 0.2
HALINE = 0.15
GRAVITY = 0.2
TIMESTEP = 0.8
VERTICAL_MIX = 0.1
VISCOSITY = 0.2
CORIOLIS_MAX = 0.3

LANES = 128
PAD = 8
EXACT = lax.Precision.HIGHEST
F32 = jnp.float32
VMEM_LIMIT = 32 * 1024 * 1024
VMEM_ALL = 62 * 1024 * 1024


def iota(shape, dim):
    return lax.broadcasted_iota(jnp.int32, shape, dim)


def dot(a, b, dims=(((1,), (0,)), ((), ()))):
    return lax.dot_general(a, b, dims, precision=EXACT, preferred_element_type=F32)


def is_even(axis):
    return lax.rem(lax.axis_index(axis), 2) == 0


def start_copies(pairs, sems):
    copies = [pltpu.make_async_copy(src, dst, sems.at[i]) for i, (src, dst) in enumerate(pairs)]
    for copy in copies:
        copy.start()
    return copies


def edge_kernel(rows, fields, tr_hbm, ve_hbm, mask_hbm, mix_hbm, lat_a, lat_b, edges, mask, mix, sems):
    half = fields // 2
    pairs = [(mask_hbm, mask), (mix_hbm, mix)]
    for n, src in enumerate((tr_hbm, ve_hbm)):
        for side, first in enumerate((0, rows - 8)):
            part = edges.at[side, n * half : (n + 1) * half]
            pairs.append((src.at[:, first : first + 8, :], part))
    for copy in start_copies(pairs, sems):
        copy.wait()
    flat = edges.reshape(2 * fields * 8, LANES)
    even = is_even("lat")
    top = ((rows - 1, 8 * fields + 7), (rows - 2, 8 * fields + 6))
    bottom = ((0, 0), (1, 1))
    for buf, first, second in ((lat_a, top, bottom), (lat_b, bottom, top)):
        (near, near_at), (far, far_at) = [
            [jnp.where(even, x, y) for x, y in zip(one, other)] for one, other in zip(first, second)
        ]
        wet_near = mask[pl.ds(near, 1), :].astype(F32)
        wet_far = mask[pl.ds(far, 1), :].astype(F32)
        buf[0:fields, :] = flat[pl.ds(near_at, fields, stride=8), :] * wet_near
        buf[fields : 2 * fields, :] = flat[pl.ds(far_at, fields, stride=8), :] * wet_far
        buf[2 * fields : 2 * fields + 8, :] = jnp.zeros((8, LANES), F32)
        buf[2 * fields : 2 * fields + 1, :] = wet_near
        buf[2 * fields + 1 : 2 * fields + 2, :] = wet_far
        buf[2 * fields + 2 : 2 * fields + 3, :] = mix[pl.ds(near, 1), :]


def pack_kernel(rows, fields, tr, ve, mask, mix, msg_a, msg_b):
    half = fields // 2
    wet = mask[...].astype(F32)
    lane = iota((rows, LANES), 1)
    pair = lane >> 1

    def columns(ref, base):
        def body(f, carry):
            to_east, to_west = carry
            x = ref[pl.ds(pl.multiple_of(f * rows, rows), rows), :]
            keep = pair == base + f
            low = 2 * (base + f)
            to_east = jnp.where(keep, pltpu.roll(x, (low + 2) & (LANES - 1), 1), to_east)
            to_west = jnp.where(keep, pltpu.roll(x, low, 1), to_west)
            return to_east, to_west

        return body

    carry = (jnp.zeros((rows, LANES), F32), jnp.zeros((rows, LANES), F32))
    for ref, base in ((tr, 0), (ve, half)):
        carry = lax.fori_loop(0, half, columns(ref, base), carry, unroll=8)
    def spread(x, i):
        return jnp.broadcast_to(x[:, i : i + 1], (rows, LANES))

    odd = (lane & 1) == 1
    to_east = carry[0] * jnp.where(odd, spread(wet, LANES - 1), spread(wet, LANES - 2))
    to_west = carry[1] * jnp.where(odd, spread(wet, 1), spread(wet, 0))
    even = is_even("lon")
    row = iota((rows, LANES), 0)
    mixing = mix[...]
    lines = []
    for near, far in ((LANES - 1, LANES - 2), (0, 1)):
        line = jnp.zeros((rows, LANES), F32)
        for part, column in enumerate((wet[:, near], wet[:, far], mixing[:, near])):
            line = jnp.where(lane == part * rows + row, column[:, None], line)
        lines.append(jnp.sum(line, axis=0, keepdims=True))
    for msg, flag in ((msg_a, even), (msg_b, jnp.logical_not(even))):
        msg[0:rows, :] = jnp.where(flag, to_east, to_west)
        msg[rows:, :] = jnp.zeros((8, LANES), F32)
        msg[rows + 4 : rows + 5, :] = jnp.where(flag, *lines)


def prepare_kernel(
    rows, levels, devices, tr, ve, mask, mix, own, atm_row,
    state, base, col_map, row_map, out, ids, used,
):
    fields = 4 * levels
    half = fields // 2
    wet = mask[...].astype(F32)
    base[0:rows, :] = wet
    base[rows : 2 * rows, :] = mix[...]
    for ref, first in ((tr, 0), (ve, half)):

        def fill(f, carry, ref=ref, first=first):
            x = ref[pl.ds(pl.multiple_of(f * rows, 8), rows), :] * wet
            state[pl.ds(pl.multiple_of((first + f) * rows, 8), rows), :] = x
            return carry

        lax.fori_loop(0, half, fill, 0, unroll=8)

    total = lax.axis_size("lat") * rows
    latitude = lax.axis_index("lat") * rows - PAD + iota((rows + 2 * PAD, LANES), 0)
    latitude = jnp.where(latitude >= total, 2 * total - 1 - latitude, latitude).astype(F32)
    table = CORIOLIS_MAX * jnp.sin(math.pi * (-0.43 + 0.93 * (latitude + 0.5) / total))
    base[2 * rows :, :] = table

    span = 2 * levels
    src, dst = iota((LANES, LANES), 0), iota((LANES, LANES), 1)
    src_group, dst_group = src // span, dst // span
    src_level, dst_level = (src // 2) % levels, (dst // 2) % levels
    same_side = (src & 1) == (dst & 1)
    mixes = VERTICAL_MIX * level_matrix("mix", levels, src_level, dst_level)
    press = level_matrix("pressure", levels, src_level, dst_level) * density_weight(src_group)
    col_map[0:LANES, :] = jnp.where(same_side & (src_group == dst_group), mixes, 0.0)
    col_map[LANES : 2 * LANES, :] = jnp.where(same_side & (dst_group == 2), -press, 0.0)
    col_map[2 * LANES :, :] = jnp.where(same_side & (dst_group == 3), -press, 0.0)

    dst, src = iota((fields, fields), 0), iota((fields, fields), 1)
    mixes = VERTICAL_MIX * level_matrix("mix", levels, src % levels, dst % levels)
    row_map[0:fields, 0:fields] = jnp.where(dst // levels == src // levels, mixes, 0.0)
    dst, src = iota((levels, fields), 0), iota((levels, fields), 1)
    press = level_matrix("pressure", levels, src % levels, dst) * density_weight(src // levels)
    row_map[fields:, 0:fields] = press

    slot_rows = out.shape[0] // devices

    def clear(d, carry):
        used[d] = 0
        return carry

    lax.fori_loop(0, devices, clear, 0, unroll=8)
    out[...] = jnp.zeros(out.shape, F32)
    lane1 = iota((1, LANES), 1)
    places = jnp.zeros((1, LANES), jnp.int32)
    for r in range(rows):
        owner = own[r]
        slot = used[owner]
        used[owner] = slot + 1
        start = owner * slot_rows
        places = jnp.where(lane1 == r, start + 4 * slot, places)
        out[pl.ds(start + 4 * CAP + slot, 1), :] = base[r : r + 1, :]
        line = out[pl.ds(start + 5 * CAP, 1), :]
        target = jnp.full((1, LANES), atm_row[r], jnp.int32).astype(F32)
        out[pl.ds(start + 5 * CAP, 1), :] = jnp.where(lane1 // (LANES // CAP) == slot, target, line)
    ids[...] = jnp.zeros(ids.shape, jnp.int32)
    ids[0:1, :] = places


def corner_kernel(lat_count, fields, got_a, got_b, tail_a, tail_b, north, south, new_a, new_b):
    fold = lax.axis_index("lat") == lat_count - 1
    even = is_even("lat")
    a, b = got_a[...], got_b[...]
    straight = jnp.where(even, a, b)
    south[...] = jnp.where(even, b, a)
    back = LANES - 1 - iota((8, LANES), 1)
    flipped = jnp.concatenate(
        [
            jnp.take_along_axis(straight[i : i + 8], back, axis=1)
            * (-1.0 if i < 2 * fields and i % fields >= fields // 2 else 1.0)
            for i in range(0, straight.shape[0], 8)
        ],
        axis=0,
    )
    north[...] = jnp.where(fold, flipped, straight)
    lane, field = iota((fields, LANES), 1), iota((fields, LANES), 0)
    lane1 = iota((1, LANES), 1)
    for old, new in ((tail_a, new_a), (tail_b, new_b)):
        new[...] = old[...]
    for i, ref in enumerate((north, south)):
        near = ref[0:fields, :]
        ends = jnp.where(
            lane == 2 * field, near[:, 0:1], jnp.where(lane == 2 * field + 1, near[:, LANES - 1 :], 0.0)
        )
        corner = jnp.sum(ends, axis=0, keepdims=True)
        wet = ref[2 * fields : 2 * fields + 1, :]
        wet = jnp.where(lane1 == 0, wet[:, 0:1], wet[:, LANES - 1 :])
        for new in (new_a, new_b):
            new[i : i + 1, :] = corner
            new[2 + i : 3 + i, :] = wet


class Sides:
    def __init__(self, rows, got_a, got_b, msg_a, msg_b):
        lane, row = iota((rows, LANES), 1), iota((rows, LANES), 0)
        self.even = (lane & 1) == 0
        self.even1 = (iota((1, LANES), 1) & 1) == 0
        even = is_even("lon")

        def ordered(a, b, place):
            return jnp.where(even, a[place, :], b[place, :]), jnp.where(even, b[place, :], a[place, :])

        self.got = ordered(got_a, got_b, slice(0, rows))
        self.mine = ordered(msg_a, msg_b, slice(0, rows))
        self.extras = ordered(got_a, got_b, slice(rows, rows + 8))
        self.columns = [
            [
                jnp.sum(jnp.where(lane == i * rows + row, x[4:5], 0.0), axis=1, keepdims=True)
                for i in range(3)
            ]
            for x in self.extras
        ]

    def near(self):
        return jnp.where(self.even, *self.got)

    def far_and_inner(self):
        east, west = self.got
        mine_e, mine_w = self.mine
        far = jnp.where(self.even, pltpu.roll(east, LANES - 1, 1), pltpu.roll(west, 1, 1))
        inner = jnp.where(self.even, pltpu.roll(mine_e, LANES - 1, 1), pltpu.roll(mine_w, 1, 1))
        return far, inner

    def corner(self, i):
        east, west = self.extras
        wets = east[2 + i : 3 + i, 0:1], west[2 + i : 3 + i, 1:2]
        return jnp.where(self.even1, east[i : i + 1], west[i : i + 1]), *wets

    def lanes(self, i):
        return jnp.where(self.even, self.columns[0][i], self.columns[1][i])


def level_matrix(kind, levels, source, target):
    if kind == "mix":
        above = (source == jnp.maximum(target - 1, 0)).astype(F32)
        below = (source == jnp.minimum(target + 1, levels - 1)).astype(F32)
        return above + below - 2.0 * (source == target).astype(F32)
    full = jnp.where(source < target, 1.0, jnp.where(source == target, 0.5, 0.0))
    return (0.5 * GRAVITY) * full


def density_weight(group):
    return jnp.where(group == 0, -THERMAL, jnp.where(group == 1, HALINE, 0.0)).astype(F32)


def advance_columns(sides, wet, coriolis, level_map):
    rows = wet.shape[0]
    mid = sides.near()
    outer, inner = sides.far_and_inner()
    (corner_n, wet_ne, wet_nw), (corner_s, wet_se, wet_sw) = sides.corner(0), sides.corner(1)
    wet_mid, wet_out = sides.lanes(0), sides.lanes(1)
    wet_in = jnp.where(sides.even, wet[:, LANES - 1 :], wet[:, 0:1])
    wet_corner_n = jnp.where(sides.even1, wet_ne, wet_nw)
    wet_corner_s = jnp.where(sides.even1, wet_se, wet_sw)
    mixing = sides.lanes(2)
    lane = iota((rows, LANES), 1)
    row = iota((rows, LANES), 0)
    span = LANES // 4
    group = lane // span

    def ends(outside, inside):
        return jnp.where(sides.even, outside, inside), jnp.where(sides.even, inside, outside)

    def shifted(x, north, south):
        n = jnp.where(row == rows - 1, north, pltpu.roll(x, rows - 1, 0))
        s = jnp.where(row == 0, south, pltpu.roll(x, 1, 0))
        return n, s

    e, w = ends(outer, inner)
    wet_e, wet_w = ends(wet_out, wet_in)
    n, s = shifted(mid, corner_n, corner_s)
    wet_n, wet_s = shifted(wet_mid, wet_corner_n, wet_corner_s)
    lap = wet_e * (e - mid) + wet_w * (w - mid) + wet_n * (n - mid) + wet_s * (s - mid)
    de, dn = e - w, n - s
    one, two, three = (pltpu.roll(mid, i * span, 1) for i in (1, 2, 3))

    def pick(a, b, c, d):
        return jnp.where(group == 0, a, jnp.where(group == 1, b, jnp.where(group == 2, c, d)))

    u = pick(two, three, mid, one)
    v = pick(one, two, three, mid)
    adv = 0.5 * (u * de + v * dn)
    zero = jnp.zeros_like(mid)
    if level_map is None:
        grad_x = HALINE * pltpu.roll(de, span, 1) - THERMAL * pltpu.roll(de, 2 * span, 1)
        grad_y = HALINE * pltpu.roll(dn, 2 * span, 1) - THERMAL * pltpu.roll(dn, 3 * span, 1)
        linear = VERTICAL_MIX * (pltpu.roll(mid, LANES - 2, 1) - mid)
        linear = linear - (0.25 * GRAVITY) * pick(zero, zero, grad_x, grad_y)
    else:
        linear = dot(jnp.concatenate([mid, de, dn], axis=1), level_map)
    turn = pick(zero, zero, coriolis * v, -coriolis * u)
    kappa = jnp.where(group < 2, mixing, VISCOSITY)
    tend = turn - adv + kappa * lap + linear
    return wet_mid * (mid + TIMESTEP * tend)


def advance_rows(levels, parts, level_map):
    fields = 4 * levels
    lane = iota((fields, LANES), 1)
    lane8 = iota((8, LANES), 1)

    def sides(x, east, west, at):
        e = jnp.where(at == LANES - 1, east, pltpu.roll(x, LANES - 1, 1))
        w = jnp.where(at == 0, west, pltpu.roll(x, 1, 1))
        return e, w

    mids, gaps = [], []
    for mid, n, s, (corner_e, corner_w), *_ in parts:
        e, w = sides(mid, corner_e, corner_w, lane)
        mids.append((mid, e, w, n, s))
        gaps += [e - w, n - s]
    vertical = dot(level_map[0:fields, 0:fields], jnp.concatenate([m[0] for m in mids], axis=1))
    grads = dot(level_map[fields:, 0:fields], jnp.concatenate(gaps, axis=1))
    done = []
    for i, (mid, e, w, n, s) in enumerate(mids):
        *_, wets, mixing, coriolis = parts[i]
        wet_mid, wet_n, wet_s, wet_corner_e, wet_corner_w = wets
        wet_e, wet_w = sides(
            jnp.broadcast_to(wet_mid, (8, LANES)), wet_corner_e, wet_corner_w, lane8
        )
        lap = wet_e[0:1] * (e - mid) + wet_w[0:1] * (w - mid)
        lap = lap + wet_n * (n - mid) + wet_s * (s - mid)
        de, dn = gaps[2 * i], gaps[2 * i + 1]
        u, v = mid[2 * levels : 3 * levels], mid[3 * levels :]
        adv = jnp.concatenate([u] * 4, axis=0) * de + jnp.concatenate([v] * 4, axis=0) * dn
        grad_x = grads[:, 2 * i * LANES : (2 * i + 1) * LANES]
        grad_y = grads[:, (2 * i + 1) * LANES : (2 * i + 2) * LANES]
        zero = jnp.zeros((2 * levels, LANES), F32)
        turn = jnp.concatenate([zero, coriolis * v - grad_x, -coriolis * u - grad_y], axis=0)
        kappa = jnp.concatenate(
            [jnp.broadcast_to(mixing, (2 * levels, LANES)), jnp.full(zero.shape, VISCOSITY)],
            axis=0,
        )
        tend = turn - 0.5 * adv + kappa * lap + vertical[:, i * LANES : (i + 1) * LANES]
        done.append(wet_mid * (mid + TIMESTEP * tend))
    return done


COEFFICIENTS = ("te", "tw", "tn", "ts", "tc", "ve", "vw", "vn", "vs", "vc", "adv", "mix", "turn")


def place_of(name, rows):
    i = COEFFICIENTS.index(name)
    return slice(i * rows, (i + 1) * rows)


def coefficients(wet, neighbours, mixing, coriolis):
    made = {}
    for name, kappa in (("t", mixing), ("v", VISCOSITY)):
        rest = wet * (1.0 - 2.0 * TIMESTEP * VERTICAL_MIX)
        for side, wet_n in zip("ewns", neighbours):
            made[name + side] = TIMESTEP * kappa * wet * wet_n
            rest = rest - made[name + side]
        made[name + "c"] = rest
    made["adv"] = (0.5 * TIMESTEP) * wet
    made["mix"] = (TIMESTEP * VERTICAL_MIX) * wet
    made["turn"] = TIMESTEP * coriolis * wet
    return made


def advance_level(k, count, levels, rows, src, sides, coef, acc):
    pitch = rows + 2 * PAD
    lane = iota((rows, LANES), 1)
    first, last = lane == 0, lane == LANES - 1
    above_k = jnp.maximum(k - 1, 0)
    below_k = jnp.minimum(k + 1, levels - 1)

    def load(q, level, shift):
        return src[pl.ds((q * count + level) * pitch + PAD + shift, rows), :]

    def base(q):
        return pl.multiple_of((q * count + k) * pitch + PAD, 8)

    center = [load(q, k, 0) for q in range(4)]
    u, v = coef("adv") * center[2], coef("adv") * center[3]
    sums, de, dn = [], [], []
    for q in range(4):
        c = center[q]
        n, s = load(q, k, 1), load(q, k, -1)
        edge = pltpu.roll(sides, (LANES - 1 - 2 * (q * levels + k)) & (LANES - 1), 1)
        e = jnp.where(last, edge, pltpu.roll(c, LANES - 1, 1))
        w = jnp.where(first, edge, pltpu.roll(c, 1, 1))
        kind = "t" if q < 2 else "v"
        lap = coef(kind + "c") * c + coef(kind + "e") * e + coef(kind + "w") * w
        lap = lap + coef(kind + "n") * n + coef(kind + "s") * s
        de.append(e - w)
        dn.append(n - s)
        sums.append(lap - (u * de[q] + v * dn[q]))
    scale = 0.5 * GRAVITY / VERTICAL_MIX
    dens_x = (scale * HALINE) * de[1] - (scale * THERMAL) * de[0]
    dens_y = (scale * HALINE) * dn[1] - (scale * THERMAL) * dn[0]
    acc_x, acc_y = acc
    grad = (None, None, acc_x + 0.5 * dens_x, acc_y + 0.5 * dens_y)
    turn = (None, None, coef("turn") * center[3], -coef("turn") * center[2])
    new = []
    for q in range(4):
        vertical = load(q, above_k, 0) + load(q, below_k, 0)
        if grad[q] is not None:
            vertical = vertical - grad[q]
        total = sums[q] + coef("mix") * vertical
        new.append(total if turn[q] is None else total + turn[q])
    return new, (acc_x + dens_x, acc_y + dens_y)


def advance_top_rows(levels, sides, north, south, state, wet, rows, table):
    fields = 4 * levels

    def both(a, b):
        return jnp.concatenate([a, b], axis=0)

    def rows_at(first):
        return both(
            north[pl.ds(first, 4, stride=levels), :], south[pl.ds(first, 4, stride=levels), :]
        )

    lane, row = iota((8, LANES), 1), iota((8, LANES), 0)
    upper = row < 4
    field = row & 3
    inside_n = state[pl.ds(rows - 1, 4, stride=levels * rows), :]
    inside_s = state[pl.ds(0, 4, stride=levels * rows), :]
    mid, below, outer = rows_at(0), rows_at(1), rows_at(fields)
    n = both(outer[0:4], inside_s)
    s = both(inside_n, outer[4:8])
    (corner_n, wet_ne, wet_nw), (corner_s, wet_se, wet_sw) = sides.corner(0), sides.corner(1)
    corner = jnp.where(upper, corner_n, corner_s)
    at = 2 * levels * field

    def end(parity):
        return jnp.sum(jnp.where(lane == at + parity, corner, 0.0), axis=1, keepdims=True)

    def west_east(x, east, west):
        return (
            jnp.where(lane == LANES - 1, east, pltpu.roll(x, LANES - 1, 1)),
            jnp.where(lane == 0, west, pltpu.roll(x, 1, 1)),
        )

    def tail(i):
        place = slice(2 * fields + i, 2 * fields + i + 1)
        return north[place, :], south[place, :]

    e, w = west_east(mid, end(0), end(1))
    wet_mid = jnp.where(upper, *tail(0))
    wet_e, wet_w = west_east(
        wet_mid, jnp.where(upper, wet_ne, wet_se), jnp.where(upper, wet_nw, wet_sw)
    )
    out_n, out_s = tail(1)
    wet_n = jnp.where(upper, out_n, wet[0:1])
    wet_s = jnp.where(upper, wet[rows - 1 : rows], out_s)
    lap = wet_e * (e - mid) + wet_w * (w - mid) + wet_n * (n - mid) + wet_s * (s - mid)
    de, dn = e - w, n - s

    def of(x, i):
        return jnp.where(upper, x[i : i + 1], x[4 + i : 5 + i])

    u, v = of(mid, 2), of(mid, 3)
    coriolis = jnp.where(upper, table[PAD + rows : PAD + rows + 1], table[PAD - 1 : PAD])
    grad_x = (0.25 * GRAVITY) * (HALINE * of(de, 1) - THERMAL * of(de, 0))
    grad_y = (0.25 * GRAVITY) * (HALINE * of(dn, 1) - THERMAL * of(dn, 0))
    turn = jnp.where(
        field < 2, 0.0, jnp.where(field == 2, coriolis * v - grad_x, -coriolis * u - grad_y)
    )
    kappa = jnp.where(field < 2, jnp.where(upper, *tail(2)), VISCOSITY)
    tend = turn - 0.5 * (u * de + v * dn) + kappa * lap + VERTICAL_MIX * (below - mid)
    return wet_mid * (mid + TIMESTEP * tend)


def surface_kernel(
    rows, levels,
    state, base, msg_a, msg_b, got_a, got_b, north, south, out_in, ids,
    coef, side, out, now, later, wet_pad, stage, places, sem,
):
    fields = 4 * levels
    pitch = rows + 2 * PAD
    to_scalars = pltpu.make_async_copy(ids, places, sem)
    to_scalars.start()
    out[...] = out_in[...]
    wet = base[0:rows, :]
    mixing = base[rows : 2 * rows, :]
    table = base[2 * rows :, :]
    coriolis = table[PAD : PAD + rows]
    lane = iota((rows, LANES), 1)
    sides = Sides(rows, got_a, got_b, msg_a, msg_b)
    wet_pad[PAD : PAD + rows, :] = wet
    wet_pad[PAD - 1 : PAD, :] = south[2 * fields : 2 * fields + 1, :]
    wet_pad[PAD + rows : PAD + rows + 1, :] = north[2 * fields : 2 * fields + 1, :]
    wet_n = wet_pad[PAD + 1 : PAD + 1 + rows, :]
    wet_s = wet_pad[PAD - 1 : PAD - 1 + rows, :]
    wet_e = jnp.where(lane == LANES - 1, sides.columns[0][0], pltpu.roll(wet, LANES - 1, 1))
    wet_w = jnp.where(lane == 0, sides.columns[1][0], pltpu.roll(wet, 1, 1))
    made = coefficients(wet, (wet_e, wet_w, wet_n, wet_s), mixing, coriolis)
    for name in COEFFICIENTS:
        coef[place_of(name, rows)] = made[name]
    near = sides.near()
    side[...] = near

    count = now.shape[0] // (4 * pitch)
    for q in range(4):
        for k in range(count):
            field = (q * levels + k) * rows
            at = (q * count + k) * pitch + PAD
            now[at : at + rows, :] = state[field : field + rows, :]
            now[at + rows : at + rows + 1, :] = north[q * levels + k : q * levels + k + 1, :]
            now[at - 1 : at, :] = south[q * levels + k : q * levels + k + 1, :]

    def read(name):
        return coef[place_of(name, rows)]

    none = jnp.zeros((rows, LANES), F32)
    acc = (none, none)
    edge_rows = advance_top_rows(levels, sides, north, south, state, wet, rows, table)
    edge_cols = advance_columns(sides, wet, coriolis, None)
    for k in range(count - 1):
        new, acc = advance_level(k, count, levels, rows, now, near, read, acc)
        for q in range(4):
            at = (q * count + k) * pitch + PAD
            later[at : at + rows, :] = new[q]
            if k == 0:
                later[at + rows : at + rows + 1, :] = edge_rows[q : q + 1]
                later[at - 1 : at, :] = edge_rows[4 + q : 5 + q]
    new, _ = advance_level(0, count, levels, rows, later, edge_cols, read, (none, none))
    for q in range(4):
        stage[pl.ds(q, rows, stride=4), :] = new[q]
    to_scalars.wait()
    for r in range(rows):
        out[pl.ds(places[0, r], 4), :] = stage[4 * r : 4 * r + 4, :]


def halo_after_first(rows, levels, sides, north, south, state, wet, table, col_map, row_map):
    fields = 4 * levels
    side_new = advance_columns(sides, wet, table[PAD : PAD + rows], col_map)
    lane, field = iota((fields, LANES), 1), iota((fields, LANES), 0)

    def to_sublanes(x, parity):
        here = lane == 2 * field + parity
        return jnp.sum(jnp.where(here, x, 0.0), axis=1, keepdims=True)

    parts = []
    for north_side, ref, line, lat_row in (
        (True, north, rows - 1, PAD + rows),
        (False, south, 0, PAD - 1),
    ):
        corner, *corner_wets = sides.corner(0 if north_side else 1)
        inside = state[pl.ds(line, fields, stride=rows), :]
        tail = ref[2 * fields :, :]
        pair = (ref[fields : 2 * fields, :], inside), (tail[1:2], wet[line : line + 1])
        (n, s), (wet_n, wet_s) = pair if north_side else [x[::-1] for x in pair]
        parts.append(
            (
                ref[0:fields, :], n, s, (to_sublanes(corner, 0), to_sublanes(corner, 1)),
                (tail[0:1], wet_n, wet_s, *corner_wets),
                tail[2:3], table[lat_row : lat_row + 1],
            )
        )
    return side_new, *advance_rows(levels, parts, row_map)


def main_kernel(
    rows, levels, chunks,
    state, base, msg_a, msg_b, got_a, got_b, north, south, col_map, row_map, coefs, side,
    tr_hbm, ve_hbm, now, later, side_new, tr_out, ve_out, sems,
):
    fields = 4 * levels
    pitch = rows + 2 * PAD
    sides = Sides(rows, got_a, got_b, msg_a, msg_b)
    side_new[...], north_new, south_new = halo_after_first(
        rows, levels, sides, north, south, state, base[0:rows, :], base[2 * rows :, :],
        col_map[...], row_map[...],
    )
    edges = (now, north[0:fields, :], south[0:fields, :]), (later, north_new, south_new)
    for buf, n, s in edges:
        buf[pl.ds(PAD - 1, fields, stride=pitch), :] = s
        buf[pl.ds(PAD + rows, fields, stride=pitch), :] = n

    def fill(f, carry):
        x = state[pl.ds(pl.multiple_of(f * rows, 8), rows), :]
        now[pl.ds(pl.multiple_of(f * pitch + PAD, 8), rows), :] = x
        return carry

    lax.fori_loop(0, fields, fill, 0, unroll=8)

    def coef(name):
        return coefs[place_of(name, rows)]

    def first(k, acc):
        new, acc = advance_level(k, levels, levels, rows, now, side[...], coef, acc)
        for q in range(4):
            place = pl.multiple_of((q * levels + k) * pitch + PAD, 8)
            later[pl.ds(place, rows), :] = new[q]
        return acc

    def second(k, acc):
        new, acc = advance_level(k, levels, levels, rows, later, side_new[...], coef, acc)
        for q in range(4):
            ref = tr_out if q < 2 else ve_out
            place = pl.multiple_of(((q % 2) * levels + k) * rows, 8)
            ref[pl.ds(place, rows), :] = new[q]
        return acc

    none = jnp.zeros((rows, LANES), F32)
    lax.fori_loop(0, levels, first, (none, none), unroll=2)
    acc = (none, none)
    size = levels // chunks
    copies = []
    for i in range(chunks):
        acc = lax.fori_loop(i * size, (i + 1) * size, second, acc, unroll=2)
        for src, dst in ((tr_out, tr_hbm), (ve_out, ve_hbm)):
            for q in range(2):
                start = (q * levels + i * size) * rows
                part = slice(start, start + size * rows)
                copy = pltpu.make_async_copy(src.at[part], dst.at[part], sems.at[len(copies)])
                copy.start()
                copies.append(copy)
    for copy in copies:
        copy.wait()


def reduce_kernel(devices, data, surface, cover):
    slot_rows = data.shape[0] // devices

    def rows_of(i):
        return data[pl.ds(i, devices, stride=slot_rows), :]

    width = LANES // CAP
    lines = rows_of(5 * CAP)
    named = (lines == (iota((devices, LANES), 1) % width).astype(F32)).astype(F32)
    to_rows, values = [], []
    for slot in range(CAP):
        to_rows.append(named[:, slot * width : slot * width + ATM_ROWS])
        parts = [rows_of(4 * slot + q) for q in range(4)] + [rows_of(4 * CAP + slot)]
        values.append(jnp.concatenate(parts, axis=1))
    totals = dot(
        jnp.concatenate(to_rows, axis=0), jnp.concatenate(values, axis=0), (((0,), (0,)), ((), ()))
    )
    ocean = totals[:, 4 * LANES :]
    cover[...] = ocean
    share = jnp.maximum(ocean, 1.0)
    for q in range(4):
        surface[q] = totals[:, q * LANES : (q + 1) * LANES] / share


def call(kernel, out_shape, limit=VMEM_LIMIT, **kwargs):
    return pl.pallas_call(
        kernel,
        out_shape=out_shape,
        compiler_params=pltpu.CompilerParams(vmem_limit_bytes=limit),
        **kwargs,
    )


def shaped(*shape, dtype=F32):
    return jax.ShapeDtypeStruct(shape, dtype)


def lat_swaps(lon_count, lat_count):
    swap_a, swap_b = [], []
    for i in range(lon_count):
        for a in range(lat_count):
            here = i * lat_count + a
            swap_a.append((here, i * lat_count + (a ^ 1)))
            if a == lat_count - 1:
                swap_b.append((here, (lon_count - 1 - i) * lat_count + a))
            elif a > 0:
                swap_b.append((here, here + 1 if a % 2 else here - 1))
    return swap_a, swap_b


def local(tracers, velocity, land_mask, mixing, owners, atm_row):
    levels = tracers.shape[1]
    rows, cols = land_mask.shape
    fields = 4 * levels
    lon_count, lat_count = lax.axis_size("lon"), lax.axis_size("lat")
    devices = lon_count * lat_count
    assert cols == LANES and rows % 8 == 0 and 2 * fields == LANES
    assert lon_count % 2 == 0 and lat_count % 2 == 0 and 3 * rows <= LANES
    length = 2 * fields + 8
    pitch = rows + 2 * PAD
    flat = 2 * levels * rows
    hbm = pl.BlockSpec(memory_space=pltpu.HBM)
    smem = pl.BlockSpec(memory_space=pltpu.SMEM)
    vmem = pl.BlockSpec(memory_space=pltpu.VMEM)

    deep = (2 * levels, rows, cols)
    lat_a, lat_b = call(
        functools.partial(edge_kernel, rows, fields),
        [shaped(length, cols)] * 2,
        limit=VMEM_ALL,
        in_specs=[hbm] * 4,
        scratch_shapes=[
            pltpu.VMEM((2, fields, 8, cols), F32),
            pltpu.VMEM((rows, cols), jnp.int32),
            pltpu.VMEM((rows, cols), F32),
            pltpu.SemaphoreType.DMA((6,)),
        ],
    )(tracers.reshape(deep), velocity.reshape(deep), land_mask, mixing)
    swap_a, swap_b = lat_swaps(lon_count, lat_count)
    got_lat_b = lax.ppermute(lat_b, ("lon", "lat"), swap_b)
    got_lat_a = lax.ppermute(lat_a, ("lon", "lat"), swap_a)

    tr, ve = tracers.reshape(flat, cols), velocity.reshape(flat, cols)
    msg_a, msg_b = call(
        functools.partial(pack_kernel, rows, fields),
        [shaped(rows + 8, cols)] * 2,
        in_specs=[vmem] * 4,
    )(tr, ve, land_mask, mixing)

    slot_rows = 5 * CAP + 1
    state, base, col_map, row_map, outgoing, ids = call(
        functools.partial(prepare_kernel, rows, levels, devices),
        [
            shaped(fields * rows, cols),
            shaped(2 * rows + pitch, cols),
            shaped(3 * cols, cols),
            shaped(fields + levels, cols),
            shaped(devices * slot_rows, cols),
            shaped(8, cols, dtype=jnp.int32),
        ],
        in_specs=[vmem] * 4 + [smem] * 2,
        scratch_shapes=[pltpu.SMEM((devices,), jnp.int32)],
    )(tr, ve, land_mask, mixing, owners.reshape(rows), atm_row)

    def full(n):
        return pl.BlockSpec((n, cols), lambda i: (0, 0))

    tail = pl.BlockSpec((8, cols), lambda i: (rows // 8, 0))
    north, south, msg_a, msg_b = call(
        functools.partial(corner_kernel, lat_count, fields),
        [shaped(length, cols)] * 2 + [shaped(rows + 8, cols)] * 2,
        grid=(1,),
        in_specs=[full(length), full(length), tail, tail],
        out_specs=[full(length), full(length), tail, tail],
        input_output_aliases={2: 2, 3: 3},
    )(got_lat_a, got_lat_b, msg_a, msg_b)
    even_pairs = [(i, i ^ 1) for i in range(lon_count)]
    odd_pairs = [(i, (i + 1 if i % 2 else i - 1) % lon_count) for i in range(lon_count)]
    got_a = lax.ppermute(msg_a, "lon", even_pairs)
    got_b = lax.ppermute(msg_b, "lon", odd_pairs)

    count = min(3, levels)
    coefs, side, outgoing = call(
        functools.partial(surface_kernel, rows, levels),
        [
            shaped(len(COEFFICIENTS) * rows, cols),
            shaped(rows, cols),
            shaped(devices * slot_rows, cols),
        ],
        scratch_shapes=[
            pltpu.VMEM((4 * count * pitch, cols), F32),
            pltpu.VMEM((4 * count * pitch, cols), F32),
            pltpu.VMEM((pitch, cols), F32),
            pltpu.VMEM((4 * rows, cols), F32),
            pltpu.SMEM((8, cols), jnp.int32),
            pltpu.SemaphoreType.DMA,
        ],
    )(state, base, msg_a, msg_b, got_a, got_b, north, south, outgoing, ids)
    incoming = lax.all_to_all(
        outgoing.reshape(devices, slot_rows, 1, cols), ("lon", "lat"), 0, 0, tiled=True
    ).reshape(devices * slot_rows, cols)

    chunks = 4
    tr_out, ve_out = call(
        functools.partial(main_kernel, rows, levels, chunks),
        [shaped(flat, cols), shaped(flat, cols)],
        in_specs=[vmem] * 12,
        out_specs=[hbm] * 2,
        scratch_shapes=[
            pltpu.VMEM((fields * pitch, cols), F32),
            pltpu.VMEM((fields * pitch, cols), F32),
            pltpu.VMEM((rows, cols), F32),
            pltpu.VMEM((flat, cols), F32),
            pltpu.VMEM((flat, cols), F32),
            pltpu.SemaphoreType.DMA((4 * chunks,)),
        ],
        cost_estimate=pl.CostEstimate(
            flops=80 * fields * rows * cols, bytes_accessed=5 << 20, transcendentals=0
        ),
    )(state, base, msg_a, msg_b, got_a, got_b, north, south, col_map, row_map, coefs, side)
    surface, cover = call(
        functools.partial(reduce_kernel, devices),
        [shaped(4, ATM_ROWS, cols), shaped(ATM_ROWS, cols)],
    )(incoming)
    shape = (2, levels, rows, cols)
    return tr_out.reshape(shape), ve_out.reshape(shape), surface, cover


def solution(mesh):
    in_specs = (
        P(None, None, "lat", "lon"),
        P(None, None, "lat", "lon"),
        P("lat", "lon"),
        P("lat", "lon"),
        P(("lon", "lat"), None),
        P(("lon", "lat")),
    )
    out_specs = (
        P(None, None, "lat", "lon"),
        P(None, None, "lat", "lon"),
        P(None, ("lon", "lat"), None),
        P(("lon", "lat"), None),
    )
    return jax.shard_map(local, mesh=mesh, in_specs=in_specs, out_specs=out_specs, check_vma=False)
```

```python
import functools
import math

import jax
import jax.numpy as jnp
from jax import lax
from jax.experimental import pallas as pl
from jax.experimental.pallas import tpu as pltpu
from jax.sharding import PartitionSpec as P

ATM_ROWS = 32
CAP = 2

THERMAL = 0.2
HALINE = 0.15
GRAVITY = 0.2
TIMESTEP = 0.8
VERTICAL_MIX = 0.1
VISCOSITY = 0.2
CORIOLIS_MAX = 0.3

LANES = 128
PAD = 8
EXACT = lax.Precision.HIGHEST
F32 = jnp.float32
VMEM_LIMIT = 32 * 1024 * 1024
VMEM_ALL = 62 * 1024 * 1024


def iota(shape, dim):
    return lax.broadcasted_iota(jnp.int32, shape, dim)


def dot(a, b, dims=(((1,), (0,)), ((), ()))):
    return lax.dot_general(a, b, dims, precision=EXACT, preferred_element_type=F32)


def is_even(axis):
    return lax.rem(lax.axis_index(axis), 2) == 0


def start_copies(pairs, sems):
    copies = [pltpu.make_async_copy(src, dst, sems.at[i]) for i, (src, dst) in enumerate(pairs)]
    for copy in copies:
        copy.start()
    return copies


def edge_kernel(rows, fields, tr_hbm, ve_hbm, mask_hbm, mix_hbm, lat_a, lat_b, edges, mask, mix, sems):
    half = fields // 2
    pairs = [(mask_hbm, mask), (mix_hbm, mix)]
    for n, src in enumerate((tr_hbm, ve_hbm)):
        for side, first in enumerate((0, rows - 8)):
            part = edges.at[side, n * half : (n + 1) * half]
            pairs.append((src.at[:, first : first + 8, :], part))
    for copy in start_copies(pairs, sems):
        copy.wait()
    flat = edges.reshape(2 * fields * 8, LANES)
    even = is_even("lat")
    top = ((rows - 1, 8 * fields + 7), (rows - 2, 8 * fields + 6))
    bottom = ((0, 0), (1, 1))
    for buf, first, second in ((lat_a, top, bottom), (lat_b, bottom, top)):
        (near, near_at), (far, far_at) = [
            [jnp.where(even, x, y) for x, y in zip(one, other)] for one, other in zip(first, second)
        ]
        wet_near = mask[pl.ds(near, 1), :].astype(F32)
        wet_far = mask[pl.ds(far, 1), :].astype(F32)
        buf[0:fields, :] = flat[pl.ds(near_at, fields, stride=8), :] * wet_near
        buf[fields : 2 * fields, :] = flat[pl.ds(far_at, fields, stride=8), :] * wet_far
        buf[2 * fields : 2 * fields + 8, :] = jnp.zeros((8, LANES), F32)
        buf[2 * fields : 2 * fields + 1, :] = wet_near
        buf[2 * fields + 1 : 2 * fields + 2, :] = wet_far
        buf[2 * fields + 2 : 2 * fields + 3, :] = mix[pl.ds(near, 1), :]


def pack_kernel(rows, fields, tr, ve, mask, mix, msg_a, msg_b):
    half = fields // 2
    wet = mask[...].astype(F32)
    lane = iota((rows, LANES), 1)
    pair = lane >> 1

    def columns(ref, base):
        def body(f, carry):
            to_east, to_west = carry
            x = ref[pl.ds(pl.multiple_of(f * rows, rows), rows), :]
            keep = pair == base + f
            low = 2 * (base + f)
            to_east = jnp.where(keep, pltpu.roll(x, (low + 2) & (LANES - 1), 1), to_east)
            to_west = jnp.where(keep, pltpu.roll(x, low, 1), to_west)
            return to_east, to_west

        return body

    carry = (jnp.zeros((rows, LANES), F32), jnp.zeros((rows, LANES), F32))
    for ref, base in ((tr, 0), (ve, half)):
        carry = lax.fori_loop(0, half, columns(ref, base), carry, unroll=8)
    def spread(x, i):
        return jnp.broadcast_to(x[:, i : i + 1], (rows, LANES))

    odd = (lane & 1) == 1
    to_east = carry[0] * jnp.where(odd, spread(wet, LANES - 1), spread(wet, LANES - 2))
    to_west = carry[1] * jnp.where(odd, spread(wet, 1), spread(wet, 0))
    even = is_even("lon")
    row = iota((rows, LANES), 0)
    mixing = mix[...]
    lines = []
    for near, far in ((LANES - 1, LANES - 2), (0, 1)):
        line = jnp.zeros((rows, LANES), F32)
        for part, column in enumerate((wet[:, near], wet[:, far], mixing[:, near])):
            line = jnp.where(lane == part * rows + row, column[:, None], line)
        lines.append(jnp.sum(line, axis=0, keepdims=True))
    for msg, flag in ((msg_a, jnp.logical_not(even)), (msg_b, even)):
        msg[0:rows, :] = jnp.where(flag, to_east, to_west)
        msg[rows:, :] = jnp.zeros((8, LANES), F32)
        msg[rows + 4 : rows + 5, :] = jnp.where(flag, *lines)


def prepare_kernel(
    rows, levels, devices, tr, ve, mask, mix, own, atm_row,
    state, base, col_map, row_map, out, ids, used,
):
    fields = 4 * levels
    half = fields // 2
    wet = mask[...].astype(F32)
    base[0:rows, :] = wet
    base[rows : 2 * rows, :] = mix[...]
    for ref, first in ((tr, 0), (ve, half)):

        def fill(f, carry, ref=ref, first=first):
            x = ref[pl.ds(pl.multiple_of(f * rows, 8), rows), :] * wet
            state[pl.ds(pl.multiple_of((first + f) * rows, 8), rows), :] = x
            return carry

        lax.fori_loop(0, half, fill, 0, unroll=8)

    total = lax.axis_size("lat") * rows
    latitude = lax.axis_index("lat") * rows - PAD + iota((rows + 2 * PAD, LANES), 0)
    latitude = jnp.where(latitude >= total, 2 * total - 1 - latitude, latitude).astype(F32)
    table = CORIOLIS_MAX * jnp.sin(math.pi * (-0.43 + 0.93 * (latitude + 0.5) / total))
    base[2 * rows :, :] = table

    span = 2 * levels
    src, dst = iota((LANES, LANES), 0), iota((LANES, LANES), 1)
    src_group, dst_group = src // span, dst // span
    src_level, dst_level = (src // 2) % levels, (dst // 2) % levels
    same_side = (src & 1) == (dst & 1)
    mixes = VERTICAL_MIX * level_matrix("mix", levels, src_level, dst_level)
    press = level_matrix("pressure", levels, src_level, dst_level) * density_weight(src_group)
    col_map[0:LANES, :] = jnp.where(same_side & (src_group == dst_group), mixes, 0.0)
    col_map[LANES : 2 * LANES, :] = jnp.where(same_side & (dst_group == 2), -press, 0.0)
    col_map[2 * LANES :, :] = jnp.where(same_side & (dst_group == 3), -press, 0.0)

    dst, src = iota((fields, fields), 0), iota((fields, fields), 1)
    mixes = VERTICAL_MIX * level_matrix("mix", levels, src % levels, dst % levels)
    row_map[0:fields, 0:fields] = jnp.where(dst // levels == src // levels, mixes, 0.0)
    dst, src = iota((levels, fields), 0), iota((levels, fields), 1)
    press = level_matrix("pressure", levels, src % levels, dst) * density_weight(src // levels)
    row_map[fields:, 0:fields] = press

    slot_rows = out.shape[0] // devices
    lon_count, lat_count = lax.axis_size("lon"), lax.axis_size("lat")

    def clear(d, carry):
        used[d] = 0
        return carry

    lax.fori_loop(0, devices, clear, 0, unroll=8)
    out[...] = jnp.zeros(out.shape, F32)
    lane1 = iota((1, LANES), 1)
    places = jnp.zeros((1, LANES), jnp.int32)
    for r in range(rows):
        owner = own[r]
        slot = used[owner]
        used[owner] = slot + 1
        start = (lax.rem(owner, lat_count) * lon_count + owner // lat_count) * slot_rows
        places = jnp.where(lane1 == r, start + 4 * slot, places)
        out[pl.ds(start + 4 * CAP + slot, 1), :] = base[r : r + 1, :]
        line = out[pl.ds(start + 5 * CAP, 1), :]
        target = jnp.full((1, LANES), atm_row[r], jnp.int32).astype(F32)
        out[pl.ds(start + 5 * CAP, 1), :] = jnp.where(lane1 // (LANES // CAP) == slot, target, line)
    ids[...] = jnp.zeros(ids.shape, jnp.int32)
    ids[0:1, :] = places


def corner_kernel(lat_count, fields, got_b, got_a, tail_a, tail_b, north, south, new_a, new_b):
    fold = lax.axis_index("lat") == lat_count - 1
    even = is_even("lat")
    a, b = got_a[...], got_b[...]
    straight = jnp.where(even, a, b)
    south[...] = jnp.where(even, b, a)
    back = LANES - 1 - iota((8, LANES), 1)
    flipped = jnp.concatenate(
        [
            jnp.take_along_axis(straight[i : i + 8], back, axis=1)
            * (-1.0 if i < 2 * fields and i % fields >= fields // 2 else 1.0)
            for i in range(0, straight.shape[0], 8)
        ],
        axis=0,
    )
    north[...] = jnp.where(fold, flipped, straight)
    lane, field = iota((fields, LANES), 1), iota((fields, LANES), 0)
    lane1 = iota((1, LANES), 1)
    for old, new in ((tail_a, new_a), (tail_b, new_b)):
        new[...] = old[...]
    for i, ref in enumerate((north, south)):
        near = ref[0:fields, :]
        ends = jnp.where(
            lane == 2 * field, near[:, 0:1], jnp.where(lane == 2 * field + 1, near[:, LANES - 1 :], 0.0)
        )
        corner = jnp.sum(ends, axis=0, keepdims=True)
        wet = ref[2 * fields : 2 * fields + 1, :]
        wet = jnp.where(lane1 == 0, wet[:, 0:1], wet[:, LANES - 1 :])
        for new in (new_a, new_b):
            new[i : i + 1, :] = corner
            new[2 + i : 3 + i, :] = wet


class Sides:
    def __init__(self, rows, got_a, got_b, msg_a, msg_b):
        lane, row = iota((rows, LANES), 1), iota((rows, LANES), 0)
        self.even = (lane & 1) == 0
        self.even1 = (iota((1, LANES), 1) & 1) == 0
        even = is_even("lon")

        def ordered(a, b, place):
            return jnp.where(even, b[place, :], a[place, :]), jnp.where(even, a[place, :], b[place, :])

        self.got = ordered(got_a, got_b, slice(0, rows))
        self.mine = ordered(msg_a, msg_b, slice(0, rows))
        self.extras = ordered(got_a, got_b, slice(rows, rows + 8))
        self.columns = [
            [
                jnp.sum(jnp.where(lane == i * rows + row, x[4:5], 0.0), axis=1, keepdims=True)
                for i in range(3)
            ]
            for x in self.extras
        ]

    def near(self):
        return jnp.where(self.even, *self.got)

    def far_and_inner(self):
        east, west = self.got
        mine_e, mine_w = self.mine
        far = jnp.where(self.even, pltpu.roll(east, LANES - 1, 1), pltpu.roll(west, 1, 1))
        inner = jnp.where(self.even, pltpu.roll(mine_e, LANES - 1, 1), pltpu.roll(mine_w, 1, 1))
        return far, inner

    def corner(self, i):
        east, west = self.extras
        wets = east[2 + i : 3 + i, 0:1], west[2 + i : 3 + i, 1:2]
        return jnp.where(self.even1, east[i : i + 1], west[i : i + 1]), *wets

    def lanes(self, i):
        return jnp.where(self.even, self.columns[0][i], self.columns[1][i])


def level_matrix(kind, levels, source, target):
    if kind == "mix":
        above = (source == jnp.maximum(target - 1, 0)).astype(F32)
        below = (source == jnp.minimum(target + 1, levels - 1)).astype(F32)
        return above + below - 2.0 * (source == target).astype(F32)
    full = jnp.where(source < target, 1.0, jnp.where(source == target, 0.5, 0.0))
    return (0.5 * GRAVITY) * full


def density_weight(group):
    return jnp.where(group == 0, -THERMAL, jnp.where(group == 1, HALINE, 0.0)).astype(F32)


def advance_columns(sides, wet, coriolis, level_map):
    rows = wet.shape[0]
    mid = sides.near()
    outer, inner = sides.far_and_inner()
    (corner_n, wet_ne, wet_nw), (corner_s, wet_se, wet_sw) = sides.corner(0), sides.corner(1)
    wet_mid, wet_out = sides.lanes(0), sides.lanes(1)
    wet_in = jnp.where(sides.even, wet[:, LANES - 1 :], wet[:, 0:1])
    wet_corner_n = jnp.where(sides.even1, wet_ne, wet_nw)
    wet_corner_s = jnp.where(sides.even1, wet_se, wet_sw)
    mixing = sides.lanes(2)
    lane = iota((rows, LANES), 1)
    row = iota((rows, LANES), 0)
    span = LANES // 4
    group = lane // span

    def ends(outside, inside):
        return jnp.where(sides.even, outside, inside), jnp.where(sides.even, inside, outside)

    def shifted(x, north, south):
        n = jnp.where(row == rows - 1, north, pltpu.roll(x, rows - 1, 0))
        s = jnp.where(row == 0, south, pltpu.roll(x, 1, 0))
        return n, s

    e, w = ends(outer, inner)
    wet_e, wet_w = ends(wet_out, wet_in)
    n, s = shifted(mid, corner_n, corner_s)
    wet_n, wet_s = shifted(wet_mid, wet_corner_n, wet_corner_s)
    lap = wet_e * (e - mid) + wet_w * (w - mid) + wet_n * (n - mid) + wet_s * (s - mid)
    de, dn = e - w, n - s
    one, two, three = (pltpu.roll(mid, i * span, 1) for i in (1, 2, 3))

    def pick(a, b, c, d):
        return jnp.where(group == 0, a, jnp.where(group == 1, b, jnp.where(group == 2, c, d)))

    u = pick(two, three, mid, one)
    v = pick(one, two, three, mid)
    adv = 0.5 * (u * de + v * dn)
    zero = jnp.zeros_like(mid)
    if level_map is None:
        grad_x = HALINE * pltpu.roll(de, span, 1) - THERMAL * pltpu.roll(de, 2 * span, 1)
        grad_y = HALINE * pltpu.roll(dn, 2 * span, 1) - THERMAL * pltpu.roll(dn, 3 * span, 1)
        linear = VERTICAL_MIX * (pltpu.roll(mid, LANES - 2, 1) - mid)
        linear = linear - (0.25 * GRAVITY) * pick(zero, zero, grad_x, grad_y)
    else:
        linear = dot(jnp.concatenate([mid, de, dn], axis=1), level_map)
    turn = pick(zero, zero, coriolis * v, -coriolis * u)
    kappa = jnp.where(group < 2, mixing, VISCOSITY)
    tend = turn - adv + kappa * lap + linear
    return wet_mid * (mid + TIMESTEP * tend)


def advance_rows(levels, parts, level_map):
    fields = 4 * levels
    lane = iota((fields, LANES), 1)
    lane8 = iota((8, LANES), 1)

    def sides(x, east, west, at):
        e = jnp.where(at == LANES - 1, east, pltpu.roll(x, LANES - 1, 1))
        w = jnp.where(at == 0, west, pltpu.roll(x, 1, 1))
        return e, w

    mids, gaps = [], []
    for mid, n, s, (corner_e, corner_w), *_ in parts:
        e, w = sides(mid, corner_e, corner_w, lane)
        mids.append((mid, e, w, n, s))
        gaps += [e - w, n - s]
    vertical = dot(level_map[0:fields, 0:fields], jnp.concatenate([m[0] for m in mids], axis=1))
    grads = dot(level_map[fields:, 0:fields], jnp.concatenate(gaps, axis=1))
    done = []
    for i, (mid, e, w, n, s) in enumerate(mids):
        *_, wets, mixing, coriolis = parts[i]
        wet_mid, wet_n, wet_s, wet_corner_e, wet_corner_w = wets
        wet_e, wet_w = sides(
            jnp.broadcast_to(wet_mid, (8, LANES)), wet_corner_e, wet_corner_w, lane8
        )
        lap = wet_e[0:1] * (e - mid) + wet_w[0:1] * (w - mid)
        lap = lap + wet_n * (n - mid) + wet_s * (s - mid)
        de, dn = gaps[2 * i], gaps[2 * i + 1]
        u, v = mid[2 * levels : 3 * levels], mid[3 * levels :]
        adv = jnp.concatenate([u] * 4, axis=0) * de + jnp.concatenate([v] * 4, axis=0) * dn
        grad_x = grads[:, 2 * i * LANES : (2 * i + 1) * LANES]
        grad_y = grads[:, (2 * i + 1) * LANES : (2 * i + 2) * LANES]
        zero = jnp.zeros((2 * levels, LANES), F32)
        turn = jnp.concatenate([zero, coriolis * v - grad_x, -coriolis * u - grad_y], axis=0)
        kappa = jnp.concatenate(
            [jnp.broadcast_to(mixing, (2 * levels, LANES)), jnp.full(zero.shape, VISCOSITY)],
            axis=0,
        )
        tend = turn - 0.5 * adv + kappa * lap + vertical[:, i * LANES : (i + 1) * LANES]
        done.append(wet_mid * (mid + TIMESTEP * tend))
    return done


COEFFICIENTS = ("te", "tw", "tn", "ts", "tc", "ve", "vw", "vn", "vs", "vc", "adv", "mix", "turn")


def place_of(name, rows):
    i = COEFFICIENTS.index(name)
    return slice(i * rows, (i + 1) * rows)


def coefficients(wet, neighbours, mixing, coriolis):
    made = {}
    for name, kappa in (("t", mixing), ("v", VISCOSITY)):
        rest = wet * (1.0 - 2.0 * TIMESTEP * VERTICAL_MIX)
        for side, wet_n in zip("ewns", neighbours):
            made[name + side] = TIMESTEP * kappa * wet * wet_n
            rest = rest - made[name + side]
        made[name + "c"] = rest
    made["adv"] = (0.5 * TIMESTEP) * wet
    made["mix"] = (TIMESTEP * VERTICAL_MIX) * wet
    made["turn"] = TIMESTEP * coriolis * wet
    return made


def advance_level(k, count, levels, rows, src, sides, coef, acc):
    pitch = rows + 2 * PAD
    lane = iota((rows, LANES), 1)
    first, last = lane == 0, lane == LANES - 1
    above_k = jnp.maximum(k - 1, 0)
    below_k = jnp.minimum(k + 1, levels - 1)

    def load(q, level, shift):
        return src[pl.ds((q * count + level) * pitch + PAD + shift, rows), :]

    def base(q):
        return pl.multiple_of((q * count + k) * pitch + PAD, 8)

    center = [load(q, k, 0) for q in range(4)]
    u, v = coef("adv") * center[2], coef("adv") * center[3]
    sums, de, dn = [], [], []
    for q in range(4):
        c = center[q]
        n, s = load(q, k, 1), load(q, k, -1)
        edge = pltpu.roll(sides, (LANES - 1 - 2 * (q * levels + k)) & (LANES - 1), 1)
        e = jnp.where(last, edge, pltpu.roll(c, LANES - 1, 1))
        w = jnp.where(first, edge, pltpu.roll(c, 1, 1))
        kind = "t" if q < 2 else "v"
        lap = coef(kind + "c") * c + coef(kind + "e") * e + coef(kind + "w") * w
        lap = lap + coef(kind + "n") * n + coef(kind + "s") * s
        de.append(e - w)
        dn.append(n - s)
        sums.append(lap - (u * de[q] + v * dn[q]))
    scale = 0.5 * GRAVITY / VERTICAL_MIX
    dens_x = (scale * HALINE) * de[1] - (scale * THERMAL) * de[0]
    dens_y = (scale * HALINE) * dn[1] - (scale * THERMAL) * dn[0]
    acc_x, acc_y = acc
    grad = (None, None, acc_x + 0.5 * dens_x, acc_y + 0.5 * dens_y)
    turn = (None, None, coef("turn") * center[3], -coef("turn") * center[2])
    new = []
    for q in range(4):
        vertical = load(q, above_k, 0) + load(q, below_k, 0)
        if grad[q] is not None:
            vertical = vertical - grad[q]
        total = sums[q] + coef("mix") * vertical
        new.append(total if turn[q] is None else total + turn[q])
    return new, (acc_x + dens_x, acc_y + dens_y)


def advance_top_rows(levels, sides, north, south, state, wet, rows, table):
    fields = 4 * levels

    def both(a, b):
        return jnp.concatenate([a, b], axis=0)

    def rows_at(first):
        return both(
            north[pl.ds(first, 4, stride=levels), :], south[pl.ds(first, 4, stride=levels), :]
        )

    lane, row = iota((8, LANES), 1), iota((8, LANES), 0)
    upper = row < 4
    field = row & 3
    inside_n = state[pl.ds(rows - 1, 4, stride=levels * rows), :]
    inside_s = state[pl.ds(0, 4, stride=levels * rows), :]
    mid, below, outer = rows_at(0), rows_at(1), rows_at(fields)
    n = both(outer[0:4], inside_s)
    s = both(inside_n, outer[4:8])
    (corner_n, wet_ne, wet_nw), (corner_s, wet_se, wet_sw) = sides.corner(0), sides.corner(1)
    corner = jnp.where(upper, corner_n, corner_s)
    at = 2 * levels * field

    def end(parity):
        return jnp.sum(jnp.where(lane == at + parity, corner, 0.0), axis=1, keepdims=True)

    def west_east(x, east, west):
        return (
            jnp.where(lane == LANES - 1, east, pltpu.roll(x, LANES - 1, 1)),
            jnp.where(lane == 0, west, pltpu.roll(x, 1, 1)),
        )

    def tail(i):
        place = slice(2 * fields + i, 2 * fields + i + 1)
        return north[place, :], south[place, :]

    e, w = west_east(mid, end(0), end(1))
    wet_mid = jnp.where(upper, *tail(0))
    wet_e, wet_w = west_east(
        wet_mid, jnp.where(upper, wet_ne, wet_se), jnp.where(upper, wet_nw, wet_sw)
    )
    out_n, out_s = tail(1)
    wet_n = jnp.where(upper, out_n, wet[0:1])
    wet_s = jnp.where(upper, wet[rows - 1 : rows], out_s)
    lap = wet_e * (e - mid) + wet_w * (w - mid) + wet_n * (n - mid) + wet_s * (s - mid)
    de, dn = e - w, n - s

    def of(x, i):
        return jnp.where(upper, x[i : i + 1], x[4 + i : 5 + i])

    u, v = of(mid, 2), of(mid, 3)
    coriolis = jnp.where(upper, table[PAD + rows : PAD + rows + 1], table[PAD - 1 : PAD])
    grad_x = (0.25 * GRAVITY) * (HALINE * of(de, 1) - THERMAL * of(de, 0))
    grad_y = (0.25 * GRAVITY) * (HALINE * of(dn, 1) - THERMAL * of(dn, 0))
    turn = jnp.where(
        field < 2, 0.0, jnp.where(field == 2, coriolis * v - grad_x, -coriolis * u - grad_y)
    )
    kappa = jnp.where(field < 2, jnp.where(upper, *tail(2)), VISCOSITY)
    tend = turn - 0.5 * (u * de + v * dn) + kappa * lap + VERTICAL_MIX * (below - mid)
    return wet_mid * (mid + TIMESTEP * tend)


def surface_kernel(
    rows, levels,
    state, base, msg_a, msg_b, got_a, got_b, north, south, out_in, ids,
    coef, side, out, now, later, wet_pad, stage, places, sem,
):
    fields = 4 * levels
    pitch = rows + 2 * PAD
    to_scalars = pltpu.make_async_copy(ids, places, sem)
    to_scalars.start()
    out[...] = out_in[...]
    wet = base[0:rows, :]
    mixing = base[rows : 2 * rows, :]
    table = base[2 * rows :, :]
    coriolis = table[PAD : PAD + rows]
    lane = iota((rows, LANES), 1)
    sides = Sides(rows, got_a, got_b, msg_a, msg_b)
    wet_pad[PAD : PAD + rows, :] = wet
    wet_pad[PAD - 1 : PAD, :] = south[2 * fields : 2 * fields + 1, :]
    wet_pad[PAD + rows : PAD + rows + 1, :] = north[2 * fields : 2 * fields + 1, :]
    wet_n = wet_pad[PAD + 1 : PAD + 1 + rows, :]
    wet_s = wet_pad[PAD - 1 : PAD - 1 + rows, :]
    wet_e = jnp.where(lane == LANES - 1, sides.columns[0][0], pltpu.roll(wet, LANES - 1, 1))
    wet_w = jnp.where(lane == 0, sides.columns[1][0], pltpu.roll(wet, 1, 1))
    made = coefficients(wet, (wet_e, wet_w, wet_n, wet_s), mixing, coriolis)
    for name in COEFFICIENTS:
        coef[place_of(name, rows)] = made[name]
    near = sides.near()
    side[...] = near

    count = now.shape[0] // (4 * pitch)
    for q in range(4):
        for k in range(count):
            field = (q * levels + k) * rows
            at = (q * count + k) * pitch + PAD
            now[at : at + rows, :] = state[field : field + rows, :]
            now[at + rows : at + rows + 1, :] = north[q * levels + k : q * levels + k + 1, :]
            now[at - 1 : at, :] = south[q * levels + k : q * levels + k + 1, :]

    def read(name):
        return coef[place_of(name, rows)]

    none = jnp.zeros((rows, LANES), F32)
    acc = (none, none)
    edge_rows = advance_top_rows(levels, sides, north, south, state, wet, rows, table)
    edge_cols = advance_columns(sides, wet, coriolis, None)
    for k in range(count - 1):
        new, acc = advance_level(k, count, levels, rows, now, near, read, acc)
        for q in range(4):
            at = (q * count + k) * pitch + PAD
            later[at : at + rows, :] = new[q]
            if k == 0:
                later[at + rows : at + rows + 1, :] = edge_rows[q : q + 1]
                later[at - 1 : at, :] = edge_rows[4 + q : 5 + q]
    new, _ = advance_level(0, count, levels, rows, later, edge_cols, read, (none, none))
    for q in range(4):
        stage[pl.ds(q, rows, stride=4), :] = new[q]
    to_scalars.wait()
    for r in range(rows):
        out[pl.ds(places[0, r], 4), :] = stage[4 * r : 4 * r + 4, :]


def halo_after_first(rows, levels, sides, north, south, state, wet, table, col_map, row_map):
    fields = 4 * levels
    side_new = advance_columns(sides, wet, table[PAD : PAD + rows], col_map)
    lane, field = iota((fields, LANES), 1), iota((fields, LANES), 0)

    def to_sublanes(x, parity):
        here = lane == 2 * field + parity
        return jnp.sum(jnp.where(here, x, 0.0), axis=1, keepdims=True)

    parts = []
    for north_side, ref, line, lat_row in (
        (True, north, rows - 1, PAD + rows),
        (False, south, 0, PAD - 1),
    ):
        corner, *corner_wets = sides.corner(0 if north_side else 1)
        inside = state[pl.ds(line, fields, stride=rows), :]
        tail = ref[2 * fields :, :]
        pair = (ref[fields : 2 * fields, :], inside), (tail[1:2], wet[line : line + 1])
        (n, s), (wet_n, wet_s) = pair if north_side else [x[::-1] for x in pair]
        parts.append(
            (
                ref[0:fields, :], n, s, (to_sublanes(corner, 0), to_sublanes(corner, 1)),
                (tail[0:1], wet_n, wet_s, *corner_wets),
                tail[2:3], table[lat_row : lat_row + 1],
            )
        )
    return side_new, *advance_rows(levels, parts, row_map)


def main_kernel(
    rows, levels, chunks,
    state, base, msg_a, msg_b, got_a, got_b, north, south, col_map, row_map, coefs, side,
    tr_hbm, ve_hbm, now, later, side_new, tr_out, ve_out, sems,
):
    fields = 4 * levels
    pitch = rows + 2 * PAD
    sides = Sides(rows, got_a, got_b, msg_a, msg_b)
    side_new[...], north_new, south_new = halo_after_first(
        rows, levels, sides, north, south, state, base[0:rows, :], base[2 * rows :, :],
        col_map[...], row_map[...],
    )
    edges = (now, north[0:fields, :], south[0:fields, :]), (later, north_new, south_new)
    for buf, n, s in edges:
        buf[pl.ds(PAD - 1, fields, stride=pitch), :] = s
        buf[pl.ds(PAD + rows, fields, stride=pitch), :] = n

    def fill(f, carry):
        x = state[pl.ds(pl.multiple_of(f * rows, 8), rows), :]
        now[pl.ds(pl.multiple_of(f * pitch + PAD, 8), rows), :] = x
        return carry

    lax.fori_loop(0, fields, fill, 0, unroll=8)

    def coef(name):
        return coefs[place_of(name, rows)]

    def first(k, acc):
        new, acc = advance_level(k, levels, levels, rows, now, side[...], coef, acc)
        for q in range(4):
            place = pl.multiple_of((q * levels + k) * pitch + PAD, 8)
            later[pl.ds(place, rows), :] = new[q]
        return acc

    def second(k, acc):
        new, acc = advance_level(k, levels, levels, rows, later, side_new[...], coef, acc)
        for q in range(4):
            ref = tr_out if q < 2 else ve_out
            place = pl.multiple_of(((q % 2) * levels + k) * rows, 8)
            ref[pl.ds(place, rows), :] = new[q]
        return acc

    none = jnp.zeros((rows, LANES), F32)
    lax.fori_loop(0, levels, first, (none, none), unroll=2)
    acc = (none, none)
    size = levels // chunks
    copies = []
    for i in range(chunks):
        acc = lax.fori_loop(i * size, (i + 1) * size, second, acc, unroll=2)
        for src, dst in ((tr_out, tr_hbm), (ve_out, ve_hbm)):
            for q in range(2):
                start = (q * levels + i * size) * rows
                part = slice(start, start + size * rows)
                copy = pltpu.make_async_copy(src.at[part], dst.at[part], sems.at[len(copies)])
                copy.start()
                copies.append(copy)
    for copy in copies:
        copy.wait()


def reduce_kernel(devices, data, surface, cover):
    slot_rows = data.shape[0] // devices

    def rows_of(i):
        return data[pl.ds(i, devices, stride=slot_rows), :]

    width = LANES // CAP
    lines = rows_of(5 * CAP)
    named = (lines == (iota((devices, LANES), 1) % width).astype(F32)).astype(F32)
    to_rows, values = [], []
    for slot in range(CAP):
        to_rows.append(named[:, slot * width : slot * width + ATM_ROWS])
        parts = [rows_of(4 * slot + q) for q in range(4)] + [rows_of(4 * CAP + slot)]
        values.append(jnp.concatenate(parts, axis=1))
    totals = dot(
        jnp.concatenate(to_rows, axis=0), jnp.concatenate(values, axis=0), (((0,), (0,)), ((), ()))
    )
    ocean = totals[:, 4 * LANES :]
    cover[...] = ocean
    share = jnp.maximum(ocean, 1.0)
    for q in range(4):
        surface[q] = totals[:, q * LANES : (q + 1) * LANES] / share


def call(kernel, out_shape, limit=VMEM_LIMIT, **kwargs):
    return pl.pallas_call(
        kernel,
        out_shape=out_shape,
        compiler_params=pltpu.CompilerParams(vmem_limit_bytes=limit),
        **kwargs,
    )


def shaped(*shape, dtype=F32):
    return jax.ShapeDtypeStruct(shape, dtype)


def lat_swaps(lon_count, lat_count):
    swap_a, swap_b = [], []
    for i in range(lon_count):
        for a in range(lat_count):
            here = i * lat_count + a
            swap_a.append((here, i * lat_count + (a ^ 1)))
            if a == lat_count - 1:
                swap_b.append((here, (lon_count - 1 - i) * lat_count + a))
            elif a > 0:
                swap_b.append((here, here + 1 if a % 2 else here - 1))
    return swap_a, swap_b


def local(tracers, velocity, land_mask, mixing, owners, atm_row):
    levels = tracers.shape[1]
    rows, cols = land_mask.shape
    fields = 4 * levels
    lon_count, lat_count = lax.axis_size("lon"), lax.axis_size("lat")
    devices = lon_count * lat_count
    assert cols == LANES and rows % 8 == 0 and 2 * fields == LANES
    assert lon_count % 2 == 0 and lat_count % 2 == 0 and 3 * rows <= LANES
    length = 2 * fields + 8
    pitch = rows + 2 * PAD
    flat = 2 * levels * rows
    hbm = pl.BlockSpec(memory_space=pltpu.HBM)
    smem = pl.BlockSpec(memory_space=pltpu.SMEM)
    vmem = pl.BlockSpec(memory_space=pltpu.VMEM)

    deep = (2 * levels, rows, cols)
    lat_a, lat_b = call(
        functools.partial(edge_kernel, rows, fields),
        [shaped(length, cols)] * 2,
        limit=VMEM_ALL,
        in_specs=[hbm] * 4,
        scratch_shapes=[
            pltpu.VMEM((2, fields, 8, cols), F32),
            pltpu.VMEM((rows, cols), jnp.int32),
            pltpu.VMEM((rows, cols), F32),
            pltpu.SemaphoreType.DMA((6,)),
        ],
    )(tracers.reshape(deep), velocity.reshape(deep), land_mask, mixing)
    swap_a, swap_b = lat_swaps(lon_count, lat_count)
    got_lat_b = lax.ppermute(lat_b, ("lon", "lat"), swap_b)
    got_lat_a = lax.ppermute(lat_a, ("lon", "lat"), swap_a)

    tr, ve = tracers.reshape(flat, cols), velocity.reshape(flat, cols)
    msg_a, msg_b = call(
        functools.partial(pack_kernel, rows, fields),
        [shaped(rows + 8, cols)] * 2,
        in_specs=[vmem] * 4,
    )(tr, ve, land_mask, mixing)

    slot_rows = 5 * CAP + 1
    state, base, col_map, row_map, outgoing, ids = call(
        functools.partial(prepare_kernel, rows, levels, devices),
        [
            shaped(fields * rows, cols),
            shaped(2 * rows + pitch, cols),
            shaped(3 * cols, cols),
            shaped(fields + levels, cols),
            shaped(devices * slot_rows, cols),
            shaped(8, cols, dtype=jnp.int32),
        ],
        in_specs=[vmem] * 4 + [smem] * 2,
        scratch_shapes=[pltpu.SMEM((devices,), jnp.int32)],
    )(tr, ve, land_mask, mixing, owners.reshape(rows), atm_row)

    def full(n):
        return pl.BlockSpec((n, cols), lambda i: (0, 0))

    tail = pl.BlockSpec((8, cols), lambda i: (rows // 8, 0))
    north, south, msg_a, msg_b = call(
        functools.partial(corner_kernel, lat_count, fields),
        [shaped(length, cols)] * 2 + [shaped(rows + 8, cols)] * 2,
        grid=(1,),
        in_specs=[full(length), full(length), tail, tail],
        out_specs=[full(length), full(length), tail, tail],
        input_output_aliases={2: 2, 3: 3},
    )(got_lat_b, got_lat_a, msg_a, msg_b)
    even_pairs = [(i, i ^ 1) for i in range(lon_count)]
    odd_pairs = [(i, (i + 1 if i % 2 else i - 1) % lon_count) for i in range(lon_count)]
    got_b = lax.ppermute(msg_b, "lon", even_pairs)
    got_a = lax.ppermute(msg_a, "lon", odd_pairs)

    count = min(3, levels)
    coefs, side, outgoing = call(
        functools.partial(surface_kernel, rows, levels),
        [
            shaped(len(COEFFICIENTS) * rows, cols),
            shaped(rows, cols),
            shaped(devices * slot_rows, cols),
        ],
        scratch_shapes=[
            pltpu.VMEM((4 * count * pitch, cols), F32),
            pltpu.VMEM((4 * count * pitch, cols), F32),
            pltpu.VMEM((pitch, cols), F32),
            pltpu.VMEM((4 * rows, cols), F32),
            pltpu.SMEM((8, cols), jnp.int32),
            pltpu.SemaphoreType.DMA,
        ],
    )(state, base, msg_a, msg_b, got_a, got_b, north, south, outgoing, ids)
    incoming = lax.all_to_all(
        outgoing.reshape(devices, slot_rows, 1, cols), ("lat", "lon"), 0, 0, tiled=True
    ).reshape(devices * slot_rows, cols)

    chunks = 4
    tr_out, ve_out = call(
        functools.partial(main_kernel, rows, levels, chunks),
        [shaped(flat, cols), shaped(flat, cols)],
        in_specs=[vmem] * 12,
        out_specs=[hbm] * 2,
        scratch_shapes=[
            pltpu.VMEM((fields * pitch, cols), F32),
            pltpu.VMEM((fields * pitch, cols), F32),
            pltpu.VMEM((rows, cols), F32),
            pltpu.VMEM((flat, cols), F32),
            pltpu.VMEM((flat, cols), F32),
            pltpu.SemaphoreType.DMA((4 * chunks,)),
        ],
        cost_estimate=pl.CostEstimate(
            flops=80 * fields * rows * cols, bytes_accessed=5 << 20, transcendentals=0
        ),
    )(state, base, msg_a, msg_b, got_a, got_b, north, south, col_map, row_map, coefs, side)
    surface, cover = call(
        functools.partial(reduce_kernel, devices),
        [shaped(4, ATM_ROWS, cols), shaped(ATM_ROWS, cols)],
    )(incoming)
    shape = (2, levels, rows, cols)
    return tr_out.reshape(shape), ve_out.reshape(shape), surface, cover


def solution(mesh):
    in_specs = (
        P(None, None, "lat", "lon"),
        P(None, None, "lat", "lon"),
        P("lat", "lon"),
        P("lat", "lon"),
        P(("lon", "lat"), None),
        P(("lon", "lat")),
    )
    out_specs = (
        P(None, None, "lat", "lon"),
        P(None, None, "lat", "lon"),
        P(None, ("lon", "lat"), None),
        P(("lon", "lat"), None),
    )
    return jax.shard_map(local, mesh=mesh, in_specs=in_specs, out_specs=out_specs, check_vma=False)
```

```python
import functools
import math

import jax
import jax.numpy as jnp
from jax import lax
from jax.experimental import pallas as pl
from jax.experimental.pallas import tpu as pltpu
from jax.sharding import PartitionSpec as P

ATM_ROWS = 32
CAP = 2

THERMAL = 0.2
HALINE = 0.15
GRAVITY = 0.2
TIMESTEP = 0.8
VERTICAL_MIX = 0.1
VISCOSITY = 0.2
CORIOLIS_MAX = 0.3

LANES = 128
PAD = 8
EXACT = lax.Precision.HIGHEST
F32 = jnp.float32
VMEM_LIMIT = 32 * 1024 * 1024
VMEM_ALL = 62 * 1024 * 1024


def iota(shape, dim):
    return lax.broadcasted_iota(jnp.int32, shape, dim)


def dot(a, b, dims=(((1,), (0,)), ((), ()))):
    return lax.dot_general(a, b, dims, precision=EXACT, preferred_element_type=F32)


def is_even(axis):
    return lax.rem(lax.axis_index(axis), 2) == 0


def start_copies(pairs, sems):
    copies = [pltpu.make_async_copy(src, dst, sems.at[i]) for i, (src, dst) in enumerate(pairs)]
    for copy in copies:
        copy.start()
    return copies


def edge_kernel(rows, fields, tr_hbm, ve_hbm, mask_hbm, mix_hbm, lat_a, lat_b, edges, mask, mix, sems):
    half = fields // 2
    pairs = [(mask_hbm, mask), (mix_hbm, mix)]
    for n, src in enumerate((tr_hbm, ve_hbm)):
        for side, first in enumerate((0, rows - 8)):
            part = edges.at[side, n * half : (n + 1) * half]
            pairs.append((src.at[:, first : first + 8, :], part))
    for copy in start_copies(pairs, sems):
        copy.wait()
    flat = edges.reshape(2 * fields * 8, LANES)
    even = is_even("lat")
    top = ((rows - 1, 8 * fields + 7), (rows - 2, 8 * fields + 6))
    bottom = ((0, 0), (1, 1))
    for buf, first, second in ((lat_a, top, bottom), (lat_b, bottom, top)):
        (near, near_at), (far, far_at) = [
            [jnp.where(even, x, y) for x, y in zip(one, other)] for one, other in zip(first, second)
        ]
        wet_near = mask[pl.ds(near, 1), :].astype(F32)
        wet_far = mask[pl.ds(far, 1), :].astype(F32)
        buf[0:fields, :] = flat[pl.ds(near_at, fields, stride=8), :] * wet_near
        buf[fields : 2 * fields, :] = flat[pl.ds(far_at, fields, stride=8), :] * wet_far
        buf[2 * fields : 2 * fields + 8, :] = jnp.zeros((8, LANES), F32)
        buf[2 * fields : 2 * fields + 1, :] = wet_near
        buf[2 * fields + 1 : 2 * fields + 2, :] = wet_far
        buf[2 * fields + 2 : 2 * fields + 3, :] = mix[pl.ds(near, 1), :]


def pack_kernel(rows, fields, tr, ve, mask, mix, msg_a, msg_b):
    half = fields // 2
    wet = mask[...].astype(F32)
    lane = iota((rows, LANES), 1)
    pair = lane >> 1

    def columns(ref, base):
        def body(f, carry):
            to_east, to_west = carry
            x = ref[pl.ds(pl.multiple_of(f * rows, rows), rows), :]
            keep = pair == base + f
            low = 2 * (base + f)
            to_east = jnp.where(keep, pltpu.roll(x, (low + 2) & (LANES - 1), 1), to_east)
            to_west = jnp.where(keep, pltpu.roll(x, low, 1), to_west)
            return to_east, to_west

        return body

    carry = (jnp.zeros((rows, LANES), F32), jnp.zeros((rows, LANES), F32))
    for ref, base in ((tr, 0), (ve, half)):
        carry = lax.fori_loop(0, half, columns(ref, base), carry, unroll=8)
    def spread(x, i):
        return jnp.broadcast_to(x[:, i : i + 1], (rows, LANES))

    odd = (lane & 1) == 1
    to_east = carry[0] * jnp.where(odd, spread(wet, LANES - 1), spread(wet, LANES - 2))
    to_west = carry[1] * jnp.where(odd, spread(wet, 1), spread(wet, 0))
    even = is_even("lon")
    row = iota((rows, LANES), 0)
    mixing = mix[...]
    lines = []
    for near, far in ((LANES - 1, LANES - 2), (0, 1)):
        line = jnp.zeros((rows, LANES), F32)
        for part, column in enumerate((wet[:, near], wet[:, far], mixing[:, near])):
            line = jnp.where(lane == part * rows + row, column[:, None], line)
        lines.append(jnp.sum(line, axis=0, keepdims=True))
    for msg, flag in ((msg_a, jnp.logical_not(even)), (msg_b, even)):
        msg[0:rows, :] = jnp.where(flag, to_east, to_west)
        msg[rows:, :] = jnp.zeros((8, LANES), F32)
        msg[rows + 4 : rows + 5, :] = jnp.where(flag, *lines)


def prepare_kernel(
    rows, levels, devices, tr, ve, mask, mix, own, atm_row,
    state, base, col_map, row_map, out, ids, used,
):
    fields = 4 * levels
    half = fields // 2
    wet = mask[...].astype(F32)
    base[0:rows, :] = wet
    base[rows : 2 * rows, :] = mix[...]
    for ref, first in ((tr, 0), (ve, half)):

        def fill(f, carry, ref=ref, first=first):
            x = ref[pl.ds(pl.multiple_of(f * rows, 8), rows), :] * wet
            state[pl.ds(pl.multiple_of((first + f) * rows, 8), rows), :] = x
            return carry

        lax.fori_loop(0, half, fill, 0, unroll=8)

    total = lax.axis_size("lat") * rows
    latitude = lax.axis_index("lat") * rows - PAD + iota((rows + 2 * PAD, LANES), 0)
    latitude = jnp.where(latitude >= total, 2 * total - 1 - latitude, latitude).astype(F32)
    table = CORIOLIS_MAX * jnp.sin(math.pi * (-0.43 + 0.93 * (latitude + 0.5) / total))
    base[2 * rows :, :] = table

    span = 2 * levels
    src, dst = iota((LANES, LANES), 0), iota((LANES, LANES), 1)
    src_group, dst_group = src // span, dst // span
    src_level, dst_level = (src // 2) % levels, (dst // 2) % levels
    same_side = (src & 1) == (dst & 1)
    mixes = VERTICAL_MIX * level_matrix("mix", levels, src_level, dst_level)
    press = level_matrix("pressure", levels, src_level, dst_level) * density_weight(src_group)
    col_map[0:LANES, :] = jnp.where(same_side & (src_group == dst_group), mixes, 0.0)
    col_map[LANES : 2 * LANES, :] = jnp.where(same_side & (dst_group == 2), -press, 0.0)
    col_map[2 * LANES :, :] = jnp.where(same_side & (dst_group == 3), -press, 0.0)

    dst, src = iota((fields, fields), 0), iota((fields, fields), 1)
    mixes = VERTICAL_MIX * level_matrix("mix", levels, src % levels, dst % levels)
    row_map[0:fields, 0:fields] = jnp.where(dst // levels == src // levels, mixes, 0.0)
    dst, src = iota((levels, fields), 0), iota((levels, fields), 1)
    press = level_matrix("pressure", levels, src % levels, dst) * density_weight(src // levels)
    row_map[fields:, 0:fields] = press

    slot_rows = out.shape[0] // devices

    def clear(d, carry):
        used[d] = 0
        return carry

    lax.fori_loop(0, devices, clear, 0, unroll=8)
    out[...] = jnp.zeros(out.shape, F32)
    lane1 = iota((1, LANES), 1)
    places = jnp.zeros((1, LANES), jnp.int32)
    for r in range(rows):
        owner = own[r]
        slot = used[owner]
        used[owner] = slot + 1
        start = (devices - 1 - owner) * slot_rows
        places = jnp.where(lane1 == r, start + 4 * slot, places)
        out[pl.ds(start + 4 * CAP + slot, 1), :] = base[r : r + 1, :]
        line = out[pl.ds(start + 5 * CAP, 1), :]
        target = jnp.full((1, LANES), atm_row[r], jnp.int32).astype(F32)
        out[pl.ds(start + 5 * CAP, 1), :] = jnp.where(lane1 // (LANES // CAP) == slot, target, line)
    ids[...] = jnp.zeros(ids.shape, jnp.int32)
    ids[0:1, :] = places


def corner_kernel(lat_count, fields, got_b, got_a, tail_a, tail_b, north, south, new_a, new_b):
    fold = lax.axis_index("lat") == lat_count - 1
    even = is_even("lat")
    a, b = got_a[...], got_b[...]
    straight = jnp.where(even, a, b)
    south[...] = jnp.where(even, b, a)
    back = LANES - 1 - iota((8, LANES), 1)
    flipped = jnp.concatenate(
        [
            jnp.take_along_axis(straight[i : i + 8], back, axis=1)
            * (-1.0 if i < 2 * fields and i % fields >= fields // 2 else 1.0)
            for i in range(0, straight.shape[0], 8)
        ],
        axis=0,
    )
    north[...] = jnp.where(fold, flipped, straight)
    lane, field = iota((fields, LANES), 1), iota((fields, LANES), 0)
    lane1 = iota((1, LANES), 1)
    for old, new in ((tail_a, new_a), (tail_b, new_b)):
        new[...] = old[...]
    for i, ref in enumerate((north, south)):
        near = ref[0:fields, :]
        ends = jnp.where(
            lane == 2 * field, near[:, 0:1], jnp.where(lane == 2 * field + 1, near[:, LANES - 1 :], 0.0)
        )
        corner = jnp.sum(ends, axis=0, keepdims=True)
        wet = ref[2 * fields : 2 * fields + 1, :]
        wet = jnp.where(lane1 == 0, wet[:, 0:1], wet[:, LANES - 1 :])
        for new in (new_a, new_b):
            new[i : i + 1, :] = corner
            new[2 + i : 3 + i, :] = wet


class Sides:
    def __init__(self, rows, got_a, got_b, msg_a, msg_b):
        lane, row = iota((rows, LANES), 1), iota((rows, LANES), 0)
        self.even = (lane & 1) == 0
        self.even1 = (iota((1, LANES), 1) & 1) == 0
        even = is_even("lon")

        def ordered(a, b, place):
            return jnp.where(even, b[place, :], a[place, :]), jnp.where(even, a[place, :], b[place, :])

        self.got = ordered(got_a, got_b, slice(0, rows))
        self.mine = ordered(msg_a, msg_b, slice(0, rows))
        self.extras = ordered(got_a, got_b, slice(rows, rows + 8))
        self.columns = [
            [
                jnp.sum(jnp.where(lane == i * rows + row, x[4:5], 0.0), axis=1, keepdims=True)
                for i in range(3)
            ]
            for x in self.extras
        ]

    def near(self):
        return jnp.where(self.even, *self.got)

    def far_and_inner(self):
        east, west = self.got
        mine_e, mine_w = self.mine
        far = jnp.where(self.even, pltpu.roll(east, LANES - 1, 1), pltpu.roll(west, 1, 1))
        inner = jnp.where(self.even, pltpu.roll(mine_e, LANES - 1, 1), pltpu.roll(mine_w, 1, 1))
        return far, inner

    def corner(self, i):
        east, west = self.extras
        wets = east[2 + i : 3 + i, 0:1], west[2 + i : 3 + i, 1:2]
        return jnp.where(self.even1, east[i : i + 1], west[i : i + 1]), *wets

    def lanes(self, i):
        return jnp.where(self.even, self.columns[0][i], self.columns[1][i])


def level_matrix(kind, levels, source, target):
    if kind == "mix":
        above = (source == jnp.maximum(target - 1, 0)).astype(F32)
        below = (source == jnp.minimum(target + 1, levels - 1)).astype(F32)
        return above + below - 2.0 * (source == target).astype(F32)
    full = jnp.where(source < target, 1.0, jnp.where(source == target, 0.5, 0.0))
    return (0.5 * GRAVITY) * full


def density_weight(group):
    return jnp.where(group == 0, -THERMAL, jnp.where(group == 1, HALINE, 0.0)).astype(F32)


def advance_columns(sides, wet, coriolis, level_map):
    rows = wet.shape[0]
    mid = sides.near()
    outer, inner = sides.far_and_inner()
    (corner_n, wet_ne, wet_nw), (corner_s, wet_se, wet_sw) = sides.corner(0), sides.corner(1)
    wet_mid, wet_out = sides.lanes(0), sides.lanes(1)
    wet_in = jnp.where(sides.even, wet[:, LANES - 1 :], wet[:, 0:1])
    wet_corner_n = jnp.where(sides.even1, wet_ne, wet_nw)
    wet_corner_s = jnp.where(sides.even1, wet_se, wet_sw)
    mixing = sides.lanes(2)
    lane = iota((rows, LANES), 1)
    row = iota((rows, LANES), 0)
    span = LANES // 4
    group = lane // span

    def ends(outside, inside):
        return jnp.where(sides.even, outside, inside), jnp.where(sides.even, inside, outside)

    def shifted(x, north, south):
        n = jnp.where(row == rows - 1, north, pltpu.roll(x, rows - 1, 0))
        s = jnp.where(row == 0, south, pltpu.roll(x, 1, 0))
        return n, s

    e, w = ends(outer, inner)
    wet_e, wet_w = ends(wet_out, wet_in)
    n, s = shifted(mid, corner_n, corner_s)
    wet_n, wet_s = shifted(wet_mid, wet_corner_n, wet_corner_s)
    lap = wet_e * (e - mid) + wet_w * (w - mid) + wet_n * (n - mid) + wet_s * (s - mid)
    de, dn = e - w, n - s
    one, two, three = (pltpu.roll(mid, i * span, 1) for i in (1, 2, 3))

    def pick(a, b, c, d):
        return jnp.where(group == 0, a, jnp.where(group == 1, b, jnp.where(group == 2, c, d)))

    u = pick(two, three, mid, one)
    v = pick(one, two, three, mid)
    adv = 0.5 * (u * de + v * dn)
    zero = jnp.zeros_like(mid)
    if level_map is None:
        grad_x = HALINE * pltpu.roll(de, span, 1) - THERMAL * pltpu.roll(de, 2 * span, 1)
        grad_y = HALINE * pltpu.roll(dn, 2 * span, 1) - THERMAL * pltpu.roll(dn, 3 * span, 1)
        linear = VERTICAL_MIX * (pltpu.roll(mid, LANES - 2, 1) - mid)
        linear = linear - (0.25 * GRAVITY) * pick(zero, zero, grad_x, grad_y)
    else:
        linear = dot(jnp.concatenate([mid, de, dn], axis=1), level_map)
    turn = pick(zero, zero, coriolis * v, -coriolis * u)
    kappa = jnp.where(group < 2, mixing, VISCOSITY)
    tend = turn - adv + kappa * lap + linear
    return wet_mid * (mid + TIMESTEP * tend)


def advance_rows(levels, parts, level_map):
    fields = 4 * levels
    lane = iota((fields, LANES), 1)
    lane8 = iota((8, LANES), 1)

    def sides(x, east, west, at):
        e = jnp.where(at == LANES - 1, east, pltpu.roll(x, LANES - 1, 1))
        w = jnp.where(at == 0, west, pltpu.roll(x, 1, 1))
        return e, w

    mids, gaps = [], []
    for mid, n, s, (corner_e, corner_w), *_ in parts:
        e, w = sides(mid, corner_e, corner_w, lane)
        mids.append((mid, e, w, n, s))
        gaps += [e - w, n - s]
    vertical = dot(level_map[0:fields, 0:fields], jnp.concatenate([m[0] for m in mids], axis=1))
    grads = dot(level_map[fields:, 0:fields], jnp.concatenate(gaps, axis=1))
    done = []
    for i, (mid, e, w, n, s) in enumerate(mids):
        *_, wets, mixing, coriolis = parts[i]
        wet_mid, wet_n, wet_s, wet_corner_e, wet_corner_w = wets
        wet_e, wet_w = sides(
            jnp.broadcast_to(wet_mid, (8, LANES)), wet_corner_e, wet_corner_w, lane8
        )
        lap = wet_e[0:1] * (e - mid) + wet_w[0:1] * (w - mid)
        lap = lap + wet_n * (n - mid) + wet_s * (s - mid)
        de, dn = gaps[2 * i], gaps[2 * i + 1]
        u, v = mid[2 * levels : 3 * levels], mid[3 * levels :]
        adv = jnp.concatenate([u] * 4, axis=0) * de + jnp.concatenate([v] * 4, axis=0) * dn
        grad_x = grads[:, 2 * i * LANES : (2 * i + 1) * LANES]
        grad_y = grads[:, (2 * i + 1) * LANES : (2 * i + 2) * LANES]
        zero = jnp.zeros((2 * levels, LANES), F32)
        turn = jnp.concatenate([zero, coriolis * v - grad_x, -coriolis * u - grad_y], axis=0)
        kappa = jnp.concatenate(
            [jnp.broadcast_to(mixing, (2 * levels, LANES)), jnp.full(zero.shape, VISCOSITY)],
            axis=0,
        )
        tend = turn - 0.5 * adv + kappa * lap + vertical[:, i * LANES : (i + 1) * LANES]
        done.append(wet_mid * (mid + TIMESTEP * tend))
    return done


COEFFICIENTS = ("te", "tw", "tn", "ts", "tc", "ve", "vw", "vn", "vs", "vc", "adv", "mix", "turn")


def place_of(name, rows):
    i = COEFFICIENTS.index(name)
    return slice(i * rows, (i + 1) * rows)


def coefficients(wet, neighbours, mixing, coriolis):
    made = {}
    for name, kappa in (("t", mixing), ("v", VISCOSITY)):
        rest = wet * (1.0 - 2.0 * TIMESTEP * VERTICAL_MIX)
        for side, wet_n in zip("ewns", neighbours):
            made[name + side] = TIMESTEP * kappa * wet * wet_n
            rest = rest - made[name + side]
        made[name + "c"] = rest
    made["adv"] = (0.5 * TIMESTEP) * wet
    made["mix"] = (TIMESTEP * VERTICAL_MIX) * wet
    made["turn"] = TIMESTEP * coriolis * wet
    return made


def advance_level(k, count, levels, rows, src, sides, coef, acc):
    pitch = rows + 2 * PAD
    lane = iota((rows, LANES), 1)
    first, last = lane == 0, lane == LANES - 1
    above_k = jnp.maximum(k - 1, 0)
    below_k = jnp.minimum(k + 1, levels - 1)

    def load(q, level, shift):
        return src[pl.ds((q * count + level) * pitch + PAD + shift, rows), :]

    def base(q):
        return pl.multiple_of((q * count + k) * pitch + PAD, 8)

    center = [load(q, k, 0) for q in range(4)]
    u, v = coef("adv") * center[2], coef("adv") * center[3]
    sums, de, dn = [], [], []
    for q in range(4):
        c = center[q]
        n, s = load(q, k, 1), load(q, k, -1)
        edge = pltpu.roll(sides, (LANES - 1 - 2 * (q * levels + k)) & (LANES - 1), 1)
        e = jnp.where(last, edge, pltpu.roll(c, LANES - 1, 1))
        w = jnp.where(first, edge, pltpu.roll(c, 1, 1))
        kind = "t" if q < 2 else "v"
        lap = coef(kind + "c") * c + coef(kind + "e") * e + coef(kind + "w") * w
        lap = lap + coef(kind + "n") * n + coef(kind + "s") * s
        de.append(e - w)
        dn.append(n - s)
        sums.append(lap - (u * de[q] + v * dn[q]))
    scale = 0.5 * GRAVITY / VERTICAL_MIX
    dens_x = (scale * HALINE) * de[1] - (scale * THERMAL) * de[0]
    dens_y = (scale * HALINE) * dn[1] - (scale * THERMAL) * dn[0]
    acc_x, acc_y = acc
    grad = (None, None, acc_x + 0.5 * dens_x, acc_y + 0.5 * dens_y)
    turn = (None, None, coef("turn") * center[3], -coef("turn") * center[2])
    new = []
    for q in range(4):
        vertical = load(q, above_k, 0) + load(q, below_k, 0)
        if grad[q] is not None:
            vertical = vertical - grad[q]
        total = sums[q] + coef("mix") * vertical
        new.append(total if turn[q] is None else total + turn[q])
    return new, (acc_x + dens_x, acc_y + dens_y)


def advance_top_rows(levels, sides, north, south, state, wet, rows, table):
    fields = 4 * levels

    def both(a, b):
        return jnp.concatenate([a, b], axis=0)

    def rows_at(first):
        return both(
            north[pl.ds(first, 4, stride=levels), :], south[pl.ds(first, 4, stride=levels), :]
        )

    lane, row = iota((8, LANES), 1), iota((8, LANES), 0)
    upper = row < 4
    field = row & 3
    inside_n = state[pl.ds(rows - 1, 4, stride=levels * rows), :]
    inside_s = state[pl.ds(0, 4, stride=levels * rows), :]
    mid, below, outer = rows_at(0), rows_at(1), rows_at(fields)
    n = both(outer[0:4], inside_s)
    s = both(inside_n, outer[4:8])
    (corner_n, wet_ne, wet_nw), (corner_s, wet_se, wet_sw) = sides.corner(0), sides.corner(1)
    corner = jnp.where(upper, corner_n, corner_s)
    at = 2 * levels * field

    def end(parity):
        return jnp.sum(jnp.where(lane == at + parity, corner, 0.0), axis=1, keepdims=True)

    def west_east(x, east, west):
        return (
            jnp.where(lane == LANES - 1, east, pltpu.roll(x, LANES - 1, 1)),
            jnp.where(lane == 0, west, pltpu.roll(x, 1, 1)),
        )

    def tail(i):
        place = slice(2 * fields + i, 2 * fields + i + 1)
        return north[place, :], south[place, :]

    e, w = west_east(mid, end(0), end(1))
    wet_mid = jnp.where(upper, *tail(0))
    wet_e, wet_w = west_east(
        wet_mid, jnp.where(upper, wet_ne, wet_se), jnp.where(upper, wet_nw, wet_sw)
    )
    out_n, out_s = tail(1)
    wet_n = jnp.where(upper, out_n, wet[0:1])
    wet_s = jnp.where(upper, wet[rows - 1 : rows], out_s)
    lap = wet_e * (e - mid) + wet_w * (w - mid) + wet_n * (n - mid) + wet_s * (s - mid)
    de, dn = e - w, n - s

    def of(x, i):
        return jnp.where(upper, x[i : i + 1], x[4 + i : 5 + i])

    u, v = of(mid, 2), of(mid, 3)
    coriolis = jnp.where(upper, table[PAD + rows : PAD + rows + 1], table[PAD - 1 : PAD])
    grad_x = (0.25 * GRAVITY) * (HALINE * of(de, 1) - THERMAL * of(de, 0))
    grad_y = (0.25 * GRAVITY) * (HALINE * of(dn, 1) - THERMAL * of(dn, 0))
    turn = jnp.where(
        field < 2, 0.0, jnp.where(field == 2, coriolis * v - grad_x, -coriolis * u - grad_y)
    )
    kappa = jnp.where(field < 2, jnp.where(upper, *tail(2)), VISCOSITY)
    tend = turn - 0.5 * (u * de + v * dn) + kappa * lap + VERTICAL_MIX * (below - mid)
    return wet_mid * (mid + TIMESTEP * tend)


def surface_kernel(
    rows, levels,
    state, base, msg_a, msg_b, got_a, got_b, north, south, out_in, ids,
    coef, side, out, now, later, wet_pad, stage, places, sem,
):
    fields = 4 * levels
    pitch = rows + 2 * PAD
    to_scalars = pltpu.make_async_copy(ids, places, sem)
    to_scalars.start()
    out[...] = out_in[...]
    wet = base[0:rows, :]
    mixing = base[rows : 2 * rows, :]
    table = base[2 * rows :, :]
    coriolis = table[PAD : PAD + rows]
    lane = iota((rows, LANES), 1)
    sides = Sides(rows, got_a, got_b, msg_a, msg_b)
    wet_pad[PAD : PAD + rows, :] = wet
    wet_pad[PAD - 1 : PAD, :] = south[2 * fields : 2 * fields + 1, :]
    wet_pad[PAD + rows : PAD + rows + 1, :] = north[2 * fields : 2 * fields + 1, :]
    wet_n = wet_pad[PAD + 1 : PAD + 1 + rows, :]
    wet_s = wet_pad[PAD - 1 : PAD - 1 + rows, :]
    wet_e = jnp.where(lane == LANES - 1, sides.columns[0][0], pltpu.roll(wet, LANES - 1, 1))
    wet_w = jnp.where(lane == 0, sides.columns[1][0], pltpu.roll(wet, 1, 1))
    made = coefficients(wet, (wet_e, wet_w, wet_n, wet_s), mixing, coriolis)
    for name in COEFFICIENTS:
        coef[place_of(name, rows)] = made[name]
    near = sides.near()
    side[...] = near

    count = now.shape[0] // (4 * pitch)
    for q in range(4):
        for k in range(count):
            field = (q * levels + k) * rows
            at = (q * count + k) * pitch + PAD
            now[at : at + rows, :] = state[field : field + rows, :]
            now[at + rows : at + rows + 1, :] = north[q * levels + k : q * levels + k + 1, :]
            now[at - 1 : at, :] = south[q * levels + k : q * levels + k + 1, :]

    def read(name):
        return coef[place_of(name, rows)]

    none = jnp.zeros((rows, LANES), F32)
    acc = (none, none)
    edge_rows = advance_top_rows(levels, sides, north, south, state, wet, rows, table)
    edge_cols = advance_columns(sides, wet, coriolis, None)
    for k in range(count - 1):
        new, acc = advance_level(k, count, levels, rows, now, near, read, acc)
        for q in range(4):
            at = (q * count + k) * pitch + PAD
            later[at : at + rows, :] = new[q]
            if k == 0:
                later[at + rows : at + rows + 1, :] = edge_rows[q : q + 1]
                later[at - 1 : at, :] = edge_rows[4 + q : 5 + q]
    new, _ = advance_level(0, count, levels, rows, later, edge_cols, read, (none, none))
    for q in range(4):
        stage[pl.ds(q, rows, stride=4), :] = new[q]
    to_scalars.wait()
    for r in range(rows):
        out[pl.ds(places[0, r], 4), :] = stage[4 * r : 4 * r + 4, :]


def halo_after_first(rows, levels, sides, north, south, state, wet, table, col_map, row_map):
    fields = 4 * levels
    side_new = advance_columns(sides, wet, table[PAD : PAD + rows], col_map)
    lane, field = iota((fields, LANES), 1), iota((fields, LANES), 0)

    def to_sublanes(x, parity):
        here = lane == 2 * field + parity
        return jnp.sum(jnp.where(here, x, 0.0), axis=1, keepdims=True)

    parts = []
    for north_side, ref, line, lat_row in (
        (True, north, rows - 1, PAD + rows),
        (False, south, 0, PAD - 1),
    ):
        corner, *corner_wets = sides.corner(0 if north_side else 1)
        inside = state[pl.ds(line, fields, stride=rows), :]
        tail = ref[2 * fields :, :]
        pair = (ref[fields : 2 * fields, :], inside), (tail[1:2], wet[line : line + 1])
        (n, s), (wet_n, wet_s) = pair if north_side else [x[::-1] for x in pair]
        parts.append(
            (
                ref[0:fields, :], n, s, (to_sublanes(corner, 0), to_sublanes(corner, 1)),
                (tail[0:1], wet_n, wet_s, *corner_wets),
                tail[2:3], table[lat_row : lat_row + 1],
            )
        )
    return side_new, *advance_rows(levels, parts, row_map)


def main_kernel(
    rows, levels, chunks,
    state, base, msg_a, msg_b, got_a, got_b, north, south, col_map, row_map, coefs, side,
    tr_hbm, ve_hbm, now, later, side_new, tr_out, ve_out, sems,
):
    fields = 4 * levels
    pitch = rows + 2 * PAD
    sides = Sides(rows, got_a, got_b, msg_a, msg_b)
    side_new[...], north_new, south_new = halo_after_first(
        rows, levels, sides, north, south, state, base[0:rows, :], base[2 * rows :, :],
        col_map[...], row_map[...],
    )
    edges = (now, north[0:fields, :], south[0:fields, :]), (later, north_new, south_new)
    for buf, n, s in edges:
        buf[pl.ds(PAD - 1, fields, stride=pitch), :] = s
        buf[pl.ds(PAD + rows, fields, stride=pitch), :] = n

    def fill(f, carry):
        x = state[pl.ds(pl.multiple_of(f * rows, 8), rows), :]
        now[pl.ds(pl.multiple_of(f * pitch + PAD, 8), rows), :] = x
        return carry

    lax.fori_loop(0, fields, fill, 0, unroll=8)

    def coef(name):
        return coefs[place_of(name, rows)]

    def first(k, acc):
        new, acc = advance_level(k, levels, levels, rows, now, side[...], coef, acc)
        for q in range(4):
            place = pl.multiple_of((q * levels + k) * pitch + PAD, 8)
            later[pl.ds(place, rows), :] = new[q]
        return acc

    def second(k, acc):
        new, acc = advance_level(k, levels, levels, rows, later, side_new[...], coef, acc)
        for q in range(4):
            ref = tr_out if q < 2 else ve_out
            place = pl.multiple_of(((q % 2) * levels + k) * rows, 8)
            ref[pl.ds(place, rows), :] = new[q]
        return acc

    none = jnp.zeros((rows, LANES), F32)
    lax.fori_loop(0, levels, first, (none, none), unroll=2)
    acc = (none, none)
    size = levels // chunks
    copies = []
    for i in range(chunks):
        acc = lax.fori_loop(i * size, (i + 1) * size, second, acc, unroll=2)
        for src, dst in ((tr_out, tr_hbm), (ve_out, ve_hbm)):
            for q in range(2):
                start = (q * levels + i * size) * rows
                part = slice(start, start + size * rows)
                copy = pltpu.make_async_copy(src.at[part], dst.at[part], sems.at[len(copies)])
                copy.start()
                copies.append(copy)
    for copy in copies:
        copy.wait()


def reduce_kernel(devices, data, surface, cover):
    slot_rows = data.shape[0] // devices

    def rows_of(i):
        return data[pl.ds(i, devices, stride=slot_rows), :]

    width = LANES // CAP
    lines = rows_of(5 * CAP)
    named = (lines == (iota((devices, LANES), 1) % width).astype(F32)).astype(F32)
    to_rows, values = [], []
    for slot in range(CAP):
        to_rows.append(named[:, slot * width : slot * width + ATM_ROWS])
        parts = [rows_of(4 * slot + q) for q in range(4)] + [rows_of(4 * CAP + slot)]
        values.append(jnp.concatenate(parts, axis=1))
    totals = dot(
        jnp.concatenate(to_rows, axis=0), jnp.concatenate(values, axis=0), (((0,), (0,)), ((), ()))
    )
    ocean = totals[:, 4 * LANES :]
    cover[...] = ocean
    share = jnp.maximum(ocean, 1.0)
    for q in range(4):
        surface[q] = totals[:, q * LANES : (q + 1) * LANES] / share


def call(kernel, out_shape, limit=VMEM_LIMIT, **kwargs):
    return pl.pallas_call(
        kernel,
        out_shape=out_shape,
        compiler_params=pltpu.CompilerParams(vmem_limit_bytes=limit),
        **kwargs,
    )


def shaped(*shape, dtype=F32):
    return jax.ShapeDtypeStruct(shape, dtype)


def lat_swaps(lon_count, lat_count):
    swap_a, swap_b = [], []
    for i in range(lon_count):
        for a in range(lat_count):
            here = i * lat_count + a
            swap_a.append((here, i * lat_count + (a ^ 1)))
            if a == lat_count - 1:
                swap_b.append((here, (lon_count - 1 - i) * lat_count + a))
            elif a > 0:
                swap_b.append((here, here + 1 if a % 2 else here - 1))
    return swap_a, swap_b


def local(tracers, velocity, land_mask, mixing, owners, atm_row):
    levels = tracers.shape[1]
    rows, cols = land_mask.shape
    fields = 4 * levels
    lon_count, lat_count = lax.axis_size("lon"), lax.axis_size("lat")
    devices = lon_count * lat_count
    assert cols == LANES and rows % 8 == 0 and 2 * fields == LANES
    assert lon_count % 2 == 0 and lat_count % 2 == 0 and 3 * rows <= LANES
    length = 2 * fields + 8
    pitch = rows + 2 * PAD
    flat = 2 * levels * rows
    hbm = pl.BlockSpec(memory_space=pltpu.HBM)
    smem = pl.BlockSpec(memory_space=pltpu.SMEM)
    vmem = pl.BlockSpec(memory_space=pltpu.VMEM)

    deep = (2 * levels, rows, cols)
    lat_a, lat_b = call(
        functools.partial(edge_kernel, rows, fields),
        [shaped(length, cols)] * 2,
        limit=VMEM_ALL,
        in_specs=[hbm] * 4,
        scratch_shapes=[
            pltpu.VMEM((2, fields, 8, cols), F32),
            pltpu.VMEM((rows, cols), jnp.int32),
            pltpu.VMEM((rows, cols), F32),
            pltpu.SemaphoreType.DMA((6,)),
        ],
    )(tracers.reshape(deep), velocity.reshape(deep), land_mask, mixing)
    swap_a, swap_b = lat_swaps(lon_count, lat_count)
    got_lat_b = lax.ppermute(lat_b, ("lon", "lat"), swap_b)
    got_lat_a = lax.ppermute(lat_a, ("lon", "lat"), swap_a)

    tr, ve = tracers.reshape(flat, cols), velocity.reshape(flat, cols)
    msg_a, msg_b = call(
        functools.partial(pack_kernel, rows, fields),
        [shaped(rows + 8, cols)] * 2,
        in_specs=[vmem] * 4,
    )(tr, ve, land_mask, mixing)

    slot_rows = 5 * CAP + 1
    state, base, col_map, row_map, outgoing, ids = call(
        functools.partial(prepare_kernel, rows, levels, devices),
        [
            shaped(fields * rows, cols),
            shaped(2 * rows + pitch, cols),
            shaped(3 * cols, cols),
            shaped(fields + levels, cols),
            shaped(devices * slot_rows, cols),
            shaped(8, cols, dtype=jnp.int32),
        ],
        in_specs=[vmem] * 4 + [smem] * 2,
        scratch_shapes=[pltpu.SMEM((devices,), jnp.int32)],
    )(tr, ve, land_mask, mixing, owners.reshape(rows), atm_row)

    def full(n):
        return pl.BlockSpec((n, cols), lambda i: (0, 0))

    tail = pl.BlockSpec((8, cols), lambda i: (rows // 8, 0))
    north, south, msg_a, msg_b = call(
        functools.partial(corner_kernel, lat_count, fields),
        [shaped(length, cols)] * 2 + [shaped(rows + 8, cols)] * 2,
        grid=(1,),
        in_specs=[full(length), full(length), tail, tail],
        out_specs=[full(length), full(length), tail, tail],
        input_output_aliases={2: 2, 3: 3},
    )(got_lat_b, got_lat_a, msg_a, msg_b)
    even_pairs = [(i, i ^ 1) for i in range(lon_count)]
    odd_pairs = [(i, (i + 1 if i % 2 else i - 1) % lon_count) for i in range(lon_count)]
    got_b = lax.ppermute(msg_b, "lon", even_pairs)
    got_a = lax.ppermute(msg_a, "lon", odd_pairs)

    count = min(3, levels)
    coefs, side, outgoing = call(
        functools.partial(surface_kernel, rows, levels),
        [
            shaped(len(COEFFICIENTS) * rows, cols),
            shaped(rows, cols),
            shaped(devices * slot_rows, cols),
        ],
        scratch_shapes=[
            pltpu.VMEM((4 * count * pitch, cols), F32),
            pltpu.VMEM((4 * count * pitch, cols), F32),
            pltpu.VMEM((pitch, cols), F32),
            pltpu.VMEM((4 * rows, cols), F32),
            pltpu.SMEM((8, cols), jnp.int32),
            pltpu.SemaphoreType.DMA,
        ],
    )(state, base, msg_a, msg_b, got_a, got_b, north, south, outgoing, ids)
    incoming = lax.all_to_all(
        outgoing.reshape(devices, slot_rows, 1, cols),
        ("lon", "lat"),
        0,
        0,
        axis_index_groups=[list(range(devices))[::-1]],
        tiled=True,
    ).reshape(devices * slot_rows, cols)

    chunks = 4
    tr_out, ve_out = call(
        functools.partial(main_kernel, rows, levels, chunks),
        [shaped(flat, cols), shaped(flat, cols)],
        in_specs=[vmem] * 12,
        out_specs=[hbm] * 2,
        scratch_shapes=[
            pltpu.VMEM((fields * pitch, cols), F32),
            pltpu.VMEM((fields * pitch, cols), F32),
            pltpu.VMEM((rows, cols), F32),
            pltpu.VMEM((flat, cols), F32),
            pltpu.VMEM((flat, cols), F32),
            pltpu.SemaphoreType.DMA((4 * chunks,)),
        ],
        cost_estimate=pl.CostEstimate(
            flops=80 * fields * rows * cols, bytes_accessed=5 << 20, transcendentals=0
        ),
    )(state, base, msg_a, msg_b, got_a, got_b, north, south, col_map, row_map, coefs, side)
    surface, cover = call(
        functools.partial(reduce_kernel, devices),
        [shaped(4, ATM_ROWS, cols), shaped(ATM_ROWS, cols)],
    )(incoming)
    shape = (2, levels, rows, cols)
    return tr_out.reshape(shape), ve_out.reshape(shape), surface, cover


def solution(mesh):
    in_specs = (
        P(None, None, "lat", "lon"),
        P(None, None, "lat", "lon"),
        P("lat", "lon"),
        P("lat", "lon"),
        P(("lon", "lat"), None),
        P(("lon", "lat")),
    )
    out_specs = (
        P(None, None, "lat", "lon"),
        P(None, None, "lat", "lon"),
        P(None, ("lon", "lat"), None),
        P(("lon", "lat"), None),
    )
    return jax.shard_map(local, mesh=mesh, in_specs=in_specs, out_specs=out_specs, check_vma=False)
```

```python
import functools
import math

import jax
import jax.numpy as jnp
from jax import lax
from jax.experimental import pallas as pl
from jax.experimental.pallas import tpu as pltpu
from jax.sharding import PartitionSpec as P

ATM_ROWS = 32
CAP = 2

THERMAL = 0.2
HALINE = 0.15
GRAVITY = 0.2
TIMESTEP = 0.8
VERTICAL_MIX = 0.1
VISCOSITY = 0.2
CORIOLIS_MAX = 0.3

LANES = 128
PAD = 8
EXACT = lax.Precision.HIGHEST
F32 = jnp.float32
VMEM_LIMIT = 32 * 1024 * 1024
VMEM_ALL = 62 * 1024 * 1024


def iota(shape, dim):
    return lax.broadcasted_iota(jnp.int32, shape, dim)


def dot(a, b, dims=(((1,), (0,)), ((), ()))):
    return lax.dot_general(a, b, dims, precision=EXACT, preferred_element_type=F32)


def is_even(axis):
    return lax.rem(lax.axis_index(axis), 2) == 0


def start_copies(pairs, sems):
    copies = [pltpu.make_async_copy(src, dst, sems.at[i]) for i, (src, dst) in enumerate(pairs)]
    for copy in copies:
        copy.start()
    return copies


def edge_kernel(rows, fields, tr_hbm, ve_hbm, mask_hbm, mix_hbm, lat_a, lat_b, edges, mask, mix, sems):
    half = fields // 2
    pairs = [(mask_hbm, mask), (mix_hbm, mix)]
    for n, src in enumerate((tr_hbm, ve_hbm)):
        for side, first in enumerate((0, rows - 8)):
            part = edges.at[side, n * half : (n + 1) * half]
            pairs.append((src.at[:, first : first + 8, :], part))
    for copy in start_copies(pairs, sems):
        copy.wait()
    flat = edges.reshape(2 * fields * 8, LANES)
    even = is_even("lat")
    top = ((rows - 1, 8 * fields + 7), (rows - 2, 8 * fields + 6))
    bottom = ((0, 0), (1, 1))
    for buf, first, second in ((lat_a, top, bottom), (lat_b, bottom, top)):
        (near, near_at), (far, far_at) = [
            [jnp.where(even, x, y) for x, y in zip(one, other)] for one, other in zip(first, second)
        ]
        wet_near = mask[pl.ds(near, 1), :].astype(F32)
        wet_far = mask[pl.ds(far, 1), :].astype(F32)
        buf[0:fields, :] = flat[pl.ds(near_at, fields, stride=8), :] * wet_near
        buf[fields : 2 * fields, :] = flat[pl.ds(far_at, fields, stride=8), :] * wet_far
        buf[2 * fields : 2 * fields + 8, :] = jnp.zeros((8, LANES), F32)
        buf[2 * fields : 2 * fields + 1, :] = wet_near
        buf[2 * fields + 1 : 2 * fields + 2, :] = wet_far
        buf[2 * fields + 2 : 2 * fields + 3, :] = mix[pl.ds(near, 1), :]


def pack_kernel(rows, fields, tr, ve, mask, mix, msg_a, msg_b):
    half = fields // 2
    wet = mask[...].astype(F32)
    lane = iota((rows, LANES), 1)
    pair = lane >> 1

    def columns(ref, base):
        def body(f, carry):
            to_east, to_west = carry
            x = ref[pl.ds(pl.multiple_of(f * rows, rows), rows), :]
            keep = pair == base + f
            low = 2 * (base + f)
            to_east = jnp.where(keep, pltpu.roll(x, (low + 2) & (LANES - 1), 1), to_east)
            to_west = jnp.where(keep, pltpu.roll(x, low, 1), to_west)
            return to_east, to_west

        return body

    carry = (jnp.zeros((rows, LANES), F32), jnp.zeros((rows, LANES), F32))
    for ref, base in ((tr, 0), (ve, half)):
        carry = lax.fori_loop(0, half, columns(ref, base), carry, unroll=8)
    def spread(x, i):
        return jnp.broadcast_to(x[:, i : i + 1], (rows, LANES))

    odd = (lane & 1) == 1
    to_east = carry[0] * jnp.where(odd, spread(wet, LANES - 1), spread(wet, LANES - 2))
    to_west = carry[1] * jnp.where(odd, spread(wet, 1), spread(wet, 0))
    even = is_even("lon")
    row = iota((rows, LANES), 0)
    mixing = mix[...]
    lines = []
    for near, far in ((LANES - 1, LANES - 2), (0, 1)):
        line = jnp.zeros((rows, LANES), F32)
        for part, column in enumerate((wet[:, near], wet[:, far], mixing[:, near])):
            line = jnp.where(lane == part * rows + row, column[:, None], line)
        lines.append(jnp.sum(line, axis=0, keepdims=True))
    for msg, flag in ((msg_a, jnp.logical_not(even)), (msg_b, even)):
        msg[0:rows, :] = jnp.where(flag, to_east, to_west)
        msg[rows:, :] = jnp.zeros((8, LANES), F32)
        msg[rows + 4 : rows + 5, :] = jnp.where(flag, *lines)


def prepare_kernel(
    rows, levels, devices, tr, ve, mask, mix, own, atm_row,
    state, base, col_map, row_map, out, ids, used,
):
    fields = 4 * levels
    half = fields // 2
    wet = mask[...].astype(F32)
    base[0:rows, :] = wet
    base[rows : 2 * rows, :] = mix[...]
    for ref, first in ((tr, 0), (ve, half)):

        def fill(f, carry, ref=ref, first=first):
            x = ref[pl.ds(pl.multiple_of(f * rows, 8), rows), :] * wet
            state[pl.ds(pl.multiple_of((first + f) * rows, 8), rows), :] = x
            return carry

        lax.fori_loop(0, half, fill, 0, unroll=8)

    total = lax.axis_size("lat") * rows
    latitude = lax.axis_index("lat") * rows - PAD + iota((rows + 2 * PAD, LANES), 0)
    latitude = jnp.where(latitude >= total, 2 * total - 1 - latitude, latitude).astype(F32)
    table = CORIOLIS_MAX * jnp.sin(math.pi * (-0.43 + 0.93 * (latitude + 0.5) / total))
    base[2 * rows :, :] = table

    span = 2 * levels
    src, dst = iota((LANES, LANES), 0), iota((LANES, LANES), 1)
    src_group, dst_group = src // span, dst // span
    src_level, dst_level = (src // 2) % levels, (dst // 2) % levels
    same_side = (src & 1) == (dst & 1)
    mixes = VERTICAL_MIX * level_matrix("mix", levels, src_level, dst_level)
    press = level_matrix("pressure", levels, src_level, dst_level) * density_weight(src_group)
    col_map[0:LANES, :] = jnp.where(same_side & (src_group == dst_group), mixes, 0.0)
    col_map[LANES : 2 * LANES, :] = jnp.where(same_side & (dst_group == 2), -press, 0.0)
    col_map[2 * LANES :, :] = jnp.where(same_side & (dst_group == 3), -press, 0.0)

    dst, src = iota((fields, fields), 0), iota((fields, fields), 1)
    mixes = VERTICAL_MIX * level_matrix("mix", levels, src % levels, dst % levels)
    row_map[0:fields, 0:fields] = jnp.where(dst // levels == src // levels, mixes, 0.0)
    dst, src = iota((levels, fields), 0), iota((levels, fields), 1)
    press = level_matrix("pressure", levels, src % levels, dst) * density_weight(src // levels)
    row_map[fields:, 0:fields] = press

    slot_rows = out.shape[0] // devices

    def clear(d, carry):
        used[d] = 0
        return carry

    lax.fori_loop(0, devices, clear, 0, unroll=8)
    out[...] = jnp.zeros(out.shape, F32)
    lane1 = iota((1, LANES), 1)
    places = jnp.zeros((1, LANES), jnp.int32)
    for r in range(rows):
        owner = own[r]
        slot = used[owner]
        used[owner] = slot + 1
        start = (devices - 1 - owner) * slot_rows
        places = jnp.where(lane1 == r, start + 4 * slot, places)
        out[pl.ds(start + 4 * CAP + slot, 1), :] = base[r : r + 1, :]
        line = out[pl.ds(start + 5 * CAP, 1), :]
        target = jnp.full((1, LANES), atm_row[r], jnp.int32).astype(F32)
        out[pl.ds(start + 5 * CAP, 1), :] = jnp.where(lane1 // (LANES // CAP) == slot, target, line)
    ids[...] = jnp.zeros(ids.shape, jnp.int32)
    ids[0:1, :] = places


def corner_kernel(lat_count, fields, got_b, got_a, tail_a, tail_b, north, south, new_a, new_b):
    fold = lax.axis_index("lat") == lat_count - 1
    even = is_even("lat")
    a, b = got_a[...], got_b[...]
    straight = jnp.where(even, a, b)
    south[...] = jnp.where(even, b, a)
    back = LANES - 1 - iota((8, LANES), 1)
    flipped = jnp.concatenate(
        [
            jnp.take_along_axis(straight[i : i + 8], back, axis=1)
            * (-1.0 if i < 2 * fields and i % fields >= fields // 2 else 1.0)
            for i in range(0, straight.shape[0], 8)
        ],
        axis=0,
    )
    north[...] = jnp.where(fold, flipped, straight)
    lane, field = iota((fields, LANES), 1), iota((fields, LANES), 0)
    lane1 = iota((1, LANES), 1)
    for old, new in ((tail_a, new_a), (tail_b, new_b)):
        new[...] = old[...]
    for i, ref in enumerate((north, south)):
        near = ref[0:fields, :]
        ends = jnp.where(
            lane == 2 * field, near[:, 0:1], jnp.where(lane == 2 * field + 1, near[:, LANES - 1 :], 0.0)
        )
        corner = jnp.sum(ends, axis=0, keepdims=True)
        wet = ref[2 * fields : 2 * fields + 1, :]
        wet = jnp.where(lane1 == 0, wet[:, 0:1], wet[:, LANES - 1 :])
        for new in (new_a, new_b):
            new[i : i + 1, :] = corner
            new[2 + i : 3 + i, :] = wet


class Sides:
    def __init__(self, rows, got_a, got_b, msg_a, msg_b):
        lane, row = iota((rows, LANES), 1), iota((rows, LANES), 0)
        self.even = (lane & 1) == 0
        self.even1 = (iota((1, LANES), 1) & 1) == 0
        even = is_even("lon")

        def ordered(a, b, place):
            return jnp.where(even, b[place, :], a[place, :]), jnp.where(even, a[place, :], b[place, :])

        self.got = ordered(got_a, got_b, slice(0, rows))
        self.mine = ordered(msg_a, msg_b, slice(0, rows))
        self.extras = ordered(got_a, got_b, slice(rows, rows + 8))
        self.columns = [
            [
                jnp.sum(jnp.where(lane == i * rows + row, x[4:5], 0.0), axis=1, keepdims=True)
                for i in range(3)
            ]
            for x in self.extras
        ]

    def near(self):
        return jnp.where(self.even, *self.got)

    def far_and_inner(self):
        east, west = self.got
        mine_e, mine_w = self.mine
        far = jnp.where(self.even, pltpu.roll(east, LANES - 1, 1), pltpu.roll(west, 1, 1))
        inner = jnp.where(self.even, pltpu.roll(mine_e, LANES - 1, 1), pltpu.roll(mine_w, 1, 1))
        return far, inner

    def corner(self, i):
        east, west = self.extras
        wets = east[2 + i : 3 + i, 0:1], west[2 + i : 3 + i, 1:2]
        return jnp.where(self.even1, east[i : i + 1], west[i : i + 1]), *wets

    def lanes(self, i):
        return jnp.where(self.even, self.columns[0][i], self.columns[1][i])


def level_matrix(kind, levels, source, target):
    if kind == "mix":
        above = (source == jnp.maximum(target - 1, 0)).astype(F32)
        below = (source == jnp.minimum(target + 1, levels - 1)).astype(F32)
        return above + below - 2.0 * (source == target).astype(F32)
    full = jnp.where(source < target, 1.0, jnp.where(source == target, 0.5, 0.0))
    return (0.5 * GRAVITY) * full


def density_weight(group):
    return jnp.where(group == 0, -THERMAL, jnp.where(group == 1, HALINE, 0.0)).astype(F32)


def advance_columns(sides, wet, coriolis, level_map):
    rows = wet.shape[0]
    mid = sides.near()
    outer, inner = sides.far_and_inner()
    (corner_n, wet_ne, wet_nw), (corner_s, wet_se, wet_sw) = sides.corner(0), sides.corner(1)
    wet_mid, wet_out = sides.lanes(0), sides.lanes(1)
    wet_in = jnp.where(sides.even, wet[:, LANES - 1 :], wet[:, 0:1])
    wet_corner_n = jnp.where(sides.even1, wet_ne, wet_nw)
    wet_corner_s = jnp.where(sides.even1, wet_se, wet_sw)
    mixing = sides.lanes(2)
    lane = iota((rows, LANES), 1)
    row = iota((rows, LANES), 0)
    span = LANES // 4
    group = lane // span

    def ends(outside, inside):
        return jnp.where(sides.even, outside, inside), jnp.where(sides.even, inside, outside)

    def shifted(x, north, south):
        n = jnp.where(row == rows - 1, north, pltpu.roll(x, rows - 1, 0))
        s = jnp.where(row == 0, south, pltpu.roll(x, 1, 0))
        return n, s

    e, w = ends(outer, inner)
    wet_e, wet_w = ends(wet_out, wet_in)
    n, s = shifted(mid, corner_n, corner_s)
    wet_n, wet_s = shifted(wet_mid, wet_corner_n, wet_corner_s)
    lap = wet_e * (e - mid) + wet_w * (w - mid) + wet_n * (n - mid) + wet_s * (s - mid)
    de, dn = e - w, n - s
    one, two, three = (pltpu.roll(mid, i * span, 1) for i in (1, 2, 3))

    def pick(a, b, c, d):
        return jnp.where(group == 0, a, jnp.where(group == 1, b, jnp.where(group == 2, c, d)))

    u = pick(two, three, mid, one)
    v = pick(one, two, three, mid)
    adv = 0.5 * (u * de + v * dn)
    zero = jnp.zeros_like(mid)
    if level_map is None:
        grad_x = HALINE * pltpu.roll(de, span, 1) - THERMAL * pltpu.roll(de, 2 * span, 1)
        grad_y = HALINE * pltpu.roll(dn, 2 * span, 1) - THERMAL * pltpu.roll(dn, 3 * span, 1)
        linear = VERTICAL_MIX * (pltpu.roll(mid, LANES - 2, 1) - mid)
        linear = linear - (0.25 * GRAVITY) * pick(zero, zero, grad_x, grad_y)
    else:
        linear = dot(jnp.concatenate([mid, de, dn], axis=1), level_map)
    turn = pick(zero, zero, coriolis * v, -coriolis * u)
    kappa = jnp.where(group < 2, mixing, VISCOSITY)
    tend = turn - adv + kappa * lap + linear
    return wet_mid * (mid + TIMESTEP * tend)


def advance_rows(levels, parts, level_map):
    fields = 4 * levels
    lane = iota((fields, LANES), 1)
    lane8 = iota((8, LANES), 1)

    def sides(x, east, west, at):
        e = jnp.where(at == LANES - 1, east, pltpu.roll(x, LANES - 1, 1))
        w = jnp.where(at == 0, west, pltpu.roll(x, 1, 1))
        return e, w

    mids, gaps = [], []
    for mid, n, s, (corner_e, corner_w), *_ in parts:
        e, w = sides(mid, corner_e, corner_w, lane)
        mids.append((mid, e, w, n, s))
        gaps += [e - w, n - s]
    vertical = dot(level_map[0:fields, 0:fields], jnp.concatenate([m[0] for m in mids], axis=1))
    grads = dot(level_map[fields:, 0:fields], jnp.concatenate(gaps, axis=1))
    done = []
    for i, (mid, e, w, n, s) in enumerate(mids):
        *_, wets, mixing, coriolis = parts[i]
        wet_mid, wet_n, wet_s, wet_corner_e, wet_corner_w = wets
        wet_e, wet_w = sides(
            jnp.broadcast_to(wet_mid, (8, LANES)), wet_corner_e, wet_corner_w, lane8
        )
        lap = wet_e[0:1] * (e - mid) + wet_w[0:1] * (w - mid)
        lap = lap + wet_n * (n - mid) + wet_s * (s - mid)
        de, dn = gaps[2 * i], gaps[2 * i + 1]
        u, v = mid[2 * levels : 3 * levels], mid[3 * levels :]
        adv = jnp.concatenate([u] * 4, axis=0) * de + jnp.concatenate([v] * 4, axis=0) * dn
        grad_x = grads[:, 2 * i * LANES : (2 * i + 1) * LANES]
        grad_y = grads[:, (2 * i + 1) * LANES : (2 * i + 2) * LANES]
        zero = jnp.zeros((2 * levels, LANES), F32)
        turn = jnp.concatenate([zero, coriolis * v - grad_x, -coriolis * u - grad_y], axis=0)
        kappa = jnp.concatenate(
            [jnp.broadcast_to(mixing, (2 * levels, LANES)), jnp.full(zero.shape, VISCOSITY)],
            axis=0,
        )
        tend = turn - 0.5 * adv + kappa * lap + vertical[:, i * LANES : (i + 1) * LANES]
        done.append(wet_mid * (mid + TIMESTEP * tend))
    return done


COEFFICIENTS = ("te", "tw", "tn", "ts", "tc", "ve", "vw", "vn", "vs", "vc", "adv", "mix", "turn")


def place_of(name, rows):
    i = COEFFICIENTS.index(name)
    return slice(i * rows, (i + 1) * rows)


def coefficients(wet, neighbours, mixing, coriolis):
    made = {}
    for name, kappa in (("t", mixing), ("v", VISCOSITY)):
        rest = wet * (1.0 - 2.0 * TIMESTEP * VERTICAL_MIX)
        for side, wet_n in zip("ewns", neighbours):
            made[name + side] = TIMESTEP * kappa * wet * wet_n
            rest = rest - made[name + side]
        made[name + "c"] = rest
    made["adv"] = (0.5 * TIMESTEP) * wet
    made["mix"] = (TIMESTEP * VERTICAL_MIX) * wet
    made["turn"] = TIMESTEP * coriolis * wet
    return made


def advance_level(k, count, levels, rows, src, sides, coef, acc):
    pitch = rows + 2 * PAD
    lane = iota((rows, LANES), 1)
    first, last = lane == 0, lane == LANES - 1
    above_k = jnp.maximum(k - 1, 0)
    below_k = jnp.minimum(k + 1, levels - 1)

    def load(q, level, shift):
        return src[pl.ds((q * count + level) * pitch + PAD + shift, rows), :]

    def base(q):
        return pl.multiple_of((q * count + k) * pitch + PAD, 8)

    center = [load(q, k, 0) for q in range(4)]
    u, v = coef("adv") * center[2], coef("adv") * center[3]
    sums, de, dn = [], [], []
    for q in range(4):
        c = center[q]
        n, s = load(q, k, 1), load(q, k, -1)
        edge = pltpu.roll(sides, (LANES - 1 - 2 * (q * levels + k)) & (LANES - 1), 1)
        e = jnp.where(last, edge, pltpu.roll(c, LANES - 1, 1))
        w = jnp.where(first, edge, pltpu.roll(c, 1, 1))
        kind = "t" if q < 2 else "v"
        lap = coef(kind + "c") * c + coef(kind + "e") * e + coef(kind + "w") * w
        lap = lap + coef(kind + "n") * n + coef(kind + "s") * s
        de.append(e - w)
        dn.append(n - s)
        sums.append(lap - (u * de[q] + v * dn[q]))
    scale = 0.5 * GRAVITY / VERTICAL_MIX
    dens_x = (scale * HALINE) * de[1] - (scale * THERMAL) * de[0]
    dens_y = (scale * HALINE) * dn[1] - (scale * THERMAL) * dn[0]
    acc_x, acc_y = acc
    grad = (None, None, acc_x + 0.5 * dens_x, acc_y + 0.5 * dens_y)
    turn = (None, None, coef("turn") * center[3], -coef("turn") * center[2])
    new = []
    for q in range(4):
        vertical = load(q, above_k, 0) + load(q, below_k, 0)
        if grad[q] is not None:
            vertical = vertical - grad[q]
        total = sums[q] + coef("mix") * vertical
        new.append(total if turn[q] is None else total + turn[q])
    return new, (acc_x + dens_x, acc_y + dens_y)


def advance_top_rows(levels, sides, north, south, state, wet, rows, table):
    fields = 4 * levels

    def both(a, b):
        return jnp.concatenate([a, b], axis=0)

    def rows_at(first):
        return both(
            north[pl.ds(first, 4, stride=levels), :], south[pl.ds(first, 4, stride=levels), :]
        )

    lane, row = iota((8, LANES), 1), iota((8, LANES), 0)
    upper = row < 4
    field = row & 3
    inside_n = state[pl.ds(rows - 1, 4, stride=levels * rows), :]
    inside_s = state[pl.ds(0, 4, stride=levels * rows), :]
    mid, below, outer = rows_at(0), rows_at(1), rows_at(fields)
    n = both(outer[0:4], inside_s)
    s = both(inside_n, outer[4:8])
    (corner_n, wet_ne, wet_nw), (corner_s, wet_se, wet_sw) = sides.corner(0), sides.corner(1)
    corner = jnp.where(upper, corner_n, corner_s)
    at = 2 * levels * field

    def end(parity):
        return jnp.sum(jnp.where(lane == at + parity, corner, 0.0), axis=1, keepdims=True)

    def west_east(x, east, west):
        return (
            jnp.where(lane == LANES - 1, east, pltpu.roll(x, LANES - 1, 1)),
            jnp.where(lane == 0, west, pltpu.roll(x, 1, 1)),
        )

    def tail(i):
        place = slice(2 * fields + i, 2 * fields + i + 1)
        return north[place, :], south[place, :]

    e, w = west_east(mid, end(0), end(1))
    wet_mid = jnp.where(upper, *tail(0))
    wet_e, wet_w = west_east(
        wet_mid, jnp.where(upper, wet_ne, wet_se), jnp.where(upper, wet_nw, wet_sw)
    )
    out_n, out_s = tail(1)
    wet_n = jnp.where(upper, out_n, wet[0:1])
    wet_s = jnp.where(upper, wet[rows - 1 : rows], out_s)
    lap = wet_e * (e - mid) + wet_w * (w - mid) + wet_n * (n - mid) + wet_s * (s - mid)
    de, dn = e - w, n - s

    def of(x, i):
        return jnp.where(upper, x[i : i + 1], x[4 + i : 5 + i])

    u, v = of(mid, 2), of(mid, 3)
    coriolis = jnp.where(upper, table[PAD + rows : PAD + rows + 1], table[PAD - 1 : PAD])
    grad_x = (0.25 * GRAVITY) * (HALINE * of(de, 1) - THERMAL * of(de, 0))
    grad_y = (0.25 * GRAVITY) * (HALINE * of(dn, 1) - THERMAL * of(dn, 0))
    turn = jnp.where(
        field < 2, 0.0, jnp.where(field == 2, coriolis * v - grad_x, -coriolis * u - grad_y)
    )
    kappa = jnp.where(field < 2, jnp.where(upper, *tail(2)), VISCOSITY)
    tend = turn - 0.5 * (u * de + v * dn) + kappa * lap + VERTICAL_MIX * (below - mid)
    return wet_mid * (mid + TIMESTEP * tend)


def surface_kernel(
    rows, levels,
    state, base, msg_a, msg_b, got_a, got_b, north, south, out_in, ids,
    coef, side, out, now, later, wet_pad, stage, places, sem,
):
    fields = 4 * levels
    pitch = rows + 2 * PAD
    to_scalars = pltpu.make_async_copy(ids, places, sem)
    to_scalars.start()
    out[...] = out_in[...]
    wet = base[0:rows, :]
    mixing = base[rows : 2 * rows, :]
    table = base[2 * rows :, :]
    coriolis = table[PAD : PAD + rows]
    lane = iota((rows, LANES), 1)
    sides = Sides(rows, got_a, got_b, msg_a, msg_b)
    wet_pad[PAD : PAD + rows, :] = wet
    wet_pad[PAD - 1 : PAD, :] = south[2 * fields : 2 * fields + 1, :]
    wet_pad[PAD + rows : PAD + rows + 1, :] = north[2 * fields : 2 * fields + 1, :]
    wet_n = wet_pad[PAD + 1 : PAD + 1 + rows, :]
    wet_s = wet_pad[PAD - 1 : PAD - 1 + rows, :]
    wet_e = jnp.where(lane == LANES - 1, sides.columns[0][0], pltpu.roll(wet, LANES - 1, 1))
    wet_w = jnp.where(lane == 0, sides.columns[1][0], pltpu.roll(wet, 1, 1))
    made = coefficients(wet, (wet_e, wet_w, wet_n, wet_s), mixing, coriolis)
    for name in COEFFICIENTS:
        coef[place_of(name, rows)] = made[name]
    near = sides.near()
    side[...] = near

    count = now.shape[0] // (4 * pitch)
    for q in range(4):
        for k in range(count):
            field = (q * levels + k) * rows
            at = (q * count + k) * pitch + PAD
            now[at : at + rows, :] = state[field : field + rows, :]
            now[at + rows : at + rows + 1, :] = north[q * levels + k : q * levels + k + 1, :]
            now[at - 1 : at, :] = south[q * levels + k : q * levels + k + 1, :]

    def read(name):
        return coef[place_of(name, rows)]

    none = jnp.zeros((rows, LANES), F32)
    acc = (none, none)
    edge_rows = advance_top_rows(levels, sides, north, south, state, wet, rows, table)
    edge_cols = advance_columns(sides, wet, coriolis, None)
    for k in range(count - 1):
        new, acc = advance_level(k, count, levels, rows, now, near, read, acc)
        for q in range(4):
            at = (q * count + k) * pitch + PAD
            later[at : at + rows, :] = new[q]
            if k == 0:
                later[at + rows : at + rows + 1, :] = edge_rows[q : q + 1]
                later[at - 1 : at, :] = edge_rows[4 + q : 5 + q]
    new, _ = advance_level(0, count, levels, rows, later, edge_cols, read, (none, none))
    for q in range(4):
        stage[pl.ds(q, rows, stride=4), :] = new[q]
    to_scalars.wait()
    for r in range(rows):
        out[pl.ds(places[0, r], 4), :] = stage[4 * r : 4 * r + 4, :]


def halo_after_first(rows, levels, sides, north, south, state, wet, table, col_map, row_map):
    fields = 4 * levels
    side_new = advance_columns(sides, wet, table[PAD : PAD + rows], col_map)
    lane, field = iota((fields, LANES), 1), iota((fields, LANES), 0)

    def to_sublanes(x, parity):
        here = lane == 2 * field + parity
        return jnp.sum(jnp.where(here, x, 0.0), axis=1, keepdims=True)

    parts = []
    for north_side, ref, line, lat_row in (
        (True, north, rows - 1, PAD + rows),
        (False, south, 0, PAD - 1),
    ):
        corner, *corner_wets = sides.corner(0 if north_side else 1)
        inside = state[pl.ds(line, fields, stride=rows), :]
        tail = ref[2 * fields :, :]
        pair = (ref[fields : 2 * fields, :], inside), (tail[1:2], wet[line : line + 1])
        (n, s), (wet_n, wet_s) = pair if north_side else [x[::-1] for x in pair]
        parts.append(
            (
                ref[0:fields, :], n, s, (to_sublanes(corner, 0), to_sublanes(corner, 1)),
                (tail[0:1], wet_n, wet_s, *corner_wets),
                tail[2:3], table[lat_row : lat_row + 1],
            )
        )
    return side_new, *advance_rows(levels, parts, row_map)


def main_kernel(
    rows, levels, chunks,
    state, base, msg_a, msg_b, got_a, got_b, north, south, col_map, row_map, coefs, side,
    tr_hbm, ve_hbm, now, later, side_new, tr_out, ve_out, sems,
):
    fields = 4 * levels
    pitch = rows + 2 * PAD
    sides = Sides(rows, got_a, got_b, msg_a, msg_b)
    side_new[...], north_new, south_new = halo_after_first(
        rows, levels, sides, north, south, state, base[0:rows, :], base[2 * rows :, :],
        col_map[...], row_map[...],
    )
    edges = (now, north[0:fields, :], south[0:fields, :]), (later, north_new, south_new)
    for buf, n, s in edges:
        buf[pl.ds(PAD - 1, fields, stride=pitch), :] = s
        buf[pl.ds(PAD + rows, fields, stride=pitch), :] = n

    def fill(f, carry):
        x = state[pl.ds(pl.multiple_of(f * rows, 8), rows), :]
        now[pl.ds(pl.multiple_of(f * pitch + PAD, 8), rows), :] = x
        return carry

    lax.fori_loop(0, fields, fill, 0, unroll=8)

    def coef(name):
        return coefs[place_of(name, rows)]

    def first(k, acc):
        new, acc = advance_level(k, levels, levels, rows, now, side[...], coef, acc)
        for q in range(4):
            place = pl.multiple_of((q * levels + k) * pitch + PAD, 8)
            later[pl.ds(place, rows), :] = new[q]
        return acc

    def second(k, acc):
        new, acc = advance_level(k, levels, levels, rows, later, side_new[...], coef, acc)
        for q in range(4):
            ref = tr_out if q < 2 else ve_out
            place = pl.multiple_of(((q % 2) * levels + k) * rows, 8)
            ref[pl.ds(place, rows), :] = new[q]
        return acc

    none = jnp.zeros((rows, LANES), F32)
    lax.fori_loop(0, levels, first, (none, none), unroll=2)
    acc = (none, none)
    size = levels // chunks
    copies = []
    for i in range(chunks):
        acc = lax.fori_loop(i * size, (i + 1) * size, second, acc, unroll=2)
        for src, dst in ((tr_out, tr_hbm), (ve_out, ve_hbm)):
            for q in range(2):
                start = (q * levels + i * size) * rows
                part = slice(start, start + size * rows)
                copy = pltpu.make_async_copy(src.at[part], dst.at[part], sems.at[len(copies)])
                copy.start()
                copies.append(copy)
    for copy in copies:
        copy.wait()


def reduce_kernel(devices, data, surface, cover):
    slot_rows = data.shape[0] // devices

    def rows_of(i):
        return data[pl.ds(i, devices, stride=slot_rows), :]

    width = LANES // CAP
    lines = rows_of(5 * CAP)
    named = (lines == (iota((devices, LANES), 1) % width).astype(F32)).astype(F32)
    to_rows, values = [], []
    for slot in range(CAP):
        to_rows.append(named[:, slot * width : slot * width + ATM_ROWS])
        parts = [rows_of(4 * slot + q) for q in range(4)] + [rows_of(4 * CAP + slot)]
        values.append(jnp.concatenate(parts, axis=1))
    rest = jnp.concatenate(values, axis=0)
    pieces = []
    for _ in range(3):
        piece = rest.astype(jnp.bfloat16)
        pieces.append(piece)
        rest = rest - piece.astype(F32)
    one = jnp.concatenate(to_rows, axis=0).astype(jnp.bfloat16)
    totals = lax.dot_general(
        jnp.concatenate([one] * 3, axis=0),
        jnp.concatenate(pieces, axis=0),
        (((0,), (0,)), ((), ())),
        preferred_element_type=F32,
    )
    ocean = totals[:, 4 * LANES :]
    cover[...] = ocean
    share = jnp.maximum(ocean, 1.0)
    for q in range(4):
        surface[q] = totals[:, q * LANES : (q + 1) * LANES] / share


def call(kernel, out_shape, limit=VMEM_LIMIT, **kwargs):
    return pl.pallas_call(
        kernel,
        out_shape=out_shape,
        compiler_params=pltpu.CompilerParams(vmem_limit_bytes=limit),
        **kwargs,
    )


def shaped(*shape, dtype=F32):
    return jax.ShapeDtypeStruct(shape, dtype)


def lat_swaps(lon_count, lat_count):
    swap_a, swap_b = [], []
    for i in range(lon_count):
        for a in range(lat_count):
            here = i * lat_count + a
            swap_a.append((here, i * lat_count + (a ^ 1)))
            if a == lat_count - 1:
                swap_b.append((here, (lon_count - 1 - i) * lat_count + a))
            elif a > 0:
                swap_b.append((here, here + 1 if a % 2 else here - 1))
    return swap_a, swap_b


def local(tracers, velocity, land_mask, mixing, owners, atm_row):
    levels = tracers.shape[1]
    rows, cols = land_mask.shape
    fields = 4 * levels
    lon_count, lat_count = lax.axis_size("lon"), lax.axis_size("lat")
    devices = lon_count * lat_count
    assert cols == LANES and rows % 8 == 0 and 2 * fields == LANES
    assert lon_count % 2 == 0 and lat_count % 2 == 0 and 3 * rows <= LANES
    length = 2 * fields + 8
    pitch = rows + 2 * PAD
    flat = 2 * levels * rows
    hbm = pl.BlockSpec(memory_space=pltpu.HBM)
    smem = pl.BlockSpec(memory_space=pltpu.SMEM)
    vmem = pl.BlockSpec(memory_space=pltpu.VMEM)

    deep = (2 * levels, rows, cols)
    lat_a, lat_b = call(
        functools.partial(edge_kernel, rows, fields),
        [pltpu.VMEM((length, cols), F32)] * 2,
        limit=VMEM_ALL,
        in_specs=[hbm] * 4,
        scratch_shapes=[
            pltpu.VMEM((2, fields, 8, cols), F32),
            pltpu.VMEM((rows, cols), jnp.int32),
            pltpu.VMEM((rows, cols), F32),
            pltpu.SemaphoreType.DMA((6,)),
        ],
    )(tracers.reshape(deep), velocity.reshape(deep), land_mask, mixing)
    swap_a, swap_b = lat_swaps(lon_count, lat_count)
    got_lat_b = lax.ppermute(lat_b, ("lon", "lat"), swap_b)
    got_lat_a = lax.ppermute(lat_a, ("lon", "lat"), swap_a)

    tr, ve = tracers.reshape(flat, cols), velocity.reshape(flat, cols)
    msg_a, msg_b = call(
        functools.partial(pack_kernel, rows, fields),
        [shaped(rows + 8, cols)] * 2,
        in_specs=[vmem] * 4,
    )(tr, ve, land_mask, mixing)

    slot_rows = 5 * CAP + 1
    state, base, col_map, row_map, outgoing, ids = call(
        functools.partial(prepare_kernel, rows, levels, devices),
        [
            shaped(fields * rows, cols),
            shaped(2 * rows + pitch, cols),
            shaped(3 * cols, cols),
            shaped(fields + levels, cols),
            shaped(devices * slot_rows, cols),
            shaped(8, cols, dtype=jnp.int32),
        ],
        in_specs=[vmem] * 4 + [smem] * 2,
        scratch_shapes=[pltpu.SMEM((devices,), jnp.int32)],
    )(tr, ve, land_mask, mixing, owners.reshape(rows), atm_row)

    def full(n):
        return pl.BlockSpec((n, cols), lambda i: (0, 0))

    tail = pl.BlockSpec((8, cols), lambda i: (rows // 8, 0))
    north, south, msg_a, msg_b = call(
        functools.partial(corner_kernel, lat_count, fields),
        [shaped(length, cols)] * 2 + [shaped(rows + 8, cols)] * 2,
        grid=(1,),
        in_specs=[full(length), full(length), tail, tail],
        out_specs=[full(length), full(length), tail, tail],
        input_output_aliases={2: 2, 3: 3},
    )(got_lat_b, got_lat_a, msg_a, msg_b)
    even_pairs = [(i, i ^ 1) for i in range(lon_count)]
    odd_pairs = [(i, (i + 1 if i % 2 else i - 1) % lon_count) for i in range(lon_count)]
    got_b = lax.ppermute(msg_b, "lon", even_pairs)
    got_a = lax.ppermute(msg_a, "lon", odd_pairs)

    count = min(3, levels)
    coefs, side, outgoing = call(
        functools.partial(surface_kernel, rows, levels),
        [
            shaped(len(COEFFICIENTS) * rows, cols),
            shaped(rows, cols),
            pltpu.VMEM((devices * slot_rows, cols), F32),
        ],
        scratch_shapes=[
            pltpu.VMEM((4 * count * pitch, cols), F32),
            pltpu.VMEM((4 * count * pitch, cols), F32),
            pltpu.VMEM((pitch, cols), F32),
            pltpu.VMEM((4 * rows, cols), F32),
            pltpu.SMEM((8, cols), jnp.int32),
            pltpu.SemaphoreType.DMA,
        ],
    )(state, base, msg_a, msg_b, got_a, got_b, north, south, outgoing, ids)
    incoming = lax.all_to_all(
        outgoing.reshape(devices, slot_rows, 1, cols),
        ("lon", "lat"),
        0,
        0,
        axis_index_groups=[list(range(devices))[::-1]],
        tiled=True,
    ).reshape(devices * slot_rows, cols)

    chunks = 4
    tr_out, ve_out = call(
        functools.partial(main_kernel, rows, levels, chunks),
        [shaped(flat, cols), shaped(flat, cols)],
        in_specs=[vmem] * 12,
        out_specs=[hbm] * 2,
        scratch_shapes=[
            pltpu.VMEM((fields * pitch, cols), F32),
            pltpu.VMEM((fields * pitch, cols), F32),
            pltpu.VMEM((rows, cols), F32),
            pltpu.VMEM((flat, cols), F32),
            pltpu.VMEM((flat, cols), F32),
            pltpu.SemaphoreType.DMA((4 * chunks,)),
        ],
        cost_estimate=pl.CostEstimate(
            flops=80 * fields * rows * cols, bytes_accessed=5 << 20, transcendentals=0
        ),
    )(state, base, msg_a, msg_b, got_a, got_b, north, south, col_map, row_map, coefs, side)
    surface, cover = call(
        functools.partial(reduce_kernel, devices),
        [shaped(4, ATM_ROWS, cols), shaped(ATM_ROWS, cols)],
    )(incoming)
    shape = (2, levels, rows, cols)
    return tr_out.reshape(shape), ve_out.reshape(shape), surface, cover


def solution(mesh):
    in_specs = (
        P(None, None, "lat", "lon"),
        P(None, None, "lat", "lon"),
        P("lat", "lon"),
        P("lat", "lon"),
        P(("lon", "lat"), None),
        P(("lon", "lat")),
    )
    out_specs = (
        P(None, None, "lat", "lon"),
        P(None, None, "lat", "lon"),
        P(None, ("lon", "lat"), None),
        P(("lon", "lat"), None),
    )
    return jax.shard_map(local, mesh=mesh, in_specs=in_specs, out_specs=out_specs, check_vma=False)
```

```python
import functools
import math

import jax
import jax.numpy as jnp
from jax import lax
from jax.experimental import pallas as pl
from jax.experimental.pallas import tpu as pltpu
from jax.sharding import PartitionSpec as P

ATM_ROWS = 32
CAP = 2

THERMAL = 0.2
HALINE = 0.15
GRAVITY = 0.2
TIMESTEP = 0.8
VERTICAL_MIX = 0.1
VISCOSITY = 0.2
CORIOLIS_MAX = 0.3

LANES = 128
PAD = 8
EXACT = lax.Precision.HIGHEST
F32 = jnp.float32
VMEM_LIMIT = 32 * 1024 * 1024
VMEM_ALL = 62 * 1024 * 1024


def iota(shape, dim):
    return lax.broadcasted_iota(jnp.int32, shape, dim)


def dot(a, b, dims=(((1,), (0,)), ((), ()))):
    return lax.dot_general(a, b, dims, precision=EXACT, preferred_element_type=F32)


def is_even(axis):
    return lax.rem(lax.axis_index(axis), 2) == 0


def is_east_first():
    return lax.rem(lax.axis_index("lon") + lax.axis_index("lat"), 2) == 1


def start_copies(pairs, sems):
    copies = [pltpu.make_async_copy(src, dst, sems.at[i]) for i, (src, dst) in enumerate(pairs)]
    for copy in copies:
        copy.start()
    return copies


def edge_kernel(rows, fields, tr_hbm, ve_hbm, mask_hbm, mix_hbm, lat_a, lat_b, edges, mask, mix, sems):
    half = fields // 2
    pairs = [(mask_hbm, mask), (mix_hbm, mix)]
    for n, src in enumerate((tr_hbm, ve_hbm)):
        for side, first in enumerate((0, rows - 8)):
            part = edges.at[side, n * half : (n + 1) * half]
            pairs.append((src.at[:, first : first + 8, :], part))
    for copy in start_copies(pairs, sems):
        copy.wait()
    flat = edges.reshape(2 * fields * 8, LANES)
    even = is_even("lat")
    top = ((rows - 1, 8 * fields + 7), (rows - 2, 8 * fields + 6))
    bottom = ((0, 0), (1, 1))
    for buf, first, second in ((lat_a, top, bottom), (lat_b, bottom, top)):
        (near, near_at), (far, far_at) = [
            [jnp.where(even, x, y) for x, y in zip(one, other)] for one, other in zip(first, second)
        ]
        wet_near = mask[pl.ds(near, 1), :].astype(F32)
        wet_far = mask[pl.ds(far, 1), :].astype(F32)
        buf[0:fields, :] = flat[pl.ds(near_at, fields, stride=8), :] * wet_near
        buf[fields : 2 * fields, :] = flat[pl.ds(far_at, fields, stride=8), :] * wet_far
        buf[2 * fields : 2 * fields + 8, :] = jnp.zeros((8, LANES), F32)
        buf[2 * fields : 2 * fields + 1, :] = wet_near
        buf[2 * fields + 1 : 2 * fields + 2, :] = wet_far
        buf[2 * fields + 2 : 2 * fields + 3, :] = mix[pl.ds(near, 1), :]


def pack_kernel(rows, fields, tr, ve, mask, mix, msg_a, msg_b):
    half = fields // 2
    wet = mask[...].astype(F32)
    lane = iota((rows, LANES), 1)
    pair = lane >> 1

    def columns(ref, base):
        def body(f, carry):
            to_east, to_west = carry
            x = ref[pl.ds(pl.multiple_of(f * rows, rows), rows), :]
            keep = pair == base + f
            low = 2 * (base + f)
            to_east = jnp.where(keep, pltpu.roll(x, (low + 2) & (LANES - 1), 1), to_east)
            to_west = jnp.where(keep, pltpu.roll(x, low, 1), to_west)
            return to_east, to_west

        return body

    carry = (jnp.zeros((rows, LANES), F32), jnp.zeros((rows, LANES), F32))
    for ref, base in ((tr, 0), (ve, half)):
        carry = lax.fori_loop(0, half, columns(ref, base), carry, unroll=8)
    def spread(x, i):
        return jnp.broadcast_to(x[:, i : i + 1], (rows, LANES))

    odd = (lane & 1) == 1
    to_east = carry[0] * jnp.where(odd, spread(wet, LANES - 1), spread(wet, LANES - 2))
    to_west = carry[1] * jnp.where(odd, spread(wet, 1), spread(wet, 0))
    east_first = is_east_first()
    row = iota((rows, LANES), 0)
    mixing = mix[...]
    lines = []
    for near, far in ((LANES - 1, LANES - 2), (0, 1)):
        line = jnp.zeros((rows, LANES), F32)
        for part, column in enumerate((wet[:, near], wet[:, far], mixing[:, near])):
            line = jnp.where(lane == part * rows + row, column[:, None], line)
        lines.append(jnp.sum(line, axis=0, keepdims=True))
    for msg, flag in ((msg_a, east_first), (msg_b, jnp.logical_not(east_first))):
        msg[0:rows, :] = jnp.where(flag, to_east, to_west)
        msg[rows:, :] = jnp.zeros((8, LANES), F32)
        msg[rows + 4 : rows + 5, :] = jnp.where(flag, *lines)


def prepare_kernel(
    rows, levels, devices, tr, ve, mask, mix, own, atm_row,
    state, base, col_map, row_map, out, ids, used,
):
    fields = 4 * levels
    half = fields // 2
    wet = mask[...].astype(F32)
    base[0:rows, :] = wet
    base[rows : 2 * rows, :] = mix[...]
    for ref, first in ((tr, 0), (ve, half)):

        def fill(f, carry, ref=ref, first=first):
            x = ref[pl.ds(pl.multiple_of(f * rows, 8), rows), :] * wet
            state[pl.ds(pl.multiple_of((first + f) * rows, 8), rows), :] = x
            return carry

        lax.fori_loop(0, half, fill, 0, unroll=8)

    total = lax.axis_size("lat") * rows
    latitude = lax.axis_index("lat") * rows - PAD + iota((rows + 2 * PAD, LANES), 0)
    latitude = jnp.where(latitude >= total, 2 * total - 1 - latitude, latitude).astype(F32)
    table = CORIOLIS_MAX * jnp.sin(math.pi * (-0.43 + 0.93 * (latitude + 0.5) / total))
    base[2 * rows :, :] = table

    span = 2 * levels
    src, dst = iota((LANES, LANES), 0), iota((LANES, LANES), 1)
    src_group, dst_group = src // span, dst // span
    src_level, dst_level = (src // 2) % levels, (dst // 2) % levels
    same_side = (src & 1) == (dst & 1)
    mixes = VERTICAL_MIX * level_matrix("mix", levels, src_level, dst_level)
    press = level_matrix("pressure", levels, src_level, dst_level) * density_weight(src_group)
    col_map[0:LANES, :] = jnp.where(same_side & (src_group == dst_group), mixes, 0.0)
    col_map[LANES : 2 * LANES, :] = jnp.where(same_side & (dst_group == 2), -press, 0.0)
    col_map[2 * LANES :, :] = jnp.where(same_side & (dst_group == 3), -press, 0.0)

    dst, src = iota((fields, fields), 0), iota((fields, fields), 1)
    mixes = VERTICAL_MIX * level_matrix("mix", levels, src % levels, dst % levels)
    row_map[0:fields, 0:fields] = jnp.where(dst // levels == src // levels, mixes, 0.0)
    dst, src = iota((levels, fields), 0), iota((levels, fields), 1)
    press = level_matrix("pressure", levels, src % levels, dst) * density_weight(src // levels)
    row_map[fields:, 0:fields] = press

    slot_rows = out.shape[0] // devices

    def clear(d, carry):
        used[d] = 0
        return carry

    lax.fori_loop(0, devices, clear, 0, unroll=8)
    out[...] = jnp.zeros(out.shape, F32)
    lane1 = iota((1, LANES), 1)
    places = jnp.zeros((1, LANES), jnp.int32)
    for r in range(rows):
        owner = own[r]
        slot = used[owner]
        used[owner] = slot + 1
        start = (devices - 1 - owner) * slot_rows
        places = jnp.where(lane1 == r, start + 4 * slot, places)
        out[pl.ds(start + 4 * CAP + slot, 1), :] = base[r : r + 1, :]
        line = out[pl.ds(start + 5 * CAP, 1), :]
        target = jnp.full((1, LANES), atm_row[r], jnp.int32).astype(F32)
        out[pl.ds(start + 5 * CAP, 1), :] = jnp.where(lane1 // (LANES // CAP) == slot, target, line)
    ids[...] = jnp.zeros(ids.shape, jnp.int32)
    ids[0:1, :] = places


def corner_kernel(lat_count, fields, got_b, got_a, tail_a, tail_b, north, south, new_a, new_b):
    fold = lax.axis_index("lat") == lat_count - 1
    even = is_even("lat")
    a, b = got_a[...], got_b[...]
    straight = jnp.where(even, a, b)
    south[...] = jnp.where(even, b, a)
    back = LANES - 1 - iota((8, LANES), 1)
    flipped = jnp.concatenate(
        [
            jnp.take_along_axis(straight[i : i + 8], back, axis=1)
            * (-1.0 if i < 2 * fields and i % fields >= fields // 2 else 1.0)
            for i in range(0, straight.shape[0], 8)
        ],
        axis=0,
    )
    north[...] = jnp.where(fold, flipped, straight)
    lane, field = iota((fields, LANES), 1), iota((fields, LANES), 0)
    lane1 = iota((1, LANES), 1)
    for old, new in ((tail_a, new_a), (tail_b, new_b)):
        new[...] = old[...]
    for i, ref in enumerate((north, south)):
        near = ref[0:fields, :]
        ends = jnp.where(
            lane == 2 * field, near[:, 0:1], jnp.where(lane == 2 * field + 1, near[:, LANES - 1 :], 0.0)
        )
        corner = jnp.sum(ends, axis=0, keepdims=True)
        wet = ref[2 * fields : 2 * fields + 1, :]
        wet = jnp.where(lane1 == 0, wet[:, 0:1], wet[:, LANES - 1 :])
        for new in (new_a, new_b):
            new[i : i + 1, :] = corner
            new[2 + i : 3 + i, :] = wet


class Sides:
    def __init__(self, rows, got_a, got_b, msg_a, msg_b):
        lane, row = iota((rows, LANES), 1), iota((rows, LANES), 0)
        self.even = (lane & 1) == 0
        self.even1 = (iota((1, LANES), 1) & 1) == 0
        first = is_east_first()

        def ordered(a, b, place):
            a, b = a[place, :], b[place, :]
            return jnp.where(first, a, b), jnp.where(first, b, a)

        self.got = ordered(got_a, got_b, slice(0, rows))
        self.mine = ordered(msg_a, msg_b, slice(0, rows))
        self.extras = ordered(got_a, got_b, slice(rows, rows + 8))
        self.columns = [
            [
                jnp.sum(jnp.where(lane == i * rows + row, x[4:5], 0.0), axis=1, keepdims=True)
                for i in range(3)
            ]
            for x in self.extras
        ]

    def near(self):
        return jnp.where(self.even, *self.got)

    def far_and_inner(self):
        east, west = self.got
        mine_e, mine_w = self.mine
        far = jnp.where(self.even, pltpu.roll(east, LANES - 1, 1), pltpu.roll(west, 1, 1))
        inner = jnp.where(self.even, pltpu.roll(mine_e, LANES - 1, 1), pltpu.roll(mine_w, 1, 1))
        return far, inner

    def corner(self, i):
        east, west = self.extras
        wets = east[2 + i : 3 + i, 0:1], west[2 + i : 3 + i, 1:2]
        return jnp.where(self.even1, east[i : i + 1], west[i : i + 1]), *wets

    def lanes(self, i):
        return jnp.where(self.even, self.columns[0][i], self.columns[1][i])


def level_matrix(kind, levels, source, target):
    if kind == "mix":
        above = (source == jnp.maximum(target - 1, 0)).astype(F32)
        below = (source == jnp.minimum(target + 1, levels - 1)).astype(F32)
        return above + below - 2.0 * (source == target).astype(F32)
    full = jnp.where(source < target, 1.0, jnp.where(source == target, 0.5, 0.0))
    return (0.5 * GRAVITY) * full


def density_weight(group):
    return jnp.where(group == 0, -THERMAL, jnp.where(group == 1, HALINE, 0.0)).astype(F32)


def advance_columns(sides, wet, coriolis, level_map):
    rows = wet.shape[0]
    mid = sides.near()
    outer, inner = sides.far_and_inner()
    (corner_n, wet_ne, wet_nw), (corner_s, wet_se, wet_sw) = sides.corner(0), sides.corner(1)
    wet_mid, wet_out = sides.lanes(0), sides.lanes(1)
    wet_in = jnp.where(sides.even, wet[:, LANES - 1 :], wet[:, 0:1])
    wet_corner_n = jnp.where(sides.even1, wet_ne, wet_nw)
    wet_corner_s = jnp.where(sides.even1, wet_se, wet_sw)
    mixing = sides.lanes(2)
    lane = iota((rows, LANES), 1)
    row = iota((rows, LANES), 0)
    span = LANES // 4
    group = lane // span

    def ends(outside, inside):
        return jnp.where(sides.even, outside, inside), jnp.where(sides.even, inside, outside)

    def shifted(x, north, south):
        n = jnp.where(row == rows - 1, north, pltpu.roll(x, rows - 1, 0))
        s = jnp.where(row == 0, south, pltpu.roll(x, 1, 0))
        return n, s

    e, w = ends(outer, inner)
    wet_e, wet_w = ends(wet_out, wet_in)
    n, s = shifted(mid, corner_n, corner_s)
    wet_n, wet_s = shifted(wet_mid, wet_corner_n, wet_corner_s)
    lap = wet_e * (e - mid) + wet_w * (w - mid) + wet_n * (n - mid) + wet_s * (s - mid)
    de, dn = e - w, n - s
    one, two, three = (pltpu.roll(mid, i * span, 1) for i in (1, 2, 3))

    def pick(a, b, c, d):
        return jnp.where(group == 0, a, jnp.where(group == 1, b, jnp.where(group == 2, c, d)))

    u = pick(two, three, mid, one)
    v = pick(one, two, three, mid)
    adv = 0.5 * (u * de + v * dn)
    zero = jnp.zeros_like(mid)
    if level_map is None:
        grad_x = HALINE * pltpu.roll(de, span, 1) - THERMAL * pltpu.roll(de, 2 * span, 1)
        grad_y = HALINE * pltpu.roll(dn, 2 * span, 1) - THERMAL * pltpu.roll(dn, 3 * span, 1)
        linear = VERTICAL_MIX * (pltpu.roll(mid, LANES - 2, 1) - mid)
        linear = linear - (0.25 * GRAVITY) * pick(zero, zero, grad_x, grad_y)
    else:
        linear = dot(jnp.concatenate([mid, de, dn], axis=1), level_map)
    turn = pick(zero, zero, coriolis * v, -coriolis * u)
    kappa = jnp.where(group < 2, mixing, VISCOSITY)
    tend = turn - adv + kappa * lap + linear
    return wet_mid * (mid + TIMESTEP * tend)


def advance_rows(levels, parts, level_map):
    fields = 4 * levels
    lane = iota((fields, LANES), 1)
    lane8 = iota((8, LANES), 1)

    def sides(x, east, west, at):
        e = jnp.where(at == LANES - 1, east, pltpu.roll(x, LANES - 1, 1))
        w = jnp.where(at == 0, west, pltpu.roll(x, 1, 1))
        return e, w

    mids, gaps = [], []
    for mid, n, s, (corner_e, corner_w), *_ in parts:
        e, w = sides(mid, corner_e, corner_w, lane)
        mids.append((mid, e, w, n, s))
        gaps += [e - w, n - s]
    vertical = dot(level_map[0:fields, 0:fields], jnp.concatenate([m[0] for m in mids], axis=1))
    grads = dot(level_map[fields:, 0:fields], jnp.concatenate(gaps, axis=1))
    done = []
    for i, (mid, e, w, n, s) in enumerate(mids):
        *_, wets, mixing, coriolis = parts[i]
        wet_mid, wet_n, wet_s, wet_corner_e, wet_corner_w = wets
        wet_e, wet_w = sides(
            jnp.broadcast_to(wet_mid, (8, LANES)), wet_corner_e, wet_corner_w, lane8
        )
        lap = wet_e[0:1] * (e - mid) + wet_w[0:1] * (w - mid)
        lap = lap + wet_n * (n - mid) + wet_s * (s - mid)
        de, dn = gaps[2 * i], gaps[2 * i + 1]
        u, v = mid[2 * levels : 3 * levels], mid[3 * levels :]
        adv = jnp.concatenate([u] * 4, axis=0) * de + jnp.concatenate([v] * 4, axis=0) * dn
        grad_x = grads[:, 2 * i * LANES : (2 * i + 1) * LANES]
        grad_y = grads[:, (2 * i + 1) * LANES : (2 * i + 2) * LANES]
        zero = jnp.zeros((2 * levels, LANES), F32)
        turn = jnp.concatenate([zero, coriolis * v - grad_x, -coriolis * u - grad_y], axis=0)
        kappa = jnp.concatenate(
            [jnp.broadcast_to(mixing, (2 * levels, LANES)), jnp.full(zero.shape, VISCOSITY)],
            axis=0,
        )
        tend = turn - 0.5 * adv + kappa * lap + vertical[:, i * LANES : (i + 1) * LANES]
        done.append(wet_mid * (mid + TIMESTEP * tend))
    return done


COEFFICIENTS = ("te", "tw", "tn", "ts", "tc", "ve", "vw", "vn", "vs", "vc", "adv", "mix", "turn")


def place_of(name, rows):
    i = COEFFICIENTS.index(name)
    return slice(i * rows, (i + 1) * rows)


def coefficients(wet, neighbours, mixing, coriolis):
    made = {}
    for name, kappa in (("t", mixing), ("v", VISCOSITY)):
        rest = wet * (1.0 - 2.0 * TIMESTEP * VERTICAL_MIX)
        for side, wet_n in zip("ewns", neighbours):
            made[name + side] = TIMESTEP * kappa * wet * wet_n
            rest = rest - made[name + side]
        made[name + "c"] = rest
    made["adv"] = (0.5 * TIMESTEP) * wet
    made["mix"] = (TIMESTEP * VERTICAL_MIX) * wet
    made["turn"] = TIMESTEP * coriolis * wet
    return made


def advance_level(k, count, levels, rows, src, sides, coef, acc):
    pitch = rows + 2 * PAD
    lane = iota((rows, LANES), 1)
    first, last = lane == 0, lane == LANES - 1
    above_k = jnp.maximum(k - 1, 0)
    below_k = jnp.minimum(k + 1, levels - 1)

    def load(q, level, shift):
        return src[pl.ds((q * count + level) * pitch + PAD + shift, rows), :]

    def base(q):
        return pl.multiple_of((q * count + k) * pitch + PAD, 8)

    center = [load(q, k, 0) for q in range(4)]
    u, v = coef("adv") * center[2], coef("adv") * center[3]
    sums, de, dn = [], [], []
    for q in range(4):
        c = center[q]
        n, s = load(q, k, 1), load(q, k, -1)
        edge = pltpu.roll(sides, (LANES - 1 - 2 * (q * levels + k)) & (LANES - 1), 1)
        e = jnp.where(last, edge, pltpu.roll(c, LANES - 1, 1))
        w = jnp.where(first, edge, pltpu.roll(c, 1, 1))
        kind = "t" if q < 2 else "v"
        lap = coef(kind + "c") * c + coef(kind + "e") * e + coef(kind + "w") * w
        lap = lap + coef(kind + "n") * n + coef(kind + "s") * s
        de.append(e - w)
        dn.append(n - s)
        sums.append(lap - (u * de[q] + v * dn[q]))
    scale = 0.5 * GRAVITY / VERTICAL_MIX
    dens_x = (scale * HALINE) * de[1] - (scale * THERMAL) * de[0]
    dens_y = (scale * HALINE) * dn[1] - (scale * THERMAL) * dn[0]
    acc_x, acc_y = acc
    grad = (None, None, acc_x + 0.5 * dens_x, acc_y + 0.5 * dens_y)
    turn = (None, None, coef("turn") * center[3], -coef("turn") * center[2])
    new = []
    for q in range(4):
        vertical = load(q, above_k, 0) + load(q, below_k, 0)
        if grad[q] is not None:
            vertical = vertical - grad[q]
        total = sums[q] + coef("mix") * vertical
        new.append(total if turn[q] is None else total + turn[q])
    return new, (acc_x + dens_x, acc_y + dens_y)


def advance_top_rows(levels, sides, north, south, state, wet, rows, table):
    fields = 4 * levels

    def both(a, b):
        return jnp.concatenate([a, b], axis=0)

    def rows_at(first):
        return both(
            north[pl.ds(first, 4, stride=levels), :], south[pl.ds(first, 4, stride=levels), :]
        )

    lane, row = iota((8, LANES), 1), iota((8, LANES), 0)
    upper = row < 4
    field = row & 3
    inside_n = state[pl.ds(rows - 1, 4, stride=levels * rows), :]
    inside_s = state[pl.ds(0, 4, stride=levels * rows), :]
    mid, below, outer = rows_at(0), rows_at(1), rows_at(fields)
    n = both(outer[0:4], inside_s)
    s = both(inside_n, outer[4:8])
    (corner_n, wet_ne, wet_nw), (corner_s, wet_se, wet_sw) = sides.corner(0), sides.corner(1)
    corner = jnp.where(upper, corner_n, corner_s)
    at = 2 * levels * field

    def end(parity):
        return jnp.sum(jnp.where(lane == at + parity, corner, 0.0), axis=1, keepdims=True)

    def west_east(x, east, west):
        return (
            jnp.where(lane == LANES - 1, east, pltpu.roll(x, LANES - 1, 1)),
            jnp.where(lane == 0, west, pltpu.roll(x, 1, 1)),
        )

    def tail(i):
        place = slice(2 * fields + i, 2 * fields + i + 1)
        return north[place, :], south[place, :]

    e, w = west_east(mid, end(0), end(1))
    wet_mid = jnp.where(upper, *tail(0))
    wet_e, wet_w = west_east(
        wet_mid, jnp.where(upper, wet_ne, wet_se), jnp.where(upper, wet_nw, wet_sw)
    )
    out_n, out_s = tail(1)
    wet_n = jnp.where(upper, out_n, wet[0:1])
    wet_s = jnp.where(upper, wet[rows - 1 : rows], out_s)
    lap = wet_e * (e - mid) + wet_w * (w - mid) + wet_n * (n - mid) + wet_s * (s - mid)
    de, dn = e - w, n - s

    def of(x, i):
        return jnp.where(upper, x[i : i + 1], x[4 + i : 5 + i])

    u, v = of(mid, 2), of(mid, 3)
    coriolis = jnp.where(upper, table[PAD + rows : PAD + rows + 1], table[PAD - 1 : PAD])
    grad_x = (0.25 * GRAVITY) * (HALINE * of(de, 1) - THERMAL * of(de, 0))
    grad_y = (0.25 * GRAVITY) * (HALINE * of(dn, 1) - THERMAL * of(dn, 0))
    turn = jnp.where(
        field < 2, 0.0, jnp.where(field == 2, coriolis * v - grad_x, -coriolis * u - grad_y)
    )
    kappa = jnp.where(field < 2, jnp.where(upper, *tail(2)), VISCOSITY)
    tend = turn - 0.5 * (u * de + v * dn) + kappa * lap + VERTICAL_MIX * (below - mid)
    return wet_mid * (mid + TIMESTEP * tend)


def surface_kernel(
    rows, levels,
    state, base, msg_a, msg_b, got_a, got_b, north, south, out_in, ids,
    coef, side, out, now, later, wet_pad, stage, places, sem,
):
    fields = 4 * levels
    pitch = rows + 2 * PAD
    to_scalars = pltpu.make_async_copy(ids, places, sem)
    to_scalars.start()
    out[...] = out_in[...]
    wet = base[0:rows, :]
    mixing = base[rows : 2 * rows, :]
    table = base[2 * rows :, :]
    coriolis = table[PAD : PAD + rows]
    lane = iota((rows, LANES), 1)
    sides = Sides(rows, got_a, got_b, msg_a, msg_b)
    wet_pad[PAD : PAD + rows, :] = wet
    wet_pad[PAD - 1 : PAD, :] = south[2 * fields : 2 * fields + 1, :]
    wet_pad[PAD + rows : PAD + rows + 1, :] = north[2 * fields : 2 * fields + 1, :]
    wet_n = wet_pad[PAD + 1 : PAD + 1 + rows, :]
    wet_s = wet_pad[PAD - 1 : PAD - 1 + rows, :]
    wet_e = jnp.where(lane == LANES - 1, sides.columns[0][0], pltpu.roll(wet, LANES - 1, 1))
    wet_w = jnp.where(lane == 0, sides.columns[1][0], pltpu.roll(wet, 1, 1))
    made = coefficients(wet, (wet_e, wet_w, wet_n, wet_s), mixing, coriolis)
    for name in COEFFICIENTS:
        coef[place_of(name, rows)] = made[name]
    near = sides.near()
    side[...] = near

    count = now.shape[0] // (4 * pitch)
    for q in range(4):
        for k in range(count):
            field = (q * levels + k) * rows
            at = (q * count + k) * pitch + PAD
            now[at : at + rows, :] = state[field : field + rows, :]
            now[at + rows : at + rows + 1, :] = north[q * levels + k : q * levels + k + 1, :]
            now[at - 1 : at, :] = south[q * levels + k : q * levels + k + 1, :]

    def read(name):
        return coef[place_of(name, rows)]

    none = jnp.zeros((rows, LANES), F32)
    acc = (none, none)
    edge_rows = advance_top_rows(levels, sides, north, south, state, wet, rows, table)
    edge_cols = advance_columns(sides, wet, coriolis, None)
    for k in range(count - 1):
        new, acc = advance_level(k, count, levels, rows, now, near, read, acc)
        for q in range(4):
            at = (q * count + k) * pitch + PAD
            later[at : at + rows, :] = new[q]
            if k == 0:
                later[at + rows : at + rows + 1, :] = edge_rows[q : q + 1]
                later[at - 1 : at, :] = edge_rows[4 + q : 5 + q]
    new, _ = advance_level(0, count, levels, rows, later, edge_cols, read, (none, none))
    for q in range(4):
        stage[pl.ds(q, rows, stride=4), :] = new[q]
    to_scalars.wait()
    for r in range(rows):
        out[pl.ds(places[0, r], 4), :] = stage[4 * r : 4 * r + 4, :]


def halo_after_first(rows, levels, sides, north, south, state, wet, table, col_map, row_map):
    fields = 4 * levels
    side_new = advance_columns(sides, wet, table[PAD : PAD + rows], col_map)
    lane, field = iota((fields, LANES), 1), iota((fields, LANES), 0)

    def to_sublanes(x, parity):
        here = lane == 2 * field + parity
        return jnp.sum(jnp.where(here, x, 0.0), axis=1, keepdims=True)

    parts = []
    for north_side, ref, line, lat_row in (
        (True, north, rows - 1, PAD + rows),
        (False, south, 0, PAD - 1),
    ):
        corner, *corner_wets = sides.corner(0 if north_side else 1)
        inside = state[pl.ds(line, fields, stride=rows), :]
        tail = ref[2 * fields :, :]
        pair = (ref[fields : 2 * fields, :], inside), (tail[1:2], wet[line : line + 1])
        (n, s), (wet_n, wet_s) = pair if north_side else [x[::-1] for x in pair]
        parts.append(
            (
                ref[0:fields, :], n, s, (to_sublanes(corner, 0), to_sublanes(corner, 1)),
                (tail[0:1], wet_n, wet_s, *corner_wets),
                tail[2:3], table[lat_row : lat_row + 1],
            )
        )
    return side_new, *advance_rows(levels, parts, row_map)


def main_kernel(
    rows, levels, chunks,
    state, base, msg_a, msg_b, got_a, got_b, north, south, col_map, row_map, coefs, side,
    tr_hbm, ve_hbm, now, later, side_new, tr_out, ve_out, sems,
):
    fields = 4 * levels
    pitch = rows + 2 * PAD
    sides = Sides(rows, got_a, got_b, msg_a, msg_b)
    side_new[...], north_new, south_new = halo_after_first(
        rows, levels, sides, north, south, state, base[0:rows, :], base[2 * rows :, :],
        col_map[...], row_map[...],
    )
    edges = (now, north[0:fields, :], south[0:fields, :]), (later, north_new, south_new)
    for buf, n, s in edges:
        buf[pl.ds(PAD - 1, fields, stride=pitch), :] = s
        buf[pl.ds(PAD + rows, fields, stride=pitch), :] = n

    def fill(f, carry):
        x = state[pl.ds(pl.multiple_of(f * rows, 8), rows), :]
        now[pl.ds(pl.multiple_of(f * pitch + PAD, 8), rows), :] = x
        return carry

    lax.fori_loop(0, fields, fill, 0, unroll=8)

    def coef(name):
        return coefs[place_of(name, rows)]

    def first(k, acc):
        new, acc = advance_level(k, levels, levels, rows, now, side[...], coef, acc)
        for q in range(4):
            place = pl.multiple_of((q * levels + k) * pitch + PAD, 8)
            later[pl.ds(place, rows), :] = new[q]
        return acc

    def second(k, acc):
        new, acc = advance_level(k, levels, levels, rows, later, side_new[...], coef, acc)
        for q in range(4):
            ref = tr_out if q < 2 else ve_out
            place = pl.multiple_of(((q % 2) * levels + k) * rows, 8)
            ref[pl.ds(place, rows), :] = new[q]
        return acc

    none = jnp.zeros((rows, LANES), F32)
    lax.fori_loop(0, levels, first, (none, none), unroll=2)
    acc = (none, none)
    size = levels // chunks
    copies = []
    for i in range(chunks):
        acc = lax.fori_loop(i * size, (i + 1) * size, second, acc, unroll=2)
        for src, dst in ((tr_out, tr_hbm), (ve_out, ve_hbm)):
            for q in range(2):
                start = (q * levels + i * size) * rows
                part = slice(start, start + size * rows)
                copy = pltpu.make_async_copy(src.at[part], dst.at[part], sems.at[len(copies)])
                copy.start()
                copies.append(copy)
    for copy in copies:
        copy.wait()


def reduce_kernel(devices, data, surface, cover):
    slot_rows = data.shape[0] // devices

    def rows_of(i):
        return data[pl.ds(i, devices, stride=slot_rows), :]

    width = LANES // CAP
    lines = rows_of(5 * CAP)
    named = (lines == (iota((devices, LANES), 1) % width).astype(F32)).astype(F32)
    to_rows, values = [], []
    for slot in range(CAP):
        to_rows.append(named[:, slot * width : slot * width + ATM_ROWS])
        parts = [rows_of(4 * slot + q) for q in range(4)] + [rows_of(4 * CAP + slot)]
        values.append(jnp.concatenate(parts, axis=1))
    rest = jnp.concatenate(values, axis=0)
    pieces = []
    for _ in range(3):
        piece = rest.astype(jnp.bfloat16)
        pieces.append(piece)
        rest = rest - piece.astype(F32)
    one = jnp.concatenate(to_rows, axis=0).astype(jnp.bfloat16)
    totals = lax.dot_general(
        jnp.concatenate([one] * 3, axis=0),
        jnp.concatenate(pieces, axis=0),
        (((0,), (0,)), ((), ())),
        preferred_element_type=F32,
    )
    ocean = totals[:, 4 * LANES :]
    cover[...] = ocean
    share = jnp.maximum(ocean, 1.0)
    for q in range(4):
        surface[q] = totals[:, q * LANES : (q + 1) * LANES] / share


def call(kernel, out_shape, limit=VMEM_LIMIT, **kwargs):
    return pl.pallas_call(
        kernel,
        out_shape=out_shape,
        compiler_params=pltpu.CompilerParams(vmem_limit_bytes=limit),
        **kwargs,
    )


def shaped(*shape, dtype=F32):
    return jax.ShapeDtypeStruct(shape, dtype)


def lat_swaps(lon_count, lat_count):
    swap_a, swap_b = [], []
    for i in range(lon_count):
        for a in range(lat_count):
            here = i * lat_count + a
            swap_a.append((here, i * lat_count + (a ^ 1)))
            if a == lat_count - 1:
                swap_b.append((here, (lon_count - 1 - i) * lat_count + a))
            elif a > 0:
                swap_b.append((here, here + 1 if a % 2 else here - 1))
    return swap_a, swap_b


def lon_swaps(lon_count, lat_count):
    swaps = [], []
    for i in range(lon_count):
        for a in range(lat_count):
            for swap, step in zip(swaps, (1, -1) if (i + a) % 2 else (-1, 1)):
                swap.append((i * lat_count + a, (i + step) % lon_count * lat_count + a))
    return swaps


def local(tracers, velocity, land_mask, mixing, owners, atm_row):
    levels = tracers.shape[1]
    rows, cols = land_mask.shape
    fields = 4 * levels
    lon_count, lat_count = lax.axis_size("lon"), lax.axis_size("lat")
    devices = lon_count * lat_count
    assert cols == LANES and rows % 8 == 0 and 2 * fields == LANES
    assert lon_count % 2 == 0 and lat_count % 2 == 0 and 3 * rows <= LANES
    length = 2 * fields + 8
    pitch = rows + 2 * PAD
    flat = 2 * levels * rows
    hbm = pl.BlockSpec(memory_space=pltpu.HBM)
    smem = pl.BlockSpec(memory_space=pltpu.SMEM)
    vmem = pl.BlockSpec(memory_space=pltpu.VMEM)

    deep = (2 * levels, rows, cols)
    lat_a, lat_b = call(
        functools.partial(edge_kernel, rows, fields),
        [pltpu.VMEM((length, cols), F32)] * 2,
        limit=VMEM_ALL,
        in_specs=[hbm] * 4,
        scratch_shapes=[
            pltpu.VMEM((2, fields, 8, cols), F32),
            pltpu.VMEM((rows, cols), jnp.int32),
            pltpu.VMEM((rows, cols), F32),
            pltpu.SemaphoreType.DMA((6,)),
        ],
    )(tracers.reshape(deep), velocity.reshape(deep), land_mask, mixing)
    swap_a, swap_b = lat_swaps(lon_count, lat_count)
    got_lat_b = lax.ppermute(lat_b, ("lon", "lat"), swap_b)
    got_lat_a = lax.ppermute(lat_a, ("lon", "lat"), swap_a)

    tr, ve = tracers.reshape(flat, cols), velocity.reshape(flat, cols)
    msg_a, msg_b = call(
        functools.partial(pack_kernel, rows, fields),
        [shaped(rows + 8, cols)] * 2,
        in_specs=[vmem] * 4,
    )(tr, ve, land_mask, mixing)

    slot_rows = 5 * CAP + 1
    state, base, col_map, row_map, outgoing, ids = call(
        functools.partial(prepare_kernel, rows, levels, devices),
        [
            shaped(fields * rows, cols),
            shaped(2 * rows + pitch, cols),
            shaped(3 * cols, cols),
            shaped(fields + levels, cols),
            shaped(devices * slot_rows, cols),
            shaped(8, cols, dtype=jnp.int32),
        ],
        in_specs=[vmem] * 4 + [smem] * 2,
        scratch_shapes=[pltpu.SMEM((devices,), jnp.int32)],
    )(tr, ve, land_mask, mixing, owners.reshape(rows), atm_row)

    def full(n):
        return pl.BlockSpec((n, cols), lambda i: (0, 0))

    tail = pl.BlockSpec((8, cols), lambda i: (rows // 8, 0))
    north, south, msg_a, msg_b = call(
        functools.partial(corner_kernel, lat_count, fields),
        [shaped(length, cols)] * 2 + [shaped(rows + 8, cols)] * 2,
        grid=(1,),
        in_specs=[full(length), full(length), tail, tail],
        out_specs=[full(length), full(length), tail, tail],
        input_output_aliases={2: 2, 3: 3},
    )(got_lat_b, got_lat_a, msg_a, msg_b)
    swap_a, swap_b = lon_swaps(lon_count, lat_count)
    got_b = lax.ppermute(msg_b, ("lon", "lat"), swap_b)
    got_a = lax.ppermute(msg_a, ("lon", "lat"), swap_a)

    count = min(3, levels)
    coefs, side, outgoing = call(
        functools.partial(surface_kernel, rows, levels),
        [
            shaped(len(COEFFICIENTS) * rows, cols),
            shaped(rows, cols),
            pltpu.VMEM((devices * slot_rows, cols), F32),
        ],
        scratch_shapes=[
            pltpu.VMEM((4 * count * pitch, cols), F32),
            pltpu.VMEM((4 * count * pitch, cols), F32),
            pltpu.VMEM((pitch, cols), F32),
            pltpu.VMEM((4 * rows, cols), F32),
            pltpu.SMEM((8, cols), jnp.int32),
            pltpu.SemaphoreType.DMA,
        ],
    )(state, base, msg_a, msg_b, got_a, got_b, north, south, outgoing, ids)
    incoming = lax.all_to_all(
        outgoing.reshape(devices, slot_rows, 1, cols),
        ("lon", "lat"),
        0,
        0,
        axis_index_groups=[list(range(devices))[::-1]],
        tiled=True,
    ).reshape(devices * slot_rows, cols)

    chunks = 4
    tr_out, ve_out = call(
        functools.partial(main_kernel, rows, levels, chunks),
        [shaped(flat, cols), shaped(flat, cols)],
        in_specs=[vmem] * 12,
        out_specs=[hbm] * 2,
        scratch_shapes=[
            pltpu.VMEM((fields * pitch, cols), F32),
            pltpu.VMEM((fields * pitch, cols), F32),
            pltpu.VMEM((rows, cols), F32),
            pltpu.VMEM((flat, cols), F32),
            pltpu.VMEM((flat, cols), F32),
            pltpu.SemaphoreType.DMA((4 * chunks,)),
        ],
        cost_estimate=pl.CostEstimate(
            flops=80 * fields * rows * cols, bytes_accessed=5 << 20, transcendentals=0
        ),
    )(state, base, msg_a, msg_b, got_a, got_b, north, south, col_map, row_map, coefs, side)
    surface, cover = call(
        functools.partial(reduce_kernel, devices),
        [shaped(4, ATM_ROWS, cols), shaped(ATM_ROWS, cols)],
    )(incoming)
    shape = (2, levels, rows, cols)
    return tr_out.reshape(shape), ve_out.reshape(shape), surface, cover


def solution(mesh):
    in_specs = (
        P(None, None, "lat", "lon"),
        P(None, None, "lat", "lon"),
        P("lat", "lon"),
        P("lat", "lon"),
        P(("lon", "lat"), None),
        P(("lon", "lat")),
    )
    out_specs = (
        P(None, None, "lat", "lon"),
        P(None, None, "lat", "lon"),
        P(None, ("lon", "lat"), None),
        P(("lon", "lat"), None),
    )
    return jax.shard_map(local, mesh=mesh, in_specs=in_specs, out_specs=out_specs, check_vma=False)
```

```python
import functools
import math

import jax
import jax.numpy as jnp
from jax import lax
from jax.experimental import pallas as pl
from jax.experimental.pallas import tpu as pltpu
from jax.sharding import PartitionSpec as P

ATM_ROWS = 32
CAP = 2

THERMAL = 0.2
HALINE = 0.15
GRAVITY = 0.2
TIMESTEP = 0.8
VERTICAL_MIX = 0.1
VISCOSITY = 0.2
CORIOLIS_MAX = 0.3

LANES = 128
PAD = 8
EXACT = lax.Precision.HIGHEST
F32 = jnp.float32
VMEM_LIMIT = 32 * 1024 * 1024
VMEM_ALL = 62 * 1024 * 1024


def iota(shape, dim):
    return lax.broadcasted_iota(jnp.int32, shape, dim)


def dot(a, b, dims=(((1,), (0,)), ((), ()))):
    return lax.dot_general(a, b, dims, precision=EXACT, preferred_element_type=F32)


def is_even(axis):
    return lax.rem(lax.axis_index(axis), 2) == 0


def start_copies(pairs, sems):
    copies = [pltpu.make_async_copy(src, dst, sems.at[i]) for i, (src, dst) in enumerate(pairs)]
    for copy in copies:
        copy.start()
    return copies


def edge_kernel(rows, fields, tr_hbm, ve_hbm, mask_hbm, mix_hbm, lat_a, lat_b, edges, mask, mix, sems):
    half = fields // 2
    pairs = [(mask_hbm, mask), (mix_hbm, mix)]
    for n, src in enumerate((tr_hbm, ve_hbm)):
        for side, first in enumerate((0, rows - 8)):
            part = edges.at[side, n * half : (n + 1) * half]
            pairs.append((src.at[:, first : first + 8, :], part))
    for copy in start_copies(pairs, sems):
        copy.wait()
    flat = edges.reshape(2 * fields * 8, LANES)
    even = is_even("lat")
    top = ((rows - 1, 8 * fields + 7), (rows - 2, 8 * fields + 6))
    bottom = ((0, 0), (1, 1))
    for buf, first, second in ((lat_a, top, bottom), (lat_b, bottom, top)):
        (near, near_at), (far, far_at) = [
            [jnp.where(even, x, y) for x, y in zip(one, other)] for one, other in zip(first, second)
        ]
        wet_near = mask[pl.ds(near, 1), :].astype(F32)
        wet_far = mask[pl.ds(far, 1), :].astype(F32)
        buf[0:fields, :] = flat[pl.ds(near_at, fields, stride=8), :] * wet_near
        buf[fields : 2 * fields, :] = flat[pl.ds(far_at, fields, stride=8), :] * wet_far
        buf[2 * fields : 2 * fields + 8, :] = jnp.zeros((8, LANES), F32)
        buf[2 * fields : 2 * fields + 1, :] = wet_near
        buf[2 * fields + 1 : 2 * fields + 2, :] = wet_far
        buf[2 * fields + 2 : 2 * fields + 3, :] = mix[pl.ds(near, 1), :]


def pack_kernel(rows, fields, tr, ve, mask, mix, msg_a, msg_b):
    half = fields // 2
    wet = mask[...].astype(F32)
    lane = iota((rows, LANES), 1)
    pair = lane >> 1

    def columns(ref, base):
        def body(f, carry):
            to_east, to_west = carry
            x = ref[pl.ds(pl.multiple_of(f * rows, rows), rows), :]
            keep = pair == base + f
            low = 2 * (base + f)
            to_east = jnp.where(keep, pltpu.roll(x, (low + 2) & (LANES - 1), 1), to_east)
            to_west = jnp.where(keep, pltpu.roll(x, low, 1), to_west)
            return to_east, to_west

        return body

    carry = (jnp.zeros((rows, LANES), F32), jnp.zeros((rows, LANES), F32))
    for ref, base in ((tr, 0), (ve, half)):
        carry = lax.fori_loop(0, half, columns(ref, base), carry, unroll=8)
    def spread(x, i):
        return jnp.broadcast_to(x[:, i : i + 1], (rows, LANES))

    odd = (lane & 1) == 1
    to_east = carry[0] * jnp.where(odd, spread(wet, LANES - 1), spread(wet, LANES - 2))
    to_west = carry[1] * jnp.where(odd, spread(wet, 1), spread(wet, 0))
    even = is_even("lon")
    row = iota((rows, LANES), 0)
    mixing = mix[...]
    lines = []
    for near, far in ((LANES - 1, LANES - 2), (0, 1)):
        line = jnp.zeros((rows, LANES), F32)
        for part, column in enumerate((wet[:, near], wet[:, far], mixing[:, near])):
            line = jnp.where(lane == part * rows + row, column[:, None], line)
        lines.append(jnp.sum(line, axis=0, keepdims=True))
    for msg, flag in ((msg_a, jnp.logical_not(even)), (msg_b, even)):
        msg[0:rows, :] = jnp.where(flag, to_east, to_west)
        msg[rows:, :] = jnp.zeros((8, LANES), F32)
        msg[rows + 4 : rows + 5, :] = jnp.where(flag, *lines)


def prepare_kernel(
    rows, levels, devices, tr, ve, mask, mix, own, atm_row,
    state, base, col_map, row_map, out, ids, used,
):
    fields = 4 * levels
    half = fields // 2
    wet = mask[...].astype(F32)
    base[0:rows, :] = wet
    base[rows : 2 * rows, :] = mix[...]
    for ref, first in ((tr, 0), (ve, half)):

        def fill(f, carry, ref=ref, first=first):
            x = ref[pl.ds(pl.multiple_of(f * rows, 8), rows), :] * wet
            state[pl.ds(pl.multiple_of((first + f) * rows, 8), rows), :] = x
            return carry

        lax.fori_loop(0, half, fill, 0, unroll=8)

    total = lax.axis_size("lat") * rows
    latitude = lax.axis_index("lat") * rows - PAD + iota((rows + 2 * PAD, LANES), 0)
    latitude = jnp.where(latitude >= total, 2 * total - 1 - latitude, latitude).astype(F32)
    table = CORIOLIS_MAX * jnp.sin(math.pi * (-0.43 + 0.93 * (latitude + 0.5) / total))
    base[2 * rows :, :] = table

    span = 2 * levels
    src, dst = iota((LANES, LANES), 0), iota((LANES, LANES), 1)
    src_group, dst_group = src // span, dst // span
    src_level, dst_level = (src // 2) % levels, (dst // 2) % levels
    same_side = (src & 1) == (dst & 1)
    mixes = VERTICAL_MIX * level_matrix("mix", levels, src_level, dst_level)
    press = level_matrix("pressure", levels, src_level, dst_level) * density_weight(src_group)
    col_map[0:LANES, :] = jnp.where(same_side & (src_group == dst_group), mixes, 0.0)
    col_map[LANES : 2 * LANES, :] = jnp.where(same_side & (dst_group == 2), -press, 0.0)
    col_map[2 * LANES :, :] = jnp.where(same_side & (dst_group == 3), -press, 0.0)

    dst, src = iota((fields, fields), 0), iota((fields, fields), 1)
    mixes = VERTICAL_MIX * level_matrix("mix", levels, src % levels, dst % levels)
    row_map[0:fields, 0:fields] = jnp.where(dst // levels == src // levels, mixes, 0.0)
    dst, src = iota((levels, fields), 0), iota((levels, fields), 1)
    press = level_matrix("pressure", levels, src % levels, dst) * density_weight(src // levels)
    row_map[fields:, 0:fields] = press

    slot_rows = out.shape[0] // devices

    def clear(d, carry):
        used[d] = 0
        return carry

    lax.fori_loop(0, devices, clear, 0, unroll=8)
    out[...] = jnp.zeros(out.shape, F32)
    lane1 = iota((1, LANES), 1)
    places = jnp.zeros((1, LANES), jnp.int32)
    for r in range(rows):
        owner = own[r]
        slot = used[owner]
        used[owner] = slot + 1
        start = (devices - 1 - owner) * slot_rows
        places = jnp.where(lane1 == r, start + 4 * slot, places)
        out[pl.ds(start + 4 * CAP + slot, 1), :] = base[r : r + 1, :]
        line = out[pl.ds(start + 5 * CAP, 1), :]
        target = jnp.full((1, LANES), atm_row[r], jnp.int32).astype(F32)
        out[pl.ds(start + 5 * CAP, 1), :] = jnp.where(lane1 // (LANES // CAP) == slot, target, line)
    ids[...] = jnp.zeros(ids.shape, jnp.int32)
    ids[0:1, :] = places


def corner_kernel(lat_count, fields, got_b, got_a, tail_a, tail_b, north, south, new_a, new_b):
    fold = lax.axis_index("lat") == lat_count - 1
    even = is_even("lat")
    a, b = got_a[...], got_b[...]
    straight = jnp.where(even, a, b)
    south[...] = jnp.where(even, b, a)
    back = LANES - 1 - iota((8, LANES), 1)
    flipped = jnp.concatenate(
        [
            jnp.take_along_axis(straight[i : i + 8], back, axis=1)
            * (-1.0 if i < 2 * fields and i % fields >= fields // 2 else 1.0)
            for i in range(0, straight.shape[0], 8)
        ],
        axis=0,
    )
    north[...] = jnp.where(fold, flipped, straight)
    lane, field = iota((fields, LANES), 1), iota((fields, LANES), 0)
    lane1 = iota((1, LANES), 1)
    for old, new in ((tail_a, new_a), (tail_b, new_b)):
        new[...] = old[...]
    for i, ref in enumerate((north, south)):
        near = ref[0:fields, :]
        ends = jnp.where(
            lane == 2 * field, near[:, 0:1], jnp.where(lane == 2 * field + 1, near[:, LANES - 1 :], 0.0)
        )
        corner = jnp.sum(ends, axis=0, keepdims=True)
        wet = ref[2 * fields : 2 * fields + 1, :]
        wet = jnp.where(lane1 == 0, wet[:, 0:1], wet[:, LANES - 1 :])
        for new in (new_a, new_b):
            new[i : i + 1, :] = corner
            new[2 + i : 3 + i, :] = wet


class Sides:
    def __init__(self, rows, got_a, got_b, msg_a, msg_b):
        lane, row = iota((rows, LANES), 1), iota((rows, LANES), 0)
        self.even = (lane & 1) == 0
        self.even1 = (iota((1, LANES), 1) & 1) == 0
        even = is_even("lon")

        def ordered(a, b, place):
            return jnp.where(even, b[place, :], a[place, :]), jnp.where(even, a[place, :], b[place, :])

        self.got = ordered(got_a, got_b, slice(0, rows))
        self.mine = ordered(msg_a, msg_b, slice(0, rows))
        self.extras = ordered(got_a, got_b, slice(rows, rows + 8))
        self.columns = [
            [
                jnp.sum(jnp.where(lane == i * rows + row, x[4:5], 0.0), axis=1, keepdims=True)
                for i in range(3)
            ]
            for x in self.extras
        ]

    def near(self):
        return jnp.where(self.even, *self.got)

    def far_and_inner(self):
        east, west = self.got
        mine_e, mine_w = self.mine
        far = jnp.where(self.even, pltpu.roll(east, LANES - 1, 1), pltpu.roll(west, 1, 1))
        inner = jnp.where(self.even, pltpu.roll(mine_e, LANES - 1, 1), pltpu.roll(mine_w, 1, 1))
        return far, inner

    def corner(self, i):
        east, west = self.extras
        wets = east[2 + i : 3 + i, 0:1], west[2 + i : 3 + i, 1:2]
        return jnp.where(self.even1, east[i : i + 1], west[i : i + 1]), *wets

    def lanes(self, i):
        return jnp.where(self.even, self.columns[0][i], self.columns[1][i])


def level_matrix(kind, levels, source, target):
    if kind == "mix":
        above = (source == jnp.maximum(target - 1, 0)).astype(F32)
        below = (source == jnp.minimum(target + 1, levels - 1)).astype(F32)
        return above + below - 2.0 * (source == target).astype(F32)
    full = jnp.where(source < target, 1.0, jnp.where(source == target, 0.5, 0.0))
    return (0.5 * GRAVITY) * full


def density_weight(group):
    return jnp.where(group == 0, -THERMAL, jnp.where(group == 1, HALINE, 0.0)).astype(F32)


def advance_columns(sides, wet, coriolis, level_map):
    rows = wet.shape[0]
    mid = sides.near()
    outer, inner = sides.far_and_inner()
    (corner_n, wet_ne, wet_nw), (corner_s, wet_se, wet_sw) = sides.corner(0), sides.corner(1)
    wet_mid, wet_out = sides.lanes(0), sides.lanes(1)
    wet_in = jnp.where(sides.even, wet[:, LANES - 1 :], wet[:, 0:1])
    wet_corner_n = jnp.where(sides.even1, wet_ne, wet_nw)
    wet_corner_s = jnp.where(sides.even1, wet_se, wet_sw)
    mixing = sides.lanes(2)
    lane = iota((rows, LANES), 1)
    row = iota((rows, LANES), 0)
    span = LANES // 4
    group = lane // span

    def ends(outside, inside):
        return jnp.where(sides.even, outside, inside), jnp.where(sides.even, inside, outside)

    def shifted(x, north, south):
        n = jnp.where(row == rows - 1, north, pltpu.roll(x, rows - 1, 0))
        s = jnp.where(row == 0, south, pltpu.roll(x, 1, 0))
        return n, s

    e, w = ends(outer, inner)
    wet_e, wet_w = ends(wet_out, wet_in)
    n, s = shifted(mid, corner_n, corner_s)
    wet_n, wet_s = shifted(wet_mid, wet_corner_n, wet_corner_s)
    lap = wet_e * (e - mid) + wet_w * (w - mid) + wet_n * (n - mid) + wet_s * (s - mid)
    de, dn = e - w, n - s
    one, two, three = (pltpu.roll(mid, i * span, 1) for i in (1, 2, 3))

    def pick(a, b, c, d):
        return jnp.where(group == 0, a, jnp.where(group == 1, b, jnp.where(group == 2, c, d)))

    u = pick(two, three, mid, one)
    v = pick(one, two, three, mid)
    adv = 0.5 * (u * de + v * dn)
    zero = jnp.zeros_like(mid)
    if level_map is None:
        grad_x = HALINE * pltpu.roll(de, span, 1) - THERMAL * pltpu.roll(de, 2 * span, 1)
        grad_y = HALINE * pltpu.roll(dn, 2 * span, 1) - THERMAL * pltpu.roll(dn, 3 * span, 1)
        linear = VERTICAL_MIX * (pltpu.roll(mid, LANES - 2, 1) - mid)
        linear = linear - (0.25 * GRAVITY) * pick(zero, zero, grad_x, grad_y)
    else:
        linear = dot(jnp.concatenate([mid, de, dn], axis=1), level_map)
    turn = pick(zero, zero, coriolis * v, -coriolis * u)
    kappa = jnp.where(group < 2, mixing, VISCOSITY)
    tend = turn - adv + kappa * lap + linear
    return wet_mid * (mid + TIMESTEP * tend)


def advance_rows(levels, parts, level_map):
    fields = 4 * levels
    lane = iota((fields, LANES), 1)
    lane8 = iota((8, LANES), 1)

    def sides(x, east, west, at):
        e = jnp.where(at == LANES - 1, east, pltpu.roll(x, LANES - 1, 1))
        w = jnp.where(at == 0, west, pltpu.roll(x, 1, 1))
        return e, w

    mids, gaps = [], []
    for mid, n, s, (corner_e, corner_w), *_ in parts:
        e, w = sides(mid, corner_e, corner_w, lane)
        mids.append((mid, e, w, n, s))
        gaps += [e - w, n - s]
    vertical = dot(level_map[0:fields, 0:fields], jnp.concatenate([m[0] for m in mids], axis=1))
    grads = dot(level_map[fields:, 0:fields], jnp.concatenate(gaps, axis=1))
    done = []
    for i, (mid, e, w, n, s) in enumerate(mids):
        *_, wets, mixing, coriolis = parts[i]
        wet_mid, wet_n, wet_s, wet_corner_e, wet_corner_w = wets
        wet_e, wet_w = sides(
            jnp.broadcast_to(wet_mid, (8, LANES)), wet_corner_e, wet_corner_w, lane8
        )
        lap = wet_e[0:1] * (e - mid) + wet_w[0:1] * (w - mid)
        lap = lap + wet_n * (n - mid) + wet_s * (s - mid)
        de, dn = gaps[2 * i], gaps[2 * i + 1]
        u, v = mid[2 * levels : 3 * levels], mid[3 * levels :]
        adv = jnp.concatenate([u] * 4, axis=0) * de + jnp.concatenate([v] * 4, axis=0) * dn
        grad_x = grads[:, 2 * i * LANES : (2 * i + 1) * LANES]
        grad_y = grads[:, (2 * i + 1) * LANES : (2 * i + 2) * LANES]
        zero = jnp.zeros((2 * levels, LANES), F32)
        turn = jnp.concatenate([zero, coriolis * v - grad_x, -coriolis * u - grad_y], axis=0)
        kappa = jnp.concatenate(
            [jnp.broadcast_to(mixing, (2 * levels, LANES)), jnp.full(zero.shape, VISCOSITY)],
            axis=0,
        )
        tend = turn - 0.5 * adv + kappa * lap + vertical[:, i * LANES : (i + 1) * LANES]
        done.append(wet_mid * (mid + TIMESTEP * tend))
    return done


COEFFICIENTS = ("te", "tw", "tn", "ts", "tc", "ve", "vw", "vn", "vs", "vc", "adv", "mix", "turn")


def place_of(name, rows):
    i = COEFFICIENTS.index(name)
    return slice(i * rows, (i + 1) * rows)


def coefficients(wet, neighbours, mixing, coriolis):
    made = {}
    for name, kappa in (("t", mixing), ("v", VISCOSITY)):
        rest = wet * (1.0 - 2.0 * TIMESTEP * VERTICAL_MIX)
        for side, wet_n in zip("ewns", neighbours):
            made[name + side] = TIMESTEP * kappa * wet * wet_n
            rest = rest - made[name + side]
        made[name + "c"] = rest
    made["adv"] = (0.5 * TIMESTEP) * wet
    made["mix"] = (TIMESTEP * VERTICAL_MIX) * wet
    made["turn"] = TIMESTEP * coriolis * wet
    return made


def advance_level(k, count, levels, rows, src, sides, coef, acc):
    pitch = rows + 2 * PAD
    lane = iota((rows, LANES), 1)
    first, last = lane == 0, lane == LANES - 1
    above_k = jnp.maximum(k - 1, 0)
    below_k = jnp.minimum(k + 1, levels - 1)

    def load(q, level, shift):
        return src[pl.ds((q * count + level) * pitch + PAD + shift, rows), :]

    def base(q):
        return pl.multiple_of((q * count + k) * pitch + PAD, 8)

    center = [load(q, k, 0) for q in range(4)]
    u, v = coef("adv") * center[2], coef("adv") * center[3]
    sums, de, dn = [], [], []
    for q in range(4):
        c = center[q]
        n, s = load(q, k, 1), load(q, k, -1)
        edge = pltpu.roll(sides, (LANES - 1 - 2 * (q * levels + k)) & (LANES - 1), 1)
        e = jnp.where(last, edge, pltpu.roll(c, LANES - 1, 1))
        w = jnp.where(first, edge, pltpu.roll(c, 1, 1))
        kind = "t" if q < 2 else "v"
        lap = coef(kind + "c") * c + coef(kind + "e") * e + coef(kind + "w") * w
        lap = lap + coef(kind + "n") * n + coef(kind + "s") * s
        de.append(e - w)
        dn.append(n - s)
        sums.append(lap - (u * de[q] + v * dn[q]))
    scale = 0.5 * GRAVITY / VERTICAL_MIX
    dens_x = (scale * HALINE) * de[1] - (scale * THERMAL) * de[0]
    dens_y = (scale * HALINE) * dn[1] - (scale * THERMAL) * dn[0]
    acc_x, acc_y = acc
    grad = (None, None, acc_x + 0.5 * dens_x, acc_y + 0.5 * dens_y)
    turn = (None, None, coef("turn") * center[3], -coef("turn") * center[2])
    new = []
    for q in range(4):
        vertical = load(q, above_k, 0) + load(q, below_k, 0)
        if grad[q] is not None:
            vertical = vertical - grad[q]
        total = sums[q] + coef("mix") * vertical
        new.append(total if turn[q] is None else total + turn[q])
    return new, (acc_x + dens_x, acc_y + dens_y)


def advance_top_rows(levels, sides, north, south, state, wet, rows, table):
    fields = 4 * levels

    def both(a, b):
        return jnp.concatenate([a, b], axis=0)

    def rows_at(first):
        return both(
            north[pl.ds(first, 4, stride=levels), :], south[pl.ds(first, 4, stride=levels), :]
        )

    lane, row = iota((8, LANES), 1), iota((8, LANES), 0)
    upper = row < 4
    field = row & 3
    inside_n = state[pl.ds(rows - 1, 4, stride=levels * rows), :]
    inside_s = state[pl.ds(0, 4, stride=levels * rows), :]
    mid, below, outer = rows_at(0), rows_at(1), rows_at(fields)
    n = both(outer[0:4], inside_s)
    s = both(inside_n, outer[4:8])
    (corner_n, wet_ne, wet_nw), (corner_s, wet_se, wet_sw) = sides.corner(0), sides.corner(1)
    corner = jnp.where(upper, corner_n, corner_s)
    at = 2 * levels * field

    def end(parity):
        return jnp.sum(jnp.where(lane == at + parity, corner, 0.0), axis=1, keepdims=True)

    def west_east(x, east, west):
        return (
            jnp.where(lane == LANES - 1, east, pltpu.roll(x, LANES - 1, 1)),
            jnp.where(lane == 0, west, pltpu.roll(x, 1, 1)),
        )

    def tail(i):
        place = slice(2 * fields + i, 2 * fields + i + 1)
        return north[place, :], south[place, :]

    e, w = west_east(mid, end(0), end(1))
    wet_mid = jnp.where(upper, *tail(0))
    wet_e, wet_w = west_east(
        wet_mid, jnp.where(upper, wet_ne, wet_se), jnp.where(upper, wet_nw, wet_sw)
    )
    out_n, out_s = tail(1)
    wet_n = jnp.where(upper, out_n, wet[0:1])
    wet_s = jnp.where(upper, wet[rows - 1 : rows], out_s)
    lap = wet_e * (e - mid) + wet_w * (w - mid) + wet_n * (n - mid) + wet_s * (s - mid)
    de, dn = e - w, n - s

    def of(x, i):
        return jnp.where(upper, x[i : i + 1], x[4 + i : 5 + i])

    u, v = of(mid, 2), of(mid, 3)
    coriolis = jnp.where(upper, table[PAD + rows : PAD + rows + 1], table[PAD - 1 : PAD])
    grad_x = (0.25 * GRAVITY) * (HALINE * of(de, 1) - THERMAL * of(de, 0))
    grad_y = (0.25 * GRAVITY) * (HALINE * of(dn, 1) - THERMAL * of(dn, 0))
    turn = jnp.where(
        field < 2, 0.0, jnp.where(field == 2, coriolis * v - grad_x, -coriolis * u - grad_y)
    )
    kappa = jnp.where(field < 2, jnp.where(upper, *tail(2)), VISCOSITY)
    tend = turn - 0.5 * (u * de + v * dn) + kappa * lap + VERTICAL_MIX * (below - mid)
    return wet_mid * (mid + TIMESTEP * tend)


def inside_kernel(rows, levels, state, base, north, south, coef, part, now, wet_pad):
    fields = 4 * levels
    pitch = rows + 2 * PAD
    wet = base[0:rows, :]
    lane = iota((rows, LANES), 1)
    wet_pad[PAD : PAD + rows, :] = wet
    wet_pad[PAD - 1 : PAD, :] = south[2 * fields : 2 * fields + 1, :]
    wet_pad[PAD + rows : PAD + rows + 1, :] = north[2 * fields : 2 * fields + 1, :]
    wet_n = wet_pad[PAD + 1 : PAD + 1 + rows, :]
    wet_s = wet_pad[PAD - 1 : PAD - 1 + rows, :]
    wet_e = jnp.where(lane == LANES - 1, 0.0, pltpu.roll(wet, LANES - 1, 1))
    wet_w = jnp.where(lane == 0, 0.0, pltpu.roll(wet, 1, 1))
    made = coefficients(
        wet, (wet_e, wet_w, wet_n, wet_s), base[rows : 2 * rows, :],
        base[2 * rows + PAD : 3 * rows + PAD, :],
    )
    for name in COEFFICIENTS:
        coef[place_of(name, rows)] = made[name]
    count = now.shape[0] // (4 * pitch)
    for q in range(4):
        for k in range(count):
            field = (q * levels + k) * rows
            at = (q * count + k) * pitch + PAD
            now[at : at + rows, :] = state[field : field + rows, :]
            now[at + rows : at + rows + 1, :] = north[q * levels + k : q * levels + k + 1, :]
            now[at - 1 : at, :] = south[q * levels + k : q * levels + k + 1, :]
    none = jnp.zeros((rows, LANES), F32)
    acc = (none, none)
    for k in range(count - 1):
        new, acc = advance_level(
            k, count, levels, rows, now, none, lambda x: coef[place_of(x, rows)], acc
        )
        for q in range(4):
            at = (q * (count - 1) + k) * rows
            part[at : at + rows, :] = new[q]


def surface_kernel(
    rows, levels,
    state, base, inner, part, msg_a, msg_b, got_b, got_a, north, south, out_in, ids,
    coef, side, out, later, stage, places, sem,
):
    pitch = rows + 2 * PAD
    to_scalars = pltpu.make_async_copy(ids, places, sem)
    to_scalars.start()
    out[...] = out_in[...]
    wet = base[0:rows, :]
    table = base[2 * rows :, :]
    lane = iota((rows, LANES), 1)
    sides = Sides(rows, got_a, got_b, msg_a, msg_b)
    near = sides.near()
    side[...] = near
    edge_rows = advance_top_rows(levels, sides, north, south, state, wet, rows, table)
    edge_cols = advance_columns(sides, wet, table[PAD : PAD + rows], None)

    east, west = lane == LANES - 1, lane == 0
    wet_out = jnp.where(east, sides.columns[0][0], jnp.where(west, sides.columns[1][0], 0.0))
    sign = jnp.where(east, -1.0, jnp.where(west, 1.0, 0.0))
    take_v = (TIMESTEP * VISCOSITY) * wet * wet_out
    take = {"t": TIMESTEP * base[rows : 2 * rows, :] * wet * wet_out, "v": take_v}
    coef[...] = inner[...]
    for kind, more in take.items():
        for name, change in (
            ("e", jnp.where(east, more, 0.0)), ("w", jnp.where(west, more, 0.0)), ("c", -more)
        ):
            place = place_of(kind + name, rows)
            coef[place] = inner[place] + change

    def read(name):
        return coef[place_of(name, rows)]

    count = later.shape[0] // (4 * pitch)
    scale = 0.5 * GRAVITY / VERTICAL_MIX
    acc = jnp.zeros((rows, LANES), F32)
    for k in range(count):
        edges = [
            pltpu.roll(near, (LANES - 1 - 2 * (q * levels + k)) & (LANES - 1), 1) for q in range(4)
        ]
        center = [
            state[(q * levels + k) * rows : (q * levels + k + 1) * rows, :] for q in range(4)
        ]
        u = sign * inner[place_of("adv", rows)] * center[2]
        dens = (scale * HALINE) * edges[1] - (scale * THERMAL) * edges[0]
        grad = sign * inner[place_of("mix", rows)] * (acc + 0.5 * dens)
        acc = acc + dens
        for q in range(4):
            more = take["t" if q < 2 else "v"] * (edges[q] - center[q]) + u * edges[q]
            if q == 2:
                more = more + grad
            at = (q * count + k) * rows
            new = part[at : at + rows, :] + more
            at = (q * count + k) * pitch + PAD
            later[at : at + rows, :] = new
            if k == 0:
                later[at + rows : at + rows + 1, :] = edge_rows[q : q + 1]
                later[at - 1 : at, :] = edge_rows[4 + q : 5 + q]
    none = jnp.zeros((rows, LANES), F32)
    new, _ = advance_level(0, count, levels, rows, later, edge_cols, read, (none, none))
    for q in range(4):
        stage[pl.ds(q, rows, stride=4), :] = new[q]
    to_scalars.wait()
    for r in range(rows):
        out[pl.ds(places[0, r], 4), :] = stage[4 * r : 4 * r + 4, :]


def halo_after_first(rows, levels, sides, north, south, state, wet, table, col_map, row_map):
    fields = 4 * levels
    side_new = advance_columns(sides, wet, table[PAD : PAD + rows], col_map)
    lane, field = iota((fields, LANES), 1), iota((fields, LANES), 0)

    def to_sublanes(x, parity):
        here = lane == 2 * field + parity
        return jnp.sum(jnp.where(here, x, 0.0), axis=1, keepdims=True)

    parts = []
    for north_side, ref, line, lat_row in (
        (True, north, rows - 1, PAD + rows),
        (False, south, 0, PAD - 1),
    ):
        corner, *corner_wets = sides.corner(0 if north_side else 1)
        inside = state[pl.ds(line, fields, stride=rows), :]
        tail = ref[2 * fields :, :]
        pair = (ref[fields : 2 * fields, :], inside), (tail[1:2], wet[line : line + 1])
        (n, s), (wet_n, wet_s) = pair if north_side else [x[::-1] for x in pair]
        parts.append(
            (
                ref[0:fields, :], n, s, (to_sublanes(corner, 0), to_sublanes(corner, 1)),
                (tail[0:1], wet_n, wet_s, *corner_wets),
                tail[2:3], table[lat_row : lat_row + 1],
            )
        )
    return side_new, *advance_rows(levels, parts, row_map)


def main_kernel(
    rows, levels, chunks,
    state, base, msg_a, msg_b, got_a, got_b, north, south, col_map, row_map, coefs, side,
    tr_hbm, ve_hbm, now, later, side_new, tr_out, ve_out, sems,
):
    fields = 4 * levels
    pitch = rows + 2 * PAD
    sides = Sides(rows, got_a, got_b, msg_a, msg_b)
    side_new[...], north_new, south_new = halo_after_first(
        rows, levels, sides, north, south, state, base[0:rows, :], base[2 * rows :, :],
        col_map[...], row_map[...],
    )
    edges = (now, north[0:fields, :], south[0:fields, :]), (later, north_new, south_new)
    for buf, n, s in edges:
        buf[pl.ds(PAD - 1, fields, stride=pitch), :] = s
        buf[pl.ds(PAD + rows, fields, stride=pitch), :] = n

    def fill(f, carry):
        x = state[pl.ds(pl.multiple_of(f * rows, 8), rows), :]
        now[pl.ds(pl.multiple_of(f * pitch + PAD, 8), rows), :] = x
        return carry

    lax.fori_loop(0, fields, fill, 0, unroll=8)

    def coef(name):
        return coefs[place_of(name, rows)]

    def first(k, acc):
        new, acc = advance_level(k, levels, levels, rows, now, side[...], coef, acc)
        for q in range(4):
            place = pl.multiple_of((q * levels + k) * pitch + PAD, 8)
            later[pl.ds(place, rows), :] = new[q]
        return acc

    def second(k, acc):
        new, acc = advance_level(k, levels, levels, rows, later, side_new[...], coef, acc)
        for q in range(4):
            ref = tr_out if q < 2 else ve_out
            place = pl.multiple_of(((q % 2) * levels + k) * rows, 8)
            ref[pl.ds(place, rows), :] = new[q]
        return acc

    none = jnp.zeros((rows, LANES), F32)
    lax.fori_loop(0, levels, first, (none, none), unroll=2)
    acc = (none, none)
    size = levels // chunks
    copies = []
    for i in range(chunks):
        acc = lax.fori_loop(i * size, (i + 1) * size, second, acc, unroll=2)
        for src, dst in ((tr_out, tr_hbm), (ve_out, ve_hbm)):
            for q in range(2):
                start = (q * levels + i * size) * rows
                part = slice(start, start + size * rows)
                copy = pltpu.make_async_copy(src.at[part], dst.at[part], sems.at[len(copies)])
                copy.start()
                copies.append(copy)
    for copy in copies:
        copy.wait()


def reduce_kernel(devices, data, surface, cover):
    slot_rows = data.shape[0] // devices

    def rows_of(i):
        return data[pl.ds(i, devices, stride=slot_rows), :]

    width = LANES // CAP
    lines = rows_of(5 * CAP)
    named = (lines == (iota((devices, LANES), 1) % width).astype(F32)).astype(F32)
    to_rows, values = [], []
    for slot in range(CAP):
        to_rows.append(named[:, slot * width : slot * width + ATM_ROWS])
        parts = [rows_of(4 * slot + q) for q in range(4)] + [rows_of(4 * CAP + slot)]
        values.append(jnp.concatenate(parts, axis=1))
    rest = jnp.concatenate(values, axis=0)
    pieces = []
    for _ in range(3):
        piece = rest.astype(jnp.bfloat16)
        pieces.append(piece)
        rest = rest - piece.astype(F32)
    one = jnp.concatenate(to_rows, axis=0).astype(jnp.bfloat16)
    totals = lax.dot_general(
        jnp.concatenate([one] * 3, axis=0),
        jnp.concatenate(pieces, axis=0),
        (((0,), (0,)), ((), ())),
        preferred_element_type=F32,
    )
    ocean = totals[:, 4 * LANES :]
    cover[...] = ocean
    share = jnp.maximum(ocean, 1.0)
    for q in range(4):
        surface[q] = totals[:, q * LANES : (q + 1) * LANES] / share


def call(kernel, out_shape, limit=VMEM_LIMIT, **kwargs):
    return pl.pallas_call(
        kernel,
        out_shape=out_shape,
        compiler_params=pltpu.CompilerParams(vmem_limit_bytes=limit),
        **kwargs,
    )


def shaped(*shape, dtype=F32):
    return jax.ShapeDtypeStruct(shape, dtype)


def lat_swaps(lon_count, lat_count):
    swap_a, swap_b = [], []
    for i in range(lon_count):
        for a in range(lat_count):
            here = i * lat_count + a
            swap_a.append((here, i * lat_count + (a ^ 1)))
            if a == lat_count - 1:
                swap_b.append((here, (lon_count - 1 - i) * lat_count + a))
            elif a > 0:
                swap_b.append((here, here + 1 if a % 2 else here - 1))
    return swap_a, swap_b


def local(tracers, velocity, land_mask, mixing, owners, atm_row):
    levels = tracers.shape[1]
    rows, cols = land_mask.shape
    fields = 4 * levels
    lon_count, lat_count = lax.axis_size("lon"), lax.axis_size("lat")
    devices = lon_count * lat_count
    assert cols == LANES and rows % 8 == 0 and 2 * fields == LANES
    assert lon_count % 2 == 0 and lat_count % 2 == 0 and 3 * rows <= LANES
    length = 2 * fields + 8
    pitch = rows + 2 * PAD
    flat = 2 * levels * rows
    hbm = pl.BlockSpec(memory_space=pltpu.HBM)
    smem = pl.BlockSpec(memory_space=pltpu.SMEM)
    vmem = pl.BlockSpec(memory_space=pltpu.VMEM)

    deep = (2 * levels, rows, cols)
    lat_a, lat_b = call(
        functools.partial(edge_kernel, rows, fields),
        [pltpu.VMEM((length, cols), F32)] * 2,
        limit=VMEM_ALL,
        in_specs=[hbm] * 4,
        scratch_shapes=[
            pltpu.VMEM((2, fields, 8, cols), F32),
            pltpu.VMEM((rows, cols), jnp.int32),
            pltpu.VMEM((rows, cols), F32),
            pltpu.SemaphoreType.DMA((6,)),
        ],
    )(tracers.reshape(deep), velocity.reshape(deep), land_mask, mixing)
    swap_a, swap_b = lat_swaps(lon_count, lat_count)
    got_lat_b = lax.ppermute(lat_b, ("lon", "lat"), swap_b)
    got_lat_a = lax.ppermute(lat_a, ("lon", "lat"), swap_a)

    tr, ve = tracers.reshape(flat, cols), velocity.reshape(flat, cols)
    msg_a, msg_b = call(
        functools.partial(pack_kernel, rows, fields),
        [shaped(rows + 8, cols)] * 2,
        in_specs=[vmem] * 4,
    )(tr, ve, land_mask, mixing)

    slot_rows = 5 * CAP + 1
    state, base, col_map, row_map, outgoing, ids = call(
        functools.partial(prepare_kernel, rows, levels, devices),
        [
            shaped(fields * rows, cols),
            shaped(2 * rows + pitch, cols),
            shaped(3 * cols, cols),
            shaped(fields + levels, cols),
            shaped(devices * slot_rows, cols),
            shaped(8, cols, dtype=jnp.int32),
        ],
        in_specs=[vmem] * 4 + [smem] * 2,
        scratch_shapes=[pltpu.SMEM((devices,), jnp.int32)],
    )(tr, ve, land_mask, mixing, owners.reshape(rows), atm_row)

    def full(n):
        return pl.BlockSpec((n, cols), lambda i: (0, 0))

    tail = pl.BlockSpec((8, cols), lambda i: (rows // 8, 0))
    north, south, msg_a, msg_b = call(
        functools.partial(corner_kernel, lat_count, fields),
        [shaped(length, cols)] * 2 + [shaped(rows + 8, cols)] * 2,
        grid=(1,),
        in_specs=[full(length), full(length), tail, tail],
        out_specs=[full(length), full(length), tail, tail],
        input_output_aliases={2: 2, 3: 3},
    )(got_lat_b, got_lat_a, msg_a, msg_b)
    even_pairs = [(i, i ^ 1) for i in range(lon_count)]
    odd_pairs = [(i, (i + 1 if i % 2 else i - 1) % lon_count) for i in range(lon_count)]
    got_b = lax.ppermute(msg_b, "lon", even_pairs)
    got_a = lax.ppermute(msg_a, "lon", odd_pairs)

    count = min(3, levels)
    inner, part = call(
        functools.partial(inside_kernel, rows, levels),
        [shaped(len(COEFFICIENTS) * rows, cols), shaped(4 * (count - 1) * rows, cols)],
        scratch_shapes=[
            pltpu.VMEM((4 * count * pitch, cols), F32),
            pltpu.VMEM((pitch, cols), F32),
        ],
    )(state, base, north, south)
    coefs, side, outgoing = call(
        functools.partial(surface_kernel, rows, levels),
        [
            shaped(len(COEFFICIENTS) * rows, cols),
            shaped(rows, cols),
            pltpu.VMEM((devices * slot_rows, cols), F32),
        ],
        scratch_shapes=[
            pltpu.VMEM((4 * (count - 1) * pitch, cols), F32),
            pltpu.VMEM((4 * rows, cols), F32),
            pltpu.SMEM((8, cols), jnp.int32),
            pltpu.SemaphoreType.DMA,
        ],
    )(state, base, inner, part, msg_a, msg_b, got_b, got_a, north, south, outgoing, ids)
    incoming = lax.all_to_all(
        outgoing.reshape(devices, slot_rows, 1, cols),
        ("lon", "lat"),
        0,
        0,
        axis_index_groups=[list(range(devices))[::-1]],
        tiled=True,
    ).reshape(devices * slot_rows, cols)

    chunks = 4
    tr_out, ve_out = call(
        functools.partial(main_kernel, rows, levels, chunks),
        [shaped(flat, cols), shaped(flat, cols)],
        in_specs=[vmem] * 12,
        out_specs=[hbm] * 2,
        scratch_shapes=[
            pltpu.VMEM((fields * pitch, cols), F32),
            pltpu.VMEM((fields * pitch, cols), F32),
            pltpu.VMEM((rows, cols), F32),
            pltpu.VMEM((flat, cols), F32),
            pltpu.VMEM((flat, cols), F32),
            pltpu.SemaphoreType.DMA((4 * chunks,)),
        ],
        cost_estimate=pl.CostEstimate(
            flops=80 * fields * rows * cols, bytes_accessed=5 << 20, transcendentals=0
        ),
    )(state, base, msg_a, msg_b, got_a, got_b, north, south, col_map, row_map, coefs, side)
    surface, cover = call(
        functools.partial(reduce_kernel, devices),
        [shaped(4, ATM_ROWS, cols), shaped(ATM_ROWS, cols)],
    )(incoming)
    shape = (2, levels, rows, cols)
    return tr_out.reshape(shape), ve_out.reshape(shape), surface, cover


def solution(mesh):
    in_specs = (
        P(None, None, "lat", "lon"),
        P(None, None, "lat", "lon"),
        P("lat", "lon"),
        P("lat", "lon"),
        P(("lon", "lat"), None),
        P(("lon", "lat")),
    )
    out_specs = (
        P(None, None, "lat", "lon"),
        P(None, None, "lat", "lon"),
        P(None, ("lon", "lat"), None),
        P(("lon", "lat"), None),
    )
    return jax.shard_map(local, mesh=mesh, in_specs=in_specs, out_specs=out_specs, check_vma=False)
```

```python
import functools
import math

import jax
import jax.numpy as jnp
from jax import lax
from jax.experimental import pallas as pl
from jax.experimental.pallas import tpu as pltpu
from jax.sharding import PartitionSpec as P

ATM_ROWS = 32
CAP = 2

THERMAL = 0.2
HALINE = 0.15
GRAVITY = 0.2
TIMESTEP = 0.8
VERTICAL_MIX = 0.1
VISCOSITY = 0.2
CORIOLIS_MAX = 0.3

LANES = 128
PAD = 8
EXACT = lax.Precision.HIGHEST
F32 = jnp.float32
VMEM_LIMIT = 32 * 1024 * 1024
VMEM_ALL = 62 * 1024 * 1024


def iota(shape, dim):
    return lax.broadcasted_iota(jnp.int32, shape, dim)


def dot(a, b, dims=(((1,), (0,)), ((), ()))):
    return lax.dot_general(a, b, dims, precision=EXACT, preferred_element_type=F32)


def exact_parts(x):
    parts = []
    for _ in range(3):
        parts.append(x.astype(jnp.bfloat16))
        x = x - parts[-1].astype(F32)
    return parts


def is_even(axis):
    return lax.rem(lax.axis_index(axis), 2) == 0


def start_copies(pairs, sems):
    copies = [pltpu.make_async_copy(src, dst, sems.at[i]) for i, (src, dst) in enumerate(pairs)]
    for copy in copies:
        copy.start()
    return copies


def edge_kernel(rows, fields, tr_hbm, ve_hbm, mask_hbm, mix_hbm, lat_a, lat_b, edges, mask, mix, sems):
    half = fields // 2
    pairs = [(mask_hbm, mask), (mix_hbm, mix)]
    for n, src in enumerate((tr_hbm, ve_hbm)):
        for side, first in enumerate((0, rows - 8)):
            part = edges.at[side, n * half : (n + 1) * half]
            pairs.append((src.at[:, first : first + 8, :], part))
    for copy in start_copies(pairs, sems):
        copy.wait()
    flat = edges.reshape(2 * fields * 8, LANES)
    even = is_even("lat")
    top = ((rows - 1, 8 * fields + 7), (rows - 2, 8 * fields + 6))
    bottom = ((0, 0), (1, 1))
    for buf, first, second in ((lat_a, top, bottom), (lat_b, bottom, top)):
        (near, near_at), (far, far_at) = [
            [jnp.where(even, x, y) for x, y in zip(one, other)] for one, other in zip(first, second)
        ]
        wet_near = mask[pl.ds(near, 1), :].astype(F32)
        wet_far = mask[pl.ds(far, 1), :].astype(F32)
        buf[0:fields, :] = flat[pl.ds(near_at, fields, stride=8), :] * wet_near
        buf[fields : 2 * fields, :] = flat[pl.ds(far_at, fields, stride=8), :] * wet_far
        buf[2 * fields : 2 * fields + 8, :] = jnp.zeros((8, LANES), F32)
        buf[2 * fields : 2 * fields + 1, :] = wet_near
        buf[2 * fields + 1 : 2 * fields + 2, :] = wet_far
        buf[2 * fields + 2 : 2 * fields + 3, :] = mix[pl.ds(near, 1), :]


def pack_kernel(rows, fields, tr, ve, mask, mix, msg_a, msg_b):
    half = fields // 2
    wet = mask[...].astype(F32)
    lane = iota((rows, LANES), 1)
    pair = lane >> 1

    def columns(ref, base):
        def body(f, carry):
            to_east, to_west = carry
            x = ref[pl.ds(pl.multiple_of(f * rows, rows), rows), :]
            keep = pair == base + f
            low = 2 * (base + f)
            to_east = jnp.where(keep, pltpu.roll(x, (low + 2) & (LANES - 1), 1), to_east)
            to_west = jnp.where(keep, pltpu.roll(x, low, 1), to_west)
            return to_east, to_west

        return body

    carry = (jnp.zeros((rows, LANES), F32), jnp.zeros((rows, LANES), F32))
    for ref, base in ((tr, 0), (ve, half)):
        carry = lax.fori_loop(0, half, columns(ref, base), carry, unroll=8)
    def spread(x, i):
        return jnp.broadcast_to(x[:, i : i + 1], (rows, LANES))

    odd = (lane & 1) == 1
    to_east = carry[0] * jnp.where(odd, spread(wet, LANES - 1), spread(wet, LANES - 2))
    to_west = carry[1] * jnp.where(odd, spread(wet, 1), spread(wet, 0))
    even = is_even("lon")
    row = iota((rows, LANES), 0)
    mixing = mix[...]
    lines = []
    for near, far in ((LANES - 1, LANES - 2), (0, 1)):
        line = jnp.zeros((rows, LANES), F32)
        for part, column in enumerate((wet[:, near], wet[:, far], mixing[:, near])):
            line = jnp.where(lane == part * rows + row, column[:, None], line)
        lines.append(jnp.sum(line, axis=0, keepdims=True))
    for msg, flag in ((msg_a, jnp.logical_not(even)), (msg_b, even)):
        msg[0:rows, :] = jnp.where(flag, to_east, to_west)
        msg[rows:, :] = jnp.zeros((8, LANES), F32)
        msg[rows + 4 : rows + 5, :] = jnp.where(flag, *lines)


def prepare_kernel(
    rows, levels, devices, tr, ve, mask, mix, own, atm_row,
    state, base, col_map, row_map, out, ids, used,
):
    fields = 4 * levels
    half = fields // 2
    wet = mask[...].astype(F32)
    base[0:rows, :] = wet
    base[rows : 2 * rows, :] = mix[...]
    for ref, first in ((tr, 0), (ve, half)):

        def fill(f, carry, ref=ref, first=first):
            x = ref[pl.ds(pl.multiple_of(f * rows, 8), rows), :] * wet
            state[pl.ds(pl.multiple_of((first + f) * rows, 8), rows), :] = x
            return carry

        lax.fori_loop(0, half, fill, 0, unroll=8)

    total = lax.axis_size("lat") * rows
    latitude = lax.axis_index("lat") * rows - PAD + iota((rows + 2 * PAD, LANES), 0)
    latitude = jnp.where(latitude >= total, 2 * total - 1 - latitude, latitude).astype(F32)
    table = CORIOLIS_MAX * jnp.sin(math.pi * (-0.43 + 0.93 * (latitude + 0.5) / total))
    base[2 * rows :, :] = table

    span = 2 * levels
    src, dst = iota((LANES, LANES), 0), iota((LANES, LANES), 1)
    src_group, dst_group = src // span, dst // span
    src_level, dst_level = (src // 2) % levels, (dst // 2) % levels
    same_side = (src & 1) == (dst & 1)
    mixes = VERTICAL_MIX * level_matrix("mix", levels, src_level, dst_level)
    press = level_matrix("pressure", levels, src_level, dst_level) * density_weight(src_group)
    col_map[0:LANES, :] = jnp.where(same_side & (src_group == dst_group), mixes, 0.0)
    col_map[LANES : 2 * LANES, :] = jnp.where(same_side & (dst_group == 2), -press, 0.0)
    col_map[2 * LANES :, :] = jnp.where(same_side & (dst_group == 3), -press, 0.0)

    dst, src = iota((fields, fields), 0), iota((fields, fields), 1)
    mixes = VERTICAL_MIX * level_matrix("mix", levels, src % levels, dst % levels)
    row_map[0:fields, 0:fields] = jnp.where(dst // levels == src // levels, mixes, 0.0)
    dst, src = iota((levels, fields), 0), iota((levels, fields), 1)
    press = level_matrix("pressure", levels, src % levels, dst) * density_weight(src // levels)
    row_map[fields:, 0:fields] = press

    slot_rows = out.shape[0] // devices

    def clear(d, carry):
        used[d] = 0
        return carry

    lax.fori_loop(0, devices, clear, 0, unroll=8)
    out[...] = jnp.zeros(out.shape, F32)
    lane1 = iota((1, LANES), 1)
    places = jnp.zeros((1, LANES), jnp.int32)
    for r in range(rows):
        owner = own[r]
        slot = used[owner]
        used[owner] = slot + 1
        start = (devices - 1 - owner) * slot_rows
        places = jnp.where(lane1 % rows == r, start + 4 * slot, places)
        out[pl.ds(start + 4 * CAP + slot, 1), :] = base[r : r + 1, :]
        line = out[pl.ds(start + 5 * CAP, 1), :]
        target = jnp.full((1, LANES), atm_row[r], jnp.int32).astype(F32)
        out[pl.ds(start + 5 * CAP, 1), :] = jnp.where(lane1 // (LANES // CAP) == slot, target, line)
    ids[...] = jnp.zeros(ids.shape, jnp.int32)
    ids[0:1, :] = places + lane1 // rows


def corner_kernel(lat_count, fields, got_b, got_a, tail_a, tail_b, north, south, new_a, new_b):
    fold = lax.axis_index("lat") == lat_count - 1
    even = is_even("lat")
    a, b = got_a[...], got_b[...]
    straight = jnp.where(even, a, b)
    south[...] = jnp.where(even, b, a)
    back = LANES - 1 - iota((8, LANES), 1)
    flipped = jnp.concatenate(
        [
            jnp.take_along_axis(straight[i : i + 8], back, axis=1)
            * (-1.0 if i < 2 * fields and i % fields >= fields // 2 else 1.0)
            for i in range(0, straight.shape[0], 8)
        ],
        axis=0,
    )
    north[...] = jnp.where(fold, flipped, straight)
    lane, field = iota((fields, LANES), 1), iota((fields, LANES), 0)
    lane1 = iota((1, LANES), 1)
    for old, new in ((tail_a, new_a), (tail_b, new_b)):
        new[...] = old[...]
    for i, ref in enumerate((north, south)):
        near = ref[0:fields, :]
        ends = jnp.where(
            lane == 2 * field, near[:, 0:1], jnp.where(lane == 2 * field + 1, near[:, LANES - 1 :], 0.0)
        )
        corner = jnp.sum(ends, axis=0, keepdims=True)
        wet = ref[2 * fields : 2 * fields + 1, :]
        wet = jnp.where(lane1 == 0, wet[:, 0:1], wet[:, LANES - 1 :])
        for new in (new_a, new_b):
            new[i : i + 1, :] = corner
            new[2 + i : 3 + i, :] = wet


class Sides:
    def __init__(self, rows, got_a, got_b, msg_a, msg_b):
        lane, row = iota((rows, LANES), 1), iota((rows, LANES), 0)
        self.even = (lane & 1) == 0
        self.even1 = (iota((1, LANES), 1) & 1) == 0
        even = is_even("lon")

        def ordered(a, b, place):
            return jnp.where(even, b[place, :], a[place, :]), jnp.where(even, a[place, :], b[place, :])

        self.got = ordered(got_a, got_b, slice(0, rows))
        self.mine = ordered(msg_a, msg_b, slice(0, rows))
        self.extras = ordered(got_a, got_b, slice(rows, rows + 8))
        self.columns = [
            [
                jnp.sum(jnp.where(lane == i * rows + row, x[4:5], 0.0), axis=1, keepdims=True)
                for i in range(3)
            ]
            for x in self.extras
        ]

    def near(self):
        return jnp.where(self.even, *self.got)

    def far_and_inner(self):
        east, west = self.got
        mine_e, mine_w = self.mine
        far = jnp.where(self.even, pltpu.roll(east, LANES - 1, 1), pltpu.roll(west, 1, 1))
        inner = jnp.where(self.even, pltpu.roll(mine_e, LANES - 1, 1), pltpu.roll(mine_w, 1, 1))
        return far, inner

    def corner(self, i):
        east, west = self.extras
        wets = east[2 + i : 3 + i, 0:1], west[2 + i : 3 + i, 1:2]
        return jnp.where(self.even1, east[i : i + 1], west[i : i + 1]), *wets

    def lanes(self, i):
        return jnp.where(self.even, self.columns[0][i], self.columns[1][i])


def level_matrix(kind, levels, source, target):
    if kind == "mix":
        above = (source == jnp.maximum(target - 1, 0)).astype(F32)
        below = (source == jnp.minimum(target + 1, levels - 1)).astype(F32)
        return above + below - 2.0 * (source == target).astype(F32)
    full = jnp.where(source < target, 1.0, jnp.where(source == target, 0.5, 0.0))
    return (0.5 * GRAVITY) * full


def density_weight(group):
    return jnp.where(group == 0, -THERMAL, jnp.where(group == 1, HALINE, 0.0)).astype(F32)


def advance_columns(sides, wet, coriolis, level_map):
    rows = wet.shape[0]
    mid = sides.near()
    outer, inner = sides.far_and_inner()
    (corner_n, wet_ne, wet_nw), (corner_s, wet_se, wet_sw) = sides.corner(0), sides.corner(1)
    wet_mid, wet_out = sides.lanes(0), sides.lanes(1)
    wet_in = jnp.where(sides.even, wet[:, LANES - 1 :], wet[:, 0:1])
    wet_corner_n = jnp.where(sides.even1, wet_ne, wet_nw)
    wet_corner_s = jnp.where(sides.even1, wet_se, wet_sw)
    mixing = sides.lanes(2)
    lane = iota((rows, LANES), 1)
    row = iota((rows, LANES), 0)
    span = LANES // 4
    group = lane // span

    def ends(outside, inside):
        return jnp.where(sides.even, outside, inside), jnp.where(sides.even, inside, outside)

    def shifted(x, north, south):
        n = jnp.where(row == rows - 1, north, pltpu.roll(x, rows - 1, 0))
        s = jnp.where(row == 0, south, pltpu.roll(x, 1, 0))
        return n, s

    e, w = ends(outer, inner)
    wet_e, wet_w = ends(wet_out, wet_in)
    n, s = shifted(mid, corner_n, corner_s)
    wet_n, wet_s = shifted(wet_mid, wet_corner_n, wet_corner_s)
    lap = wet_e * (e - mid) + wet_w * (w - mid) + wet_n * (n - mid) + wet_s * (s - mid)
    de, dn = e - w, n - s
    one, two, three = (pltpu.roll(mid, i * span, 1) for i in (1, 2, 3))

    def pick(a, b, c, d):
        return jnp.where(group == 0, a, jnp.where(group == 1, b, jnp.where(group == 2, c, d)))

    u = pick(two, three, mid, one)
    v = pick(one, two, three, mid)
    adv = 0.5 * (u * de + v * dn)
    zero = jnp.zeros_like(mid)
    if level_map is None:
        grad_x = HALINE * pltpu.roll(de, span, 1) - THERMAL * pltpu.roll(de, 2 * span, 1)
        grad_y = HALINE * pltpu.roll(dn, 2 * span, 1) - THERMAL * pltpu.roll(dn, 3 * span, 1)
        linear = VERTICAL_MIX * (pltpu.roll(mid, LANES - 2, 1) - mid)
        linear = linear - (0.25 * GRAVITY) * pick(zero, zero, grad_x, grad_y)
    else:
        linear = dot(jnp.concatenate([mid, de, dn], axis=1), level_map)
    turn = pick(zero, zero, coriolis * v, -coriolis * u)
    kappa = jnp.where(group < 2, mixing, VISCOSITY)
    tend = turn - adv + kappa * lap + linear
    return wet_mid * (mid + TIMESTEP * tend)


def advance_rows(levels, parts, level_map):
    fields = 4 * levels
    lane = iota((fields, LANES), 1)
    lane8 = iota((8, LANES), 1)

    def sides(x, east, west, at):
        e = jnp.where(at == LANES - 1, east, pltpu.roll(x, LANES - 1, 1))
        w = jnp.where(at == 0, west, pltpu.roll(x, 1, 1))
        return e, w

    mids, gaps = [], []
    for mid, n, s, (corner_e, corner_w), *_ in parts:
        e, w = sides(mid, corner_e, corner_w, lane)
        mids.append((mid, e, w, n, s))
        gaps += [e - w, n - s]
    vertical = dot(level_map[0:fields, 0:fields], jnp.concatenate([m[0] for m in mids], axis=1))
    grads = dot(level_map[fields:, 0:fields], jnp.concatenate(gaps, axis=1))
    done = []
    for i, (mid, e, w, n, s) in enumerate(mids):
        *_, wets, mixing, coriolis = parts[i]
        wet_mid, wet_n, wet_s, wet_corner_e, wet_corner_w = wets
        wet_e, wet_w = sides(
            jnp.broadcast_to(wet_mid, (8, LANES)), wet_corner_e, wet_corner_w, lane8
        )
        lap = wet_e[0:1] * (e - mid) + wet_w[0:1] * (w - mid)
        lap = lap + wet_n * (n - mid) + wet_s * (s - mid)
        de, dn = gaps[2 * i], gaps[2 * i + 1]
        u, v = mid[2 * levels : 3 * levels], mid[3 * levels :]
        adv = jnp.concatenate([u] * 4, axis=0) * de + jnp.concatenate([v] * 4, axis=0) * dn
        grad_x = grads[:, 2 * i * LANES : (2 * i + 1) * LANES]
        grad_y = grads[:, (2 * i + 1) * LANES : (2 * i + 2) * LANES]
        zero = jnp.zeros((2 * levels, LANES), F32)
        turn = jnp.concatenate([zero, coriolis * v - grad_x, -coriolis * u - grad_y], axis=0)
        kappa = jnp.concatenate(
            [jnp.broadcast_to(mixing, (2 * levels, LANES)), jnp.full(zero.shape, VISCOSITY)],
            axis=0,
        )
        tend = turn - 0.5 * adv + kappa * lap + vertical[:, i * LANES : (i + 1) * LANES]
        done.append(wet_mid * (mid + TIMESTEP * tend))
    return done


COEFFICIENTS = ("te", "tw", "tn", "ts", "tc", "ve", "vw", "vn", "vs", "vc", "adv", "mix", "turn")


def place_of(name, rows):
    i = COEFFICIENTS.index(name)
    return slice(i * rows, (i + 1) * rows)


def coefficients(wet, neighbours, mixing, coriolis):
    made = {}
    for name, kappa in (("t", mixing), ("v", VISCOSITY)):
        rest = wet * (1.0 - 2.0 * TIMESTEP * VERTICAL_MIX)
        for side, wet_n in zip("ewns", neighbours):
            made[name + side] = TIMESTEP * kappa * wet * wet_n
            rest = rest - made[name + side]
        made[name + "c"] = rest
    made["adv"] = (0.5 * TIMESTEP) * wet
    made["mix"] = (TIMESTEP * VERTICAL_MIX) * wet
    made["turn"] = TIMESTEP * coriolis * wet
    return made


def advance_level(k, count, levels, rows, src, sides, coef, acc):
    pitch = rows + 2 * PAD
    lane = iota((rows, LANES), 1)
    first, last = lane == 0, lane == LANES - 1
    above_k = jnp.maximum(k - 1, 0)
    below_k = jnp.minimum(k + 1, levels - 1)

    def load(q, level, shift):
        return src[pl.ds((q * count + level) * pitch + PAD + shift, rows), :]

    def base(q):
        return pl.multiple_of((q * count + k) * pitch + PAD, 8)

    center = [load(q, k, 0) for q in range(4)]
    u, v = coef("adv") * center[2], coef("adv") * center[3]
    sums, de, dn = [], [], []
    for q in range(4):
        c = center[q]
        n, s = load(q, k, 1), load(q, k, -1)
        edge = pltpu.roll(sides, (LANES - 1 - 2 * (q * levels + k)) & (LANES - 1), 1)
        e = jnp.where(last, edge, pltpu.roll(c, LANES - 1, 1))
        w = jnp.where(first, edge, pltpu.roll(c, 1, 1))
        kind = "t" if q < 2 else "v"
        lap = coef(kind + "c") * c + coef(kind + "e") * e + coef(kind + "w") * w
        lap = lap + coef(kind + "n") * n + coef(kind + "s") * s
        de.append(e - w)
        dn.append(n - s)
        sums.append(lap - (u * de[q] + v * dn[q]))
    scale = 0.5 * GRAVITY / VERTICAL_MIX
    dens_x = (scale * HALINE) * de[1] - (scale * THERMAL) * de[0]
    dens_y = (scale * HALINE) * dn[1] - (scale * THERMAL) * dn[0]
    acc_x, acc_y = acc
    grad = (None, None, acc_x + 0.5 * dens_x, acc_y + 0.5 * dens_y)
    turn = (None, None, coef("turn") * center[3], -coef("turn") * center[2])
    new = []
    for q in range(4):
        vertical = load(q, above_k, 0) + load(q, below_k, 0)
        if grad[q] is not None:
            vertical = vertical - grad[q]
        total = sums[q] + coef("mix") * vertical
        new.append(total if turn[q] is None else total + turn[q])
    return new, (acc_x + dens_x, acc_y + dens_y)


def advance_top_rows(levels, sides, north, south, state, wet, rows, table):
    fields = 4 * levels

    def both(a, b):
        return jnp.concatenate([a, b], axis=0)

    def rows_at(first):
        return both(
            north[pl.ds(first, 4, stride=levels), :], south[pl.ds(first, 4, stride=levels), :]
        )

    lane, row = iota((8, LANES), 1), iota((8, LANES), 0)
    upper = row < 4
    field = row & 3
    inside_n = state[pl.ds(rows - 1, 4, stride=levels * rows), :]
    inside_s = state[pl.ds(0, 4, stride=levels * rows), :]
    mid, below, outer = rows_at(0), rows_at(1), rows_at(fields)
    n = both(outer[0:4], inside_s)
    s = both(inside_n, outer[4:8])
    (corner_n, wet_ne, wet_nw), (corner_s, wet_se, wet_sw) = sides.corner(0), sides.corner(1)
    corner = jnp.where(upper, corner_n, corner_s)
    at = 2 * levels * field

    def end(parity):
        return jnp.sum(jnp.where(lane == at + parity, corner, 0.0), axis=1, keepdims=True)

    def west_east(x, east, west):
        return (
            jnp.where(lane == LANES - 1, east, pltpu.roll(x, LANES - 1, 1)),
            jnp.where(lane == 0, west, pltpu.roll(x, 1, 1)),
        )

    def tail(i):
        place = slice(2 * fields + i, 2 * fields + i + 1)
        return north[place, :], south[place, :]

    e, w = west_east(mid, end(0), end(1))
    wet_mid = jnp.where(upper, *tail(0))
    wet_e, wet_w = west_east(
        wet_mid, jnp.where(upper, wet_ne, wet_se), jnp.where(upper, wet_nw, wet_sw)
    )
    out_n, out_s = tail(1)
    wet_n = jnp.where(upper, out_n, wet[0:1])
    wet_s = jnp.where(upper, wet[rows - 1 : rows], out_s)
    lap = wet_e * (e - mid) + wet_w * (w - mid) + wet_n * (n - mid) + wet_s * (s - mid)
    de, dn = e - w, n - s

    def of(x, i):
        return jnp.where(upper, x[i : i + 1], x[4 + i : 5 + i])

    u, v = of(mid, 2), of(mid, 3)
    coriolis = jnp.where(upper, table[PAD + rows : PAD + rows + 1], table[PAD - 1 : PAD])
    grad_x = (0.25 * GRAVITY) * (HALINE * of(de, 1) - THERMAL * of(de, 0))
    grad_y = (0.25 * GRAVITY) * (HALINE * of(dn, 1) - THERMAL * of(dn, 0))
    turn = jnp.where(
        field < 2, 0.0, jnp.where(field == 2, coriolis * v - grad_x, -coriolis * u - grad_y)
    )
    kappa = jnp.where(field < 2, jnp.where(upper, *tail(2)), VISCOSITY)
    tend = turn - 0.5 * (u * de + v * dn) + kappa * lap + VERTICAL_MIX * (below - mid)
    return wet_mid * (mid + TIMESTEP * tend)


def surface_kernel(
    rows, levels,
    state, base, msg_a, msg_b, got_a, got_b, north, south, out_in, ids,
    coef, side, out, now, later, wet_pad,
):
    fields = 4 * levels
    pitch = rows + 2 * PAD
    wet = base[0:rows, :]
    mixing = base[rows : 2 * rows, :]
    table = base[2 * rows :, :]
    coriolis = table[PAD : PAD + rows]
    lane = iota((rows, LANES), 1)
    sides = Sides(rows, got_a, got_b, msg_a, msg_b)
    wet_pad[PAD : PAD + rows, :] = wet
    wet_pad[PAD - 1 : PAD, :] = south[2 * fields : 2 * fields + 1, :]
    wet_pad[PAD + rows : PAD + rows + 1, :] = north[2 * fields : 2 * fields + 1, :]
    wet_n = wet_pad[PAD + 1 : PAD + 1 + rows, :]
    wet_s = wet_pad[PAD - 1 : PAD - 1 + rows, :]
    wet_e = jnp.where(lane == LANES - 1, sides.columns[0][0], pltpu.roll(wet, LANES - 1, 1))
    wet_w = jnp.where(lane == 0, sides.columns[1][0], pltpu.roll(wet, 1, 1))
    made = coefficients(wet, (wet_e, wet_w, wet_n, wet_s), mixing, coriolis)
    for name in COEFFICIENTS:
        coef[place_of(name, rows)] = made[name]
    near = sides.near()
    side[...] = near

    count = now.shape[0] // (4 * pitch)
    for q in range(4):
        for k in range(count):
            field = (q * levels + k) * rows
            at = (q * count + k) * pitch + PAD
            now[at : at + rows, :] = state[field : field + rows, :]
            now[at + rows : at + rows + 1, :] = north[q * levels + k : q * levels + k + 1, :]
            now[at - 1 : at, :] = south[q * levels + k : q * levels + k + 1, :]

    def read(name):
        return coef[place_of(name, rows)]

    none = jnp.zeros((rows, LANES), F32)
    acc = (none, none)
    edge_rows = advance_top_rows(levels, sides, north, south, state, wet, rows, table)
    edge_cols = advance_columns(sides, wet, coriolis, None)
    for k in range(count - 1):
        new, acc = advance_level(k, count, levels, rows, now, near, read, acc)
        for q in range(4):
            at = (q * count + k) * pitch + PAD
            later[at : at + rows, :] = new[q]
            if k == 0:
                later[at + rows : at + rows + 1, :] = edge_rows[q : q + 1]
                later[at - 1 : at, :] = edge_rows[4 + q : 5 + q]
    new, _ = advance_level(0, count, levels, rows, later, edge_cols, read, (none, none))
    length = out.shape[0]
    here = (iota((length, LANES), 0) == ids[0:1, :]).astype(F32).astype(jnp.bfloat16)
    out[...] = out_in[...] + jnp.dot(
        jnp.concatenate([here] * 3, axis=1),
        jnp.concatenate(exact_parts(jnp.concatenate(new, axis=0)), axis=0),
        preferred_element_type=F32,
    )


def halo_after_first(rows, levels, sides, north, south, state, wet, table, col_map, row_map):
    fields = 4 * levels
    side_new = advance_columns(sides, wet, table[PAD : PAD + rows], col_map)
    lane, field = iota((fields, LANES), 1), iota((fields, LANES), 0)

    def to_sublanes(x, parity):
        here = lane == 2 * field + parity
        return jnp.sum(jnp.where(here, x, 0.0), axis=1, keepdims=True)

    parts = []
    for north_side, ref, line, lat_row in (
        (True, north, rows - 1, PAD + rows),
        (False, south, 0, PAD - 1),
    ):
        corner, *corner_wets = sides.corner(0 if north_side else 1)
        inside = state[pl.ds(line, fields, stride=rows), :]
        tail = ref[2 * fields :, :]
        pair = (ref[fields : 2 * fields, :], inside), (tail[1:2], wet[line : line + 1])
        (n, s), (wet_n, wet_s) = pair if north_side else [x[::-1] for x in pair]
        parts.append(
            (
                ref[0:fields, :], n, s, (to_sublanes(corner, 0), to_sublanes(corner, 1)),
                (tail[0:1], wet_n, wet_s, *corner_wets),
                tail[2:3], table[lat_row : lat_row + 1],
            )
        )
    return side_new, *advance_rows(levels, parts, row_map)


def main_kernel(
    rows, levels, chunks,
    state, base, msg_a, msg_b, got_a, got_b, north, south, col_map, row_map, coefs, side,
    tr_hbm, ve_hbm, now, later, side_new, tr_out, ve_out, sems,
):
    fields = 4 * levels
    pitch = rows + 2 * PAD
    sides = Sides(rows, got_a, got_b, msg_a, msg_b)
    side_new[...], north_new, south_new = halo_after_first(
        rows, levels, sides, north, south, state, base[0:rows, :], base[2 * rows :, :],
        col_map[...], row_map[...],
    )
    edges = (now, north[0:fields, :], south[0:fields, :]), (later, north_new, south_new)
    for buf, n, s in edges:
        buf[pl.ds(PAD - 1, fields, stride=pitch), :] = s
        buf[pl.ds(PAD + rows, fields, stride=pitch), :] = n

    def fill(f, carry):
        x = state[pl.ds(pl.multiple_of(f * rows, 8), rows), :]
        now[pl.ds(pl.multiple_of(f * pitch + PAD, 8), rows), :] = x
        return carry

    lax.fori_loop(0, fields, fill, 0, unroll=8)

    def coef(name):
        return coefs[place_of(name, rows)]

    def first(k, acc):
        new, acc = advance_level(k, levels, levels, rows, now, side[...], coef, acc)
        for q in range(4):
            place = pl.multiple_of((q * levels + k) * pitch + PAD, 8)
            later[pl.ds(place, rows), :] = new[q]
        return acc

    def second(k, acc):
        new, acc = advance_level(k, levels, levels, rows, later, side_new[...], coef, acc)
        for q in range(4):
            ref = tr_out if q < 2 else ve_out
            place = pl.multiple_of(((q % 2) * levels + k) * rows, 8)
            ref[pl.ds(place, rows), :] = new[q]
        return acc

    none = jnp.zeros((rows, LANES), F32)
    lax.fori_loop(0, levels, first, (none, none), unroll=2)
    acc = (none, none)
    size = levels // chunks
    copies = []
    for i in range(chunks):
        acc = lax.fori_loop(i * size, (i + 1) * size, second, acc, unroll=2)
        for src, dst in ((tr_out, tr_hbm), (ve_out, ve_hbm)):
            for q in range(2):
                start = (q * levels + i * size) * rows
                part = slice(start, start + size * rows)
                copy = pltpu.make_async_copy(src.at[part], dst.at[part], sems.at[len(copies)])
                copy.start()
                copies.append(copy)
    for copy in copies:
        copy.wait()


def reduce_kernel(devices, data, surface, cover):
    slot_rows = data.shape[0] // devices

    def rows_of(i):
        return data[pl.ds(i, devices, stride=slot_rows), :]

    width = LANES // CAP
    lines = rows_of(5 * CAP)
    named = (lines == (iota((devices, LANES), 1) % width).astype(F32)).astype(F32)
    to_rows, values = [], []
    for slot in range(CAP):
        to_rows.append(named[:, slot * width : slot * width + ATM_ROWS])
        parts = [rows_of(4 * slot + q) for q in range(4)] + [rows_of(4 * CAP + slot)]
        values.append(jnp.concatenate(parts, axis=1))
    rest = jnp.concatenate(values, axis=0)
    pieces = exact_parts(rest)
    one = jnp.concatenate(to_rows, axis=0).astype(jnp.bfloat16)
    totals = lax.dot_general(
        jnp.concatenate([one] * 3, axis=0),
        jnp.concatenate(pieces, axis=0),
        (((0,), (0,)), ((), ())),
        preferred_element_type=F32,
    )
    ocean = totals[:, 4 * LANES :]
    cover[...] = ocean
    share = jnp.maximum(ocean, 1.0)
    for q in range(4):
        surface[q] = totals[:, q * LANES : (q + 1) * LANES] / share


def call(kernel, out_shape, limit=VMEM_LIMIT, **kwargs):
    return pl.pallas_call(
        kernel,
        out_shape=out_shape,
        compiler_params=pltpu.CompilerParams(vmem_limit_bytes=limit),
        **kwargs,
    )


def shaped(*shape, dtype=F32):
    return jax.ShapeDtypeStruct(shape, dtype)


def lat_swaps(lon_count, lat_count):
    swap_a, swap_b = [], []
    for i in range(lon_count):
        for a in range(lat_count):
            here = i * lat_count + a
            swap_a.append((here, i * lat_count + (a ^ 1)))
            if a == lat_count - 1:
                swap_b.append((here, (lon_count - 1 - i) * lat_count + a))
            elif a > 0:
                swap_b.append((here, here + 1 if a % 2 else here - 1))
    return swap_a, swap_b


def local(tracers, velocity, land_mask, mixing, owners, atm_row):
    levels = tracers.shape[1]
    rows, cols = land_mask.shape
    fields = 4 * levels
    lon_count, lat_count = lax.axis_size("lon"), lax.axis_size("lat")
    devices = lon_count * lat_count
    assert cols == LANES and 4 * rows == LANES and 2 * fields == LANES
    assert lon_count % 2 == 0 and lat_count % 2 == 0 and 3 * rows <= LANES
    length = 2 * fields + 8
    pitch = rows + 2 * PAD
    flat = 2 * levels * rows
    hbm = pl.BlockSpec(memory_space=pltpu.HBM)
    smem = pl.BlockSpec(memory_space=pltpu.SMEM)
    vmem = pl.BlockSpec(memory_space=pltpu.VMEM)

    deep = (2 * levels, rows, cols)
    lat_a, lat_b = call(
        functools.partial(edge_kernel, rows, fields),
        [pltpu.VMEM((length, cols), F32)] * 2,
        limit=VMEM_ALL,
        in_specs=[hbm] * 4,
        scratch_shapes=[
            pltpu.VMEM((2, fields, 8, cols), F32),
            pltpu.VMEM((rows, cols), jnp.int32),
            pltpu.VMEM((rows, cols), F32),
            pltpu.SemaphoreType.DMA((6,)),
        ],
    )(tracers.reshape(deep), velocity.reshape(deep), land_mask, mixing)
    swap_a, swap_b = lat_swaps(lon_count, lat_count)
    got_lat_b = lax.ppermute(lat_b, ("lon", "lat"), swap_b)
    got_lat_a = lax.ppermute(lat_a, ("lon", "lat"), swap_a)

    tr, ve = tracers.reshape(flat, cols), velocity.reshape(flat, cols)
    msg_a, msg_b = call(
        functools.partial(pack_kernel, rows, fields),
        [shaped(rows + 8, cols)] * 2,
        in_specs=[vmem] * 4,
    )(tr, ve, land_mask, mixing)

    slot_rows = 5 * CAP + 1
    state, base, col_map, row_map, outgoing, ids = call(
        functools.partial(prepare_kernel, rows, levels, devices),
        [
            shaped(fields * rows, cols),
            shaped(2 * rows + pitch, cols),
            shaped(3 * cols, cols),
            shaped(fields + levels, cols),
            shaped(devices * slot_rows, cols),
            shaped(8, cols, dtype=jnp.int32),
        ],
        in_specs=[vmem] * 4 + [smem] * 2,
        scratch_shapes=[pltpu.SMEM((devices,), jnp.int32)],
    )(tr, ve, land_mask, mixing, owners.reshape(rows), atm_row)

    def full(n):
        return pl.BlockSpec((n, cols), lambda i: (0, 0))

    tail = pl.BlockSpec((8, cols), lambda i: (rows // 8, 0))
    north, south, msg_a, msg_b = call(
        functools.partial(corner_kernel, lat_count, fields),
        [shaped(length, cols)] * 2 + [shaped(rows + 8, cols)] * 2,
        grid=(1,),
        in_specs=[full(length), full(length), tail, tail],
        out_specs=[full(length), full(length), tail, tail],
        input_output_aliases={2: 2, 3: 3},
    )(got_lat_b, got_lat_a, msg_a, msg_b)
    even_pairs = [(i, i ^ 1) for i in range(lon_count)]
    odd_pairs = [(i, (i + 1 if i % 2 else i - 1) % lon_count) for i in range(lon_count)]
    got_b = lax.ppermute(msg_b, "lon", even_pairs)
    got_a = lax.ppermute(msg_a, "lon", odd_pairs)

    count = min(3, levels)
    coefs, side, outgoing = call(
        functools.partial(surface_kernel, rows, levels),
        [
            shaped(len(COEFFICIENTS) * rows, cols),
            shaped(rows, cols),
            pltpu.VMEM((devices * slot_rows, cols), F32),
        ],
        scratch_shapes=[
            pltpu.VMEM((4 * count * pitch, cols), F32),
            pltpu.VMEM((4 * count * pitch, cols), F32),
            pltpu.VMEM((pitch, cols), F32),
        ],
    )(state, base, msg_a, msg_b, got_a, got_b, north, south, outgoing, ids)
    incoming = lax.all_to_all(
        outgoing.reshape(devices, slot_rows, 1, cols),
        ("lon", "lat"),
        0,
        0,
        axis_index_groups=[list(range(devices))[::-1]],
        tiled=True,
    ).reshape(devices * slot_rows, cols)

    chunks = 4
    tr_out, ve_out = call(
        functools.partial(main_kernel, rows, levels, chunks),
        [shaped(flat, cols), shaped(flat, cols)],
        in_specs=[vmem] * 12,
        out_specs=[hbm] * 2,
        scratch_shapes=[
            pltpu.VMEM((fields * pitch, cols), F32),
            pltpu.VMEM((fields * pitch, cols), F32),
            pltpu.VMEM((rows, cols), F32),
            pltpu.VMEM((flat, cols), F32),
            pltpu.VMEM((flat, cols), F32),
            pltpu.SemaphoreType.DMA((4 * chunks,)),
        ],
        cost_estimate=pl.CostEstimate(
            flops=80 * fields * rows * cols, bytes_accessed=5 << 20, transcendentals=0
        ),
    )(state, base, msg_a, msg_b, got_a, got_b, north, south, col_map, row_map, coefs, side)
    surface, cover = call(
        functools.partial(reduce_kernel, devices),
        [shaped(4, ATM_ROWS, cols), shaped(ATM_ROWS, cols)],
    )(incoming)
    shape = (2, levels, rows, cols)
    return tr_out.reshape(shape), ve_out.reshape(shape), surface, cover


def solution(mesh):
    in_specs = (
        P(None, None, "lat", "lon"),
        P(None, None, "lat", "lon"),
        P("lat", "lon"),
        P("lat", "lon"),
        P(("lon", "lat"), None),
        P(("lon", "lat")),
    )
    out_specs = (
        P(None, None, "lat", "lon"),
        P(None, None, "lat", "lon"),
        P(None, ("lon", "lat"), None),
        P(("lon", "lat"), None),
    )
    return jax.shard_map(local, mesh=mesh, in_specs=in_specs, out_specs=out_specs, check_vma=False)
```

```python
import functools
import math

import jax
import jax.numpy as jnp
from jax import lax
from jax.experimental import pallas as pl
from jax.experimental.pallas import tpu as pltpu
from jax.sharding import PartitionSpec as P

ATM_ROWS = 32
CAP = 2

THERMAL = 0.2
HALINE = 0.15
GRAVITY = 0.2
TIMESTEP = 0.8
VERTICAL_MIX = 0.1
VISCOSITY = 0.2
CORIOLIS_MAX = 0.3

LANES = 128
PAD = 8
EXACT = lax.Precision.HIGHEST
F32 = jnp.float32
VMEM_LIMIT = 32 * 1024 * 1024
VMEM_ALL = 62 * 1024 * 1024


def iota(shape, dim):
    return lax.broadcasted_iota(jnp.int32, shape, dim)


def dot(a, b, dims=(((1,), (0,)), ((), ()))):
    return lax.dot_general(a, b, dims, precision=EXACT, preferred_element_type=F32)


def is_even(axis):
    return lax.rem(lax.axis_index(axis), 2) == 0


def start_copies(pairs, sems):
    copies = [pltpu.make_async_copy(src, dst, sems.at[i]) for i, (src, dst) in enumerate(pairs)]
    for copy in copies:
        copy.start()
    return copies


def edge_kernel(rows, fields, tr_hbm, ve_hbm, mask_hbm, mix_hbm, lat_a, lat_b, edges, mask, mix, sems):
    half = fields // 2
    pairs = [(mask_hbm, mask), (mix_hbm, mix)]
    for n, src in enumerate((tr_hbm, ve_hbm)):
        for side, first in enumerate((0, rows - 8)):
            part = edges.at[side, n * half : (n + 1) * half]
            pairs.append((src.at[:, first : first + 8, :], part))
    for copy in start_copies(pairs, sems):
        copy.wait()
    flat = edges.reshape(2 * fields * 8, LANES)
    even = is_even("lat")
    top = ((rows - 1, 8 * fields + 7), (rows - 2, 8 * fields + 6))
    bottom = ((0, 0), (1, 1))
    for buf, first, second in ((lat_a, top, bottom), (lat_b, bottom, top)):
        (near, near_at), (far, far_at) = [
            [jnp.where(even, x, y) for x, y in zip(one, other)] for one, other in zip(first, second)
        ]
        wet_near = mask[pl.ds(near, 1), :].astype(F32)
        wet_far = mask[pl.ds(far, 1), :].astype(F32)
        buf[0:fields, :] = flat[pl.ds(near_at, fields, stride=8), :] * wet_near
        buf[fields : 2 * fields, :] = flat[pl.ds(far_at, fields, stride=8), :] * wet_far
        buf[2 * fields : 2 * fields + 8, :] = jnp.zeros((8, LANES), F32)
        buf[2 * fields : 2 * fields + 1, :] = wet_near
        buf[2 * fields + 1 : 2 * fields + 2, :] = wet_far
        buf[2 * fields + 2 : 2 * fields + 3, :] = mix[pl.ds(near, 1), :]


def pack_kernel(rows, fields, tr, ve, mask, mix, msg_a, msg_b):
    half = fields // 2
    wet = mask[...].astype(F32)
    lane = iota((rows, LANES), 1)
    pair = lane >> 1

    def columns(ref, base):
        def body(f, carry):
            to_east, to_west = carry
            x = ref[pl.ds(pl.multiple_of(f * rows, rows), rows), :]
            keep = pair == base + f
            low = 2 * (base + f)
            to_east = jnp.where(keep, pltpu.roll(x, (low + 2) & (LANES - 1), 1), to_east)
            to_west = jnp.where(keep, pltpu.roll(x, low, 1), to_west)
            return to_east, to_west

        return body

    carry = (jnp.zeros((rows, LANES), F32), jnp.zeros((rows, LANES), F32))
    for ref, base in ((tr, 0), (ve, half)):
        carry = lax.fori_loop(0, half, columns(ref, base), carry, unroll=8)
    def spread(x, i):
        return jnp.broadcast_to(x[:, i : i + 1], (rows, LANES))

    odd = (lane & 1) == 1
    to_east = carry[0] * jnp.where(odd, spread(wet, LANES - 1), spread(wet, LANES - 2))
    to_west = carry[1] * jnp.where(odd, spread(wet, 1), spread(wet, 0))
    even = is_even("lon")
    row = iota((rows, LANES), 0)
    mixing = mix[...]
    lines = []
    for near, far in ((LANES - 1, LANES - 2), (0, 1)):
        line = jnp.zeros((rows, LANES), F32)
        for part, column in enumerate((wet[:, near], wet[:, far], mixing[:, near])):
            line = jnp.where(lane == part * rows + row, column[:, None], line)
        lines.append(jnp.sum(line, axis=0, keepdims=True))
    for msg, flag in ((msg_a, jnp.logical_not(even)), (msg_b, even)):
        msg[0:rows, :] = jnp.where(flag, to_east, to_west)
        msg[rows:, :] = jnp.zeros((8, LANES), F32)
        msg[rows + 4 : rows + 5, :] = jnp.where(flag, *lines)


def prepare_kernel(
    rows, levels, devices, tr, ve, mask, mix, own, atm_row,
    state, base, col_map, row_map, out, ids, used,
):
    fields = 4 * levels
    half = fields // 2
    wet = mask[...].astype(F32)
    base[0:rows, :] = wet
    base[rows : 2 * rows, :] = mix[...]
    for ref, first in ((tr, 0), (ve, half)):

        def fill(f, carry, ref=ref, first=first):
            x = ref[pl.ds(pl.multiple_of(f * rows, 8), rows), :] * wet
            state[pl.ds(pl.multiple_of((first + f) * rows, 8), rows), :] = x
            return carry

        lax.fori_loop(0, half, fill, 0, unroll=8)

    total = lax.axis_size("lat") * rows
    latitude = lax.axis_index("lat") * rows - PAD + iota((rows + 2 * PAD, LANES), 0)
    latitude = jnp.where(latitude >= total, 2 * total - 1 - latitude, latitude).astype(F32)
    table = CORIOLIS_MAX * jnp.sin(math.pi * (-0.43 + 0.93 * (latitude + 0.5) / total))
    base[2 * rows :, :] = table

    span = 2 * levels
    src, dst = iota((LANES, LANES), 0), iota((LANES, LANES), 1)
    src_group, dst_group = src // span, dst // span
    src_level, dst_level = (src // 2) % levels, (dst // 2) % levels
    same_side = (src & 1) == (dst & 1)
    mixes = VERTICAL_MIX * level_matrix("mix", levels, src_level, dst_level)
    press = level_matrix("pressure", levels, src_level, dst_level) * density_weight(src_group)
    col_map[0:LANES, :] = jnp.where(same_side & (src_group == dst_group), mixes, 0.0)
    col_map[LANES : 2 * LANES, :] = jnp.where(same_side & (dst_group == 2), -press, 0.0)
    col_map[2 * LANES :, :] = jnp.where(same_side & (dst_group == 3), -press, 0.0)

    dst, src = iota((fields, fields), 0), iota((fields, fields), 1)
    mixes = VERTICAL_MIX * level_matrix("mix", levels, src % levels, dst % levels)
    row_map[0:fields, 0:fields] = jnp.where(dst // levels == src // levels, mixes, 0.0)
    dst, src = iota((levels, fields), 0), iota((levels, fields), 1)
    press = level_matrix("pressure", levels, src % levels, dst) * density_weight(src // levels)
    row_map[fields:, 0:fields] = press

    slot_rows = out.shape[0] // devices

    def clear(d, carry):
        used[d] = 0
        return carry

    lax.fori_loop(0, devices, clear, 0, unroll=8)
    out[...] = jnp.zeros(out.shape, F32)
    lane1 = iota((1, LANES), 1)
    places = jnp.zeros((1, LANES), jnp.int32)
    for r in range(rows):
        owner = own[r]
        slot = used[owner]
        used[owner] = slot + 1
        start = (devices - 1 - owner) * slot_rows
        places = jnp.where(lane1 == r, start + 4 * slot, places)
        out[pl.ds(start + 4 * CAP + slot, 1), :] = base[r : r + 1, :]
        line = out[pl.ds(start + 5 * CAP, 1), :]
        target = jnp.full((1, LANES), atm_row[r], jnp.int32).astype(F32)
        out[pl.ds(start + 5 * CAP, 1), :] = jnp.where(lane1 // (LANES // CAP) == slot, target, line)
    ids[...] = jnp.zeros(ids.shape, jnp.int32)
    ids[0:1, :] = places


def corner_kernel(lat_count, fields, got_b, got_a, tail_a, tail_b, north, south, new_a, new_b):
    fold = lax.axis_index("lat") == lat_count - 1
    even = is_even("lat")
    a, b = got_a[...], got_b[...]
    straight = jnp.where(even, a, b)
    south[...] = jnp.where(even, b, a)
    back = LANES - 1 - iota((8, LANES), 1)
    flipped = jnp.concatenate(
        [
            jnp.take_along_axis(straight[i : i + 8], back, axis=1)
            * (-1.0 if i < 2 * fields and i % fields >= fields // 2 else 1.0)
            for i in range(0, straight.shape[0], 8)
        ],
        axis=0,
    )
    north[...] = jnp.where(fold, flipped, straight)
    lane, field = iota((fields, LANES), 1), iota((fields, LANES), 0)
    lane1 = iota((1, LANES), 1)
    for old, new in ((tail_a, new_a), (tail_b, new_b)):
        new[...] = old[...]
    for i, ref in enumerate((north, south)):
        near = ref[0:fields, :]
        ends = jnp.where(
            lane == 2 * field, near[:, 0:1], jnp.where(lane == 2 * field + 1, near[:, LANES - 1 :], 0.0)
        )
        corner = jnp.sum(ends, axis=0, keepdims=True)
        wet = ref[2 * fields : 2 * fields + 1, :]
        wet = jnp.where(lane1 == 0, wet[:, 0:1], wet[:, LANES - 1 :])
        for new in (new_a, new_b):
            new[i : i + 1, :] = corner
            new[2 + i : 3 + i, :] = wet


class Sides:
    def __init__(self, rows, got_a, got_b, msg_a, msg_b):
        lane = iota((rows, LANES), 1)
        self.even = (lane & 1) == 0
        self.even1 = (iota((1, LANES), 1) & 1) == 0
        even = is_even("lon")

        def ordered(a, b, place):
            return jnp.where(even, b[place, :], a[place, :]), jnp.where(even, a[place, :], b[place, :])

        self.got = ordered(got_a, got_b, slice(0, rows))
        self.mine = ordered(msg_a, msg_b, slice(0, rows))
        self.extras = ordered(got_a, got_b, slice(rows, rows + 8))
        both = jnp.where((iota((LANES, LANES), 0) & 1) == 0, *[x[4:5] for x in self.extras])
        turned = jnp.transpose(both)
        self.columns = [turned[i * rows : (i + 1) * rows] for i in range(3)]

    def near(self):
        return jnp.where(self.even, *self.got)

    def far_and_inner(self):
        east, west = self.got
        mine_e, mine_w = self.mine
        far = jnp.where(self.even, pltpu.roll(east, LANES - 1, 1), pltpu.roll(west, 1, 1))
        inner = jnp.where(self.even, pltpu.roll(mine_e, LANES - 1, 1), pltpu.roll(mine_w, 1, 1))
        return far, inner

    def corner(self, i):
        east, west = self.extras
        wets = east[2 + i : 3 + i, 0:1], west[2 + i : 3 + i, 1:2]
        return jnp.where(self.even1, east[i : i + 1], west[i : i + 1]), *wets

    def lanes(self, i):
        return self.columns[i]


def level_matrix(kind, levels, source, target):
    if kind == "mix":
        above = (source == jnp.maximum(target - 1, 0)).astype(F32)
        below = (source == jnp.minimum(target + 1, levels - 1)).astype(F32)
        return above + below - 2.0 * (source == target).astype(F32)
    full = jnp.where(source < target, 1.0, jnp.where(source == target, 0.5, 0.0))
    return (0.5 * GRAVITY) * full


def density_weight(group):
    return jnp.where(group == 0, -THERMAL, jnp.where(group == 1, HALINE, 0.0)).astype(F32)


def advance_columns(sides, wet, coriolis, level_map):
    rows = wet.shape[0]
    mid = sides.near()
    outer, inner = sides.far_and_inner()
    (corner_n, wet_ne, wet_nw), (corner_s, wet_se, wet_sw) = sides.corner(0), sides.corner(1)
    wet_mid, wet_out = sides.lanes(0), sides.lanes(1)
    wet_in = jnp.where(sides.even, wet[:, LANES - 1 :], wet[:, 0:1])
    wet_corner_n = jnp.where(sides.even1, wet_ne, wet_nw)
    wet_corner_s = jnp.where(sides.even1, wet_se, wet_sw)
    mixing = sides.lanes(2)
    lane = iota((rows, LANES), 1)
    row = iota((rows, LANES), 0)
    span = LANES // 4
    group = lane // span

    def ends(outside, inside):
        return jnp.where(sides.even, outside, inside), jnp.where(sides.even, inside, outside)

    def shifted(x, north, south):
        n = jnp.where(row == rows - 1, north, pltpu.roll(x, rows - 1, 0))
        s = jnp.where(row == 0, south, pltpu.roll(x, 1, 0))
        return n, s

    e, w = ends(outer, inner)
    wet_e, wet_w = ends(wet_out, wet_in)
    n, s = shifted(mid, corner_n, corner_s)
    wet_n, wet_s = shifted(wet_mid, wet_corner_n, wet_corner_s)
    lap = wet_e * (e - mid) + wet_w * (w - mid) + wet_n * (n - mid) + wet_s * (s - mid)
    de, dn = e - w, n - s
    one, two, three = (pltpu.roll(mid, i * span, 1) for i in (1, 2, 3))

    def pick(a, b, c, d):
        return jnp.where(group == 0, a, jnp.where(group == 1, b, jnp.where(group == 2, c, d)))

    u = pick(two, three, mid, one)
    v = pick(one, two, three, mid)
    adv = 0.5 * (u * de + v * dn)
    zero = jnp.zeros_like(mid)
    if level_map is None:
        grad_x = HALINE * pltpu.roll(de, span, 1) - THERMAL * pltpu.roll(de, 2 * span, 1)
        grad_y = HALINE * pltpu.roll(dn, 2 * span, 1) - THERMAL * pltpu.roll(dn, 3 * span, 1)
        linear = VERTICAL_MIX * (pltpu.roll(mid, LANES - 2, 1) - mid)
        linear = linear - (0.25 * GRAVITY) * pick(zero, zero, grad_x, grad_y)
    else:
        linear = dot(jnp.concatenate([mid, de, dn], axis=1), level_map)
    turn = pick(zero, zero, coriolis * v, -coriolis * u)
    kappa = jnp.where(group < 2, mixing, VISCOSITY)
    tend = turn - adv + kappa * lap + linear
    return wet_mid * (mid + TIMESTEP * tend)


def advance_rows(levels, parts, level_map):
    fields = 4 * levels
    lane = iota((fields, LANES), 1)
    lane8 = iota((8, LANES), 1)

    def sides(x, east, west, at):
        e = jnp.where(at == LANES - 1, east, pltpu.roll(x, LANES - 1, 1))
        w = jnp.where(at == 0, west, pltpu.roll(x, 1, 1))
        return e, w

    mids, gaps = [], []
    for mid, n, s, (corner_e, corner_w), *_ in parts:
        e, w = sides(mid, corner_e, corner_w, lane)
        mids.append((mid, e, w, n, s))
        gaps += [e - w, n - s]
    vertical = dot(level_map[0:fields, 0:fields], jnp.concatenate([m[0] for m in mids], axis=1))
    grads = dot(level_map[fields:, 0:fields], jnp.concatenate(gaps, axis=1))
    done = []
    for i, (mid, e, w, n, s) in enumerate(mids):
        *_, wets, mixing, coriolis = parts[i]
        wet_mid, wet_n, wet_s, wet_corner_e, wet_corner_w = wets
        wet_e, wet_w = sides(
            jnp.broadcast_to(wet_mid, (8, LANES)), wet_corner_e, wet_corner_w, lane8
        )
        lap = wet_e[0:1] * (e - mid) + wet_w[0:1] * (w - mid)
        lap = lap + wet_n * (n - mid) + wet_s * (s - mid)
        de, dn = gaps[2 * i], gaps[2 * i + 1]
        u, v = mid[2 * levels : 3 * levels], mid[3 * levels :]
        adv = jnp.concatenate([u] * 4, axis=0) * de + jnp.concatenate([v] * 4, axis=0) * dn
        grad_x = grads[:, 2 * i * LANES : (2 * i + 1) * LANES]
        grad_y = grads[:, (2 * i + 1) * LANES : (2 * i + 2) * LANES]
        zero = jnp.zeros((2 * levels, LANES), F32)
        turn = jnp.concatenate([zero, coriolis * v - grad_x, -coriolis * u - grad_y], axis=0)
        kappa = jnp.concatenate(
            [jnp.broadcast_to(mixing, (2 * levels, LANES)), jnp.full(zero.shape, VISCOSITY)],
            axis=0,
        )
        tend = turn - 0.5 * adv + kappa * lap + vertical[:, i * LANES : (i + 1) * LANES]
        done.append(wet_mid * (mid + TIMESTEP * tend))
    return done


COEFFICIENTS = ("te", "tw", "tn", "ts", "tc", "ve", "vw", "vn", "vs", "vc", "adv", "mix", "turn")


def place_of(name, rows):
    i = COEFFICIENTS.index(name)
    return slice(i * rows, (i + 1) * rows)


def coefficients(wet, neighbours, mixing, coriolis):
    made = {}
    for name, kappa in (("t", mixing), ("v", VISCOSITY)):
        rest = wet * (1.0 - 2.0 * TIMESTEP * VERTICAL_MIX)
        for side, wet_n in zip("ewns", neighbours):
            made[name + side] = TIMESTEP * kappa * wet * wet_n
            rest = rest - made[name + side]
        made[name + "c"] = rest
    made["adv"] = (0.5 * TIMESTEP) * wet
    made["mix"] = (TIMESTEP * VERTICAL_MIX) * wet
    made["turn"] = TIMESTEP * coriolis * wet
    return made


def advance_level(k, count, levels, rows, src, sides, coef, acc):
    pitch = rows + 2 * PAD
    lane = iota((rows, LANES), 1)
    first, last = lane == 0, lane == LANES - 1
    above_k = jnp.maximum(k - 1, 0)
    below_k = jnp.minimum(k + 1, levels - 1)

    def load(q, level, shift):
        return src[pl.ds((q * count + level) * pitch + PAD + shift, rows), :]

    def base(q):
        return pl.multiple_of((q * count + k) * pitch + PAD, 8)

    center = [load(q, k, 0) for q in range(4)]
    u, v = coef("adv") * center[2], coef("adv") * center[3]
    sums, de, dn = [], [], []
    for q in range(4):
        c = center[q]
        n, s = load(q, k, 1), load(q, k, -1)
        edge = pltpu.roll(sides, (LANES - 1 - 2 * (q * levels + k)) & (LANES - 1), 1)
        e = jnp.where(last, edge, pltpu.roll(c, LANES - 1, 1))
        w = jnp.where(first, edge, pltpu.roll(c, 1, 1))
        kind = "t" if q < 2 else "v"
        lap = coef(kind + "c") * c + coef(kind + "e") * e + coef(kind + "w") * w
        lap = lap + coef(kind + "n") * n + coef(kind + "s") * s
        de.append(e - w)
        dn.append(n - s)
        sums.append(lap - (u * de[q] + v * dn[q]))
    scale = 0.5 * GRAVITY / VERTICAL_MIX
    dens_x = (scale * HALINE) * de[1] - (scale * THERMAL) * de[0]
    dens_y = (scale * HALINE) * dn[1] - (scale * THERMAL) * dn[0]
    acc_x, acc_y = acc
    grad = (None, None, acc_x + 0.5 * dens_x, acc_y + 0.5 * dens_y)
    turn = (None, None, coef("turn") * center[3], -coef("turn") * center[2])
    new = []
    for q in range(4):
        vertical = load(q, above_k, 0) + load(q, below_k, 0)
        if grad[q] is not None:
            vertical = vertical - grad[q]
        total = sums[q] + coef("mix") * vertical
        new.append(total if turn[q] is None else total + turn[q])
    return new, (acc_x + dens_x, acc_y + dens_y)


def advance_top_rows(levels, sides, north, south, state, wet, rows, table):
    fields = 4 * levels

    def both(a, b):
        return jnp.concatenate([a, b], axis=0)

    def rows_at(first):
        return both(
            north[pl.ds(first, 4, stride=levels), :], south[pl.ds(first, 4, stride=levels), :]
        )

    lane, row = iota((8, LANES), 1), iota((8, LANES), 0)
    upper = row < 4
    field = row & 3
    inside_n = state[pl.ds(rows - 1, 4, stride=levels * rows), :]
    inside_s = state[pl.ds(0, 4, stride=levels * rows), :]
    mid, below, outer = rows_at(0), rows_at(1), rows_at(fields)
    n = both(outer[0:4], inside_s)
    s = both(inside_n, outer[4:8])
    (corner_n, wet_ne, wet_nw), (corner_s, wet_se, wet_sw) = sides.corner(0), sides.corner(1)
    corner = jnp.where(upper, corner_n, corner_s)
    at = 2 * levels * field

    def end(parity):
        return jnp.sum(jnp.where(lane == at + parity, corner, 0.0), axis=1, keepdims=True)

    def west_east(x, east, west):
        return (
            jnp.where(lane == LANES - 1, east, pltpu.roll(x, LANES - 1, 1)),
            jnp.where(lane == 0, west, pltpu.roll(x, 1, 1)),
        )

    def tail(i):
        place = slice(2 * fields + i, 2 * fields + i + 1)
        return north[place, :], south[place, :]

    e, w = west_east(mid, end(0), end(1))
    wet_mid = jnp.where(upper, *tail(0))
    wet_e, wet_w = west_east(
        wet_mid, jnp.where(upper, wet_ne, wet_se), jnp.where(upper, wet_nw, wet_sw)
    )
    out_n, out_s = tail(1)
    wet_n = jnp.where(upper, out_n, wet[0:1])
    wet_s = jnp.where(upper, wet[rows - 1 : rows], out_s)
    lap = wet_e * (e - mid) + wet_w * (w - mid) + wet_n * (n - mid) + wet_s * (s - mid)
    de, dn = e - w, n - s

    def of(x, i):
        return jnp.where(upper, x[i : i + 1], x[4 + i : 5 + i])

    u, v = of(mid, 2), of(mid, 3)
    coriolis = jnp.where(upper, table[PAD + rows : PAD + rows + 1], table[PAD - 1 : PAD])
    grad_x = (0.25 * GRAVITY) * (HALINE * of(de, 1) - THERMAL * of(de, 0))
    grad_y = (0.25 * GRAVITY) * (HALINE * of(dn, 1) - THERMAL * of(dn, 0))
    turn = jnp.where(
        field < 2, 0.0, jnp.where(field == 2, coriolis * v - grad_x, -coriolis * u - grad_y)
    )
    kappa = jnp.where(field < 2, jnp.where(upper, *tail(2)), VISCOSITY)
    tend = turn - 0.5 * (u * de + v * dn) + kappa * lap + VERTICAL_MIX * (below - mid)
    return wet_mid * (mid + TIMESTEP * tend)


def surface_kernel(
    rows, levels,
    state, base, msg_a, msg_b, got_a, got_b, north, south, out_in, ids,
    coef, side, out, now, later, wet_pad, stage, places, sem,
):
    fields = 4 * levels
    pitch = rows + 2 * PAD
    to_scalars = pltpu.make_async_copy(ids, places, sem)
    to_scalars.start()
    out[...] = out_in[...]
    wet = base[0:rows, :]
    mixing = base[rows : 2 * rows, :]
    table = base[2 * rows :, :]
    coriolis = table[PAD : PAD + rows]
    lane = iota((rows, LANES), 1)
    sides = Sides(rows, got_a, got_b, msg_a, msg_b)
    wet_pad[PAD : PAD + rows, :] = wet
    wet_pad[PAD - 1 : PAD, :] = south[2 * fields : 2 * fields + 1, :]
    wet_pad[PAD + rows : PAD + rows + 1, :] = north[2 * fields : 2 * fields + 1, :]
    wet_n = wet_pad[PAD + 1 : PAD + 1 + rows, :]
    wet_s = wet_pad[PAD - 1 : PAD - 1 + rows, :]
    ends = pltpu.roll(sides.lanes(0), LANES - 1, 1)
    wet_e = jnp.where(lane == LANES - 1, ends, pltpu.roll(wet, LANES - 1, 1))
    wet_w = jnp.where(lane == 0, ends, pltpu.roll(wet, 1, 1))
    made = coefficients(wet, (wet_e, wet_w, wet_n, wet_s), mixing, coriolis)
    for name in COEFFICIENTS:
        coef[place_of(name, rows)] = made[name]
    near = sides.near()
    side[...] = near

    count = now.shape[0] // (4 * pitch)
    for q in range(4):
        for k in range(count):
            field = (q * levels + k) * rows
            at = (q * count + k) * pitch + PAD
            now[at : at + rows, :] = state[field : field + rows, :]
            now[at + rows : at + rows + 1, :] = north[q * levels + k : q * levels + k + 1, :]
            now[at - 1 : at, :] = south[q * levels + k : q * levels + k + 1, :]

    def read(name):
        return coef[place_of(name, rows)]

    none = jnp.zeros((rows, LANES), F32)
    acc = (none, none)
    edge_rows = advance_top_rows(levels, sides, north, south, state, wet, rows, table)
    edge_cols = advance_columns(sides, wet, coriolis, None)
    for k in range(count - 1):
        new, acc = advance_level(k, count, levels, rows, now, near, read, acc)
        for q in range(4):
            at = (q * count + k) * pitch + PAD
            later[at : at + rows, :] = new[q]
            if k == 0:
                later[at + rows : at + rows + 1, :] = edge_rows[q : q + 1]
                later[at - 1 : at, :] = edge_rows[4 + q : 5 + q]
    new, _ = advance_level(0, count, levels, rows, later, edge_cols, read, (none, none))
    for q in range(4):
        stage[pl.ds(q, rows, stride=4), :] = new[q]
    to_scalars.wait()
    for r in range(rows):
        out[pl.ds(places[0, r], 4), :] = stage[4 * r : 4 * r + 4, :]


def halo_after_first(rows, levels, sides, north, south, state, wet, table, col_map, row_map):
    fields = 4 * levels
    side_new = advance_columns(sides, wet, table[PAD : PAD + rows], col_map)
    lane, field = iota((fields, LANES), 1), iota((fields, LANES), 0)

    def to_sublanes(x, parity):
        here = lane == 2 * field + parity
        return jnp.sum(jnp.where(here, x, 0.0), axis=1, keepdims=True)

    parts = []
    for north_side, ref, line, lat_row in (
        (True, north, rows - 1, PAD + rows),
        (False, south, 0, PAD - 1),
    ):
        corner, *corner_wets = sides.corner(0 if north_side else 1)
        inside = state[pl.ds(line, fields, stride=rows), :]
        tail = ref[2 * fields :, :]
        pair = (ref[fields : 2 * fields, :], inside), (tail[1:2], wet[line : line + 1])
        (n, s), (wet_n, wet_s) = pair if north_side else [x[::-1] for x in pair]
        parts.append(
            (
                ref[0:fields, :], n, s, (to_sublanes(corner, 0), to_sublanes(corner, 1)),
                (tail[0:1], wet_n, wet_s, *corner_wets),
                tail[2:3], table[lat_row : lat_row + 1],
            )
        )
    return side_new, *advance_rows(levels, parts, row_map)


def main_kernel(
    rows, levels, chunks,
    state, base, msg_a, msg_b, got_a, got_b, north, south, col_map, row_map, coefs, side,
    tr_hbm, ve_hbm, now, later, side_new, tr_out, ve_out, sems,
):
    fields = 4 * levels
    pitch = rows + 2 * PAD
    sides = Sides(rows, got_a, got_b, msg_a, msg_b)
    side_new[...], north_new, south_new = halo_after_first(
        rows, levels, sides, north, south, state, base[0:rows, :], base[2 * rows :, :],
        col_map[...], row_map[...],
    )
    edges = (now, north[0:fields, :], south[0:fields, :]), (later, north_new, south_new)
    for buf, n, s in edges:
        buf[pl.ds(PAD - 1, fields, stride=pitch), :] = s
        buf[pl.ds(PAD + rows, fields, stride=pitch), :] = n

    def fill(f, carry):
        x = state[pl.ds(pl.multiple_of(f * rows, 8), rows), :]
        now[pl.ds(pl.multiple_of(f * pitch + PAD, 8), rows), :] = x
        return carry

    lax.fori_loop(0, fields, fill, 0, unroll=8)

    def coef(name):
        return coefs[place_of(name, rows)]

    def first(k, acc):
        new, acc = advance_level(k, levels, levels, rows, now, side[...], coef, acc)
        for q in range(4):
            place = pl.multiple_of((q * levels + k) * pitch + PAD, 8)
            later[pl.ds(place, rows), :] = new[q]
        return acc

    def second(k, acc):
        new, acc = advance_level(k, levels, levels, rows, later, side_new[...], coef, acc)
        for q in range(4):
            ref = tr_out if q < 2 else ve_out
            place = pl.multiple_of(((q % 2) * levels + k) * rows, 8)
            ref[pl.ds(place, rows), :] = new[q]
        return acc

    none = jnp.zeros((rows, LANES), F32)
    lax.fori_loop(0, levels, first, (none, none), unroll=2)
    acc = (none, none)
    size = levels // chunks
    copies = []
    for i in range(chunks):
        acc = lax.fori_loop(i * size, (i + 1) * size, second, acc, unroll=2)
        for src, dst in ((tr_out, tr_hbm), (ve_out, ve_hbm)):
            for q in range(2):
                start = (q * levels + i * size) * rows
                part = slice(start, start + size * rows)
                copy = pltpu.make_async_copy(src.at[part], dst.at[part], sems.at[len(copies)])
                copy.start()
                copies.append(copy)
    for copy in copies:
        copy.wait()


def reduce_kernel(devices, data, surface, cover):
    slot_rows = data.shape[0] // devices

    def rows_of(i):
        return data[pl.ds(i, devices, stride=slot_rows), :]

    width = LANES // CAP
    lines = rows_of(5 * CAP)
    named = (lines == (iota((devices, LANES), 1) % width).astype(F32)).astype(F32)
    to_rows, values = [], []
    for slot in range(CAP):
        to_rows.append(named[:, slot * width : slot * width + ATM_ROWS])
        parts = [rows_of(4 * slot + q) for q in range(4)] + [rows_of(4 * CAP + slot)]
        values.append(jnp.concatenate(parts, axis=1))
    rest = jnp.concatenate(values, axis=0)
    pieces = []
    for _ in range(3):
        piece = rest.astype(jnp.bfloat16)
        pieces.append(piece)
        rest = rest - piece.astype(F32)
    one = jnp.concatenate(to_rows, axis=0).astype(jnp.bfloat16)
    totals = lax.dot_general(
        jnp.concatenate([one] * 3, axis=0),
        jnp.concatenate(pieces, axis=0),
        (((0,), (0,)), ((), ())),
        preferred_element_type=F32,
    )
    ocean = totals[:, 4 * LANES :]
    cover[...] = ocean
    share = jnp.maximum(ocean, 1.0)
    for q in range(4):
        surface[q] = totals[:, q * LANES : (q + 1) * LANES] / share


def call(kernel, out_shape, limit=VMEM_LIMIT, **kwargs):
    return pl.pallas_call(
        kernel,
        out_shape=out_shape,
        compiler_params=pltpu.CompilerParams(vmem_limit_bytes=limit),
        **kwargs,
    )


def shaped(*shape, dtype=F32):
    return jax.ShapeDtypeStruct(shape, dtype)


def lat_swaps(lon_count, lat_count):
    swap_a, swap_b = [], []
    for i in range(lon_count):
        for a in range(lat_count):
            here = i * lat_count + a
            swap_a.append((here, i * lat_count + (a ^ 1)))
            if a == lat_count - 1:
                swap_b.append((here, (lon_count - 1 - i) * lat_count + a))
            elif a > 0:
                swap_b.append((here, here + 1 if a % 2 else here - 1))
    return swap_a, swap_b


def local(tracers, velocity, land_mask, mixing, owners, atm_row):
    levels = tracers.shape[1]
    rows, cols = land_mask.shape
    fields = 4 * levels
    lon_count, lat_count = lax.axis_size("lon"), lax.axis_size("lat")
    devices = lon_count * lat_count
    assert cols == LANES and rows % 8 == 0 and 2 * fields == LANES
    assert lon_count % 2 == 0 and lat_count % 2 == 0 and 3 * rows <= LANES
    length = 2 * fields + 8
    pitch = rows + 2 * PAD
    flat = 2 * levels * rows
    hbm = pl.BlockSpec(memory_space=pltpu.HBM)
    smem = pl.BlockSpec(memory_space=pltpu.SMEM)
    vmem = pl.BlockSpec(memory_space=pltpu.VMEM)

    deep = (2 * levels, rows, cols)
    lat_a, lat_b = call(
        functools.partial(edge_kernel, rows, fields),
        [pltpu.VMEM((length, cols), F32)] * 2,
        limit=VMEM_ALL,
        in_specs=[hbm] * 4,
        scratch_shapes=[
            pltpu.VMEM((2, fields, 8, cols), F32),
            pltpu.VMEM((rows, cols), jnp.int32),
            pltpu.VMEM((rows, cols), F32),
            pltpu.SemaphoreType.DMA((6,)),
        ],
    )(tracers.reshape(deep), velocity.reshape(deep), land_mask, mixing)
    swap_a, swap_b = lat_swaps(lon_count, lat_count)
    got_lat_b = lax.ppermute(lat_b, ("lon", "lat"), swap_b)
    got_lat_a = lax.ppermute(lat_a, ("lon", "lat"), swap_a)

    tr, ve = tracers.reshape(flat, cols), velocity.reshape(flat, cols)
    msg_a, msg_b = call(
        functools.partial(pack_kernel, rows, fields),
        [shaped(rows + 8, cols)] * 2,
        in_specs=[vmem] * 4,
    )(tr, ve, land_mask, mixing)

    slot_rows = 5 * CAP + 1
    state, base, col_map, row_map, outgoing, ids = call(
        functools.partial(prepare_kernel, rows, levels, devices),
        [
            shaped(fields * rows, cols),
            shaped(2 * rows + pitch, cols),
            shaped(3 * cols, cols),
            shaped(fields + levels, cols),
            shaped(devices * slot_rows, cols),
            shaped(8, cols, dtype=jnp.int32),
        ],
        in_specs=[vmem] * 4 + [smem] * 2,
        scratch_shapes=[pltpu.SMEM((devices,), jnp.int32)],
    )(tr, ve, land_mask, mixing, owners.reshape(rows), atm_row)

    def full(n):
        return pl.BlockSpec((n, cols), lambda i: (0, 0))

    tail = pl.BlockSpec((8, cols), lambda i: (rows // 8, 0))
    north, south, msg_a, msg_b = call(
        functools.partial(corner_kernel, lat_count, fields),
        [shaped(length, cols)] * 2 + [shaped(rows + 8, cols)] * 2,
        grid=(1,),
        in_specs=[full(length), full(length), tail, tail],
        out_specs=[full(length), full(length), tail, tail],
        input_output_aliases={2: 2, 3: 3},
    )(got_lat_b, got_lat_a, msg_a, msg_b)
    even_pairs = [(i, i ^ 1) for i in range(lon_count)]
    odd_pairs = [(i, (i + 1 if i % 2 else i - 1) % lon_count) for i in range(lon_count)]
    got_b = lax.ppermute(msg_b, "lon", even_pairs)
    got_a = lax.ppermute(msg_a, "lon", odd_pairs)

    count = min(3, levels)
    coefs, side, outgoing = call(
        functools.partial(surface_kernel, rows, levels),
        [
            shaped(len(COEFFICIENTS) * rows, cols),
            shaped(rows, cols),
            pltpu.VMEM((devices * slot_rows, cols), F32),
        ],
        scratch_shapes=[
            pltpu.VMEM((4 * count * pitch, cols), F32),
            pltpu.VMEM((4 * count * pitch, cols), F32),
            pltpu.VMEM((pitch, cols), F32),
            pltpu.VMEM((4 * rows, cols), F32),
            pltpu.SMEM((8, cols), jnp.int32),
            pltpu.SemaphoreType.DMA,
        ],
    )(state, base, msg_a, msg_b, got_a, got_b, north, south, outgoing, ids)
    incoming = lax.all_to_all(
        outgoing.reshape(devices, slot_rows, 1, cols),
        ("lon", "lat"),
        0,
        0,
        axis_index_groups=[list(range(devices))[::-1]],
        tiled=True,
    ).reshape(devices * slot_rows, cols)

    chunks = 4
    tr_out, ve_out = call(
        functools.partial(main_kernel, rows, levels, chunks),
        [shaped(flat, cols), shaped(flat, cols)],
        in_specs=[vmem] * 12,
        out_specs=[hbm] * 2,
        scratch_shapes=[
            pltpu.VMEM((fields * pitch, cols), F32),
            pltpu.VMEM((fields * pitch, cols), F32),
            pltpu.VMEM((rows, cols), F32),
            pltpu.VMEM((flat, cols), F32),
            pltpu.VMEM((flat, cols), F32),
            pltpu.SemaphoreType.DMA((4 * chunks,)),
        ],
        cost_estimate=pl.CostEstimate(
            flops=80 * fields * rows * cols, bytes_accessed=5 << 20, transcendentals=0
        ),
    )(state, base, msg_a, msg_b, got_a, got_b, north, south, col_map, row_map, coefs, side)
    surface, cover = call(
        functools.partial(reduce_kernel, devices),
        [shaped(4, ATM_ROWS, cols), shaped(ATM_ROWS, cols)],
    )(incoming)
    shape = (2, levels, rows, cols)
    return tr_out.reshape(shape), ve_out.reshape(shape), surface, cover


def solution(mesh):
    in_specs = (
        P(None, None, "lat", "lon"),
        P(None, None, "lat", "lon"),
        P("lat", "lon"),
        P("lat", "lon"),
        P(("lon", "lat"), None),
        P(("lon", "lat")),
    )
    out_specs = (
        P(None, None, "lat", "lon"),
        P(None, None, "lat", "lon"),
        P(None, ("lon", "lat"), None),
        P(("lon", "lat"), None),
    )
    return jax.shard_map(local, mesh=mesh, in_specs=in_specs, out_specs=out_specs, check_vma=False)
```

```python
import functools
import math

import jax
import jax.numpy as jnp
from jax import lax
from jax.experimental import pallas as pl
from jax.experimental.pallas import tpu as pltpu
from jax.sharding import PartitionSpec as P

ATM_ROWS = 32
CAP = 2

THERMAL = 0.2
HALINE = 0.15
GRAVITY = 0.2
TIMESTEP = 0.8
VERTICAL_MIX = 0.1
VISCOSITY = 0.2
CORIOLIS_MAX = 0.3

LANES = 128
PAD = 8
EXACT = lax.Precision.HIGHEST
F32 = jnp.float32
VMEM_LIMIT = 32 * 1024 * 1024
VMEM_ALL = 62 * 1024 * 1024


def iota(shape, dim):
    return lax.broadcasted_iota(jnp.int32, shape, dim)


def dot(a, b, dims=(((1,), (0,)), ((), ()))):
    return lax.dot_general(a, b, dims, precision=EXACT, preferred_element_type=F32)


def is_even(axis):
    return lax.rem(lax.axis_index(axis), 2) == 0


def start_copies(pairs, sems):
    copies = [pltpu.make_async_copy(src, dst, sems.at[i]) for i, (src, dst) in enumerate(pairs)]
    for copy in copies:
        copy.start()
    return copies


def edge_kernel(rows, fields, tr_hbm, ve_hbm, mask_hbm, mix_hbm, lat_a, lat_b, edges, mask, mix, sems):
    half = fields // 2
    pairs = [(mask_hbm, mask), (mix_hbm, mix)]
    for n, src in enumerate((tr_hbm, ve_hbm)):
        for side, first in enumerate((0, rows - 8)):
            part = edges.at[side, n * half : (n + 1) * half]
            pairs.append((src.at[:, first : first + 8, :], part))
    for copy in start_copies(pairs, sems):
        copy.wait()
    flat = edges.reshape(2 * fields * 8, LANES)
    even = is_even("lat")
    top = ((rows - 1, 8 * fields + 7), (rows - 2, 8 * fields + 6))
    bottom = ((0, 0), (1, 1))
    for buf, first, second in ((lat_a, top, bottom), (lat_b, bottom, top)):
        (near, near_at), (far, far_at) = [
            [jnp.where(even, x, y) for x, y in zip(one, other)] for one, other in zip(first, second)
        ]
        wet_near = mask[pl.ds(near, 1), :].astype(F32)
        wet_far = mask[pl.ds(far, 1), :].astype(F32)
        buf[0:fields, :] = flat[pl.ds(near_at, fields, stride=8), :] * wet_near
        buf[fields : 2 * fields, :] = flat[pl.ds(far_at, fields, stride=8), :] * wet_far
        buf[2 * fields : 2 * fields + 8, :] = jnp.zeros((8, LANES), F32)
        buf[2 * fields : 2 * fields + 1, :] = wet_near
        buf[2 * fields + 1 : 2 * fields + 2, :] = wet_far
        buf[2 * fields + 2 : 2 * fields + 3, :] = mix[pl.ds(near, 1), :]


def pack_kernel(rows, fields, tr, ve, mask, mix, msg_a, msg_b):
    half = fields // 2
    wet = mask[...].astype(F32)
    lane = iota((rows, LANES), 1)
    pair = lane >> 1

    def columns(ref, base):
        def body(f, carry):
            to_east, to_west = carry
            x = ref[pl.ds(pl.multiple_of(f * rows, rows), rows), :]
            keep = pair == base + f
            low = 2 * (base + f)
            to_east = jnp.where(keep, pltpu.roll(x, (low + 2) & (LANES - 1), 1), to_east)
            to_west = jnp.where(keep, pltpu.roll(x, low, 1), to_west)
            return to_east, to_west

        return body

    carry = (jnp.zeros((rows, LANES), F32), jnp.zeros((rows, LANES), F32))
    for ref, base in ((tr, 0), (ve, half)):
        carry = lax.fori_loop(0, half, columns(ref, base), carry, unroll=8)
    def spread(x, i):
        return jnp.broadcast_to(x[:, i : i + 1], (rows, LANES))

    odd = (lane & 1) == 1
    to_east = carry[0] * jnp.where(odd, spread(wet, LANES - 1), spread(wet, LANES - 2))
    to_west = carry[1] * jnp.where(odd, spread(wet, 1), spread(wet, 0))
    even = is_even("lon")
    row = iota((rows, LANES), 0)
    mixing = mix[...]
    lines = []
    for near, far in ((LANES - 1, LANES - 2), (0, 1)):
        line = jnp.zeros((rows, LANES), F32)
        for part, column in enumerate((wet[:, near], wet[:, far], mixing[:, near])):
            line = jnp.where(lane == part * rows + row, column[:, None], line)
        lines.append(jnp.sum(line, axis=0, keepdims=True))
    for msg, flag in ((msg_a, jnp.logical_not(even)), (msg_b, even)):
        msg[0:rows, :] = jnp.where(flag, to_east, to_west)
        msg[rows:, :] = jnp.zeros((8, LANES), F32)
        msg[rows + 4 : rows + 5, :] = jnp.where(flag, *lines)


def prepare_kernel(
    rows, levels, devices, tr, ve, mask, mix, own, atm_row,
    state, base, col_map, row_map, out, ids, used,
):
    fields = 4 * levels
    half = fields // 2
    wet = mask[...].astype(F32)
    base[0:rows, :] = wet
    base[rows : 2 * rows, :] = mix[...]
    for ref, first in ((tr, 0), (ve, half)):

        def fill(f, carry, ref=ref, first=first):
            x = ref[pl.ds(pl.multiple_of(f * rows, 8), rows), :] * wet
            state[pl.ds(pl.multiple_of((first + f) * rows, 8), rows), :] = x
            return carry

        lax.fori_loop(0, half, fill, 0, unroll=8)

    total = lax.axis_size("lat") * rows
    latitude = lax.axis_index("lat") * rows - PAD + iota((rows + 2 * PAD, LANES), 0)
    latitude = jnp.where(latitude >= total, 2 * total - 1 - latitude, latitude).astype(F32)
    table = CORIOLIS_MAX * jnp.sin(math.pi * (-0.43 + 0.93 * (latitude + 0.5) / total))
    base[2 * rows :, :] = table

    span = 2 * levels
    src, dst = iota((LANES, LANES), 0), iota((LANES, LANES), 1)
    src_group, dst_group = src // span, dst // span
    src_level, dst_level = (src // 2) % levels, (dst // 2) % levels
    same_side = (src & 1) == (dst & 1)
    mixes = VERTICAL_MIX * level_matrix("mix", levels, src_level, dst_level)
    press = level_matrix("pressure", levels, src_level, dst_level) * density_weight(src_group)
    col_map[0:LANES, :] = jnp.where(same_side & (src_group == dst_group), mixes, 0.0)
    col_map[LANES : 2 * LANES, :] = jnp.where(same_side & (dst_group == 2), -press, 0.0)
    col_map[2 * LANES :, :] = jnp.where(same_side & (dst_group == 3), -press, 0.0)

    dst, src = iota((fields, fields), 0), iota((fields, fields), 1)
    mixes = VERTICAL_MIX * level_matrix("mix", levels, src % levels, dst % levels)
    row_map[0:fields, 0:fields] = jnp.where(dst // levels == src // levels, mixes, 0.0)
    dst, src = iota((levels, fields), 0), iota((levels, fields), 1)
    press = level_matrix("pressure", levels, src % levels, dst) * density_weight(src // levels)
    row_map[fields:, 0:fields] = press

    slot_rows = out.shape[0] // devices

    def clear(d, carry):
        used[d] = 0
        return carry

    lax.fori_loop(0, devices, clear, 0, unroll=8)
    out[...] = jnp.zeros(out.shape, F32)
    lane1 = iota((1, LANES), 1)
    places = jnp.zeros((1, LANES), jnp.int32)
    for r in range(rows):
        owner = own[r]
        slot = used[owner]
        used[owner] = slot + 1
        start = owner * slot_rows
        places = jnp.where(lane1 == r, start + 4 * slot, places)
        out[pl.ds(start + 4 * CAP + slot, 1), :] = base[r : r + 1, :]
        line = out[pl.ds(start + 5 * CAP, 1), :]
        target = jnp.full((1, LANES), atm_row[r], jnp.int32).astype(F32)
        out[pl.ds(start + 5 * CAP, 1), :] = jnp.where(lane1 // (LANES // CAP) == slot, target, line)
    ids[...] = jnp.zeros(ids.shape, jnp.int32)
    ids[0:1, :] = places


def corner_kernel(lat_count, fields, got_b, got_a, tail_a, tail_b, north, south, new_a, new_b):
    fold = lax.axis_index("lat") == lat_count - 1
    even = is_even("lat")
    a, b = got_a[...], got_b[...]
    straight = jnp.where(even, a, b)
    south[...] = jnp.where(even, b, a)
    back = LANES - 1 - iota((8, LANES), 1)
    flipped = jnp.concatenate(
        [
            jnp.take_along_axis(straight[i : i + 8], back, axis=1)
            * (-1.0 if i < 2 * fields and i % fields >= fields // 2 else 1.0)
            for i in range(0, straight.shape[0], 8)
        ],
        axis=0,
    )
    north[...] = jnp.where(fold, flipped, straight)
    lane, field = iota((fields, LANES), 1), iota((fields, LANES), 0)
    lane1 = iota((1, LANES), 1)
    for old, new in ((tail_a, new_a), (tail_b, new_b)):
        new[...] = old[...]
    for i, ref in enumerate((north, south)):
        near = ref[0:fields, :]
        ends = jnp.where(
            lane == 2 * field, near[:, 0:1], jnp.where(lane == 2 * field + 1, near[:, LANES - 1 :], 0.0)
        )
        corner = jnp.sum(ends, axis=0, keepdims=True)
        wet = ref[2 * fields : 2 * fields + 1, :]
        wet = jnp.where(lane1 == 0, wet[:, 0:1], wet[:, LANES - 1 :])
        for new in (new_a, new_b):
            new[i : i + 1, :] = corner
            new[2 + i : 3 + i, :] = wet


class Sides:
    def __init__(self, rows, got_a, got_b, msg_a, msg_b):
        lane, row = iota((rows, LANES), 1), iota((rows, LANES), 0)
        self.even = (lane & 1) == 0
        self.even1 = (iota((1, LANES), 1) & 1) == 0
        even = is_even("lon")

        def ordered(a, b, place):
            return jnp.where(even, b[place, :], a[place, :]), jnp.where(even, a[place, :], b[place, :])

        self.got = ordered(got_a, got_b, slice(0, rows))
        self.mine = ordered(msg_a, msg_b, slice(0, rows))
        self.extras = ordered(got_a, got_b, slice(rows, rows + 8))
        self.columns = [
            [
                jnp.sum(jnp.where(lane == i * rows + row, x[4:5], 0.0), axis=1, keepdims=True)
                for i in range(3)
            ]
            for x in self.extras
        ]

    def near(self):
        return jnp.where(self.even, *self.got)

    def far_and_inner(self):
        east, west = self.got
        mine_e, mine_w = self.mine
        far = jnp.where(self.even, pltpu.roll(east, LANES - 1, 1), pltpu.roll(west, 1, 1))
        inner = jnp.where(self.even, pltpu.roll(mine_e, LANES - 1, 1), pltpu.roll(mine_w, 1, 1))
        return far, inner

    def corner(self, i):
        east, west = self.extras
        wets = east[2 + i : 3 + i, 0:1], west[2 + i : 3 + i, 1:2]
        return jnp.where(self.even1, east[i : i + 1], west[i : i + 1]), *wets

    def lanes(self, i):
        return jnp.where(self.even, self.columns[0][i], self.columns[1][i])


def level_matrix(kind, levels, source, target):
    if kind == "mix":
        above = (source == jnp.maximum(target - 1, 0)).astype(F32)
        below = (source == jnp.minimum(target + 1, levels - 1)).astype(F32)
        return above + below - 2.0 * (source == target).astype(F32)
    full = jnp.where(source < target, 1.0, jnp.where(source == target, 0.5, 0.0))
    return (0.5 * GRAVITY) * full


def density_weight(group):
    return jnp.where(group == 0, -THERMAL, jnp.where(group == 1, HALINE, 0.0)).astype(F32)


def advance_columns(sides, wet, coriolis, level_map):
    rows = wet.shape[0]
    mid = sides.near()
    outer, inner = sides.far_and_inner()
    (corner_n, wet_ne, wet_nw), (corner_s, wet_se, wet_sw) = sides.corner(0), sides.corner(1)
    wet_mid, wet_out = sides.lanes(0), sides.lanes(1)
    wet_in = jnp.where(sides.even, wet[:, LANES - 1 :], wet[:, 0:1])
    wet_corner_n = jnp.where(sides.even1, wet_ne, wet_nw)
    wet_corner_s = jnp.where(sides.even1, wet_se, wet_sw)
    mixing = sides.lanes(2)
    lane = iota((rows, LANES), 1)
    row = iota((rows, LANES), 0)
    span = LANES // 4
    group = lane // span

    def ends(outside, inside):
        return jnp.where(sides.even, outside, inside), jnp.where(sides.even, inside, outside)

    def shifted(x, north, south):
        n = jnp.where(row == rows - 1, north, pltpu.roll(x, rows - 1, 0))
        s = jnp.where(row == 0, south, pltpu.roll(x, 1, 0))
        return n, s

    e, w = ends(outer, inner)
    wet_e, wet_w = ends(wet_out, wet_in)
    n, s = shifted(mid, corner_n, corner_s)
    wet_n, wet_s = shifted(wet_mid, wet_corner_n, wet_corner_s)
    lap = wet_e * (e - mid) + wet_w * (w - mid) + wet_n * (n - mid) + wet_s * (s - mid)
    de, dn = e - w, n - s
    one, two, three = (pltpu.roll(mid, i * span, 1) for i in (1, 2, 3))

    def pick(a, b, c, d):
        return jnp.where(group == 0, a, jnp.where(group == 1, b, jnp.where(group == 2, c, d)))

    u = pick(two, three, mid, one)
    v = pick(one, two, three, mid)
    adv = 0.5 * (u * de + v * dn)
    zero = jnp.zeros_like(mid)
    if level_map is None:
        grad_x = HALINE * pltpu.roll(de, span, 1) - THERMAL * pltpu.roll(de, 2 * span, 1)
        grad_y = HALINE * pltpu.roll(dn, 2 * span, 1) - THERMAL * pltpu.roll(dn, 3 * span, 1)
        linear = VERTICAL_MIX * (pltpu.roll(mid, LANES - 2, 1) - mid)
        linear = linear - (0.25 * GRAVITY) * pick(zero, zero, grad_x, grad_y)
    else:
        linear = dot(jnp.concatenate([mid, de, dn], axis=1), level_map)
    turn = pick(zero, zero, coriolis * v, -coriolis * u)
    kappa = jnp.where(group < 2, mixing, VISCOSITY)
    tend = turn - adv + kappa * lap + linear
    return wet_mid * (mid + TIMESTEP * tend)


def advance_rows(levels, parts, level_map):
    fields = 4 * levels
    lane = iota((fields, LANES), 1)
    lane8 = iota((8, LANES), 1)

    def sides(x, east, west, at):
        e = jnp.where(at == LANES - 1, east, pltpu.roll(x, LANES - 1, 1))
        w = jnp.where(at == 0, west, pltpu.roll(x, 1, 1))
        return e, w

    mids, gaps = [], []
    for mid, n, s, (corner_e, corner_w), *_ in parts:
        e, w = sides(mid, corner_e, corner_w, lane)
        mids.append((mid, e, w, n, s))
        gaps += [e - w, n - s]
    vertical = dot(level_map[0:fields, 0:fields], jnp.concatenate([m[0] for m in mids], axis=1))
    grads = dot(level_map[fields:, 0:fields], jnp.concatenate(gaps, axis=1))
    done = []
    for i, (mid, e, w, n, s) in enumerate(mids):
        *_, wets, mixing, coriolis = parts[i]
        wet_mid, wet_n, wet_s, wet_corner_e, wet_corner_w = wets
        wet_e, wet_w = sides(
            jnp.broadcast_to(wet_mid, (8, LANES)), wet_corner_e, wet_corner_w, lane8
        )
        lap = wet_e[0:1] * (e - mid) + wet_w[0:1] * (w - mid)
        lap = lap + wet_n * (n - mid) + wet_s * (s - mid)
        de, dn = gaps[2 * i], gaps[2 * i + 1]
        u, v = mid[2 * levels : 3 * levels], mid[3 * levels :]
        adv = jnp.concatenate([u] * 4, axis=0) * de + jnp.concatenate([v] * 4, axis=0) * dn
        grad_x = grads[:, 2 * i * LANES : (2 * i + 1) * LANES]
        grad_y = grads[:, (2 * i + 1) * LANES : (2 * i + 2) * LANES]
        zero = jnp.zeros((2 * levels, LANES), F32)
        turn = jnp.concatenate([zero, coriolis * v - grad_x, -coriolis * u - grad_y], axis=0)
        kappa = jnp.concatenate(
            [jnp.broadcast_to(mixing, (2 * levels, LANES)), jnp.full(zero.shape, VISCOSITY)],
            axis=0,
        )
        tend = turn - 0.5 * adv + kappa * lap + vertical[:, i * LANES : (i + 1) * LANES]
        done.append(wet_mid * (mid + TIMESTEP * tend))
    return done


COEFFICIENTS = ("te", "tw", "tn", "ts", "tc", "ve", "vw", "vn", "vs", "vc", "adv", "mix", "turn")


def place_of(name, rows):
    i = COEFFICIENTS.index(name)
    return slice(i * rows, (i + 1) * rows)


def coefficients(wet, neighbours, mixing, coriolis):
    made = {}
    for name, kappa in (("t", mixing), ("v", VISCOSITY)):
        rest = wet * (1.0 - 2.0 * TIMESTEP * VERTICAL_MIX)
        for side, wet_n in zip("ewns", neighbours):
            made[name + side] = TIMESTEP * kappa * wet * wet_n
            rest = rest - made[name + side]
        made[name + "c"] = rest
    made["adv"] = (0.5 * TIMESTEP) * wet
    made["mix"] = (TIMESTEP * VERTICAL_MIX) * wet
    made["turn"] = TIMESTEP * coriolis * wet
    return made


def advance_level(k, count, levels, rows, src, sides, coef, acc):
    pitch = rows + 2 * PAD
    lane = iota((rows, LANES), 1)
    first, last = lane == 0, lane == LANES - 1
    above_k = jnp.maximum(k - 1, 0)
    below_k = jnp.minimum(k + 1, levels - 1)

    def load(q, level, shift):
        return src[pl.ds((q * count + level) * pitch + PAD + shift, rows), :]

    def base(q):
        return pl.multiple_of((q * count + k) * pitch + PAD, 8)

    center = [load(q, k, 0) for q in range(4)]
    u, v = coef("adv") * center[2], coef("adv") * center[3]
    sums, de, dn = [], [], []
    for q in range(4):
        c = center[q]
        n, s = load(q, k, 1), load(q, k, -1)
        edge = pltpu.roll(sides, (LANES - 1 - 2 * (q * levels + k)) & (LANES - 1), 1)
        e = jnp.where(last, edge, pltpu.roll(c, LANES - 1, 1))
        w = jnp.where(first, edge, pltpu.roll(c, 1, 1))
        kind = "t" if q < 2 else "v"
        lap = coef(kind + "c") * c + coef(kind + "e") * e + coef(kind + "w") * w
        lap = lap + coef(kind + "n") * n + coef(kind + "s") * s
        de.append(e - w)
        dn.append(n - s)
        sums.append(lap - (u * de[q] + v * dn[q]))
    scale = 0.5 * GRAVITY / VERTICAL_MIX
    dens_x = (scale * HALINE) * de[1] - (scale * THERMAL) * de[0]
    dens_y = (scale * HALINE) * dn[1] - (scale * THERMAL) * dn[0]
    acc_x, acc_y = acc
    grad = (None, None, acc_x + 0.5 * dens_x, acc_y + 0.5 * dens_y)
    turn = (None, None, coef("turn") * center[3], -coef("turn") * center[2])
    new = []
    for q in range(4):
        vertical = load(q, above_k, 0) + load(q, below_k, 0)
        if grad[q] is not None:
            vertical = vertical - grad[q]
        total = sums[q] + coef("mix") * vertical
        new.append(total if turn[q] is None else total + turn[q])
    return new, (acc_x + dens_x, acc_y + dens_y)


def advance_top_rows(levels, sides, north, south, state, wet, rows, table):
    fields = 4 * levels

    def both(a, b):
        return jnp.concatenate([a, b], axis=0)

    def rows_at(first):
        return both(
            north[pl.ds(first, 4, stride=levels), :], south[pl.ds(first, 4, stride=levels), :]
        )

    lane, row = iota((8, LANES), 1), iota((8, LANES), 0)
    upper = row < 4
    field = row & 3
    inside_n = state[pl.ds(rows - 1, 4, stride=levels * rows), :]
    inside_s = state[pl.ds(0, 4, stride=levels * rows), :]
    mid, below, outer = rows_at(0), rows_at(1), rows_at(fields)
    n = both(outer[0:4], inside_s)
    s = both(inside_n, outer[4:8])
    (corner_n, wet_ne, wet_nw), (corner_s, wet_se, wet_sw) = sides.corner(0), sides.corner(1)
    corner = jnp.where(upper, corner_n, corner_s)
    at = 2 * levels * field

    def end(parity):
        return jnp.sum(jnp.where(lane == at + parity, corner, 0.0), axis=1, keepdims=True)

    def west_east(x, east, west):
        return (
            jnp.where(lane == LANES - 1, east, pltpu.roll(x, LANES - 1, 1)),
            jnp.where(lane == 0, west, pltpu.roll(x, 1, 1)),
        )

    def tail(i):
        place = slice(2 * fields + i, 2 * fields + i + 1)
        return north[place, :], south[place, :]

    e, w = west_east(mid, end(0), end(1))
    wet_mid = jnp.where(upper, *tail(0))
    wet_e, wet_w = west_east(
        wet_mid, jnp.where(upper, wet_ne, wet_se), jnp.where(upper, wet_nw, wet_sw)
    )
    out_n, out_s = tail(1)
    wet_n = jnp.where(upper, out_n, wet[0:1])
    wet_s = jnp.where(upper, wet[rows - 1 : rows], out_s)
    lap = wet_e * (e - mid) + wet_w * (w - mid) + wet_n * (n - mid) + wet_s * (s - mid)
    de, dn = e - w, n - s

    def of(x, i):
        return jnp.where(upper, x[i : i + 1], x[4 + i : 5 + i])

    u, v = of(mid, 2), of(mid, 3)
    coriolis = jnp.where(upper, table[PAD + rows : PAD + rows + 1], table[PAD - 1 : PAD])
    grad_x = (0.25 * GRAVITY) * (HALINE * of(de, 1) - THERMAL * of(de, 0))
    grad_y = (0.25 * GRAVITY) * (HALINE * of(dn, 1) - THERMAL * of(dn, 0))
    turn = jnp.where(
        field < 2, 0.0, jnp.where(field == 2, coriolis * v - grad_x, -coriolis * u - grad_y)
    )
    kappa = jnp.where(field < 2, jnp.where(upper, *tail(2)), VISCOSITY)
    tend = turn - 0.5 * (u * de + v * dn) + kappa * lap + VERTICAL_MIX * (below - mid)
    return wet_mid * (mid + TIMESTEP * tend)


def surface_kernel(
    rows, levels,
    state, base, msg_a, msg_b, got_a, got_b, north, south, out_in, ids,
    coef, side, out, now, later, wet_pad, stage, places, sem,
):
    fields = 4 * levels
    pitch = rows + 2 * PAD
    to_scalars = pltpu.make_async_copy(ids, places, sem)
    to_scalars.start()
    out[...] = out_in[...]
    wet = base[0:rows, :]
    mixing = base[rows : 2 * rows, :]
    table = base[2 * rows :, :]
    coriolis = table[PAD : PAD + rows]
    lane = iota((rows, LANES), 1)
    sides = Sides(rows, got_a, got_b, msg_a, msg_b)
    wet_pad[PAD : PAD + rows, :] = wet
    wet_pad[PAD - 1 : PAD, :] = south[2 * fields : 2 * fields + 1, :]
    wet_pad[PAD + rows : PAD + rows + 1, :] = north[2 * fields : 2 * fields + 1, :]
    wet_n = wet_pad[PAD + 1 : PAD + 1 + rows, :]
    wet_s = wet_pad[PAD - 1 : PAD - 1 + rows, :]
    wet_e = jnp.where(lane == LANES - 1, sides.columns[0][0], pltpu.roll(wet, LANES - 1, 1))
    wet_w = jnp.where(lane == 0, sides.columns[1][0], pltpu.roll(wet, 1, 1))
    made = coefficients(wet, (wet_e, wet_w, wet_n, wet_s), mixing, coriolis)
    for name in COEFFICIENTS:
        coef[place_of(name, rows)] = made[name]
    near = sides.near()
    side[...] = near

    count = now.shape[0] // (4 * pitch)
    for q in range(4):
        for k in range(count):
            field = (q * levels + k) * rows
            at = (q * count + k) * pitch + PAD
            now[at : at + rows, :] = state[field : field + rows, :]
            now[at + rows : at + rows + 1, :] = north[q * levels + k : q * levels + k + 1, :]
            now[at - 1 : at, :] = south[q * levels + k : q * levels + k + 1, :]

    def read(name):
        return coef[place_of(name, rows)]

    none = jnp.zeros((rows, LANES), F32)
    acc = (none, none)
    edge_rows = advance_top_rows(levels, sides, north, south, state, wet, rows, table)
    edge_cols = advance_columns(sides, wet, coriolis, None)
    for k in range(count - 1):
        new, acc = advance_level(k, count, levels, rows, now, near, read, acc)
        for q in range(4):
            at = (q * count + k) * pitch + PAD
            later[at : at + rows, :] = new[q]
            if k == 0:
                later[at + rows : at + rows + 1, :] = edge_rows[q : q + 1]
                later[at - 1 : at, :] = edge_rows[4 + q : 5 + q]
    new, _ = advance_level(0, count, levels, rows, later, edge_cols, read, (none, none))
    for q in range(4):
        stage[pl.ds(q, rows, stride=4), :] = new[q]
    to_scalars.wait()
    for r in range(rows):
        out[pl.ds(places[0, r], 4), :] = stage[4 * r : 4 * r + 4, :]


def halo_after_first(rows, levels, sides, north, south, state, wet, table, col_map, row_map):
    fields = 4 * levels
    side_new = advance_columns(sides, wet, table[PAD : PAD + rows], col_map)
    lane, field = iota((fields, LANES), 1), iota((fields, LANES), 0)

    def to_sublanes(x, parity):
        here = lane == 2 * field + parity
        return jnp.sum(jnp.where(here, x, 0.0), axis=1, keepdims=True)

    parts = []
    for north_side, ref, line, lat_row in (
        (True, north, rows - 1, PAD + rows),
        (False, south, 0, PAD - 1),
    ):
        corner, *corner_wets = sides.corner(0 if north_side else 1)
        inside = state[pl.ds(line, fields, stride=rows), :]
        tail = ref[2 * fields :, :]
        pair = (ref[fields : 2 * fields, :], inside), (tail[1:2], wet[line : line + 1])
        (n, s), (wet_n, wet_s) = pair if north_side else [x[::-1] for x in pair]
        parts.append(
            (
                ref[0:fields, :], n, s, (to_sublanes(corner, 0), to_sublanes(corner, 1)),
                (tail[0:1], wet_n, wet_s, *corner_wets),
                tail[2:3], table[lat_row : lat_row + 1],
            )
        )
    return side_new, *advance_rows(levels, parts, row_map)


def main_kernel(
    rows, levels, chunks,
    state, base, msg_a, msg_b, got_a, got_b, north, south, col_map, row_map, coefs, side,
    tr_hbm, ve_hbm, now, later, side_new, tr_out, ve_out, sems,
):
    fields = 4 * levels
    pitch = rows + 2 * PAD
    sides = Sides(rows, got_a, got_b, msg_a, msg_b)
    side_new[...], north_new, south_new = halo_after_first(
        rows, levels, sides, north, south, state, base[0:rows, :], base[2 * rows :, :],
        col_map[...], row_map[...],
    )
    edges = (now, north[0:fields, :], south[0:fields, :]), (later, north_new, south_new)
    for buf, n, s in edges:
        buf[pl.ds(PAD - 1, fields, stride=pitch), :] = s
        buf[pl.ds(PAD + rows, fields, stride=pitch), :] = n

    def fill(f, carry):
        x = state[pl.ds(pl.multiple_of(f * rows, 8), rows), :]
        now[pl.ds(pl.multiple_of(f * pitch + PAD, 8), rows), :] = x
        return carry

    lax.fori_loop(0, fields, fill, 0, unroll=8)

    def coef(name):
        return coefs[place_of(name, rows)]

    def first(k, acc):
        new, acc = advance_level(k, levels, levels, rows, now, side[...], coef, acc)
        for q in range(4):
            place = pl.multiple_of((q * levels + k) * pitch + PAD, 8)
            later[pl.ds(place, rows), :] = new[q]
        return acc

    def second(k, acc):
        new, acc = advance_level(k, levels, levels, rows, later, side_new[...], coef, acc)
        for q in range(4):
            ref = tr_out if q < 2 else ve_out
            place = pl.multiple_of(((q % 2) * levels + k) * rows, 8)
            ref[pl.ds(place, rows), :] = new[q]
        return acc

    none = jnp.zeros((rows, LANES), F32)
    lax.fori_loop(0, levels, first, (none, none), unroll=4)
    acc = (none, none)
    size = levels // chunks
    copies = []
    for i in range(chunks):
        acc = lax.fori_loop(i * size, (i + 1) * size, second, acc, unroll=4)
        for src, dst in ((tr_out, tr_hbm), (ve_out, ve_hbm)):
            for q in range(2):
                start = (q * levels + i * size) * rows
                part = slice(start, start + size * rows)
                copy = pltpu.make_async_copy(src.at[part], dst.at[part], sems.at[len(copies)])
                copy.start()
                copies.append(copy)
    for copy in copies:
        copy.wait()


def reduce_kernel(devices, data, surface, cover):
    slot_rows = data.shape[0] // devices

    def rows_of(i):
        return data[pl.ds(i, devices, stride=slot_rows), :]

    width = LANES // CAP
    lines = rows_of(5 * CAP)
    named = (lines == (iota((devices, LANES), 1) % width).astype(F32)).astype(F32)
    to_rows, values = [], []
    for slot in range(CAP):
        to_rows.append(named[:, slot * width : slot * width + ATM_ROWS])
        parts = [rows_of(4 * slot + q) for q in range(4)] + [rows_of(4 * CAP + slot)]
        values.append(jnp.concatenate(parts, axis=1))
    rest = jnp.concatenate(values, axis=0)
    pieces = []
    for _ in range(3):
        piece = rest.astype(jnp.bfloat16)
        pieces.append(piece)
        rest = rest - piece.astype(F32)
    one = jnp.concatenate(to_rows, axis=0).astype(jnp.bfloat16)
    totals = lax.dot_general(
        jnp.concatenate([one] * 3, axis=0),
        jnp.concatenate(pieces, axis=0),
        (((0,), (0,)), ((), ())),
        preferred_element_type=F32,
    )
    ocean = totals[:, 4 * LANES :]
    cover[...] = ocean
    share = jnp.maximum(ocean, 1.0)
    for q in range(4):
        surface[q] = totals[:, q * LANES : (q + 1) * LANES] / share


def call(kernel, out_shape, limit=VMEM_LIMIT, **kwargs):
    return pl.pallas_call(
        kernel,
        out_shape=out_shape,
        compiler_params=pltpu.CompilerParams(vmem_limit_bytes=limit),
        **kwargs,
    )


def shaped(*shape, dtype=F32):
    return jax.ShapeDtypeStruct(shape, dtype)


def lat_swaps(lon_count, lat_count):
    swap_a, swap_b = [], []
    for i in range(lon_count):
        for a in range(lat_count):
            here = i * lat_count + a
            swap_a.append((here, i * lat_count + (a ^ 1)))
            if a == lat_count - 1:
                swap_b.append((here, (lon_count - 1 - i) * lat_count + a))
            elif a > 0:
                swap_b.append((here, here + 1 if a % 2 else here - 1))
    return swap_a, swap_b


def local(tracers, velocity, land_mask, mixing, owners, atm_row):
    levels = tracers.shape[1]
    rows, cols = land_mask.shape
    fields = 4 * levels
    lon_count, lat_count = lax.axis_size("lon"), lax.axis_size("lat")
    devices = lon_count * lat_count
    assert cols == LANES and rows % 8 == 0 and 2 * fields == LANES
    assert lon_count % 2 == 0 and lat_count % 2 == 0 and 3 * rows <= LANES
    length = 2 * fields + 8
    pitch = rows + 2 * PAD
    flat = 2 * levels * rows
    hbm = pl.BlockSpec(memory_space=pltpu.HBM)
    smem = pl.BlockSpec(memory_space=pltpu.SMEM)
    vmem = pl.BlockSpec(memory_space=pltpu.VMEM)

    deep = (2 * levels, rows, cols)
    lat_a, lat_b = call(
        functools.partial(edge_kernel, rows, fields),
        [pltpu.VMEM((length, cols), F32)] * 2,
        limit=VMEM_ALL,
        in_specs=[hbm] * 4,
        scratch_shapes=[
            pltpu.VMEM((2, fields, 8, cols), F32),
            pltpu.VMEM((rows, cols), jnp.int32),
            pltpu.VMEM((rows, cols), F32),
            pltpu.SemaphoreType.DMA((6,)),
        ],
    )(tracers.reshape(deep), velocity.reshape(deep), land_mask, mixing)
    swap_a, swap_b = lat_swaps(lon_count, lat_count)
    got_lat_b = lax.ppermute(lat_b, ("lon", "lat"), swap_b)
    got_lat_a = lax.ppermute(lat_a, ("lon", "lat"), swap_a)

    tr, ve = tracers.reshape(flat, cols), velocity.reshape(flat, cols)
    msg_a, msg_b = call(
        functools.partial(pack_kernel, rows, fields),
        [shaped(rows + 8, cols)] * 2,
        in_specs=[vmem] * 4,
    )(tr, ve, land_mask, mixing)

    slot_rows = 5 * CAP + 1
    state, base, col_map, row_map, outgoing, ids = call(
        functools.partial(prepare_kernel, rows, levels, devices),
        [
            shaped(fields * rows, cols),
            shaped(2 * rows + pitch, cols),
            shaped(3 * cols, cols),
            shaped(fields + levels, cols),
            shaped(devices * slot_rows, cols),
            shaped(8, cols, dtype=jnp.int32),
        ],
        in_specs=[vmem] * 4 + [smem] * 2,
        scratch_shapes=[pltpu.SMEM((devices,), jnp.int32)],
    )(tr, ve, land_mask, mixing, owners.reshape(rows), atm_row)

    def full(n):
        return pl.BlockSpec((n, cols), lambda i: (0, 0))

    tail = pl.BlockSpec((8, cols), lambda i: (rows // 8, 0))
    north, south, msg_a, msg_b = call(
        functools.partial(corner_kernel, lat_count, fields),
        [shaped(length, cols)] * 2 + [shaped(rows + 8, cols)] * 2,
        grid=(1,),
        in_specs=[full(length), full(length), tail, tail],
        out_specs=[full(length), full(length), tail, tail],
        input_output_aliases={2: 2, 3: 3},
    )(got_lat_b, got_lat_a, msg_a, msg_b)
    even_pairs = [(i, i ^ 1) for i in range(lon_count)]
    odd_pairs = [(i, (i + 1 if i % 2 else i - 1) % lon_count) for i in range(lon_count)]
    got_b = lax.ppermute(msg_b, "lon", even_pairs)
    got_a = lax.ppermute(msg_a, "lon", odd_pairs)

    count = min(3, levels)
    coefs, side, outgoing = call(
        functools.partial(surface_kernel, rows, levels),
        [
            shaped(len(COEFFICIENTS) * rows, cols),
            shaped(rows, cols),
            pltpu.VMEM((devices * slot_rows, cols), F32),
        ],
        scratch_shapes=[
            pltpu.VMEM((4 * count * pitch, cols), F32),
            pltpu.VMEM((4 * count * pitch, cols), F32),
            pltpu.VMEM((pitch, cols), F32),
            pltpu.VMEM((4 * rows, cols), F32),
            pltpu.SMEM((8, cols), jnp.int32),
            pltpu.SemaphoreType.DMA,
        ],
    )(state, base, msg_a, msg_b, got_a, got_b, north, south, outgoing, ids)
    incoming = lax.all_to_all(
        outgoing.reshape(devices, slot_rows, 1, cols),
        ("lon", "lat"),
        0,
        0,
        tiled=True,
    ).reshape(devices * slot_rows, cols)

    chunks = 4
    tr_out, ve_out = call(
        functools.partial(main_kernel, rows, levels, chunks),
        [shaped(flat, cols), shaped(flat, cols)],
        in_specs=[vmem] * 12,
        out_specs=[hbm] * 2,
        scratch_shapes=[
            pltpu.VMEM((fields * pitch, cols), F32),
            pltpu.VMEM((fields * pitch, cols), F32),
            pltpu.VMEM((rows, cols), F32),
            pltpu.VMEM((flat, cols), F32),
            pltpu.VMEM((flat, cols), F32),
            pltpu.SemaphoreType.DMA((4 * chunks,)),
        ],
        cost_estimate=pl.CostEstimate(
            flops=80 * fields * rows * cols, bytes_accessed=5 << 20, transcendentals=0
        ),
    )(state, base, msg_a, msg_b, got_a, got_b, north, south, col_map, row_map, coefs, side)
    surface, cover = call(
        functools.partial(reduce_kernel, devices),
        [shaped(4, ATM_ROWS, cols), shaped(ATM_ROWS, cols)],
    )(incoming)
    shape = (2, levels, rows, cols)
    return tr_out.reshape(shape), ve_out.reshape(shape), surface, cover


def solution(mesh):
    in_specs = (
        P(None, None, "lat", "lon"),
        P(None, None, "lat", "lon"),
        P("lat", "lon"),
        P("lat", "lon"),
        P(("lon", "lat"), None),
        P(("lon", "lat")),
    )
    out_specs = (
        P(None, None, "lat", "lon"),
        P(None, None, "lat", "lon"),
        P(None, ("lon", "lat"), None),
        P(("lon", "lat"), None),
    )
    return jax.shard_map(local, mesh=mesh, in_specs=in_specs, out_specs=out_specs, check_vma=False)
```
